32 devices in a mesh: dp: 8 (over y, x, core), tp: 4 (over z).
Axes of the slice: x: 2, y: 2, z: 4, core: 2. Of those that a mesh axis runs over, the one named last changes fastest.
Arguments:
- residual: bfloat16 [128, 7168], P(('dp', 'tp')), may hold values from -6 to 6
- queries: bfloat16 [128, 73728], P(('dp', 'tp')), may hold values from -240 to 240
- paged_latent_cache: bfloat16 [458752, 576], P(('dp', 'tp')), may hold values from -6 to 6
- lengths: int32 [128], replicated, may hold values from 1 to 14144, as said below
- w_uv: bfloat16 [128, 512, 128], P(('dp', 'tp')), may hold values from -1.5 to 1.5
- w_o: bfloat16 [16384, 7168], P('dp', 'tp'), may hold values from -0.046875 to 0.046875
- norm_gain: bfloat16 [7168], replicated, may hold values from 0.099609375 to 1.8984375
- w_gate: bfloat16 [7168, 18432], P('tp', 'dp'), may hold values from -0.0625 to 0.0625
- w_up: bfloat16 [7168, 18432], P('tp', 'dp'), may hold values from -0.0625 to 0.0625
- w_down: bfloat16 [18432, 7168], P('dp', 'tp'), may hold values from -0.125 to 0.125
Outputs:
- layer_out: bfloat16 [128, 7168], P(('dp', 'tp'))
The draws below stay inside these ranges and needn't reach their ends.
Inputs may be any that keep to these rules, and one draw needn't show every extreme that they name: `lengths`: requests are owned 4 after one another by the ranks in rank order. On every rank, the sum over its requests of ceil(length / 64) is at most 224, and it is exactly 224 on at least one rank. One request has exactly the largest length.
All inputs are finite; a program needn't handle non-finite values.
Results may differ from the reference program's by a relative error of at most 0.018.
Values may be sent and summed in bfloat16 or wider, within the bound.
No kernel may reach another device: no remote copies, remote signals or barrier semaphores. Data moves between devices by JAX's collectives and lax.ppermute only.
A program may use at most 192 MiB of HBM per device.

```python
import jax
import jax.numpy as jnp
from jax import lax

D = 7168
FF = 18432
H = 128
C = 512
RD = 64
VD = 128
BLOCK_TOKENS = 64
REQ_DEV = 4
CAPB = 224
REQUESTS = 128
POOL = 458752


def draw_queries(key, part):
    key = jax.random.fold_in(key, 11)
    base = jax.random.normal(key, (REQUESTS, H, C + RD), jnp.float32)
    base = jnp.clip(base, -240.0, 240.0)
    return base.reshape(REQUESTS, H * (C + RD)).astype(jnp.bfloat16)


def draw_lengths(key, part):
    key = jax.random.fold_in(key, 23)
    first, second, third, fourth = jax.random.split(key, 4)
    ranks = REQUESTS // REQ_DEV
    lowest = max(REQ_DEV, CAPB // 8)
    used = jax.random.randint(first, (ranks,), lowest, CAPB // 2 + 1, jnp.int32)
    fullest = jax.random.randint(second, (), 0, ranks, jnp.int32)
    is_full = jnp.arange(ranks, dtype=jnp.int32) == fullest
    used = jnp.where(is_full, CAPB, used)
    shares = jax.random.randint(third, (ranks, REQ_DEV), 1, 8, jnp.int32)
    extra = used - REQ_DEV
    split = extra[:, None] * shares // jnp.sum(shares, 1, keepdims=True)
    leftover = extra - jnp.sum(split, 1)
    is_first = jnp.arange(REQ_DEV, dtype=jnp.int32)[None, :] == 0
    split = split + jnp.where(is_first, leftover[:, None], 0)
    cache_blocks = 1 + split
    longest = jnp.where(is_first, CAPB - REQ_DEV + 1, 1)
    cache_blocks = jnp.where(is_full[:, None], longest, cache_blocks)
    cut = jax.random.randint(fourth, (ranks, REQ_DEV), 0, BLOCK_TOKENS, jnp.int32)
    cut = jnp.where(is_full[:, None] & is_first, 0, cut)
    return (cache_blocks * BLOCK_TOKENS - cut).reshape(REQUESTS).astype(jnp.int32)


def block_scale(key, extent, shards, least, top_value):
    factor_of, own = 1.0, jax.random.fold_in(key, 6)
    for axis_at, shards_of in shards:
        draws = jnp.exp(jax.random.uniform(jax.random.fold_in(own, axis_at), (shards_of,), jnp.float32, least / len(shards), top_value / len(shards)))
        factor_of = factor_of * jnp.repeat(draws, extent[axis_at] // shards_of).reshape([-1 if axis == axis_at else 1 for axis in range(len(extent))])
    return factor_of


def noise(rng, shape, scale, limit, shards=(), kind=jnp.bfloat16):
    result = jax.random.normal(rng, shape, jnp.float32) * scale
    if len(shards) > 0:
        result = block_scale(rng, shape, shards, -0.22, 0.18) * result
    return jnp.clip(result, min=-limit, max=limit).astype(kind)


def setup_inputs(seed: int = 0) -> dict:
    arg_keys = jax.random.split(jax.random.key(seed), 11)
    return {
        "residual": noise(arg_keys[0], (REQUESTS, D), 1.0, 6.0, ((0, 32),)),
        "queries": draw_queries(jax.random.fold_in(arg_keys[10], 71), 0),
        "paged_latent_cache": noise(arg_keys[2], (POOL, C + RD), 1.0, 6.0, ((0, 32),)),
        "lengths": draw_lengths(jax.random.fold_in(arg_keys[10], 71), 0),
        "w_uv": noise(arg_keys[4], (H, C, VD), (C // 32) ** -0.5, 1.5, ((0, 32),)),
        "w_o": noise(arg_keys[5], (H * VD, D), (H * VD) ** -0.5, 0.046875, ((0, 8), (1, 4))),
        "norm_gain": jnp.clip(1.0 + 0.18 * jax.random.normal(arg_keys[6], (D,), jnp.float32), 0.099609375, 1.8984375).astype(jnp.bfloat16),
        "w_gate": noise(arg_keys[7], (D, FF), D ** -0.5, 0.0625, ((0, 4), (1, 8))),
        "w_up": noise(arg_keys[8], (D, FF), D ** -0.5, 0.0625, ((0, 4), (1, 8))),
        "w_down": noise(arg_keys[9], (FF, D), (FF // 8) ** -0.5, 0.125, ((0, 8), (1, 4))),
    }


score_scale = 192.0 ** (-0.5)
negative = -1e+30
blocks_each_step = 8

def block_table(lens, count_blocks, width):
    nreq = lens.shape[0]
    need = ((lens + width - 1) // width).astype(jnp.int32)
    ends = jnp.cumsum(need).astype(jnp.int32)
    starts = (ends - need).astype(jnp.int32)
    index = jnp.arange(count_blocks, dtype=jnp.int32)[:, None]
    inside = (index >= starts[None, :]) & (index < ends[None, :])
    owners = jnp.arange(nreq, dtype=jnp.int32)[None, :]
    which = jnp.where(jnp.any(inside, 1), lax.optimization_barrier(jnp.sum(jnp.where(inside, owners, 0), 1)), -1).astype(jnp.int32)
    filled = jnp.clip(lens[None, :] - width * (index - starts[None, :]), 0, width)
    valid = lax.optimization_barrier(jnp.sum(jnp.where(inside, filled, 0), 1)).astype(jnp.int32)
    return (which, valid, ends[-1])

def attend(query_matrix, cache_blocks, which, valid, count):
    nreq = query_matrix.shape[0]
    width = cache_blocks.shape[1]
    row_length = cache_blocks.shape[2]
    query_heads = query_matrix.shape[1] // row_length
    init = (jnp.full((nreq, query_heads), negative, jnp.float32), jnp.zeros((nreq, query_heads), jnp.float32), jnp.zeros((nreq, query_heads, C), jnp.float32))

    def step(i, carry):
        best, total, acc = carry
        start = (i * blocks_each_step).astype(jnp.int32)
        part = lax.dynamic_slice_in_dim(cache_blocks, start, blocks_each_step, 0).astype(jnp.float32)
        owner = lax.dynamic_slice_in_dim(which, start, blocks_each_step, 0)
        filled = lax.dynamic_slice_in_dim(valid, start, blocks_each_step, 0)
        onehot = owner[:, None] == jnp.arange(nreq, dtype=jnp.int32)[None, :]
        selected_blocks = jnp.dot(onehot.astype(jnp.float32), query_matrix.astype(jnp.float32))
        selected_blocks = selected_blocks.reshape(blocks_each_step, query_heads, row_length)
        scores = jnp.einsum('ghc,gtc->ght', selected_blocks, part) * score_scale
        live = jnp.arange(width, dtype=jnp.int32)[None, :] < filled[:, None]
        scores = jnp.where(live[:, None, :], scores, negative)
        peak = lax.optimization_barrier(jnp.max(scores, 2))
        weights = jnp.exp(scores - peak[..., None])
        mass = lax.optimization_barrier(jnp.sum(weights, 2))
        rounded = lax.optimization_barrier(weights.astype(jnp.bfloat16)).astype(jnp.float32)
        values = jnp.einsum('ght,gtc->ghc', rounded, part[:, :, :C])
        mine = onehot[:, :, None]
        newbest = jnp.maximum(best, lax.optimization_barrier(jnp.max(jnp.where(mine, peak[:, None, :], negative), 0)))
        factor = jnp.where(mine, jnp.exp(peak[:, None, :] - newbest[None]), 0.0)
        keep = jnp.exp(best - newbest)
        total = total * keep + lax.optimization_barrier(jnp.sum(factor * mass[:, None, :], 0))
        acc = acc * keep[..., None] + jnp.einsum('grh,ghc->rhc', factor, values, precision=lax.Precision.HIGHEST)
        return (newbest, total, acc)
    steps = (count + blocks_each_step - 1) // blocks_each_step
    return lax.fori_loop(0, steps, step, init)

def finish(total, acc):
    return (acc / total[..., None]).astype(jnp.bfloat16)

def reference(residual, queries, paged_latent_cache, lengths, w_uv, w_o, norm_gain, w_gate, w_up, w_down):
    ranks = REQUESTS // REQ_DEV
    query_all = queries.reshape(ranks, REQ_DEV, H * (C + RD))
    pools = paged_latent_cache.reshape(ranks, CAPB, BLOCK_TOKENS, C + RD)
    lens_all = lengths.reshape(ranks, REQ_DEV)

    def one_rank(args):
        query_rank, pool_rank, lens_rank = args
        which, valid, used = block_table(lens_rank, CAPB, BLOCK_TOKENS)
        best, total, acc = attend(query_rank, pool_rank, which, valid, used)
        return finish(total, acc)
    latent_out = lax.map(one_rank, (query_all, pools, lens_all)).reshape(REQUESTS, H, C)
    head_values = jnp.einsum('rhc,hcv->rhv', latent_out.astype(jnp.float32), w_uv.astype(jnp.float32)).astype(jnp.bfloat16)
    attn = jnp.dot(head_values.reshape(REQUESTS, H * VD), w_o, preferred_element_type=jnp.float32)
    hidden = (residual.astype(jnp.float32) + attn).astype(jnp.bfloat16)
    hidden_f = hidden.astype(jnp.float32)
    normed = hidden_f * lax.rsqrt(lax.optimization_barrier(jnp.mean(hidden_f * hidden_f, 1, keepdims=True)) + 1e-06) * norm_gain.astype(jnp.float32)
    normed = normed.astype(jnp.bfloat16)
    gate = jnp.dot(normed, w_gate, preferred_element_type=jnp.float32)
    up = jnp.dot(normed, w_up, preferred_element_type=jnp.float32)
    inner = (jax.nn.silu(gate) * up).astype(jnp.bfloat16)
    ffn = jnp.dot(inner, w_down, preferred_element_type=jnp.float32)
    return (hidden_f + ffn).astype(jnp.bfloat16)
```

```python
import functools

import jax
import jax.numpy as jnp
from jax import lax
from jax.experimental import pallas as pl
from jax.experimental.pallas import tpu as pltpu
from jax.sharding import PartitionSpec as P

C = 512
BLOCK_TOKENS = 64
TILE = 1024
VMEM_BYTES = 48 * 1024 * 1024

score_scale = 192.0 ** (-0.5)
log2_e = 1.4426950408889634
negative = -1e30


def attention_kernel(
    lens_ref, q_ref, cache_ref, out_ref, held, score0, score1, acc, best, mass, lo, hi, first, last, sems
):
    nreq = q_ref.shape[0]
    tiles = held.shape[0]
    tile = held.shape[2]
    heads = q_ref.shape[1]

    begin = jnp.int32(0)
    pairs = jnp.int32(0)
    for r in range(nreq):
        length = lens_ref[r]
        lo[r] = begin
        hi[r] = begin + length
        first[r] = begin // tile
        last[r] = (begin + length - 1) // tile
        pairs = pairs + (last[r] - first[r] + 1)
        begin = begin + ((length + BLOCK_TOKENS - 1) // BLOCK_TOKENS) * BLOCK_TOKENS
    used = last[nreq - 1] + 1

    def copy(i):
        return pltpu.make_async_copy(
            cache_ref.at[:, pl.ds(pl.multiple_of(i * tile, tile), tile)], held.at[i], sems.at[i]
        )

    @pl.loop(0, used)
    def _(i):
        copy(i).start()

    def reset():
        acc[...] = jnp.zeros_like(acc)
        best[...] = jnp.full_like(best, negative)
        mass[...] = jnp.zeros_like(mass)

    def scores(r, i, live, target):
        begin_at = jnp.where(live, lo[r], 0)
        end_at = jnp.where(live, hi[r], 0)
        s = jnp.dot(q_ref[r], held[i], preferred_element_type=jnp.float32)
        token = i * tile + lax.broadcasted_iota(jnp.int32, (1, tile), 1)
        s = jnp.where((token >= begin_at) & (token < end_at), s, negative)
        target[...] = s

    def advance(p, r, i):
        ends = i == last[r]
        live = p + 1 < pairs
        nr = jnp.where(ends & live, r + 1, r)
        ni = jnp.where(ends, jnp.where(live, first[nr], i), i + 1)
        return nr, ni, live

    def fetch(i, r, live):
        fresh = live & ((r == 0) | (i > last[jnp.maximum(r - 1, 0)]))

        @pl.when(fresh)
        def _():
            copy(i).wait()

    def absorb(r, i, live, source):
        factor = score_scale * log2_e
        s = source[...]
        old = best[...]
        new = jnp.maximum(old, jnp.max(s, axis=1, keepdims=True))
        weight = jnp.exp2((s - new[:, :1]) * factor)
        keep = jnp.exp2((old - new) * factor)
        part = weight[:, :128]
        for at in range(128, tile, 128):
            part = part + weight[:, at : at + 128]
        mass[...] = mass[...] * keep + part
        best[...] = new
        values = lax.dot_general(
            weight.astype(jnp.bfloat16),
            held[i, :C, :],
            (((1,), (1,)), ((), ())),
            preferred_element_type=jnp.float32,
        )
        acc[...] = acc[...] * keep[:, :1] + values

    def close(r, i, live):
        @pl.when(live & (i == last[r]))
        def _():
            total = jnp.sum(mass[...], axis=1, keepdims=True)
            out_ref[r] = (acc[...] / total).astype(out_ref.dtype)
            reset()

    reset()
    fetch(jnp.int32(0), jnp.int32(0), pairs > 0)
    scores(jnp.int32(0), jnp.int32(0), pairs > 0, score0)

    def step(j, carry):
        r, i, live = carry
        p = 2 * j
        for now, later in ((score0, score1), (score1, score0)):
            nr, ni, nlive = advance(p, r, i)
            fetch(ni, nr, nlive)
            scores(nr, ni, nlive, later)
            absorb(r, i, live, now)
            close(r, i, live)
            r, i, live, p = nr, ni, nlive, p + 1
        return r, i, live

    lax.fori_loop(0, (pairs + 1) // 2, step, (jnp.int32(0), jnp.int32(0), pairs > 0))


def attend(own_lens, queries, cache_t):
    nreq, heads, width = queries.shape
    tokens = cache_t.shape[1]
    tile = TILE
    tiles = tokens // tile
    return pl.pallas_call(
        attention_kernel,
        out_shape=jax.ShapeDtypeStruct((nreq, heads, C), jnp.bfloat16),
        in_specs=[
            pl.BlockSpec(memory_space=pltpu.SMEM),
            pl.BlockSpec(memory_space=pltpu.VMEM),
            pl.BlockSpec(memory_space=pl.ANY),
        ],
        out_specs=pl.BlockSpec(memory_space=pltpu.VMEM),
        scratch_shapes=[
            pltpu.VMEM((tiles, width, tile), jnp.bfloat16),
            pltpu.VMEM((heads, tile), jnp.float32),
            pltpu.VMEM((heads, tile), jnp.float32),
            pltpu.VMEM((heads, C), jnp.float32),
            pltpu.VMEM((heads, 128), jnp.float32),
            pltpu.VMEM((heads, 128), jnp.float32),
            pltpu.SMEM((nreq,), jnp.int32),
            pltpu.SMEM((nreq,), jnp.int32),
            pltpu.SMEM((nreq,), jnp.int32),
            pltpu.SMEM((nreq,), jnp.int32),
            pltpu.SemaphoreType.DMA((tiles,)),
        ],
        compiler_params=pltpu.CompilerParams(vmem_limit_bytes=VMEM_BYTES),
        cost_estimate=pl.CostEstimate(
            flops=2 * heads * tokens * (width + C),
            bytes_accessed=2 * tokens * width,
            transcendentals=heads * tokens,
        ),
        name="attention",
    )(own_lens, queries, cache_t)


def exchange_columns(rows, axis):
    size = lax.axis_size(axis)
    me = lax.axis_index(axis)
    width = rows.shape[1] // size
    slices = rows.reshape(rows.shape[0], size, width)
    out = jnp.zeros((size, rows.shape[0], width), rows.dtype)
    own = lax.dynamic_index_in_dim(slices, me, 1, keepdims=False)
    out = lax.dynamic_update_index_in_dim(out, own, me, 0)
    for shift in range(1, size):
        piece = lax.dynamic_index_in_dim(slices, (me + shift) % size, 1, keepdims=False)
        got = lax.ppermute(piece, axis, [(k, (k + shift) % size) for k in range(size)])
        out = lax.dynamic_update_index_in_dim(out, got, (me - shift) % size, 0)
    return out


def scatter_sum(part, axis):
    size = lax.axis_size(axis)
    pieces = part.reshape(size, part.shape[0] // size, part.shape[1])
    pieces = lax.all_to_all(pieces, axis, split_axis=0, concat_axis=0, tiled=True)
    return jnp.sum(pieces.astype(jnp.float32), 0)


def local(
    residual, queries, paged_latent_cache, lengths, w_uv, w_o, norm_gain, w_gate, w_up, w_down
):
    ranks_dp = lax.axis_size("dp")
    ranks_tp = lax.axis_size("tp")
    me_dp = lax.axis_index("dp")
    me_tp = lax.axis_index("tp")
    per_rank, model = residual.shape
    row_length = paged_latent_cache.shape[1]
    heads_all = queries.shape[1] // row_length
    heads_here = w_uv.shape[0]
    units = w_gate.shape[1]
    width = w_o.shape[1]
    rank = me_dp * ranks_tp + me_tp

    residual_slice = exchange_columns(residual, "tp").reshape(ranks_tp * per_rank, width)
    gain_slice = lax.dynamic_slice_in_dim(norm_gain, me_tp * width, width, 0)

    own_lens = lax.dynamic_slice_in_dim(lengths, rank * per_rank, per_rank, 0)
    query = queries.reshape(per_rank, heads_all, row_length)
    latent_out = attend(own_lens, query, paged_latent_cache.T)

    local_heads = lax.all_to_all(latent_out, ("dp", "tp"), split_axis=1, concat_axis=0, tiled=True)
    head_values = jnp.einsum("rhc,hcv->rhv", local_heads, w_uv, preferred_element_type=jnp.float32)
    head_values = head_values.astype(jnp.bfloat16)
    flat_values = head_values.reshape(head_values.shape[0], heads_here * w_uv.shape[2])
    group_values = lax.all_gather(flat_values, "tp", axis=1, tiled=True)
    attn_part = jnp.dot(group_values, w_o, preferred_element_type=jnp.float32).astype(jnp.bfloat16)
    attn = scatter_sum(attn_part, "dp")

    hidden = (residual_slice.astype(jnp.float32) + attn).astype(jnp.bfloat16)
    piece = lax.all_gather(hidden, "dp", axis=0, tiled=True).astype(jnp.float32)
    square = jnp.sum(piece * piece, 1, keepdims=True)
    scaled = (piece * gain_slice.astype(jnp.float32)).astype(jnp.bfloat16)
    gate_part = jnp.dot(scaled, w_gate, preferred_element_type=jnp.float32).astype(jnp.bfloat16)
    up_part = jnp.dot(scaled, w_up, preferred_element_type=jnp.float32).astype(jnp.bfloat16)
    top = square.astype(jnp.bfloat16)
    rest = square - top.astype(jnp.float32)
    middle = rest.astype(jnp.bfloat16)
    low = (rest - middle.astype(jnp.float32)).astype(jnp.bfloat16)
    extra = jnp.concatenate(
        [top, middle, low, jnp.zeros((top.shape[0], 125), jnp.bfloat16)], 1
    )
    both = scatter_sum(jnp.concatenate([gate_part, up_part, extra], 1), "tp")
    mean = jnp.sum(both[:, 2 * units :], 1, keepdims=True) / model
    factor = lax.rsqrt(mean + 1e-06)
    gate = both[:, :units] * factor
    up = both[:, units : 2 * units] * factor
    inner = (jax.nn.silu(gate) * up).astype(jnp.bfloat16)
    inner = lax.all_gather(inner, "tp", axis=0, tiled=True)
    ffn_part = jnp.dot(inner, w_down, preferred_element_type=jnp.float32).astype(jnp.bfloat16)
    ffn = scatter_sum(ffn_part, "dp")
    layer = (hidden.astype(jnp.float32) + ffn).astype(jnp.bfloat16)
    return lax.all_to_all(layer, "tp", split_axis=0, concat_axis=1, tiled=True)


def solution(mesh):
    placed = (
        P(("dp", "tp"), None),
        P(("dp", "tp"), None),
        P(("dp", "tp"), None),
        P(),
        P(("dp", "tp"), None, None),
        P("dp", "tp"),
        P(),
        P("tp", "dp"),
        P("tp", "dp"),
        P("dp", "tp"),
    )
    return jax.shard_map(
        local, mesh=mesh, in_specs=placed, out_specs=P(("dp", "tp"), None), check_vma=False
    )
```

```python
import jax
import jax.numpy as jnp
from jax import lax
from jax.experimental import pallas as pl
from jax.experimental.pallas import tpu as pltpu
from jax.sharding import PartitionSpec as P

C = 512
BLOCK_TOKENS = 64
TILE = 1024
CHUNKS = 2
VMEM_BYTES = 48 * 1024 * 1024

score_scale = 192.0 ** (-0.5)
log2_e = 1.4426950408889634
negative = -1e30


def attention_kernel(
    lens_ref, q_ref, cache_ref, out_ref, held, score0, score1, acc, best, mass, lo, hi, first, last, sems
):
    nreq = q_ref.shape[0]
    tiles = held.shape[0]
    tile = held.shape[2]
    heads = q_ref.shape[1]

    rank = lax.axis_index("dp") * lax.axis_size("tp") + lax.axis_index("tp")
    begin = jnp.int32(0)
    pairs = jnp.int32(0)
    for r in range(nreq):
        length = lens_ref[rank * nreq + r]
        lo[r] = begin
        hi[r] = begin + length
        first[r] = begin // tile
        last[r] = (begin + length - 1) // tile
        pairs = pairs + (last[r] - first[r] + 1)
        begin = begin + ((length + BLOCK_TOKENS - 1) // BLOCK_TOKENS) * BLOCK_TOKENS
    used = last[nreq - 1] + 1

    def copy(i):
        return pltpu.make_async_copy(
            cache_ref.at[:, pl.ds(pl.multiple_of(i * tile, tile), tile)], held.at[i], sems.at[i]
        )

    @pl.loop(0, used)
    def _(i):
        copy(i).start()

    def reset():
        acc[...] = jnp.zeros_like(acc)
        best[...] = jnp.full_like(best, negative)
        mass[...] = jnp.zeros_like(mass)

    def scores(r, i, live, target):
        begin_at = jnp.where(live, lo[r], 0)
        end_at = jnp.where(live, hi[r], 0)
        s = jnp.dot(q_ref[r], held[i], preferred_element_type=jnp.float32)
        token = i * tile + lax.broadcasted_iota(jnp.int32, (1, tile), 1)
        s = jnp.where((token >= begin_at) & (token < end_at), s, negative)
        target[...] = s

    def advance(p, r, i):
        ends = i == last[r]
        live = p + 1 < pairs
        nr = jnp.where(ends & live, r + 1, r)
        ni = jnp.where(ends, jnp.where(live, first[nr], i), i + 1)
        return nr, ni, live

    def fetch(i, r, live):
        fresh = live & ((r == 0) | (i > last[jnp.maximum(r - 1, 0)]))

        @pl.when(fresh)
        def _():
            copy(i).wait()

    def absorb(r, i, live, source):
        factor = score_scale * log2_e
        s = source[...]
        old = best[...]
        new = jnp.maximum(old, jnp.max(s, axis=1, keepdims=True))
        weight = jnp.exp2((s - new[:, :1]) * factor)
        keep = jnp.exp2((old - new) * factor)
        part = weight[:, :128]
        for at in range(128, tile, 128):
            part = part + weight[:, at : at + 128]
        mass[...] = mass[...] * keep + part
        best[...] = new
        values = lax.dot_general(
            weight.astype(jnp.bfloat16),
            held[i, :C, :],
            (((1,), (1,)), ((), ())),
            preferred_element_type=jnp.float32,
        )
        acc[...] = acc[...] * keep[:, :1] + values

    def close(r, i, live):
        @pl.when(live & (i == last[r]))
        def _():
            total = jnp.sum(mass[...], axis=1, keepdims=True)
            out_ref[r] = (acc[...] / total).astype(out_ref.dtype)
            reset()

    reset()
    fetch(jnp.int32(0), jnp.int32(0), pairs > 0)
    scores(jnp.int32(0), jnp.int32(0), pairs > 0, score0)

    def step(j, carry):
        r, i, live = carry
        p = 2 * j
        for now, later in ((score0, score1), (score1, score0)):
            nr, ni, nlive = advance(p, r, i)
            fetch(ni, nr, nlive)
            scores(nr, ni, nlive, later)
            absorb(r, i, live, now)
            close(r, i, live)
            r, i, live, p = nr, ni, nlive, p + 1
        return r, i, live

    lax.fori_loop(0, (pairs + 1) // 2, step, (jnp.int32(0), jnp.int32(0), pairs > 0))


def attend(lengths, queries, cache_t):
    nreq, heads, width = queries.shape
    tokens = cache_t.shape[1]
    tile = TILE
    tiles = tokens // tile
    return pl.pallas_call(
        attention_kernel,
        out_shape=jax.ShapeDtypeStruct((nreq, heads, C), jnp.bfloat16),
        in_specs=[
            pl.BlockSpec(memory_space=pltpu.SMEM),
            pl.BlockSpec(memory_space=pltpu.VMEM),
            pl.BlockSpec(memory_space=pl.ANY),
        ],
        out_specs=pl.BlockSpec(memory_space=pltpu.VMEM),
        scratch_shapes=[
            pltpu.VMEM((tiles, width, tile), jnp.bfloat16),
            pltpu.VMEM((heads, tile), jnp.float32),
            pltpu.VMEM((heads, tile), jnp.float32),
            pltpu.VMEM((heads, C), jnp.float32),
            pltpu.VMEM((heads, 128), jnp.float32),
            pltpu.VMEM((heads, 128), jnp.float32),
            pltpu.SMEM((nreq,), jnp.int32),
            pltpu.SMEM((nreq,), jnp.int32),
            pltpu.SMEM((nreq,), jnp.int32),
            pltpu.SMEM((nreq,), jnp.int32),
            pltpu.SemaphoreType.DMA((tiles,)),
        ],
        compiler_params=pltpu.CompilerParams(vmem_limit_bytes=VMEM_BYTES),
        cost_estimate=pl.CostEstimate(
            flops=2 * heads * tokens * (width + C),
            bytes_accessed=2 * tokens * width,
            transcendentals=heads * tokens,
        ),
        name="attention",
    )(lengths, queries, cache_t)


def dynamic_piece(pieces, at):
    return lax.dynamic_index_in_dim(pieces, at, 0, keepdims=False)


def exchange(pieces, axis):
    size = lax.axis_size(axis)
    me = lax.axis_index(axis)
    got = [dynamic_piece(pieces, me)]
    for shift in range(1, size):
        piece = dynamic_piece(pieces, (me + shift) % size)
        got.append(lax.ppermute(piece, axis, [(k, (k + shift) % size) for k in range(size)]))
    return got


def ordered(got, axis):
    size = lax.axis_size(axis)
    me = lax.axis_index(axis)
    out = jnp.zeros((size,) + got[0].shape, got[0].dtype)
    for shift, piece in enumerate(got):
        out = lax.dynamic_update_index_in_dim(out, piece, (me - shift) % size, 0)
    return out


def gather(piece, axis):
    size = lax.axis_size(axis)
    return [piece] + [
        lax.ppermute(piece, axis, [(k, (k + shift) % size) for k in range(size)])
        for shift in range(1, size)
    ]


def scatter_sum(part, axis):
    size = lax.axis_size(axis)
    pieces = part.reshape(size, part.shape[0] // size, part.shape[1])
    pieces = lax.all_to_all(pieces, axis, split_axis=0, concat_axis=0, tiled=True)
    return jnp.sum(pieces.astype(jnp.float32), 0)


def local(
    residual, queries, paged_latent_cache, lengths, w_uv, w_o, norm_gain, w_gate, w_up, w_down
):
    ranks_dp = lax.axis_size("dp")
    ranks_tp = lax.axis_size("tp")
    me_tp = lax.axis_index("tp")
    per_rank, model = residual.shape
    row_length = paged_latent_cache.shape[1]
    heads_all = queries.shape[1] // row_length
    heads_here = w_uv.shape[0]
    units = w_gate.shape[1]
    width = w_o.shape[1]

    query = queries.reshape(per_rank, heads_all, row_length)
    latent_out = attend(lengths, query, paged_latent_cache.T)

    local_heads = lax.all_to_all(latent_out, ("dp", "tp"), split_axis=1, concat_axis=0, tiled=True)
    local_heads, residual = lax.optimization_barrier((local_heads, residual))
    head_values = jnp.einsum("rhc,hcv->rhv", local_heads, w_uv, preferred_element_type=jnp.float32)
    head_values = head_values.astype(jnp.bfloat16)
    flat_values = head_values.reshape(head_values.shape[0], heads_here * w_uv.shape[2])
    depth = flat_values.shape[1]
    attn_part = None
    for shift, values in enumerate(gather(flat_values, "tp")):
        rows = lax.dynamic_slice_in_dim(w_o, ((me_tp - shift) % ranks_tp) * depth, depth, 0)
        term = jnp.dot(values, rows, preferred_element_type=jnp.float32)
        attn_part = term if attn_part is None else attn_part + term
    residual_pieces = residual.reshape(per_rank, ranks_tp, width).transpose(1, 0, 2)
    residual_slice = ordered(exchange(residual_pieces, "tp"), "tp").reshape(-1, width)
    attn = scatter_sum(attn_part.astype(jnp.bfloat16), "dp")

    hidden = (residual_slice.astype(jnp.float32) + attn).astype(jnp.bfloat16)
    hidden_got = exchange(hidden.reshape(ranks_tp, per_rank, width), "tp")
    gain_slice = lax.dynamic_slice_in_dim(norm_gain, me_tp * width, width, 0)
    piece = lax.all_gather(hidden, "dp", axis=0, tiled=True).astype(jnp.float32)
    square = jnp.sum(piece * piece, 1, keepdims=True)
    scaled = (piece * gain_slice.astype(jnp.float32)).astype(jnp.bfloat16)
    top = square.astype(jnp.bfloat16)
    rest = square - top.astype(jnp.float32)
    middle = rest.astype(jnp.bfloat16)
    low = (rest - middle.astype(jnp.float32)).astype(jnp.bfloat16)
    extra = jnp.concatenate([top, middle, low, jnp.zeros((top.shape[0], 125), jnp.bfloat16)], 1)

    chunk = units // CHUNKS
    factor = None
    sums = []
    for c in range(CHUNKS):
        columns = slice(c * chunk, (c + 1) * chunk)
        parts = [
            jnp.dot(scaled, w[:, columns], preferred_element_type=jnp.float32).astype(jnp.bfloat16)
            for w in (w_gate, w_up)
        ]
        if c == 0:
            parts.append(extra)
        both = jnp.concatenate(parts, 1).reshape(ranks_tp, -1, 2 * chunk + 128 * (c == 0))
        sums.append(sum(got.astype(jnp.float32) for got in exchange(both, "tp")))
    ffn_part = None
    for c, both in enumerate(sums):
        if c == 0:
            mean = jnp.sum(both[:, 2 * chunk :], 1, keepdims=True) / model
            factor = lax.rsqrt(mean + 1e-06)
        gate = both[:, :chunk] * factor
        up = both[:, chunk : 2 * chunk] * factor
        inner = (jax.nn.silu(gate) * up).astype(jnp.bfloat16)
        inner = ordered(gather(inner, "tp"), "tp").reshape(-1, chunk)
        term = jnp.dot(
            inner, w_down[c * chunk : (c + 1) * chunk], preferred_element_type=jnp.float32
        )
        ffn_part = term if ffn_part is None else ffn_part + term
    ffn_pieces = ffn_part.astype(jnp.bfloat16).reshape(ranks_dp * ranks_tp, per_rank, width)
    ffn_pieces = lax.all_to_all(
        ffn_pieces, ("dp", "tp"), split_axis=0, concat_axis=0, tiled=True
    )
    ffn = jnp.sum(ffn_pieces.astype(jnp.float32).reshape(ranks_dp, ranks_tp, per_rank, width), 0)
    layer = ordered(hidden_got, "tp").astype(jnp.float32) + ffn
    return layer.astype(jnp.bfloat16).transpose(1, 0, 2).reshape(per_rank, model)


def solution(mesh):
    placed = (
        P(("dp", "tp"), None),
        P(("dp", "tp"), None),
        P(("dp", "tp"), None),
        P(),
        P(("dp", "tp"), None, None),
        P("dp", "tp"),
        P(),
        P("tp", "dp"),
        P("tp", "dp"),
        P("dp", "tp"),
    )
    return jax.shard_map(
        local, mesh=mesh, in_specs=placed, out_specs=P(("dp", "tp"), None), check_vma=False
    )
```

```python
import jax
import jax.numpy as jnp
from jax import lax
from jax.experimental import pallas as pl
from jax.experimental.pallas import tpu as pltpu
from jax.sharding import PartitionSpec as P

C = 512
BLOCK_TOKENS = 64
TILE = 1024
CHUNKS = 2
VMEM_BYTES = 24 * 1024 * 1024

score_scale = 192.0 ** (-0.5)
log2_e = 1.4426950408889634
negative = -1e30


def attention_kernel(
    lens_ref,
    q_ref,
    cache_ref,
    *refs,
):
    weights = (len(refs) - 12) // 2
    sources, (out_ref, *staged) = refs[:weights], refs[weights : 2 * weights + 1]
    held, score0, score1, acc, best, mass, lo, hi, first, last, sems = refs[2 * weights + 1 :]
    nreq = q_ref.shape[0]
    tiles = held.shape[0]
    tile = held.shape[2]
    heads = q_ref.shape[1]

    rank = lax.axis_index("dp") * lax.axis_size("tp") + lax.axis_index("tp")
    begin = jnp.int32(0)
    pairs = jnp.int32(0)
    for r in range(nreq):
        length = lens_ref[rank * nreq + r]
        lo[r] = begin
        hi[r] = begin + length
        first[r] = begin // tile
        last[r] = (begin + length - 1) // tile
        pairs = pairs + (last[r] - first[r] + 1)
        begin = begin + ((length + BLOCK_TOKENS - 1) // BLOCK_TOKENS) * BLOCK_TOKENS
    used = last[nreq - 1] + 1

    def copy(i):
        return pltpu.make_async_copy(
            cache_ref.at[:, pl.ds(pl.multiple_of(i * tile, tile), tile)], held.at[i], sems.at[i]
        )

    @pl.loop(0, used)
    def _(i):
        copy(i).start()

    copies = [
        pltpu.make_async_copy(source, target, sems.at[tiles + k])
        for k, (source, target) in enumerate(zip(sources, staged))
    ]
    for each in copies:
        each.start()

    def reset():
        acc[...] = jnp.zeros_like(acc)
        best[...] = jnp.full_like(best, negative)
        mass[...] = jnp.zeros_like(mass)

    def scores(r, i, live, target):
        begin_at = jnp.where(live, lo[r], 0)
        end_at = jnp.where(live, hi[r], 0)
        s = jnp.dot(q_ref[r], held[i], preferred_element_type=jnp.float32)
        token = i * tile + lax.broadcasted_iota(jnp.int32, (1, tile), 1)
        s = jnp.where((token >= begin_at) & (token < end_at), s, negative)
        target[...] = s

    def advance(p, r, i):
        ends = i == last[r]
        live = p + 1 < pairs
        nr = jnp.where(ends & live, r + 1, r)
        ni = jnp.where(ends, jnp.where(live, first[nr], i), i + 1)
        return nr, ni, live

    def fetch(i, r, live):
        fresh = live & ((r == 0) | (i > last[jnp.maximum(r - 1, 0)]))

        @pl.when(fresh)
        def _():
            copy(i).wait()

    def absorb(r, i, live, source):
        factor = score_scale * log2_e
        s = source[...]
        old = best[...]
        new = jnp.maximum(old, jnp.max(s, axis=1, keepdims=True))
        weight = jnp.exp2((s - new[:, :1]) * factor)
        keep = jnp.exp2((old - new) * factor)
        part = weight[:, :128]
        for at in range(128, tile, 128):
            part = part + weight[:, at : at + 128]
        mass[...] = mass[...] * keep + part
        best[...] = new
        values = lax.dot_general(
            held[i, :C, :],
            weight.astype(jnp.bfloat16),
            (((1,), (1,)), ((), ())),
            preferred_element_type=jnp.float32,
        )
        acc[...] = acc[...] * keep.T[:1, :] + values

    def close(r, i, live):
        @pl.when(live & (i == last[r]))
        def _():
            total = jnp.sum(mass[...], axis=1, keepdims=True)
            out_ref[r] = (acc[...].T / total).astype(out_ref.dtype)
            reset()

    reset()
    fetch(jnp.int32(0), jnp.int32(0), pairs > 0)
    scores(jnp.int32(0), jnp.int32(0), pairs > 0, score0)

    def step(j, carry):
        r, i, live = carry
        p = 2 * j
        for now, later in ((score0, score1), (score1, score0)):
            nr, ni, nlive = advance(p, r, i)
            fetch(ni, nr, nlive)
            scores(nr, ni, nlive, later)
            absorb(r, i, live, now)
            close(r, i, live)
            r, i, live, p = nr, ni, nlive, p + 1
        return r, i, live

    lax.fori_loop(0, (pairs + 1) // 2, step, (jnp.int32(0), jnp.int32(0), pairs > 0))
    for each in copies:
        each.wait()


def attend(lengths, queries, cache_t, *weights):
    nreq, heads, width = queries.shape
    tokens = cache_t.shape[1]
    tile = TILE
    tiles = tokens // tile
    return pl.pallas_call(
        attention_kernel,
        out_shape=[jax.ShapeDtypeStruct((nreq, heads, C), jnp.bfloat16)]
        + [pltpu.VMEM(w.shape, w.dtype) for w in weights],
        in_specs=[
            pl.BlockSpec(memory_space=pltpu.SMEM),
            pl.BlockSpec(memory_space=pltpu.VMEM),
        ]
        + [pl.BlockSpec(memory_space=pl.ANY)] * (1 + len(weights)),
        out_specs=[pl.BlockSpec(memory_space=pltpu.VMEM)] * (1 + len(weights)),
        scratch_shapes=[
            pltpu.VMEM((tiles, width, tile), jnp.bfloat16),
            pltpu.VMEM((heads, tile), jnp.float32),
            pltpu.VMEM((heads, tile), jnp.float32),
            pltpu.VMEM((C, heads), jnp.float32),
            pltpu.VMEM((heads, 128), jnp.float32),
            pltpu.VMEM((heads, 128), jnp.float32),
            pltpu.SMEM((nreq,), jnp.int32),
            pltpu.SMEM((nreq,), jnp.int32),
            pltpu.SMEM((nreq,), jnp.int32),
            pltpu.SMEM((nreq,), jnp.int32),
            pltpu.SemaphoreType.DMA((tiles + len(weights),)),
        ],
        compiler_params=pltpu.CompilerParams(vmem_limit_bytes=VMEM_BYTES),
        cost_estimate=pl.CostEstimate(
            flops=2 * heads * tokens * (width + C),
            bytes_accessed=2 * tokens * width + sum(2 * w.size for w in weights),
            transcendentals=heads * tokens,
        ),
        name="attention",
    )(lengths, queries, cache_t, *weights)


def dynamic_piece(pieces, at):
    return lax.dynamic_index_in_dim(pieces, at, 0, keepdims=False)


def exchange(pieces, axis):
    size = lax.axis_size(axis)
    me = lax.axis_index(axis)
    got = [dynamic_piece(pieces, me)]
    for shift in range(1, size):
        piece = dynamic_piece(pieces, (me + shift) % size)
        got.append(lax.ppermute(piece, axis, [(k, (k + shift) % size) for k in range(size)]))
    return got


def ordered(got, axis):
    size = lax.axis_size(axis)
    me = lax.axis_index(axis)
    out = jnp.zeros((size,) + got[0].shape, got[0].dtype)
    for shift, piece in enumerate(got):
        out = lax.dynamic_update_index_in_dim(out, piece, (me - shift) % size, 0)
    return out


def gather(piece, axis):
    size = lax.axis_size(axis)
    return [piece] + [
        lax.ppermute(piece, axis, [(k, (k + shift) % size) for k in range(size)])
        for shift in range(1, size)
    ]


def scatter_sum(part, axis):
    size = lax.axis_size(axis)
    pieces = part.reshape(size, part.shape[0] // size, part.shape[1])
    pieces = lax.all_to_all(pieces, axis, split_axis=0, concat_axis=0, tiled=True)
    return jnp.sum(pieces.astype(jnp.float32), 0)


def local(
    residual, queries, paged_latent_cache, lengths, w_uv, w_o, norm_gain, w_gate, w_up, w_down
):
    ranks_dp = lax.axis_size("dp")
    ranks_tp = lax.axis_size("tp")
    me_tp = lax.axis_index("tp")
    per_rank, model = residual.shape
    row_length = paged_latent_cache.shape[1]
    heads_all = queries.shape[1] // row_length
    heads_here = w_uv.shape[0]
    units = w_gate.shape[1]
    width = w_o.shape[1]

    query = queries.reshape(per_rank, heads_all, row_length)
    latent_out, w_o, w_gate, w_up, w_down = attend(
        lengths, query, paged_latent_cache.T, w_o, w_gate, w_up, w_down
    )

    local_heads = lax.all_to_all(latent_out, ("dp", "tp"), split_axis=1, concat_axis=0, tiled=True)
    local_heads, residual = lax.optimization_barrier((local_heads, residual))
    head_values = jnp.einsum("rhc,hcv->rhv", local_heads, w_uv, preferred_element_type=jnp.float32)
    head_values = head_values.astype(jnp.bfloat16)
    flat_values = head_values.reshape(head_values.shape[0], heads_here * w_uv.shape[2])
    depth = flat_values.shape[1]
    attn_part = None
    for shift, values in enumerate(gather(flat_values, "tp")):
        rows = lax.dynamic_slice_in_dim(w_o, ((me_tp - shift) % ranks_tp) * depth, depth, 0)
        term = jnp.dot(values, rows, preferred_element_type=jnp.float32)
        attn_part = term if attn_part is None else attn_part + term
    residual_pieces = residual.reshape(per_rank, ranks_tp, width).transpose(1, 0, 2)
    residual_slice = ordered(exchange(residual_pieces, "tp"), "tp").reshape(-1, width)
    attn = scatter_sum(attn_part.astype(jnp.bfloat16), "dp")

    hidden = (residual_slice.astype(jnp.float32) + attn).astype(jnp.bfloat16)
    hidden_got = exchange(hidden.reshape(ranks_tp, per_rank, width), "tp")
    gain_slice = lax.dynamic_slice_in_dim(norm_gain, me_tp * width, width, 0)
    piece = lax.all_gather(hidden, "dp", axis=0, tiled=True).astype(jnp.float32)
    square = jnp.sum(piece * piece, 1, keepdims=True)
    scaled = (piece * gain_slice.astype(jnp.float32)).astype(jnp.bfloat16)
    top = square.astype(jnp.bfloat16)
    rest = square - top.astype(jnp.float32)
    middle = rest.astype(jnp.bfloat16)
    low = (rest - middle.astype(jnp.float32)).astype(jnp.bfloat16)
    extra = jnp.concatenate([top, middle, low, jnp.zeros((top.shape[0], 125), jnp.bfloat16)], 1)

    chunk = units // CHUNKS
    factor = None
    sums = []
    for c in range(CHUNKS):
        columns = slice(c * chunk, (c + 1) * chunk)
        parts = [
            jnp.dot(scaled, w[:, columns], preferred_element_type=jnp.float32).astype(jnp.bfloat16)
            for w in (w_gate, w_up)
        ]
        if c == 0:
            parts.append(extra)
        sums.append(scatter_sum(jnp.concatenate(parts, 1), "tp"))
    ffn_part = None
    for c, both in enumerate(sums):
        if c == 0:
            mean = jnp.sum(both[:, 2 * chunk :], 1, keepdims=True) / model
            factor = lax.rsqrt(mean + 1e-06)
        gate = both[:, :chunk] * factor
        up = both[:, chunk : 2 * chunk] * factor
        inner = (jax.nn.silu(gate) * up).astype(jnp.bfloat16)
        inner = ordered(gather(inner, "tp"), "tp").reshape(-1, chunk)
        term = jnp.dot(
            inner, w_down[c * chunk : (c + 1) * chunk], preferred_element_type=jnp.float32
        )
        ffn_part = term if ffn_part is None else ffn_part + term
    ffn_pieces = ffn_part.astype(jnp.bfloat16).reshape(ranks_dp * ranks_tp, per_rank, width)
    ffn_pieces = lax.all_to_all(
        ffn_pieces, ("dp", "tp"), split_axis=0, concat_axis=0, tiled=True
    )
    ffn = jnp.sum(ffn_pieces.astype(jnp.float32).reshape(ranks_dp, ranks_tp, per_rank, width), 0)
    layer = ordered(hidden_got, "tp").astype(jnp.float32) + ffn
    return layer.astype(jnp.bfloat16).transpose(1, 0, 2).reshape(per_rank, model)


def solution(mesh):
    placed = (
        P(("dp", "tp"), None),
        P(("dp", "tp"), None),
        P(("dp", "tp"), None),
        P(),
        P(("dp", "tp"), None, None),
        P("dp", "tp"),
        P(),
        P("tp", "dp"),
        P("tp", "dp"),
        P("dp", "tp"),
    )
    return jax.shard_map(
        local, mesh=mesh, in_specs=placed, out_specs=P(("dp", "tp"), None), check_vma=False
    )
```

```python
import functools

import jax
import jax.numpy as jnp
from jax import lax
from jax.experimental import pallas as pl
from jax.experimental.pallas import tpu as pltpu
from jax.sharding import PartitionSpec as P

C = 512
BLOCK_TOKENS = 64
TILE = 1024

score_scale = 192.0 ** (-0.5)
log2_e = 1.4426950408889634
negative = -1e30


def attention_kernel(
    lens_ref,
    q_ref,
    cache_ref,
    out_ref,
    held,
    score0,
    score1,
    acc,
    done,
    best,
    mass,
    lo,
    hi,
    first,
    last,
    sems,
):
    nreq = q_ref.shape[0]
    tiles = held.shape[0]
    tile = held.shape[2]
    heads = q_ref.shape[1]

    rank = lax.axis_index("dp") * lax.axis_size("tp") + lax.axis_index("tp")
    begin = jnp.int32(0)
    pairs = jnp.int32(0)
    for r in range(nreq):
        length = lens_ref[rank * nreq + r]
        lo[r] = begin
        hi[r] = begin + length
        first[r] = begin // tile
        last[r] = (begin + length - 1) // tile
        pairs = pairs + (last[r] - first[r] + 1)
        begin = begin + ((length + BLOCK_TOKENS - 1) // BLOCK_TOKENS) * BLOCK_TOKENS
    used = last[nreq - 1] + 1

    def copy(i):
        return pltpu.make_async_copy(
            cache_ref.at[:, pl.ds(pl.multiple_of(i * tile, tile), tile)], held.at[i], sems.at[i]
        )

    @pl.loop(0, used)
    def _(i):
        copy(i).start()

    def reset():
        acc[...] = jnp.zeros_like(acc)
        best[...] = jnp.full_like(best, negative)
        mass[...] = jnp.zeros_like(mass)

    def scores(r, i, live, target):
        begin_at = jnp.where(live, lo[r], 0)
        end_at = jnp.where(live, hi[r], 0)
        s = jnp.dot(q_ref[r], held[i], preferred_element_type=jnp.float32)
        token = i * tile + lax.broadcasted_iota(jnp.int32, (1, tile), 1)
        s = jnp.where((token >= begin_at) & (token < end_at), s, negative)
        target[...] = s

    def advance(p, r, i):
        ends = i == last[r]
        live = p + 1 < pairs
        nr = jnp.where(ends & live, r + 1, r)
        ni = jnp.where(ends, jnp.where(live, first[nr], i), i + 1)
        return nr, ni, live

    def fetch(i, r, live):
        fresh = live & ((r == 0) | (i > last[jnp.maximum(r - 1, 0)]))

        @pl.when(fresh)
        def _():
            copy(i).wait()

    def absorb(r, i, live, source):
        factor = score_scale * log2_e
        s = source[...]
        old = best[...]
        new = jnp.maximum(old, jnp.max(s, axis=1, keepdims=True))
        weight = jnp.exp2((s - new[:, :1]) * factor)
        keep = jnp.exp2((old - new) * factor)
        part = weight[:, :128]
        for at in range(128, tile, 128):
            part = part + weight[:, at : at + 128]
        mass[...] = mass[...] * keep + part
        best[...] = new
        values = lax.dot_general(
            held[i, :C, :],
            weight.astype(jnp.bfloat16),
            (((1,), (1,)), ((), ())),
            preferred_element_type=jnp.float32,
        )
        acc[...] = acc[...] * keep.T[:1, :] + values

    def close(r, i, live):
        @pl.when(live & (i == last[r]))
        def _():
            total = jnp.sum(mass[...], axis=1, keepdims=True)
            done[r] = acc[...].T / total
            reset()

    reset()
    fetch(jnp.int32(0), jnp.int32(0), pairs > 0)
    scores(jnp.int32(0), jnp.int32(0), pairs > 0, score0)

    def step(j, carry):
        r, i, live = carry
        p = 2 * j
        for now, later in ((score0, score1), (score1, score0)):
            nr, ni, nlive = advance(p, r, i)
            fetch(ni, nr, nlive)
            scores(nr, ni, nlive, later)
            absorb(r, i, live, now)
            close(r, i, live)
            r, i, live, p = nr, ni, nlive, p + 1
        return r, i, live

    lax.fori_loop(0, (pairs + 1) // 2, step, (jnp.int32(0), jnp.int32(0), pairs > 0))
    share = heads // out_ref.shape[0]
    for d in range(out_ref.shape[0]):
        rows = [done[r, d * share : (d + 1) * share, :] for r in range(nreq)]
        out_ref[d] = jnp.concatenate(rows, 0).astype(out_ref.dtype)


def kernel_params(limit):
    return pltpu.CompilerParams(vmem_limit_bytes=limit * 1024 * 1024)


def in_vmem(count):
    return [pl.BlockSpec(memory_space=pltpu.VMEM)] * count


def in_any(count):
    return [pl.BlockSpec(memory_space=pl.ANY)] * count


def attend(lengths, queries, cache_t, ranks):
    nreq, heads, width = queries.shape
    tokens = cache_t.shape[1]
    tile = TILE
    tiles = tokens // tile
    return pl.pallas_call(
        attention_kernel,
        out_shape=jax.ShapeDtypeStruct((ranks, nreq * heads // ranks, C), jnp.bfloat16),
        in_specs=[pl.BlockSpec(memory_space=pltpu.SMEM)] + in_vmem(1) + in_any(1),
        out_specs=pl.BlockSpec(memory_space=pltpu.VMEM),
        scratch_shapes=[
            pltpu.VMEM((tiles, width, tile), jnp.bfloat16),
            pltpu.VMEM((heads, tile), jnp.float32),
            pltpu.VMEM((heads, tile), jnp.float32),
            pltpu.VMEM((C, heads), jnp.float32),
            pltpu.VMEM((nreq, heads, C), jnp.float32),
            pltpu.VMEM((heads, 128), jnp.float32),
            pltpu.VMEM((heads, 128), jnp.float32),
            pltpu.SMEM((nreq,), jnp.int32),
            pltpu.SMEM((nreq,), jnp.int32),
            pltpu.SMEM((nreq,), jnp.int32),
            pltpu.SMEM((nreq,), jnp.int32),
            pltpu.SemaphoreType.DMA((tiles,)),
        ],
        compiler_params=kernel_params(28),
        cost_estimate=pl.CostEstimate(
            flops=2 * heads * tokens * (width + C),
            bytes_accessed=2 * tokens * width,
            transcendentals=heads * tokens,
        ),
        name="attention",
    )(lengths, queries, cache_t)


def head_values_kernel(latent_ref, w_ref, residual_ref, out_ref, values, slots):
    heads, _, wide = w_ref.shape
    per_rank, model = residual_ref.shape
    requests = latent_ref.shape[0] // heads
    latent = latent_ref[...]
    for h in range(heads):
        values[...] = jnp.dot(latent, w_ref[h], preferred_element_type=jnp.float32)
        picked = values[pl.ds(h, requests, stride=heads), :]
        out_ref[:requests, h * wide : (h + 1) * wide] = picked.astype(out_ref.dtype)
    ranks = lax.axis_size("tp")
    groups = model // ranks // 128
    rows = (out_ref.shape[0] - requests) // ranks
    across = out_ref.shape[1] // 128
    slots[...] = jnp.zeros_like(slots)
    for t in range(ranks):
        for g in range(groups):
            at = (t * groups + g) * 128
            row = t * rows + (g // across) * per_rank
            column = (g % across) * 128
            slots[row : row + per_rank, column : column + 128] = residual_ref[
                :, at : at + 128
            ].astype(jnp.float32)
    out_ref[requests:, :] = slots[...].astype(out_ref.dtype)


def head_values(latent, w_uv, residual, slot_rows):
    heads, _, wide = w_uv.shape
    requests = latent.shape[0] // heads
    return pl.pallas_call(
        head_values_kernel,
        out_shape=jax.ShapeDtypeStruct((requests + slot_rows, heads * wide), jnp.bfloat16),
        in_specs=in_vmem(3),
        out_specs=pl.BlockSpec(memory_space=pltpu.VMEM),
        scratch_shapes=[
            pltpu.VMEM((latent.shape[0], wide), jnp.float32),
            pltpu.VMEM((slot_rows, heads * wide), jnp.float32),
        ],
        compiler_params=kernel_params(12),
        name="head_values",
    )(latent, w_uv, residual)


def stream(sources, target, sems):
    copies = [pltpu.make_async_copy(s, target.at[k], sems.at[k]) for k, s in enumerate(sources)]
    for copy in copies:
        copy.start()
    return copies


def output_kernel(values_ref, w_ref, out_ref, held, total, sems):
    steps, depth, _ = held.shape
    requests = out_ref.shape[0]
    copies = stream([w_ref.at[pl.ds(k * depth, depth), :] for k in range(steps)], held, sems)
    for k in range(steps):
        copies[k].wait()
        term = jnp.dot(values_ref[k, :requests, :], held[k], preferred_element_type=jnp.float32)
        if k == 0:
            total[...] = term
        else:
            total[...] += term
    out_ref[...] = total[...].astype(out_ref.dtype)


def project_out(values, w_o, requests):
    steps, _, depth = values.shape
    width = w_o.shape[1]
    return pl.pallas_call(
        output_kernel,
        out_shape=jax.ShapeDtypeStruct((requests, width), jnp.bfloat16),
        in_specs=in_vmem(1) + in_any(1),
        out_specs=pl.BlockSpec(memory_space=pltpu.VMEM),
        scratch_shapes=[
            pltpu.VMEM((steps, depth, width), w_o.dtype),
            pltpu.VMEM((requests, width), jnp.float32),
            pltpu.SemaphoreType.DMA((steps,)),
        ],
        compiler_params=kernel_params(20),
        name="project_out",
    )(values, w_o)


def hidden_kernel(parts_ref, values_ref, out_ref, slots):
    ranks = values_ref.shape[0]
    width = out_ref.shape[1]
    per_rank = out_ref.shape[0] // ranks
    across = values_ref.shape[2] // 128
    rows = slots.shape[1]
    requests = values_ref.shape[1] - ranks * rows
    start = pl.multiple_of(requests + lax.axis_index("tp") * rows, 16)
    for s in range(ranks):
        slots[s] = values_ref[s, pl.ds(start, rows), :].astype(jnp.float32)
    for g in range(width // 128):
        at = slice(g * 128, (g + 1) * 128)
        row = (g // across) * per_rank
        column = (g % across) * 128
        terms = [
            slots[s, row : row + per_rank, column : column + 128] for s in range(ranks)
        ]
        total = parts_ref[0, :, at].astype(jnp.float32)
        for d in range(1, parts_ref.shape[0]):
            total = total + parts_ref[d, :, at].astype(jnp.float32)
        total = total + jnp.concatenate(terms, 0)
        out_ref[:, at] = total.astype(out_ref.dtype)


def make_hidden(parts, values, slot_rows):
    ranks = values.shape[0]
    return pl.pallas_call(
        hidden_kernel,
        out_shape=jax.ShapeDtypeStruct(parts.shape[1:], jnp.bfloat16),
        in_specs=in_vmem(2),
        out_specs=pl.BlockSpec(memory_space=pltpu.VMEM),
        scratch_shapes=[pltpu.VMEM((ranks, slot_rows // ranks, values.shape[2]), jnp.float32)],
        compiler_params=kernel_params(12),
        name="hidden",
    )(parts, values)


def gate_up_kernel(
    hidden_ref, gain_ref, gate_ref, up_ref, out_ref, held, scaled, gains, own, sems
):
    steps, _, chunk = held.shape
    half = steps // 2
    requests, width = hidden_ref.shape
    units = gate_ref.shape[1]
    ranks = lax.axis_size("tp")
    groups = width // 128
    copies = stream(
        [w.at[:, pl.ds(k * chunk, chunk)] for w in (gate_ref, up_ref) for k in range(half)],
        held,
        sems,
    )
    gains[...] = gain_ref[...].astype(jnp.float32)
    base = lax.axis_index("tp") * groups
    square = jnp.zeros((requests, 128), jnp.float32)
    for g in range(groups):
        at = slice(g * 128, (g + 1) * 128)
        x = hidden_ref[:, at].astype(jnp.float32)
        square = square + x * x
        scaled[:, at] = (x * gains[pl.ds(base + g, 1), :]).astype(scaled.dtype)
    square = jnp.sum(square, 1, keepdims=True)
    top = square.astype(jnp.bfloat16).astype(jnp.float32)
    middle = (square - top).astype(jnp.bfloat16).astype(jnp.float32)
    low = square - top - middle
    lane = lax.broadcasted_iota(jnp.int32, (requests, 128), 1)
    digits = jnp.where(lane == 0, top, jnp.where(lane == 1, middle, jnp.where(lane == 2, low, 0.0)))
    out_ref[:, 2 * units : 2 * units + 128] = digits.astype(out_ref.dtype)

    rows = own.shape[0]
    per_rank = rows // ranks
    start = pl.multiple_of(lax.axis_index("dp") * rows, 16)
    own[...] = hidden_ref[pl.ds(start, rows), :].astype(jnp.float32)
    share = requests // ranks
    high = share // per_rank
    for t in range(ranks):
        for block in range((groups + high - 1) // high):
            pieces = []
            for g in range(block * high, (block + 1) * high):
                g = min(g, groups - 1)
                pieces.append(
                    own[t * per_rank : (t + 1) * per_rank, g * 128 : (g + 1) * 128]
                )
            column = 2 * units + 128 * (1 + block)
            out_ref[t * share : (t + 1) * share, column : column + 128] = jnp.concatenate(
                pieces, 0
            ).astype(out_ref.dtype)

    for k in range(steps):
        copies[k].wait()
        term = jnp.dot(scaled[...], held[k], preferred_element_type=jnp.float32)
        out_ref[:, k * chunk : (k + 1) * chunk] = term.astype(out_ref.dtype)


def gate_up(hidden, gain, w_gate, w_up, own_rows, columns):
    requests, width = hidden.shape
    units = w_gate.shape[1]
    chunk = units // 3
    return pl.pallas_call(
        gate_up_kernel,
        out_shape=jax.ShapeDtypeStruct((requests, columns), jnp.bfloat16),
        in_specs=in_vmem(2) + in_any(2),
        out_specs=pl.BlockSpec(memory_space=pltpu.VMEM),
        scratch_shapes=[
            pltpu.VMEM((6, width, chunk), w_gate.dtype),
            pltpu.VMEM((requests, width), jnp.bfloat16),
            pltpu.VMEM(gain.shape, jnp.float32),
            pltpu.VMEM((own_rows, width), jnp.float32),
            pltpu.SemaphoreType.DMA((6,)),
        ],
        compiler_params=kernel_params(32),
        name="gate_up",
    )(hidden, gain, w_gate, w_up)


def inner_kernel(model, parts_ref, out_ref, slots_ref):
    ranks = parts_ref.shape[0]
    units = out_ref.shape[1]

    def total(at):
        return sum(parts_ref[s, :, at].astype(jnp.float32) for s in range(ranks))

    square = jnp.sum(total(slice(2 * units, 2 * units + 128)), 1, keepdims=True)
    factor = lax.rsqrt(square / model + 1e-06)
    for at in range(0, units, 128):
        gate = total(slice(at, at + 128)) * factor
        up = total(slice(units + at, units + at + 128)) * factor
        out_ref[:, at : at + 128] = (gate / (1.0 + jnp.exp(-gate)) * up).astype(out_ref.dtype)
    slots_ref[...] = parts_ref[:, :, 2 * units + 128 :]


def make_inner(parts, units, model):
    ranks, rows, columns = parts.shape
    return pl.pallas_call(
        functools.partial(inner_kernel, model),
        out_shape=[
            jax.ShapeDtypeStruct((rows, units), jnp.bfloat16),
            jax.ShapeDtypeStruct((ranks, rows, columns - 2 * units - 128), jnp.bfloat16),
        ],
        in_specs=in_vmem(1),
        out_specs=in_vmem(2),
        compiler_params=kernel_params(12),
        name="inner",
    )(parts)


def down_kernel(inner_ref, w_ref, out_ref, held, total, sems):
    steps, depth, width = held.shape
    copies = stream([w_ref.at[pl.ds(k * depth, depth), :] for k in range(steps)], held, sems)
    for k in range(steps):
        copies[k].wait()
        term = jnp.dot(
            inner_ref[:, k * depth : (k + 1) * depth], held[k], preferred_element_type=jnp.float32
        )
        if k == 0:
            total[...] = term
        else:
            total[...] += term
    groups = width // 128
    per_rank = out_ref.shape[1] // groups
    for d in range(out_ref.shape[0]):
        pieces = [
            total[d * per_rank : (d + 1) * per_rank, g * 128 : (g + 1) * 128]
            for g in range(groups)
        ]
        out_ref[d] = jnp.concatenate(pieces, 0).astype(out_ref.dtype)


def project_down(inner, w_down, ranks):
    requests, units = inner.shape
    width = w_down.shape[1]
    return pl.pallas_call(
        down_kernel,
        out_shape=jax.ShapeDtypeStruct(
            (ranks, requests // ranks * (width // 128), 128), jnp.bfloat16
        ),
        in_specs=in_vmem(1) + in_any(1),
        out_specs=pl.BlockSpec(memory_space=pltpu.VMEM),
        scratch_shapes=[
            pltpu.VMEM((3, units // 3, width), w_down.dtype),
            pltpu.VMEM((requests, width), jnp.float32),
            pltpu.SemaphoreType.DMA((3,)),
        ],
        compiler_params=kernel_params(20),
        name="project_down",
    )(inner, w_down)


def layer_kernel(parts_ref, slots_ref, out_ref, total, hidden):
    ranks = slots_ref.shape[0]
    per_rank, model = out_ref.shape
    groups = model // ranks // 128
    high = slots_ref.shape[1] // per_rank
    hidden[...] = slots_ref[...].astype(jnp.float32)
    for t in range(ranks):
        ffn = sum(
            parts_ref[d, :, :].astype(jnp.float32) for d in range(t, parts_ref.shape[0], ranks)
        )
        for g in range(groups):
            row = (g % high) * per_rank
            column = (g // high) * 128
            at = (t * groups + g) * 128
            total[:, at : at + 128] = (
                ffn[g * per_rank : (g + 1) * per_rank, :]
                + hidden[t, row : row + per_rank, column : column + 128]
            )
    out_ref[...] = total[...].astype(out_ref.dtype)


def make_layer(parts, slots, per_rank, model):
    return pl.pallas_call(
        layer_kernel,
        out_shape=jax.ShapeDtypeStruct((per_rank, model), jnp.bfloat16),
        in_specs=in_vmem(2),
        out_specs=pl.BlockSpec(memory_space=pltpu.VMEM),
        scratch_shapes=[
            pltpu.VMEM((per_rank, model), jnp.float32),
            pltpu.VMEM(slots.shape, jnp.float32),
        ],
        compiler_params=kernel_params(12),
        name="layer",
    )(parts, slots)


def round_up(value, step):
    return (value + step - 1) // step * step


def swap(parts, axes):
    return lax.all_to_all(parts, axes, split_axis=0, concat_axis=0, tiled=True)


def local(
    residual, queries, paged_latent_cache, lengths, w_uv, w_o, norm_gain, w_gate, w_up, w_down
):
    ranks_dp = lax.axis_size("dp")
    ranks_tp = lax.axis_size("tp")
    ranks = ranks_dp * ranks_tp
    per_rank, model = residual.shape
    requests = per_rank * ranks
    row_length = paged_latent_cache.shape[1]
    heads_all = queries.shape[1] // row_length
    heads_here = w_uv.shape[0]
    units = w_gate.shape[1]
    width = w_o.shape[1]
    groups = width // 128

    query = queries.reshape(per_rank, heads_all, row_length)
    latent = swap(attend(lengths, query, paged_latent_cache.T, ranks), ("dp", "tp"))

    across = heads_here * w_uv.shape[2] // 128
    slot_rows = ranks_tp * round_up(per_rank * ((groups + across - 1) // across), 16)
    values = head_values(latent.reshape(requests * heads_here, C), w_uv, residual, slot_rows)
    values = lax.all_gather(values, "tp", axis=0)
    attn = project_out(values, w_o, requests)
    attn = swap(attn.reshape(ranks_dp, requests // ranks_dp, width), "dp")
    hidden = make_hidden(attn, values, slot_rows)
    hidden = lax.all_gather(hidden, "dp", axis=0, tiled=True)

    share = requests // ranks_tp
    high = share // per_rank
    columns = 2 * units + 128 + 128 * ((groups + high - 1) // high)
    both = gate_up(
        hidden, norm_gain.reshape(-1, 128), w_gate, w_up, requests // ranks_dp, columns
    )
    both = swap(both.reshape(ranks_tp, share, columns), "tp")
    inner, slots = make_inner(both, units, model)
    inner = lax.all_gather(inner, "tp", axis=0, tiled=True)
    ffn = swap(project_down(inner, w_down, ranks), ("dp", "tp"))
    return make_layer(ffn, slots, per_rank, model)


def solution(mesh):
    placed = (
        P(("dp", "tp"), None),
        P(("dp", "tp"), None),
        P(("dp", "tp"), None),
        P(),
        P(("dp", "tp"), None, None),
        P("dp", "tp"),
        P(),
        P("tp", "dp"),
        P("tp", "dp"),
        P("dp", "tp"),
    )
    return jax.shard_map(
        local, mesh=mesh, in_specs=placed, out_specs=P(("dp", "tp"), None), check_vma=False
    )
```

```python
import functools

import jax
import jax.numpy as jnp
from jax import lax
from jax.experimental import pallas as pl
from jax.experimental.pallas import tpu as pltpu
from jax.sharding import PartitionSpec as P

C = 512
BLOCK_TOKENS = 64
TILE = 1024

score_scale = 192.0 ** (-0.5)
log2_e = 1.4426950408889634
negative = -1e30


def attention_kernel(
    lens_ref,
    q_ref,
    cache_ref,
    out_ref,
    held,
    score0,
    score1,
    weight0,
    weight1,
    keep0,
    keep1,
    acc,
    done,
    best,
    mass,
    lo,
    hi,
    first,
    last,
    sems,
):
    nreq, heads, _ = q_ref.shape
    tile = held.shape[2]
    factor = score_scale * log2_e

    rank = lax.axis_index("dp") * lax.axis_size("tp") + lax.axis_index("tp")
    begin = jnp.int32(0)
    pairs = jnp.int32(0)
    for r in range(nreq):
        length = lens_ref[rank * nreq + r]
        lo[r] = begin
        hi[r] = begin + length
        first[r] = begin // tile
        last[r] = (begin + length - 1) // tile
        pairs = pairs + (last[r] - first[r] + 1)
        begin = begin + ((length + BLOCK_TOKENS - 1) // BLOCK_TOKENS) * BLOCK_TOKENS
    used = last[nreq - 1] + 1

    def copy(i):
        return pltpu.make_async_copy(
            cache_ref.at[:, pl.ds(pl.multiple_of(i * tile, tile), tile)], held.at[i], sems.at[i]
        )

    @pl.loop(0, used)
    def _(i):
        copy(i).start()

    acc[...] = jnp.zeros_like(acc)
    best[...] = jnp.full_like(best, negative)
    mass[...] = jnp.zeros_like(mass)
    weight1[...] = jnp.zeros_like(weight1)
    keep1[...] = jnp.ones_like(keep1)

    def advance(p, r, i):
        live = p + 1 < pairs
        step = (i == last[r]) & live
        nr = jnp.where(step, r + 1, r)
        ni = jnp.where(step, first[nr], jnp.where(live, i + 1, i))
        return nr, ni, live

    def fetch(r, i, live):
        fresh = live & ((r == 0) | (i > last[jnp.maximum(r - 1, 0)]))

        @pl.when(fresh)
        def _():
            copy(i).wait()

    def scores(r, i, live, target):
        begin_at = jnp.where(live, lo[r], 0)
        end_at = jnp.where(live, hi[r], 0)
        s = jnp.dot(q_ref[r], held[i], preferred_element_type=jnp.float32)
        token = i * tile + lax.broadcasted_iota(jnp.int32, (1, tile), 1)
        target[...] = jnp.where((token >= begin_at) & (token < end_at), s, negative)

    def soften(r, source, weights, keeps):
        s = source[...]
        old = best[r]
        new = jnp.maximum(old, jnp.max(s, axis=1, keepdims=True))
        weight = jnp.exp2((s - new[:, :1]) * factor)
        keep = jnp.exp2((old - new) * factor)
        part = weight[:, :128]
        for at in range(128, tile, 128):
            part = part + weight[:, at : at + 128]
        mass[r] = mass[r] * keep + part
        best[r] = new
        weights[...] = weight.astype(weights.dtype)
        keeps[...] = keep.T[:8, :]

    def gather(r, i, weights, keeps):
        values = lax.dot_general(
            held[i, :C, :],
            weights[...],
            (((1,), (1,)), ((), ())),
            preferred_element_type=jnp.float32,
        )
        acc[r] = acc[r] * keeps[:1, :] + values

    zero = jnp.int32(0)
    fetch(zero, zero, pairs > 0)
    scores(zero, zero, pairs > 0, score0)

    def step(j, carry):
        r0, i0, r1, i1 = carry
        p = 2 * j
        r2, i2, live2 = advance(p, r1, i1)
        r3, i3, live3 = advance(p + 1, r2, i2)
        fetch(r2, i2, live2)
        fetch(r3, i3, live3)
        gather(r0, i0, weight1, keep1)
        scores(r2, i2, live2, score1)
        soften(r1, score0, weight0, keep0)
        gather(r1, i1, weight0, keep0)
        scores(r3, i3, live3, score0)
        soften(r2, score1, weight1, keep1)
        return r2, i2, r3, i3

    r0, i0, _, _ = lax.fori_loop(0, (pairs + 1) // 2, step, (zero, zero, zero, zero))
    gather(r0, i0, weight1, keep1)

    share = heads // out_ref.shape[0]
    for r in range(nreq):
        total = jnp.sum(mass[r], axis=1, keepdims=True)
        score0[:, :C] = acc[r].T / total
        for d in range(out_ref.shape[0]):
            done[d, r * share : (r + 1) * share, :] = score0[d * share : (d + 1) * share, :C]
    out_ref[...] = done[...].astype(out_ref.dtype)


def kernel_params(limit):
    return pltpu.CompilerParams(vmem_limit_bytes=limit * 1024 * 1024)


def in_vmem(count):
    return [pl.BlockSpec(memory_space=pltpu.VMEM)] * count


def fetched(weight):
    return pltpu.with_memory_space_constraint(weight, pltpu.VMEM)


def attend(lengths, queries, cache_t, ranks):
    nreq, heads, width = queries.shape
    tokens = cache_t.shape[1]
    tile = TILE
    tiles = tokens // tile
    return pl.pallas_call(
        attention_kernel,
        out_shape=jax.ShapeDtypeStruct((ranks, nreq * heads // ranks, C), jnp.bfloat16),
        in_specs=[pl.BlockSpec(memory_space=pltpu.SMEM)]
        + in_vmem(1)
        + [pl.BlockSpec(memory_space=pltpu.HBM)],
        out_specs=pl.BlockSpec(memory_space=pltpu.VMEM),
        scratch_shapes=[
            pltpu.VMEM((tiles, width, tile), jnp.bfloat16),
            pltpu.VMEM((heads, tile), jnp.float32),
            pltpu.VMEM((heads, tile), jnp.float32),
            pltpu.VMEM((heads, tile), jnp.bfloat16),
            pltpu.VMEM((heads, tile), jnp.bfloat16),
            pltpu.VMEM((8, heads), jnp.float32),
            pltpu.VMEM((8, heads), jnp.float32),
            pltpu.VMEM((nreq, C, heads), jnp.float32),
            pltpu.VMEM((ranks, nreq * heads // ranks, C), jnp.float32),
            pltpu.VMEM((nreq, heads, 128), jnp.float32),
            pltpu.VMEM((nreq, heads, 128), jnp.float32),
            pltpu.SMEM((nreq,), jnp.int32),
            pltpu.SMEM((nreq,), jnp.int32),
            pltpu.SMEM((nreq,), jnp.int32),
            pltpu.SMEM((nreq,), jnp.int32),
            pltpu.SemaphoreType.DMA((tiles,)),
        ],
        compiler_params=kernel_params(26),
        cost_estimate=pl.CostEstimate(
            flops=2 * heads * tokens * (width + C),
            bytes_accessed=2 * tokens * width,
            transcendentals=heads * tokens,
        ),
        name="attention",
    )(lengths, queries, pltpu.with_memory_space_constraint(cache_t, pltpu.HBM))


def head_values_kernel(latent_ref, w_ref, residual_ref, out_ref, values, slots):
    heads, _, wide = w_ref.shape
    per_rank, model = residual_ref.shape
    requests = latent_ref.shape[0] // heads
    latent = latent_ref[...]
    for h in range(heads):
        values[...] = jnp.dot(latent, w_ref[h], preferred_element_type=jnp.float32)
        picked = values[pl.ds(h, requests, stride=heads), :]
        out_ref[:requests, h * wide : (h + 1) * wide] = picked.astype(out_ref.dtype)
    ranks = lax.axis_size("tp")
    groups = model // ranks // 128
    rows = (out_ref.shape[0] - requests) // ranks
    across = out_ref.shape[1] // 128
    slots[...] = jnp.zeros_like(slots)
    for t in range(ranks):
        for g in range(groups):
            at = (t * groups + g) * 128
            row = t * rows + (g // across) * per_rank
            column = (g % across) * 128
            slots[row : row + per_rank, column : column + 128] = residual_ref[
                :, at : at + 128
            ].astype(jnp.float32)
    out_ref[requests:, :] = slots[...].astype(out_ref.dtype)


def head_values(latent, w_uv, residual, slot_rows):
    heads, _, wide = w_uv.shape
    requests = latent.shape[0] // heads
    return pl.pallas_call(
        head_values_kernel,
        out_shape=jax.ShapeDtypeStruct((requests + slot_rows, heads * wide), jnp.bfloat16),
        in_specs=in_vmem(3),
        out_specs=pl.BlockSpec(memory_space=pltpu.VMEM),
        scratch_shapes=[
            pltpu.VMEM((latent.shape[0], wide), jnp.float32),
            pltpu.VMEM((slot_rows, heads * wide), jnp.float32),
        ],
        compiler_params=kernel_params(12),
        name="head_values",
    )(latent, w_uv, residual)


def output_kernel(values_ref, w_ref, out_ref, total):
    steps, _, depth = values_ref.shape
    requests = out_ref.shape[0]
    for k in range(steps):
        term = jnp.dot(
            values_ref[k, :requests, :],
            w_ref[k * depth : (k + 1) * depth, :],
            preferred_element_type=jnp.float32,
        )
        if k == 0:
            total[...] = term
        else:
            total[...] += term
    out_ref[...] = total[...].astype(out_ref.dtype)


def project_out(values, w_o, requests):
    width = w_o.shape[1]
    return pl.pallas_call(
        output_kernel,
        out_shape=jax.ShapeDtypeStruct((requests, width), jnp.bfloat16),
        in_specs=in_vmem(2),
        out_specs=pl.BlockSpec(memory_space=pltpu.VMEM),
        scratch_shapes=[pltpu.VMEM((requests, width), jnp.float32)],
        compiler_params=kernel_params(12),
        name="project_out",
    )(values, fetched(w_o))


def hidden_kernel(parts_ref, values_ref, out_ref, slots):
    ranks = values_ref.shape[0]
    width = out_ref.shape[1]
    per_rank = out_ref.shape[0] // ranks
    across = values_ref.shape[2] // 128
    rows = slots.shape[1]
    requests = values_ref.shape[1] - ranks * rows
    start = pl.multiple_of(requests + lax.axis_index("tp") * rows, 16)
    for s in range(ranks):
        slots[s] = values_ref[s, pl.ds(start, rows), :].astype(jnp.float32)
    for g in range(width // 128):
        at = slice(g * 128, (g + 1) * 128)
        row = (g // across) * per_rank
        column = (g % across) * 128
        terms = [
            slots[s, row : row + per_rank, column : column + 128] for s in range(ranks)
        ]
        total = parts_ref[0, :, at].astype(jnp.float32)
        for d in range(1, parts_ref.shape[0]):
            total = total + parts_ref[d, :, at].astype(jnp.float32)
        total = total + jnp.concatenate(terms, 0)
        out_ref[:, at] = total.astype(out_ref.dtype)


def make_hidden(parts, values, slot_rows):
    ranks = values.shape[0]
    return pl.pallas_call(
        hidden_kernel,
        out_shape=jax.ShapeDtypeStruct(parts.shape[1:], jnp.bfloat16),
        in_specs=in_vmem(2),
        out_specs=pl.BlockSpec(memory_space=pltpu.VMEM),
        scratch_shapes=[pltpu.VMEM((ranks, slot_rows // ranks, values.shape[2]), jnp.float32)],
        compiler_params=kernel_params(12),
        name="hidden",
    )(parts, values)


def gate_up_kernel(
    hidden_ref, gain_ref, gate_ref, up_ref, out_ref, scaled, gains, own
):
    requests, width = hidden_ref.shape
    units = gate_ref.shape[1]
    ranks = lax.axis_size("tp")
    groups = width // 128
    gains[...] = gain_ref[...].astype(jnp.float32)
    base = lax.axis_index("tp") * groups
    square = jnp.zeros((requests, 128), jnp.float32)
    for g in range(groups):
        at = slice(g * 128, (g + 1) * 128)
        x = hidden_ref[:, at].astype(jnp.float32)
        square = square + x * x
        scaled[:, at] = (x * gains[pl.ds(base + g, 1), :]).astype(scaled.dtype)
    square = jnp.sum(square, 1, keepdims=True)
    top = square.astype(jnp.bfloat16).astype(jnp.float32)
    middle = (square - top).astype(jnp.bfloat16).astype(jnp.float32)
    low = square - top - middle
    lane = lax.broadcasted_iota(jnp.int32, (requests, 128), 1)
    digits = jnp.where(lane == 0, top, jnp.where(lane == 1, middle, jnp.where(lane == 2, low, 0.0)))
    out_ref[:, 2 * units : 2 * units + 128] = digits.astype(out_ref.dtype)

    rows = own.shape[0]
    per_rank = rows // ranks
    start = pl.multiple_of(lax.axis_index("dp") * rows, 16)
    own[...] = hidden_ref[pl.ds(start, rows), :].astype(jnp.float32)
    share = requests // ranks
    high = share // per_rank
    for t in range(ranks):
        for block in range((groups + high - 1) // high):
            pieces = []
            for g in range(block * high, (block + 1) * high):
                g = min(g, groups - 1)
                pieces.append(
                    own[t * per_rank : (t + 1) * per_rank, g * 128 : (g + 1) * 128]
                )
            column = 2 * units + 128 * (1 + block)
            out_ref[t * share : (t + 1) * share, column : column + 128] = jnp.concatenate(
                pieces, 0
            ).astype(out_ref.dtype)

    chunk = units // 3
    for k, w_ref in enumerate((gate_ref, up_ref)):
        for at in range(0, units, chunk):
            term = jnp.dot(
                scaled[...], w_ref[:, at : at + chunk], preferred_element_type=jnp.float32
            )
            out_ref[:, k * units + at : k * units + at + chunk] = term.astype(out_ref.dtype)


def gate_up(hidden, gain, w_gate, w_up, own_rows, columns):
    requests, width = hidden.shape
    return pl.pallas_call(
        gate_up_kernel,
        out_shape=jax.ShapeDtypeStruct((requests, columns), jnp.bfloat16),
        in_specs=in_vmem(4),
        out_specs=pl.BlockSpec(memory_space=pltpu.VMEM),
        scratch_shapes=[
            pltpu.VMEM((requests, width), jnp.bfloat16),
            pltpu.VMEM(gain.shape, jnp.float32),
            pltpu.VMEM((own_rows, width), jnp.float32),
        ],
        compiler_params=kernel_params(12),
        name="gate_up",
    )(hidden, gain, fetched(w_gate), fetched(w_up))


def inner_kernel(model, parts_ref, out_ref, slots_ref):
    ranks = parts_ref.shape[0]
    units = out_ref.shape[1]

    def total(at):
        return sum(parts_ref[s, :, at].astype(jnp.float32) for s in range(ranks))

    square = jnp.sum(total(slice(2 * units, 2 * units + 128)), 1, keepdims=True)
    factor = lax.rsqrt(square / model + 1e-06)
    for at in range(0, units, 128):
        gate = total(slice(at, at + 128)) * factor
        up = total(slice(units + at, units + at + 128)) * factor
        out_ref[:, at : at + 128] = (gate / (1.0 + jnp.exp(-gate)) * up).astype(out_ref.dtype)
    slots_ref[...] = parts_ref[:, :, 2 * units + 128 :]


def make_inner(parts, units, model):
    ranks, rows, columns = parts.shape
    return pl.pallas_call(
        functools.partial(inner_kernel, model),
        out_shape=[
            jax.ShapeDtypeStruct((rows, units), jnp.bfloat16),
            jax.ShapeDtypeStruct((ranks, rows, columns - 2 * units - 128), jnp.bfloat16),
        ],
        in_specs=in_vmem(1),
        out_specs=in_vmem(2),
        compiler_params=kernel_params(12),
        name="inner",
    )(parts)


def down_kernel(inner_ref, w_ref, out_ref, total):
    width = w_ref.shape[1]
    total[...] = jnp.dot(inner_ref[...], w_ref[...], preferred_element_type=jnp.float32)
    groups = width // 128
    per_rank = out_ref.shape[1] // groups
    for d in range(out_ref.shape[0]):
        pieces = [
            total[d * per_rank : (d + 1) * per_rank, g * 128 : (g + 1) * 128]
            for g in range(groups)
        ]
        out_ref[d] = jnp.concatenate(pieces, 0).astype(out_ref.dtype)


def project_down(inner, w_down, ranks):
    requests, units = inner.shape
    width = w_down.shape[1]
    return pl.pallas_call(
        down_kernel,
        out_shape=jax.ShapeDtypeStruct(
            (ranks, requests // ranks * (width // 128), 128), jnp.bfloat16
        ),
        in_specs=in_vmem(2),
        out_specs=pl.BlockSpec(memory_space=pltpu.VMEM),
        scratch_shapes=[pltpu.VMEM((requests, width), jnp.float32)],
        compiler_params=kernel_params(12),
        name="project_down",
    )(inner, fetched(w_down))


def layer_kernel(parts_ref, slots_ref, out_ref, total, hidden):
    ranks = slots_ref.shape[0]
    per_rank, model = out_ref.shape
    groups = model // ranks // 128
    high = slots_ref.shape[1] // per_rank
    hidden[...] = slots_ref[...].astype(jnp.float32)
    for t in range(ranks):
        ffn = sum(
            parts_ref[d, :, :].astype(jnp.float32) for d in range(t, parts_ref.shape[0], ranks)
        )
        for g in range(groups):
            row = (g % high) * per_rank
            column = (g // high) * 128
            at = (t * groups + g) * 128
            total[:, at : at + 128] = (
                ffn[g * per_rank : (g + 1) * per_rank, :]
                + hidden[t, row : row + per_rank, column : column + 128]
            )
    out_ref[...] = total[...].astype(out_ref.dtype)


def make_layer(parts, slots, per_rank, model):
    return pl.pallas_call(
        layer_kernel,
        out_shape=jax.ShapeDtypeStruct((per_rank, model), jnp.bfloat16),
        in_specs=in_vmem(2),
        out_specs=pl.BlockSpec(memory_space=pltpu.VMEM),
        scratch_shapes=[
            pltpu.VMEM((per_rank, model), jnp.float32),
            pltpu.VMEM(slots.shape, jnp.float32),
        ],
        compiler_params=kernel_params(12),
        name="layer",
    )(parts, slots)


def round_up(value, step):
    return (value + step - 1) // step * step


def swap(parts, axes):
    return lax.all_to_all(parts, axes, split_axis=0, concat_axis=0, tiled=True)


def local(
    residual, queries, paged_latent_cache, lengths, w_uv, w_o, norm_gain, w_gate, w_up, w_down
):
    ranks_dp = lax.axis_size("dp")
    ranks_tp = lax.axis_size("tp")
    ranks = ranks_dp * ranks_tp
    per_rank, model = residual.shape
    requests = per_rank * ranks
    row_length = paged_latent_cache.shape[1]
    heads_all = queries.shape[1] // row_length
    heads_here = w_uv.shape[0]
    units = w_gate.shape[1]
    width = w_o.shape[1]
    groups = width // 128

    query = queries.reshape(per_rank, heads_all, row_length)
    latent = swap(attend(lengths, query, paged_latent_cache.T, ranks), ("dp", "tp"))

    across = heads_here * w_uv.shape[2] // 128
    slot_rows = ranks_tp * round_up(per_rank * ((groups + across - 1) // across), 16)
    values = head_values(latent.reshape(requests * heads_here, C), w_uv, residual, slot_rows)
    values = lax.all_gather(values, "tp", axis=0)
    attn = project_out(values, w_o, requests)
    attn = swap(attn.reshape(ranks_dp, requests // ranks_dp, width), "dp")
    hidden = make_hidden(attn, values, slot_rows)
    hidden = lax.all_gather(hidden, "dp", axis=0, tiled=True)

    share = requests // ranks_tp
    high = share // per_rank
    columns = 2 * units + 128 + 128 * ((groups + high - 1) // high)
    both = gate_up(
        hidden, norm_gain.reshape(-1, 128), w_gate, w_up, requests // ranks_dp, columns
    )
    both = swap(both.reshape(ranks_tp, share, columns), "tp")
    inner, slots = make_inner(both, units, model)
    inner = lax.all_gather(inner, "tp", axis=0, tiled=True)
    ffn = swap(project_down(inner, w_down, ranks), ("dp", "tp"))
    return make_layer(ffn, slots, per_rank, model)


def solution(mesh):
    placed = (
        P(("dp", "tp"), None),
        P(("dp", "tp"), None),
        P(("dp", "tp"), None),
        P(),
        P(("dp", "tp"), None, None),
        P("dp", "tp"),
        P(),
        P("tp", "dp"),
        P("tp", "dp"),
        P("dp", "tp"),
    )
    return jax.shard_map(
        local, mesh=mesh, in_specs=placed, out_specs=P(("dp", "tp"), None), check_vma=False
    )
```

```python
import functools

import jax
import jax.numpy as jnp
from jax import lax
from jax.experimental import pallas as pl
from jax.experimental.pallas import tpu as pltpu
from jax.sharding import PartitionSpec as P

C = 512
BLOCK_TOKENS = 64
TILE = 1024

score_scale = 192.0 ** (-0.5)
log2_e = 1.4426950408889634
negative = -1e30


def attention_kernel(
    lens_ref,
    q_ref,
    cache_ref,
    out_ref,
    held,
    score0,
    score1,
    weight0,
    weight1,
    keep0,
    keep1,
    acc,
    done,
    best,
    mass,
    lo,
    hi,
    first,
    last,
    sems,
):
    nreq, heads, _ = q_ref.shape
    tile = held.shape[2]
    factor = score_scale * log2_e

    rank = lax.axis_index("dp") * lax.axis_size("tp") + lax.axis_index("tp")
    begin = jnp.int32(0)
    pairs = jnp.int32(0)
    for r in range(nreq):
        length = lens_ref[rank * nreq + r]
        lo[r] = begin
        hi[r] = begin + length
        first[r] = begin // tile
        last[r] = (begin + length - 1) // tile
        pairs = pairs + (last[r] - first[r] + 1)
        begin = begin + ((length + BLOCK_TOKENS - 1) // BLOCK_TOKENS) * BLOCK_TOKENS
    used = last[nreq - 1] + 1

    def copy(i):
        return pltpu.make_async_copy(
            cache_ref.at[:, pl.ds(pl.multiple_of(i * tile, tile), tile)], held.at[i], sems.at[i]
        )

    @pl.loop(0, used)
    def _(i):
        copy(i).start()

    acc[...] = jnp.zeros_like(acc)
    best[...] = jnp.full_like(best, negative)
    mass[...] = jnp.zeros_like(mass)
    weight1[...] = jnp.zeros_like(weight1)
    keep1[...] = jnp.ones_like(keep1)

    def advance(p, r, i):
        live = p + 1 < pairs
        step = (i == last[r]) & live
        nr = jnp.where(step, r + 1, r)
        ni = jnp.where(step, first[nr], jnp.where(live, i + 1, i))
        return nr, ni, live

    def fetch(r, i, live):
        fresh = live & ((r == 0) | (i > last[jnp.maximum(r - 1, 0)]))

        @pl.when(fresh)
        def _():
            copy(i).wait()

    def scores(r, i, live, target):
        begin_at = jnp.where(live, lo[r], 0)
        end_at = jnp.where(live, hi[r], 0)
        s = jnp.dot(q_ref[r], held[i], preferred_element_type=jnp.float32)
        token = i * tile + lax.broadcasted_iota(jnp.int32, (1, tile), 1)
        target[...] = jnp.where((token >= begin_at) & (token < end_at), s, negative)

    def soften(r, source, weights, keeps):
        s = source[...]
        old = best[r]
        new = jnp.maximum(old, jnp.max(s, axis=1, keepdims=True))
        weight = jnp.exp2((s - new[:, :1]) * factor)
        keep = jnp.exp2((old - new) * factor)
        part = weight[:, :128]
        for at in range(128, tile, 128):
            part = part + weight[:, at : at + 128]
        mass[r] = mass[r] * keep + part
        best[r] = new
        weights[...] = weight.astype(weights.dtype)
        keeps[...] = keep.T[:8, :]

    def gather(r, i, weights, keeps):
        values = lax.dot_general(
            held[i, :C, :],
            weights[...],
            (((1,), (1,)), ((), ())),
            preferred_element_type=jnp.float32,
        )
        acc[r] = acc[r] * keeps[:1, :] + values

    zero = jnp.int32(0)
    fetch(zero, zero, pairs > 0)
    scores(zero, zero, pairs > 0, score0)

    def step(j, carry):
        r0, i0, r1, i1 = carry
        p = 2 * j
        r2, i2, live2 = advance(p, r1, i1)
        r3, i3, live3 = advance(p + 1, r2, i2)
        fetch(r2, i2, live2)
        fetch(r3, i3, live3)
        gather(r0, i0, weight1, keep1)
        scores(r2, i2, live2, score1)
        soften(r1, score0, weight0, keep0)
        gather(r1, i1, weight0, keep0)
        scores(r3, i3, live3, score0)
        soften(r2, score1, weight1, keep1)
        return r2, i2, r3, i3

    r0, i0, _, _ = lax.fori_loop(0, (pairs + 1) // 2, step, (zero, zero, zero, zero))
    gather(r0, i0, weight1, keep1)

    share = heads // out_ref.shape[0]
    for r in range(nreq):
        total = jnp.sum(mass[r], axis=1, keepdims=True)
        score0[:, :C] = acc[r].T / total
        for d in range(out_ref.shape[0]):
            done[d, r * share : (r + 1) * share, :] = score0[d * share : (d + 1) * share, :C]
    out_ref[...] = done[...].astype(out_ref.dtype)


def kernel_params(limit):
    return pltpu.CompilerParams(vmem_limit_bytes=limit * 1024 * 1024)


def in_vmem(count):
    return [pl.BlockSpec(memory_space=pltpu.VMEM)] * count


def fetched(weight):
    return pltpu.with_memory_space_constraint(weight, pltpu.VMEM)


def attend(lengths, queries, cache_t, ranks):
    nreq, heads, width = queries.shape
    tokens = cache_t.shape[1]
    tile = TILE
    tiles = tokens // tile
    return pl.pallas_call(
        attention_kernel,
        out_shape=jax.ShapeDtypeStruct((ranks, nreq * heads // ranks, C), jnp.bfloat16),
        in_specs=[pl.BlockSpec(memory_space=pltpu.SMEM)]
        + in_vmem(1)
        + [pl.BlockSpec(memory_space=pltpu.HBM)],
        out_specs=pl.BlockSpec(memory_space=pltpu.VMEM),
        scratch_shapes=[
            pltpu.VMEM((tiles, width, tile), jnp.bfloat16),
            pltpu.VMEM((heads, tile), jnp.float32),
            pltpu.VMEM((heads, tile), jnp.float32),
            pltpu.VMEM((heads, tile), jnp.bfloat16),
            pltpu.VMEM((heads, tile), jnp.bfloat16),
            pltpu.VMEM((8, heads), jnp.float32),
            pltpu.VMEM((8, heads), jnp.float32),
            pltpu.VMEM((nreq, C, heads), jnp.float32),
            pltpu.VMEM((ranks, nreq * heads // ranks, C), jnp.float32),
            pltpu.VMEM((nreq, heads, 128), jnp.float32),
            pltpu.VMEM((nreq, heads, 128), jnp.float32),
            pltpu.SMEM((nreq,), jnp.int32),
            pltpu.SMEM((nreq,), jnp.int32),
            pltpu.SMEM((nreq,), jnp.int32),
            pltpu.SMEM((nreq,), jnp.int32),
            pltpu.SemaphoreType.DMA((tiles,)),
        ],
        compiler_params=kernel_params(26),
        cost_estimate=pl.CostEstimate(
            flops=2 * heads * tokens * (width + C),
            bytes_accessed=2 * tokens * width,
            transcendentals=heads * tokens,
        ),
        name="attention",
    )(lengths, queries, pltpu.with_memory_space_constraint(cache_t, pltpu.HBM))


def head_values_kernel(latent_ref, w_ref, out_ref, values):
    heads, _, wide = w_ref.shape
    requests = out_ref.shape[0]
    latent = latent_ref[...]
    for h in range(heads):
        values[...] = jnp.dot(latent, w_ref[h], preferred_element_type=jnp.float32)
        picked = values[pl.ds(h, requests, stride=heads), :]
        out_ref[:, h * wide : (h + 1) * wide] = picked.astype(out_ref.dtype)


def head_values(latent, w_uv):
    heads, _, wide = w_uv.shape
    requests = latent.shape[0] // heads
    return pl.pallas_call(
        head_values_kernel,
        out_shape=jax.ShapeDtypeStruct((requests, heads * wide), jnp.bfloat16),
        in_specs=in_vmem(2),
        out_specs=pl.BlockSpec(memory_space=pltpu.VMEM),
        scratch_shapes=[pltpu.VMEM((latent.shape[0], wide), jnp.float32)],
        compiler_params=kernel_params(12),
        name="head_values",
    )(latent, w_uv)


def split_kernel(rows_ref, *out_refs):
    width = out_refs[0].shape[1]
    me = lax.axis_index("tp")
    for k, out_ref in enumerate(out_refs):
        start = pl.multiple_of((me ^ k) * width, 128)
        out_ref[...] = rows_ref[:, pl.ds(start, width)]


def split_columns(rows, ranks):
    shape = jax.ShapeDtypeStruct((rows.shape[0], rows.shape[1] // ranks), rows.dtype)
    return pl.pallas_call(
        split_kernel,
        out_shape=[shape] * ranks,
        in_specs=in_vmem(1),
        out_specs=in_vmem(ranks),
        compiler_params=kernel_params(8),
        name="split_columns",
    )(rows)


def across(piece, axis, distance):
    return lax.ppermute(piece, axis, [(k, k ^ distance) for k in range(lax.axis_size(axis))])


def output_kernel(values_ref, w_ref, out_ref, total):
    steps, _, depth = values_ref.shape
    requests = out_ref.shape[0]
    for k in range(steps):
        term = jnp.dot(
            values_ref[k],
            w_ref[k * depth : (k + 1) * depth, :],
            preferred_element_type=jnp.float32,
        )
        if k == 0:
            total[...] = term
        else:
            total[...] += term
    out_ref[...] = total[...].astype(out_ref.dtype)


def project_out(values, w_o, requests):
    width = w_o.shape[1]
    return pl.pallas_call(
        output_kernel,
        out_shape=jax.ShapeDtypeStruct((requests, width), jnp.bfloat16),
        in_specs=in_vmem(2),
        out_specs=pl.BlockSpec(memory_space=pltpu.VMEM),
        scratch_shapes=[pltpu.VMEM((requests, width), jnp.float32)],
        compiler_params=kernel_params(12),
        name="project_out",
    )(values, fetched(w_o))


def hidden_kernel(parts_ref, *refs):
    *slices, out_ref, added = refs
    per_rank = slices[0].shape[0]
    me = lax.axis_index("tp")
    for k, piece in enumerate(slices):
        added[me ^ k] = piece[...].astype(jnp.float32)
    width = out_ref.shape[1]
    for at in range(0, width, 128):
        at = slice(at, at + 128)
        total = parts_ref[0, :, at].astype(jnp.float32)
        for d in range(1, parts_ref.shape[0]):
            total = total + parts_ref[d, :, at].astype(jnp.float32)
        terms = [added[s, :, at] for s in range(len(slices))]
        out_ref[:, at] = (total + jnp.concatenate(terms, 0)).astype(out_ref.dtype)


def make_hidden(parts, slices):
    return pl.pallas_call(
        hidden_kernel,
        out_shape=jax.ShapeDtypeStruct(parts.shape[1:], jnp.bfloat16),
        in_specs=in_vmem(1 + len(slices)),
        out_specs=pl.BlockSpec(memory_space=pltpu.VMEM),
        scratch_shapes=[pltpu.VMEM((len(slices),) + slices[0].shape, jnp.float32)],
        compiler_params=kernel_params(12),
        name="hidden",
    )(parts, *slices)


def gate_up_kernel(hidden_ref, gain_ref, gate_ref, up_ref, *refs):
    ranks = lax.axis_size("tp")
    *outs, scaled, gains, own = refs
    gate_outs, up_outs, rows_out = outs[:-ranks][0::2], outs[:-ranks][1::2], outs[-ranks:]
    requests, width = hidden_ref.shape
    units = gate_ref.shape[1]
    share = requests // ranks
    groups = width // 128
    me = lax.axis_index("tp")
    if len(gate_outs) == 1:
        orders = [[0 * me + t for t in range(ranks)]] * 2
    else:
        orders = [[me ^ 3, me ^ 1, me ^ 2, me], [me ^ 3, me ^ 2, me ^ 1, me]]

    gains[...] = gain_ref[...].astype(jnp.float32)
    squares = []
    for k, order in enumerate(orders[:1] if len(gate_outs) == 1 else orders):
        square = [jnp.zeros((share, 128), jnp.float32) for _ in order]
        for t, block in enumerate(order):
            start = pl.multiple_of(block * share, 16)
            for g in range(groups):
                at = slice(g * 128, (g + 1) * 128)
                x = hidden_ref[pl.ds(start, share), at].astype(jnp.float32)
                square[t] = square[t] + x * x
                gain = gains[pl.ds(me * groups + g, 1), :]
                scaled[k, t * share : (t + 1) * share, at] = (x * gain).astype(scaled.dtype)
        squares.append(square)
    square = jnp.sum(jnp.concatenate(squares[0], 0), 1, keepdims=True)
    top = square.astype(jnp.bfloat16).astype(jnp.float32)
    middle = (square - top).astype(jnp.bfloat16).astype(jnp.float32)
    low = square - top - middle
    lane = lax.broadcasted_iota(jnp.int32, (requests, 128), 1)
    digits = jnp.where(lane == 0, top, jnp.where(lane == 1, middle, jnp.where(lane == 2, low, 0.0)))

    def store(targets, at, value):
        rows = requests // len(targets)
        for n, target in enumerate(targets):
            block = value[n * rows : (n + 1) * rows].astype(target.dtype)
            target[:, at : at + value.shape[1]] = block

    store(gate_outs, units, digits)
    per_rank = own.shape[1]
    rows = ranks * per_rank
    start = pl.multiple_of(lax.axis_index("dp") * rows, 16)
    own[...] = (
        hidden_ref[pl.ds(start, rows), :].astype(jnp.float32).reshape(ranks, per_rank, width)
    )
    for k, target in enumerate(rows_out):
        target[...] = own[me ^ k].astype(target.dtype)

    chunk = units // 3
    for w_ref, left, targets in ((gate_ref, 0, gate_outs), (up_ref, scaled.shape[0] - 1, up_outs)):
        for at in range(0, units, chunk):
            term = jnp.dot(
                scaled[left], w_ref[:, at : at + chunk], preferred_element_type=jnp.float32
            )
            store(targets, at, term)


def gate_up(hidden, gain, w_gate, w_up, ranks_dp, ranks_tp, halves):
    requests, width = hidden.shape
    units = w_gate.shape[1]
    rows = requests // ranks_dp
    per_rank = rows // ranks_tp
    shapes = [
        jax.ShapeDtypeStruct((requests // halves, columns), jnp.bfloat16)
        for _ in range(halves)
        for columns in (units + 128, units)
    ] + [jax.ShapeDtypeStruct((per_rank, width), jnp.bfloat16)] * ranks_tp
    outs = pl.pallas_call(
        gate_up_kernel,
        out_shape=shapes,
        in_specs=in_vmem(4),
        out_specs=in_vmem(len(shapes)),
        scratch_shapes=[
            pltpu.VMEM((halves, requests, width), jnp.bfloat16),
            pltpu.VMEM(gain.shape, jnp.float32),
            pltpu.VMEM((ranks_tp, per_rank, width), jnp.float32),
        ],
        compiler_params=kernel_params(12),
        name="gate_up",
    )(hidden, gain, fetched(w_gate), fetched(w_up))
    return outs[: 2 * halves], outs[2 * halves :]


def halve_kernel(*refs):
    count = len(refs) // 4
    for n in range(count):
        kept, came, send, keep = refs[n], refs[count + n], refs[2 * count + n], refs[3 * count + n]
        rows = send.shape[0]
        for at in range(0, send.shape[1], 128):
            at = slice(at, at + 128)
            total = kept[:, at].astype(jnp.float32) + came[:, at].astype(jnp.float32)
            send[:, at] = total[:rows].astype(send.dtype)
            keep[:, at] = total[rows:]


def halve(kept, came):
    half = [(k.shape[0] // 2, k.shape[1]) for k in kept]
    outs = pl.pallas_call(
        halve_kernel,
        out_shape=[jax.ShapeDtypeStruct(shape, jnp.bfloat16) for shape in half]
        + [jax.ShapeDtypeStruct(shape, jnp.float32) for shape in half],
        in_specs=in_vmem(2 * len(kept)),
        out_specs=in_vmem(2 * len(kept)),
        compiler_params=kernel_params(12),
        name="halve",
    )(*kept, *came)
    return outs[: len(kept)], outs[len(kept) :]


def inner_kernel(model, *refs):
    *parts, out_ref = refs
    gates, ups = parts[0::2], parts[1::2]
    units = out_ref.shape[1]

    def total(parts, at):
        terms = [
            part[n, :, at].astype(jnp.float32) for part in parts for n in range(part.shape[0])
        ]
        return sum(terms[1:], terms[0])

    square = jnp.sum(total(gates, slice(units, units + 128)), 1, keepdims=True)
    factor = lax.rsqrt(square / model + 1e-06)
    for at in range(0, units, 128):
        at = slice(at, at + 128)
        gate = total(gates, at) * factor
        up = total(ups, at) * factor
        out_ref[:, at] = (gate / (1.0 + jnp.exp(-gate)) * up).astype(out_ref.dtype)


def make_inner(parts, units, model):
    return pl.pallas_call(
        functools.partial(inner_kernel, model),
        out_shape=jax.ShapeDtypeStruct((parts[0].shape[1], units), jnp.bfloat16),
        in_specs=in_vmem(len(parts)),
        out_specs=pl.BlockSpec(memory_space=pltpu.VMEM),
        compiler_params=kernel_params(12),
        name="inner",
    )(*parts)


def down_kernel(inner_ref, w_ref, out_ref, total):
    width = w_ref.shape[1]
    total[...] = jnp.dot(inner_ref[...], w_ref[...], preferred_element_type=jnp.float32)
    groups = width // 128
    per_rank = out_ref.shape[1] // groups
    for d in range(out_ref.shape[0]):
        pieces = [
            total[d * per_rank : (d + 1) * per_rank, g * 128 : (g + 1) * 128]
            for g in range(groups)
        ]
        out_ref[d] = jnp.concatenate(pieces, 0).astype(out_ref.dtype)


def project_down(inner, w_down, ranks):
    requests, units = inner.shape
    width = w_down.shape[1]
    return pl.pallas_call(
        down_kernel,
        out_shape=jax.ShapeDtypeStruct(
            (ranks, requests // ranks * (width // 128), 128), jnp.bfloat16
        ),
        in_specs=in_vmem(2),
        out_specs=pl.BlockSpec(memory_space=pltpu.VMEM),
        scratch_shapes=[pltpu.VMEM((requests, width), jnp.float32)],
        compiler_params=kernel_params(12),
        name="project_down",
    )(inner, fetched(w_down))


def layer_kernel(parts_ref, *refs):
    *slices, out_ref, total = refs
    ranks = len(slices)
    per_rank, model = out_ref.shape
    width = model // ranks
    groups = width // 128
    me = lax.axis_index("tp")
    for t in range(ranks):
        ffn = sum(
            parts_ref[d, :, :].astype(jnp.float32) for d in range(t, parts_ref.shape[0], ranks)
        )
        for g in range(groups):
            at = (t * groups + g) * 128
            total[:, at : at + 128] = ffn[g * per_rank : (g + 1) * per_rank, :]
    for k, piece in enumerate(slices):
        at = pl.ds(pl.multiple_of((me ^ k) * width, 128), width)
        total[:, at] += piece[...].astype(jnp.float32)
    out_ref[...] = total[...].astype(out_ref.dtype)


def make_layer(parts, slices, model):
    per_rank = slices[0].shape[0]
    return pl.pallas_call(
        layer_kernel,
        out_shape=jax.ShapeDtypeStruct((per_rank, model), jnp.bfloat16),
        in_specs=in_vmem(1 + len(slices)),
        out_specs=pl.BlockSpec(memory_space=pltpu.VMEM),
        scratch_shapes=[pltpu.VMEM((per_rank, model), jnp.float32)],
        compiler_params=kernel_params(12),
        name="layer",
    )(parts, *slices)


def swap(parts, axes):
    return lax.all_to_all(parts, axes, split_axis=0, concat_axis=0, tiled=True)


def local(
    residual, queries, paged_latent_cache, lengths, w_uv, w_o, norm_gain, w_gate, w_up, w_down
):
    ranks_dp = lax.axis_size("dp")
    ranks_tp = lax.axis_size("tp")
    ranks = ranks_dp * ranks_tp
    per_rank, model = residual.shape
    requests = per_rank * ranks
    row_length = paged_latent_cache.shape[1]
    heads_all = queries.shape[1] // row_length
    heads_here = w_uv.shape[0]
    units = w_gate.shape[1]
    width = w_o.shape[1]

    query = queries.reshape(per_rank, heads_all, row_length)
    latent = attend(lengths, query, paged_latent_cache.T, ranks)
    latent, residual, w_o, w_gate, w_up, w_down = lax.optimization_barrier(
        (latent, residual, w_o, w_gate, w_up, w_down)
    )
    added = split_columns(residual, ranks_tp)
    added = [added[0]] + [across(added[k], "tp", k) for k in range(1, ranks_tp)]
    latent = swap(latent, ("dp", "tp"))

    values = head_values(latent.reshape(requests * heads_here, C), w_uv)
    values = lax.all_gather(values, "tp", axis=0)
    attn = project_out(values, w_o, requests)
    attn = swap(attn.reshape(ranks_dp, requests // ranks_dp, width), "dp")
    hidden = make_hidden(attn, added)
    hidden = lax.all_gather(hidden, "dp", axis=0, tiled=True)

    halves = 2 if ranks_tp == 4 else 1
    parts, rows = gate_up(
        hidden, norm_gain.reshape(-1, 128), w_gate, w_up, ranks_dp, ranks_tp, halves
    )
    if halves == 2:
        gate_send, up_send, gate_keep, up_keep = parts
        came = [across(gate_send, "tp", 1), across(up_send, "tp", 2)]
        rows = [rows[0]] + [across(rows[k], "tp", k) for k in range(1, ranks_tp)]
        (gate_send, up_send), (gate_keep, up_keep) = halve([gate_keep, up_keep], came)
        parts = [gate_keep, up_keep, across(gate_send, "tp", 2), across(up_send, "tp", 1)]
        parts = [part[None] for part in parts]
    else:
        rows = [rows[0]] + [across(rows[k], "tp", k) for k in range(1, ranks_tp)]
        parts = [swap(part.reshape(ranks_tp, -1, part.shape[1]), "tp") for part in parts]
    inner = make_inner(parts, units, model)
    inner = lax.all_gather(inner, "tp", axis=0, tiled=True)
    ffn = swap(project_down(inner, w_down, ranks), ("dp", "tp"))
    return make_layer(ffn, rows, model)


def solution(mesh):
    placed = (
        P(("dp", "tp"), None),
        P(("dp", "tp"), None),
        P(("dp", "tp"), None),
        P(),
        P(("dp", "tp"), None, None),
        P("dp", "tp"),
        P(),
        P("tp", "dp"),
        P("tp", "dp"),
        P("dp", "tp"),
    )
    return jax.shard_map(
        local, mesh=mesh, in_specs=placed, out_specs=P(("dp", "tp"), None), check_vma=False
    )
```

```python
import functools

import jax
import jax.numpy as jnp
from jax import lax
from jax.experimental import pallas as pl
from jax.experimental.pallas import tpu as pltpu
from jax.sharding import PartitionSpec as P

C = 512
BLOCK_TOKENS = 64
TILE = 1024

score_scale = 192.0 ** (-0.5)
log2_e = 1.4426950408889634
negative = -1e30


def attention_kernel(
    lens_ref,
    q_ref,
    cache_ref,
    out_ref,
    held,
    score0,
    score1,
    weight0,
    weight1,
    keep0,
    keep1,
    acc,
    done,
    best,
    mass,
    lo,
    hi,
    first,
    last,
    sems,
):
    nreq, heads, _ = q_ref.shape
    tile = held.shape[2]
    factor = score_scale * log2_e

    rank = lax.axis_index("dp") * lax.axis_size("tp") + lax.axis_index("tp")
    begin = jnp.int32(0)
    pairs = jnp.int32(0)
    for r in range(nreq):
        length = lens_ref[rank * nreq + r]
        lo[r] = begin
        hi[r] = begin + length
        first[r] = begin // tile
        last[r] = (begin + length - 1) // tile
        pairs = pairs + (last[r] - first[r] + 1)
        begin = begin + ((length + BLOCK_TOKENS - 1) // BLOCK_TOKENS) * BLOCK_TOKENS
    used = last[nreq - 1] + 1

    def copy(i):
        return pltpu.make_async_copy(
            cache_ref.at[:, pl.ds(pl.multiple_of(i * tile, tile), tile)], held.at[i], sems.at[i]
        )

    @pl.loop(0, used)
    def _(i):
        copy(i).start()

    acc[...] = jnp.zeros_like(acc)
    best[...] = jnp.full_like(best, negative)
    mass[...] = jnp.zeros_like(mass)
    weight1[...] = jnp.zeros_like(weight1)
    keep1[...] = jnp.ones_like(keep1)

    def advance(p, r, i):
        live = p + 1 < pairs
        step = (i == last[r]) & live
        nr = jnp.where(step, r + 1, r)
        ni = jnp.where(step, first[nr], jnp.where(live, i + 1, i))
        return nr, ni, live

    def fetch(r, i, live):
        fresh = live & ((r == 0) | (i > last[jnp.maximum(r - 1, 0)]))

        @pl.when(fresh)
        def _():
            copy(i).wait()

    def scores(r, i, live, target):
        begin_at = jnp.where(live, lo[r], 0)
        end_at = jnp.where(live, hi[r], 0)
        s = jnp.dot(q_ref[r], held[i], preferred_element_type=jnp.float32)
        token = i * tile + lax.broadcasted_iota(jnp.int32, (1, tile), 1)
        target[...] = jnp.where((token >= begin_at) & (token < end_at), s, negative)

    def soften(r, source, weights, keeps):
        s = source[...]
        old = best[r]
        new = jnp.maximum(old, jnp.max(s, axis=1, keepdims=True))
        weight = jnp.exp2((s - new[:, :1]) * factor)
        keep = jnp.exp2((old - new) * factor)
        part = weight[:, :128]
        for at in range(128, tile, 128):
            part = part + weight[:, at : at + 128]
        mass[r] = mass[r] * keep + part
        best[r] = new
        weights[...] = weight.astype(weights.dtype)
        keeps[...] = keep

    def gather(r, i, weights, keeps):
        values = lax.dot_general(
            weights[...],
            held[i, :C, :],
            (((1,), (1,)), ((), ())),
            preferred_element_type=jnp.float32,
        )
        acc[r] = acc[r] * keeps[:, :1] + values

    zero = jnp.int32(0)
    fetch(zero, zero, pairs > 0)
    scores(zero, zero, pairs > 0, score0)

    def step(j, carry):
        r0, i0, r1, i1 = carry
        p = 2 * j
        r2, i2, live2 = advance(p, r1, i1)
        r3, i3, live3 = advance(p + 1, r2, i2)
        fetch(r2, i2, live2)
        fetch(r3, i3, live3)
        gather(r0, i0, weight1, keep1)
        scores(r2, i2, live2, score1)
        soften(r1, score0, weight0, keep0)
        gather(r1, i1, weight0, keep0)
        scores(r3, i3, live3, score0)
        soften(r2, score1, weight1, keep1)
        return r2, i2, r3, i3

    r0, i0, _, _ = lax.fori_loop(0, (pairs + 1) // 2, step, (zero, zero, zero, zero))
    gather(r0, i0, weight1, keep1)

    share = heads // out_ref.shape[0]
    for r in range(nreq):
        total = jnp.sum(mass[r], axis=1, keepdims=True)
        score0[:, :C] = acc[r] / total
        for d in range(out_ref.shape[0]):
            done[d, r * share : (r + 1) * share, :] = score0[d * share : (d + 1) * share, :C]
    out_ref[...] = done[...].astype(out_ref.dtype)


def kernel_params(limit):
    return pltpu.CompilerParams(vmem_limit_bytes=limit * 1024 * 1024)


def in_vmem(count):
    return [pl.BlockSpec(memory_space=pltpu.VMEM)] * count


def fetched(weight):
    return pltpu.with_memory_space_constraint(weight, pltpu.VMEM)


def attend(lengths, queries, cache_t, ranks):
    nreq, heads, width = queries.shape
    tokens = cache_t.shape[1]
    tile = TILE
    tiles = tokens // tile
    return pl.pallas_call(
        attention_kernel,
        out_shape=jax.ShapeDtypeStruct((ranks, nreq * heads // ranks, C), jnp.bfloat16),
        in_specs=[pl.BlockSpec(memory_space=pltpu.SMEM)]
        + in_vmem(1)
        + [pl.BlockSpec(memory_space=pltpu.HBM)],
        out_specs=pl.BlockSpec(memory_space=pltpu.VMEM),
        scratch_shapes=[
            pltpu.VMEM((tiles, width, tile), jnp.bfloat16),
            pltpu.VMEM((heads, tile), jnp.float32),
            pltpu.VMEM((heads, tile), jnp.float32),
            pltpu.VMEM((heads, tile), jnp.bfloat16),
            pltpu.VMEM((heads, tile), jnp.bfloat16),
            pltpu.VMEM((heads, 128), jnp.float32),
            pltpu.VMEM((heads, 128), jnp.float32),
            pltpu.VMEM((nreq, heads, C), jnp.float32),
            pltpu.VMEM((ranks, nreq * heads // ranks, C), jnp.float32),
            pltpu.VMEM((nreq, heads, 128), jnp.float32),
            pltpu.VMEM((nreq, heads, 128), jnp.float32),
            pltpu.SMEM((nreq,), jnp.int32),
            pltpu.SMEM((nreq,), jnp.int32),
            pltpu.SMEM((nreq,), jnp.int32),
            pltpu.SMEM((nreq,), jnp.int32),
            pltpu.SemaphoreType.DMA((tiles,)),
        ],
        compiler_params=kernel_params(26),
        cost_estimate=pl.CostEstimate(
            flops=2 * heads * tokens * (width + C),
            bytes_accessed=2 * tokens * width,
            transcendentals=heads * tokens,
        ),
        name="attention",
    )(
        pltpu.with_memory_space_constraint(lengths, pltpu.HBM),
        fetched(queries),
        pltpu.with_memory_space_constraint(cache_t, pltpu.HBM),
    )


def head_values_kernel(latent_ref, w_ref, out_ref, values):
    heads, _, wide = w_ref.shape
    requests = out_ref.shape[0]
    latent = latent_ref[...]
    for h in range(heads):
        values[...] = jnp.dot(latent, w_ref[h], preferred_element_type=jnp.float32)
        picked = values[pl.ds(h, requests, stride=heads), :]
        out_ref[:, h * wide : (h + 1) * wide] = picked.astype(out_ref.dtype)


def head_values(latent, w_uv):
    heads, _, wide = w_uv.shape
    requests = latent.shape[0] // heads
    return pl.pallas_call(
        head_values_kernel,
        out_shape=jax.ShapeDtypeStruct((requests, heads * wide), jnp.bfloat16),
        in_specs=in_vmem(2),
        out_specs=pl.BlockSpec(memory_space=pltpu.VMEM),
        scratch_shapes=[pltpu.VMEM((latent.shape[0], wide), jnp.float32)],
        compiler_params=kernel_params(12),
        name="head_values",
    )(latent, w_uv)


def split_kernel(rows_ref, *out_refs):
    width = out_refs[0].shape[1]
    me = lax.axis_index("tp")
    for k, out_ref in enumerate(out_refs):
        start = pl.multiple_of((me ^ k) * width, 128)
        out_ref[...] = rows_ref[:, pl.ds(start, width)]


def split_columns(rows, ranks):
    shape = jax.ShapeDtypeStruct((rows.shape[0], rows.shape[1] // ranks), rows.dtype)
    return pl.pallas_call(
        split_kernel,
        out_shape=[shape] * ranks,
        in_specs=in_vmem(1),
        out_specs=in_vmem(ranks),
        compiler_params=kernel_params(8),
        name="split_columns",
    )(rows)


def across(piece, axis, distance):
    return lax.ppermute(piece, axis, [(k, k ^ distance) for k in range(lax.axis_size(axis))])


def output_kernel(values_ref, w_ref, out_ref, total):
    steps, _, depth = values_ref.shape
    requests = out_ref.shape[0]
    for k in range(steps):
        term = jnp.dot(
            values_ref[k],
            w_ref[k * depth : (k + 1) * depth, :],
            preferred_element_type=jnp.float32,
        )
        if k == 0:
            total[...] = term
        else:
            total[...] += term
    out_ref[...] = total[...].astype(out_ref.dtype)


def project_out(values, w_o, requests):
    width = w_o.shape[1]
    return pl.pallas_call(
        output_kernel,
        out_shape=jax.ShapeDtypeStruct((requests, width), jnp.bfloat16),
        in_specs=in_vmem(2),
        out_specs=pl.BlockSpec(memory_space=pltpu.VMEM),
        scratch_shapes=[pltpu.VMEM((requests, width), jnp.float32)],
        compiler_params=kernel_params(12),
        name="project_out",
    )(values, fetched(w_o))


def hidden_kernel(parts_ref, *refs):
    *slices, out_ref, added = refs
    per_rank = slices[0].shape[0]
    me = lax.axis_index("tp")
    for k, piece in enumerate(slices):
        added[me ^ k] = piece[...].astype(jnp.float32)
    width = out_ref.shape[1]
    for at in range(0, width, 128):
        at = slice(at, at + 128)
        total = parts_ref[0, :, at].astype(jnp.float32)
        for d in range(1, parts_ref.shape[0]):
            total = total + parts_ref[d, :, at].astype(jnp.float32)
        terms = [added[s, :, at] for s in range(len(slices))]
        out_ref[:, at] = (total + jnp.concatenate(terms, 0)).astype(out_ref.dtype)


def make_hidden(parts, slices):
    return pl.pallas_call(
        hidden_kernel,
        out_shape=jax.ShapeDtypeStruct(parts.shape[1:], jnp.bfloat16),
        in_specs=in_vmem(1 + len(slices)),
        out_specs=pl.BlockSpec(memory_space=pltpu.VMEM),
        scratch_shapes=[pltpu.VMEM((len(slices),) + slices[0].shape, jnp.float32)],
        compiler_params=kernel_params(12),
        name="hidden",
    )(parts, *slices)


def gate_up_kernel(hidden_ref, gain_ref, gate_ref, up_ref, *refs):
    ranks = lax.axis_size("tp")
    *outs, scaled, gains, own = refs
    gate_outs, up_outs, rows_out = outs[:-ranks][0::2], outs[:-ranks][1::2], outs[-ranks:]
    requests, width = hidden_ref.shape
    units = gate_ref.shape[1]
    share = requests // ranks
    groups = width // 128
    me = lax.axis_index("tp")
    if len(gate_outs) == 1:
        orders = [[0 * me + t for t in range(ranks)]] * 2
    else:
        orders = [[me ^ 3, me ^ 1, me ^ 2, me], [me ^ 3, me ^ 2, me ^ 1, me]]

    gains[...] = gain_ref[...].astype(jnp.float32)
    squares = []
    for k, order in enumerate(orders[:1] if len(gate_outs) == 1 else orders):
        square = [jnp.zeros((share, 128), jnp.float32) for _ in order]
        for t, block in enumerate(order):
            start = pl.multiple_of(block * share, 16)
            for g in range(groups):
                at = slice(g * 128, (g + 1) * 128)
                x = hidden_ref[pl.ds(start, share), at].astype(jnp.float32)
                square[t] = square[t] + x * x
                gain = gains[pl.ds(me * groups + g, 1), :]
                scaled[k, t * share : (t + 1) * share, at] = (x * gain).astype(scaled.dtype)
        squares.append(square)
    square = jnp.sum(jnp.concatenate(squares[0], 0), 1, keepdims=True)
    top = square.astype(jnp.bfloat16).astype(jnp.float32)
    middle = (square - top).astype(jnp.bfloat16).astype(jnp.float32)
    low = square - top - middle
    lane = lax.broadcasted_iota(jnp.int32, (requests, 128), 1)
    digits = jnp.where(lane == 0, top, jnp.where(lane == 1, middle, jnp.where(lane == 2, low, 0.0)))

    def store(targets, at, value):
        rows = requests // len(targets)
        for n, target in enumerate(targets):
            block = value[n * rows : (n + 1) * rows].astype(target.dtype)
            target[:, at : at + value.shape[1]] = block

    store(gate_outs, units, digits)
    per_rank = own.shape[1]
    rows = ranks * per_rank
    start = pl.multiple_of(lax.axis_index("dp") * rows, 16)
    own[...] = (
        hidden_ref[pl.ds(start, rows), :].astype(jnp.float32).reshape(ranks, per_rank, width)
    )
    for k, target in enumerate(rows_out):
        target[...] = own[me ^ k].astype(target.dtype)

    chunk = units // 3
    for w_ref, left, targets in ((gate_ref, 0, gate_outs), (up_ref, scaled.shape[0] - 1, up_outs)):
        for at in range(0, units, chunk):
            term = jnp.dot(
                scaled[left], w_ref[:, at : at + chunk], preferred_element_type=jnp.float32
            )
            store(targets, at, term)


def gate_up(hidden, gain, w_gate, w_up, ranks_dp, ranks_tp, halves):
    requests, width = hidden.shape
    units = w_gate.shape[1]
    rows = requests // ranks_dp
    per_rank = rows // ranks_tp
    shapes = [
        jax.ShapeDtypeStruct((requests // halves, columns), jnp.bfloat16)
        for _ in range(halves)
        for columns in (units + 128, units)
    ] + [jax.ShapeDtypeStruct((per_rank, width), jnp.bfloat16)] * ranks_tp
    outs = pl.pallas_call(
        gate_up_kernel,
        out_shape=shapes,
        in_specs=in_vmem(4),
        out_specs=in_vmem(len(shapes)),
        scratch_shapes=[
            pltpu.VMEM((halves, requests, width), jnp.bfloat16),
            pltpu.VMEM(gain.shape, jnp.float32),
            pltpu.VMEM((ranks_tp, per_rank, width), jnp.float32),
        ],
        compiler_params=kernel_params(12),
        name="gate_up",
    )(hidden, gain, fetched(w_gate), fetched(w_up))
    return outs[: 2 * halves], outs[2 * halves :]


def halve_kernel(*refs):
    count = len(refs) // 4
    for n in range(count):
        kept, came, send, keep = refs[n], refs[count + n], refs[2 * count + n], refs[3 * count + n]
        rows = send.shape[0]
        for at in range(0, send.shape[1], 128):
            at = slice(at, at + 128)
            total = kept[:, at].astype(jnp.float32) + came[:, at].astype(jnp.float32)
            send[:, at] = total[:rows].astype(send.dtype)
            keep[:, at] = total[rows:]


def halve(kept, came):
    half = [(k.shape[0] // 2, k.shape[1]) for k in kept]
    outs = pl.pallas_call(
        halve_kernel,
        out_shape=[jax.ShapeDtypeStruct(shape, jnp.bfloat16) for shape in half]
        + [jax.ShapeDtypeStruct(shape, jnp.float32) for shape in half],
        in_specs=in_vmem(2 * len(kept)),
        out_specs=in_vmem(2 * len(kept)),
        compiler_params=kernel_params(12),
        name="halve",
    )(*kept, *came)
    return outs[: len(kept)], outs[len(kept) :]


def inner_kernel(model, *refs):
    *parts, out_ref = refs
    gates, ups = parts[0::2], parts[1::2]
    units = out_ref.shape[1]

    def total(parts, at):
        terms = [
            part[n, :, at].astype(jnp.float32) for part in parts for n in range(part.shape[0])
        ]
        return sum(terms[1:], terms[0])

    square = jnp.sum(total(gates, slice(units, units + 128)), 1, keepdims=True)
    factor = lax.rsqrt(square / model + 1e-06)
    for at in range(0, units, 128):
        at = slice(at, at + 128)
        gate = total(gates, at) * factor
        up = total(ups, at) * factor
        out_ref[:, at] = (gate / (1.0 + jnp.exp(-gate)) * up).astype(out_ref.dtype)


def make_inner(parts, units, model):
    return pl.pallas_call(
        functools.partial(inner_kernel, model),
        out_shape=jax.ShapeDtypeStruct((parts[0].shape[1], units), jnp.bfloat16),
        in_specs=in_vmem(len(parts)),
        out_specs=pl.BlockSpec(memory_space=pltpu.VMEM),
        compiler_params=kernel_params(12),
        name="inner",
    )(*parts)


def down_kernel(inner_ref, w_ref, out_ref, total):
    width = w_ref.shape[1]
    total[...] = jnp.dot(inner_ref[...], w_ref[...], preferred_element_type=jnp.float32)
    groups = width // 128
    per_rank = out_ref.shape[1] // groups
    for d in range(out_ref.shape[0]):
        pieces = [
            total[d * per_rank : (d + 1) * per_rank, g * 128 : (g + 1) * 128]
            for g in range(groups)
        ]
        out_ref[d] = jnp.concatenate(pieces, 0).astype(out_ref.dtype)


def project_down(inner, w_down, ranks):
    requests, units = inner.shape
    width = w_down.shape[1]
    return pl.pallas_call(
        down_kernel,
        out_shape=jax.ShapeDtypeStruct(
            (ranks, requests // ranks * (width // 128), 128), jnp.bfloat16
        ),
        in_specs=in_vmem(2),
        out_specs=pl.BlockSpec(memory_space=pltpu.VMEM),
        scratch_shapes=[pltpu.VMEM((requests, width), jnp.float32)],
        compiler_params=kernel_params(12),
        name="project_down",
    )(inner, fetched(w_down))


def layer_kernel(parts_ref, *refs):
    *slices, out_ref, total = refs
    ranks = len(slices)
    per_rank, model = out_ref.shape
    width = model // ranks
    groups = width // 128
    me = lax.axis_index("tp")
    for t in range(ranks):
        ffn = sum(
            parts_ref[d, :, :].astype(jnp.float32) for d in range(t, parts_ref.shape[0], ranks)
        )
        for g in range(groups):
            at = (t * groups + g) * 128
            total[:, at : at + 128] = ffn[g * per_rank : (g + 1) * per_rank, :]
    for k, piece in enumerate(slices):
        at = pl.ds(pl.multiple_of((me ^ k) * width, 128), width)
        total[:, at] += piece[...].astype(jnp.float32)
    out_ref[...] = total[...].astype(out_ref.dtype)


def make_layer(parts, slices, model):
    per_rank = slices[0].shape[0]
    return pl.pallas_call(
        layer_kernel,
        out_shape=jax.ShapeDtypeStruct((per_rank, model), jnp.bfloat16),
        in_specs=in_vmem(1 + len(slices)),
        out_specs=pl.BlockSpec(memory_space=pltpu.VMEM),
        scratch_shapes=[pltpu.VMEM((per_rank, model), jnp.float32)],
        compiler_params=kernel_params(12),
        name="layer",
    )(parts, *slices)


def swap(parts, axes):
    return lax.all_to_all(parts, axes, split_axis=0, concat_axis=0, tiled=True)


def local(
    residual, queries, paged_latent_cache, lengths, w_uv, w_o, norm_gain, w_gate, w_up, w_down
):
    ranks_dp = lax.axis_size("dp")
    ranks_tp = lax.axis_size("tp")
    ranks = ranks_dp * ranks_tp
    per_rank, model = residual.shape
    requests = per_rank * ranks
    row_length = paged_latent_cache.shape[1]
    heads_all = queries.shape[1] // row_length
    heads_here = w_uv.shape[0]
    units = w_gate.shape[1]
    width = w_o.shape[1]

    query = queries.reshape(per_rank, heads_all, row_length)
    latent = attend(lengths, query, paged_latent_cache.T, ranks)
    latent, residual = lax.optimization_barrier((latent, residual))
    added = split_columns(residual, ranks_tp)
    added = [added[0]] + [across(added[k], "tp", k) for k in range(1, ranks_tp)]
    latent = swap(latent, ("dp", "tp"))

    values = head_values(latent.reshape(requests * heads_here, C), w_uv)
    values = lax.all_gather(values, "tp", axis=0)
    attn = project_out(values, w_o, requests)
    attn, added = lax.optimization_barrier((attn, added))
    attn = swap(attn.reshape(ranks_dp, requests // ranks_dp, width), "dp")
    hidden = make_hidden(attn, added)
    hidden = lax.all_gather(hidden, "dp", axis=0, tiled=True)

    halves = 2 if ranks_tp == 4 else 1
    parts, rows = gate_up(
        hidden, norm_gain.reshape(-1, 128), w_gate, w_up, ranks_dp, ranks_tp, halves
    )
    if halves == 2:
        gate_send, up_send, gate_keep, up_keep = parts
        came = [across(gate_send, "tp", 1), across(up_send, "tp", 2)]
        rows = [rows[0]] + [across(rows[k], "tp", k) for k in range(1, ranks_tp)]
        (gate_send, up_send), (gate_keep, up_keep) = halve([gate_keep, up_keep], came)
        parts = [gate_keep, up_keep, across(gate_send, "tp", 2), across(up_send, "tp", 1)]
        parts = [part[None] for part in parts]
    else:
        rows = [rows[0]] + [across(rows[k], "tp", k) for k in range(1, ranks_tp)]
        parts = [swap(part.reshape(ranks_tp, -1, part.shape[1]), "tp") for part in parts]
    inner = make_inner(parts, units, model)
    inner, rows = lax.optimization_barrier((inner, rows))
    inner = lax.all_gather(inner, "tp", axis=0, tiled=True)
    ffn = swap(project_down(inner, w_down, ranks), ("dp", "tp"))
    return make_layer(ffn, rows, model)


def solution(mesh):
    placed = (
        P(("dp", "tp"), None),
        P(("dp", "tp"), None),
        P(("dp", "tp"), None),
        P(),
        P(("dp", "tp"), None, None),
        P("dp", "tp"),
        P(),
        P("tp", "dp"),
        P("tp", "dp"),
        P("dp", "tp"),
    )
    return jax.shard_map(
        local, mesh=mesh, in_specs=placed, out_specs=P(("dp", "tp"), None), check_vma=False
    )
```

```python
import functools

import jax
import jax.numpy as jnp
from jax import lax
from jax.experimental import pallas as pl
from jax.experimental.pallas import tpu as pltpu
from jax.sharding import PartitionSpec as P

C = 512
BLOCK_TOKENS = 64
TILE = 1024

score_scale = 192.0 ** (-0.5)
log2_e = 1.4426950408889634
negative = -1e30


def attention_kernel(
    lens_ref,
    q_ref,
    cache_ref,
    out_ref,
    held,
    score0,
    score1,
    weight0,
    weight1,
    keep0,
    keep1,
    acc,
    done,
    best,
    mass,
    lo,
    hi,
    first,
    last,
    sems,
):
    nreq, heads, _ = q_ref.shape
    tile = held.shape[2]
    factor = score_scale * log2_e

    rank = lax.axis_index("dp") * lax.axis_size("tp") + lax.axis_index("tp")
    begin = jnp.int32(0)
    pairs = jnp.int32(0)
    for r in range(nreq):
        length = lens_ref[rank * nreq + r]
        lo[r] = begin
        hi[r] = begin + length
        first[r] = begin // tile
        last[r] = (begin + length - 1) // tile
        pairs = pairs + (last[r] - first[r] + 1)
        begin = begin + ((length + BLOCK_TOKENS - 1) // BLOCK_TOKENS) * BLOCK_TOKENS
    used = last[nreq - 1] + 1

    def copy(i):
        return pltpu.make_async_copy(
            cache_ref.at[:, pl.ds(pl.multiple_of(i * tile, tile), tile)], held.at[i], sems.at[i]
        )

    @pl.loop(0, used)
    def _(i):
        copy(i).start()

    acc[...] = jnp.zeros_like(acc)
    best[...] = jnp.full_like(best, negative)
    mass[...] = jnp.zeros_like(mass)
    weight1[...] = jnp.zeros_like(weight1)
    keep1[...] = jnp.ones_like(keep1)

    def advance(p, r, i):
        live = p + 1 < pairs
        step = (i == last[r]) & live
        nr = jnp.where(step, r + 1, r)
        ni = jnp.where(step, first[nr], jnp.where(live, i + 1, i))
        return nr, ni, live

    def fetch(r, i, live):
        fresh = live & ((r == 0) | (i > last[jnp.maximum(r - 1, 0)]))

        @pl.when(fresh)
        def _():
            copy(i).wait()

    def scores(r, i, live, target):
        begin_at = jnp.where(live, lo[r], 0)
        end_at = jnp.where(live, hi[r], 0)
        s = jnp.dot(q_ref[r], held[i], preferred_element_type=jnp.float32)
        token = i * tile + lax.broadcasted_iota(jnp.int32, (1, tile), 1)
        target[...] = jnp.where((token >= begin_at) & (token < end_at), s, negative)

    def soften(r, source, weights, keeps):
        s = source[...]
        old = best[r]
        new = jnp.maximum(old, jnp.max(s, axis=1, keepdims=True))
        weight = jnp.exp2((s - new[:, :1]) * factor)
        keep = jnp.exp2((old - new) * factor)
        part = weight[:, :128]
        for at in range(128, tile, 128):
            part = part + weight[:, at : at + 128]
        mass[r] = mass[r] * keep + part
        best[r] = new
        weights[...] = weight.astype(weights.dtype)
        keeps[...] = keep.T[:8, :]

    def gather(r, i, weights, keeps):
        values = lax.dot_general(
            held[i, :C, :],
            weights[...],
            (((1,), (1,)), ((), ())),
            preferred_element_type=jnp.float32,
        )
        acc[r] = acc[r] * keeps[:1, :] + values

    zero = jnp.int32(0)
    fetch(zero, zero, pairs > 0)
    scores(zero, zero, pairs > 0, score0)

    def step(j, carry):
        r0, i0, r1, i1 = carry
        p = 2 * j
        r2, i2, live2 = advance(p, r1, i1)
        r3, i3, live3 = advance(p + 1, r2, i2)
        fetch(r2, i2, live2)
        fetch(r3, i3, live3)
        gather(r0, i0, weight1, keep1)
        scores(r2, i2, live2, score1)
        soften(r1, score0, weight0, keep0)
        gather(r1, i1, weight0, keep0)
        scores(r3, i3, live3, score0)
        soften(r2, score1, weight1, keep1)
        return r2, i2, r3, i3

    r0, i0, _, _ = lax.fori_loop(0, (pairs + 1) // 2, step, (zero, zero, zero, zero))
    gather(r0, i0, weight1, keep1)

    share = heads // out_ref.shape[0]
    for r in range(nreq):
        total = jnp.sum(mass[r], axis=1, keepdims=True)
        score0[:, :C] = acc[r].T / total
        for d in range(out_ref.shape[0]):
            done[d, r * share : (r + 1) * share, :] = score0[d * share : (d + 1) * share, :C]
    out_ref[...] = done[...].astype(out_ref.dtype)


def kernel_params(limit):
    return pltpu.CompilerParams(vmem_limit_bytes=limit * 1024 * 1024)


def in_vmem(count):
    return [pl.BlockSpec(memory_space=pltpu.VMEM)] * count


def fetched(weight):
    return pltpu.with_memory_space_constraint(weight, pltpu.VMEM)


def attend(lengths, queries, cache_t, ranks):
    nreq, heads, width = queries.shape
    tokens = cache_t.shape[1]
    tile = TILE
    tiles = tokens // tile
    return pl.pallas_call(
        attention_kernel,
        out_shape=jax.ShapeDtypeStruct((ranks, nreq * heads // ranks, C), jnp.bfloat16),
        in_specs=[pl.BlockSpec(memory_space=pltpu.SMEM)]
        + in_vmem(1)
        + [pl.BlockSpec(memory_space=pltpu.HBM)],
        out_specs=pl.BlockSpec(memory_space=pltpu.VMEM),
        scratch_shapes=[
            pltpu.VMEM((tiles, width, tile), jnp.bfloat16),
            pltpu.VMEM((heads, tile), jnp.float32),
            pltpu.VMEM((heads, tile), jnp.float32),
            pltpu.VMEM((heads, tile), jnp.bfloat16),
            pltpu.VMEM((heads, tile), jnp.bfloat16),
            pltpu.VMEM((8, heads), jnp.float32),
            pltpu.VMEM((8, heads), jnp.float32),
            pltpu.VMEM((nreq, C, heads), jnp.float32),
            pltpu.VMEM((ranks, nreq * heads // ranks, C), jnp.float32),
            pltpu.VMEM((nreq, heads, 128), jnp.float32),
            pltpu.VMEM((nreq, heads, 128), jnp.float32),
            pltpu.SMEM((nreq,), jnp.int32),
            pltpu.SMEM((nreq,), jnp.int32),
            pltpu.SMEM((nreq,), jnp.int32),
            pltpu.SMEM((nreq,), jnp.int32),
            pltpu.SemaphoreType.DMA((tiles,)),
        ],
        compiler_params=kernel_params(26),
        cost_estimate=pl.CostEstimate(
            flops=2 * heads * tokens * (width + C),
            bytes_accessed=2 * tokens * width,
            transcendentals=heads * tokens,
        ),
        name="attention",
    )(
        pltpu.with_memory_space_constraint(lengths, pltpu.HBM),
        fetched(queries),
        pltpu.with_memory_space_constraint(cache_t, pltpu.HBM),
    )


def head_values_kernel(latent_ref, w_ref, residual_ref, out_ref, values, slots):
    heads, _, wide = w_ref.shape
    per_rank, model = residual_ref.shape
    requests = latent_ref.shape[0] // heads
    latent = latent_ref[...]
    for h in range(heads):
        values[...] = jnp.dot(latent, w_ref[h], preferred_element_type=jnp.float32)
        picked = values[pl.ds(h, requests, stride=heads), :]
        out_ref[:requests, h * wide : (h + 1) * wide] = picked.astype(out_ref.dtype)
    ranks = lax.axis_size("tp")
    groups = model // ranks // 128
    rows = (out_ref.shape[0] - requests) // ranks
    across = out_ref.shape[1] // 128
    slots[...] = jnp.zeros_like(slots)
    for t in range(ranks):
        for g in range(groups):
            at = (t * groups + g) * 128
            row = t * rows + (g // across) * per_rank
            column = (g % across) * 128
            slots[row : row + per_rank, column : column + 128] = residual_ref[
                :, at : at + 128
            ].astype(jnp.float32)
    out_ref[requests:, :] = slots[...].astype(out_ref.dtype)


def head_values(latent, w_uv, residual, slot_rows):
    heads, _, wide = w_uv.shape
    requests = latent.shape[0] // heads
    return pl.pallas_call(
        head_values_kernel,
        out_shape=jax.ShapeDtypeStruct((requests + slot_rows, heads * wide), jnp.bfloat16),
        in_specs=in_vmem(3),
        out_specs=pl.BlockSpec(memory_space=pltpu.VMEM),
        scratch_shapes=[
            pltpu.VMEM((latent.shape[0], wide), jnp.float32),
            pltpu.VMEM((slot_rows, heads * wide), jnp.float32),
        ],
        compiler_params=kernel_params(12),
        name="head_values",
    )(latent, w_uv, residual)


def from_distance(piece, axis, distance):
    return lax.ppermute(piece, axis, [(k, k ^ distance) for k in range(lax.axis_size(axis))])


def output_kernel(values_ref, w_ref, out_ref, total):
    steps, _, depth = values_ref.shape
    requests = out_ref.shape[0]
    for k in range(steps):
        term = jnp.dot(
            values_ref[k, :requests, :],
            w_ref[k * depth : (k + 1) * depth, :],
            preferred_element_type=jnp.float32,
        )
        if k == 0:
            total[...] = term
        else:
            total[...] += term
    out_ref[...] = total[...].astype(out_ref.dtype)


def project_out(values, w_o, requests):
    width = w_o.shape[1]
    return pl.pallas_call(
        output_kernel,
        out_shape=jax.ShapeDtypeStruct((requests, width), jnp.bfloat16),
        in_specs=in_vmem(2),
        out_specs=pl.BlockSpec(memory_space=pltpu.VMEM),
        scratch_shapes=[pltpu.VMEM((requests, width), jnp.float32)],
        compiler_params=kernel_params(12),
        name="project_out",
    )(values, fetched(w_o))


def hidden_kernel(parts_ref, values_ref, out_ref, slots):
    ranks = values_ref.shape[0]
    width = out_ref.shape[1]
    per_rank = out_ref.shape[0] // ranks
    across = values_ref.shape[2] // 128
    rows = slots.shape[1]
    requests = values_ref.shape[1] - ranks * rows
    start = pl.multiple_of(requests + lax.axis_index("tp") * rows, 16)
    for s in range(ranks):
        slots[s] = values_ref[s, pl.ds(start, rows), :].astype(jnp.float32)
    for g in range(width // 128):
        at = slice(g * 128, (g + 1) * 128)
        row = (g // across) * per_rank
        column = (g % across) * 128
        terms = [
            slots[s, row : row + per_rank, column : column + 128] for s in range(ranks)
        ]
        total = parts_ref[0, :, at].astype(jnp.float32)
        for d in range(1, parts_ref.shape[0]):
            total = total + parts_ref[d, :, at].astype(jnp.float32)
        total = total + jnp.concatenate(terms, 0)
        out_ref[:, at] = total.astype(out_ref.dtype)


def make_hidden(parts, values, slot_rows):
    ranks = values.shape[0]
    return pl.pallas_call(
        hidden_kernel,
        out_shape=jax.ShapeDtypeStruct(parts.shape[1:], jnp.bfloat16),
        in_specs=in_vmem(2),
        out_specs=pl.BlockSpec(memory_space=pltpu.VMEM),
        scratch_shapes=[pltpu.VMEM((ranks, slot_rows // ranks, values.shape[2]), jnp.float32)],
        compiler_params=kernel_params(12),
        name="hidden",
    )(parts, values)


def gate_up_kernel(hidden_ref, gain_ref, gate_ref, up_ref, *refs):
    ranks = lax.axis_size("tp")
    *outs, scaled, gains = refs
    gate_outs, up_outs = outs[0::2], outs[1::2]
    requests, width = hidden_ref.shape
    units = gate_ref.shape[1]
    share = requests // ranks
    groups = width // 128
    me = lax.axis_index("tp")
    if len(gate_outs) == 1:
        orders = [[0 * me + t for t in range(ranks)]] * 2
    else:
        orders = [[me ^ 3, me ^ 1, me ^ 2, me], [me ^ 3, me ^ 2, me ^ 1, me]]

    gains[...] = gain_ref[...].astype(jnp.float32)
    squares = []
    for k, order in enumerate(orders[:1] if len(gate_outs) == 1 else orders):
        square = [jnp.zeros((share, 128), jnp.float32) for _ in order]
        for t, block in enumerate(order):
            start = pl.multiple_of(block * share, 16)
            for g in range(groups):
                at = slice(g * 128, (g + 1) * 128)
                x = hidden_ref[pl.ds(start, share), at].astype(jnp.float32)
                square[t] = square[t] + x * x
                gain = gains[pl.ds(me * groups + g, 1), :]
                scaled[k, t * share : (t + 1) * share, at] = (x * gain).astype(scaled.dtype)
        squares.append(square)
    square = jnp.sum(jnp.concatenate(squares[0], 0), 1, keepdims=True)
    top = square.astype(jnp.bfloat16).astype(jnp.float32)
    middle = (square - top).astype(jnp.bfloat16).astype(jnp.float32)
    low = square - top - middle
    lane = lax.broadcasted_iota(jnp.int32, (requests, 128), 1)
    digits = jnp.where(lane == 0, top, jnp.where(lane == 1, middle, jnp.where(lane == 2, low, 0.0)))

    def store(targets, at, value):
        rows = requests // len(targets)
        for n, target in enumerate(targets):
            block = value[n * rows : (n + 1) * rows].astype(target.dtype)
            target[:, at : at + value.shape[1]] = block

    store(gate_outs, units, digits)
    chunk = units // 3
    for w_ref, left, targets in ((gate_ref, 0, gate_outs), (up_ref, scaled.shape[0] - 1, up_outs)):
        for at in range(0, units, chunk):
            term = jnp.dot(
                scaled[left], w_ref[:, at : at + chunk], preferred_element_type=jnp.float32
            )
            store(targets, at, term)


def gate_up(hidden, gain, w_gate, w_up, halves):
    requests, width = hidden.shape
    units = w_gate.shape[1]
    shapes = [
        jax.ShapeDtypeStruct((requests // halves, columns), jnp.bfloat16)
        for _ in range(halves)
        for columns in (units + 128, units)
    ]
    return pl.pallas_call(
        gate_up_kernel,
        out_shape=shapes,
        in_specs=in_vmem(4),
        out_specs=in_vmem(len(shapes)),
        scratch_shapes=[
            pltpu.VMEM((halves, requests, width), jnp.bfloat16),
            pltpu.VMEM(gain.shape, jnp.float32),
        ],
        compiler_params=kernel_params(12),
        name="gate_up",
    )(hidden, gain, fetched(w_gate), fetched(w_up))


def halve_kernel(*refs):
    count = len(refs) // 4
    for n in range(count):
        kept, came, send, keep = refs[n], refs[count + n], refs[2 * count + n], refs[3 * count + n]
        rows = send.shape[0]
        for at in range(0, send.shape[1], 128):
            at = slice(at, at + 128)
            total = kept[:, at].astype(jnp.float32) + came[:, at].astype(jnp.float32)
            send[:, at] = total[:rows].astype(send.dtype)
            keep[:, at] = total[rows:]


def halve(kept, came):
    half = [(k.shape[0] // 2, k.shape[1]) for k in kept]
    outs = pl.pallas_call(
        halve_kernel,
        out_shape=[jax.ShapeDtypeStruct(shape, jnp.bfloat16) for shape in half]
        + [jax.ShapeDtypeStruct(shape, jnp.float32) for shape in half],
        in_specs=in_vmem(2 * len(kept)),
        out_specs=in_vmem(2 * len(kept)),
        compiler_params=kernel_params(12),
        name="halve",
    )(*kept, *came)
    return outs[: len(kept)], outs[len(kept) :]


def inner_kernel(model, *refs):
    *parts, out_ref = refs
    gates, ups = parts[0::2], parts[1::2]
    units = out_ref.shape[1]

    def total(parts, at):
        terms = [
            part[n, :, at].astype(jnp.float32) for part in parts for n in range(part.shape[0])
        ]
        return sum(terms[1:], terms[0])

    square = jnp.sum(total(gates, slice(units, units + 128)), 1, keepdims=True)
    factor = lax.rsqrt(square / model + 1e-06)
    for at in range(0, units, 128):
        at = slice(at, at + 128)
        gate = total(gates, at) * factor
        up = total(ups, at) * factor
        out_ref[:, at] = (gate / (1.0 + jnp.exp(-gate)) * up).astype(out_ref.dtype)


def make_inner(parts, units, model):
    return pl.pallas_call(
        functools.partial(inner_kernel, model),
        out_shape=jax.ShapeDtypeStruct((parts[0].shape[1], units), jnp.bfloat16),
        in_specs=in_vmem(len(parts)),
        out_specs=pl.BlockSpec(memory_space=pltpu.VMEM),
        compiler_params=kernel_params(12),
        name="inner",
    )(*parts)


def down_kernel(inner_ref, w_ref, hidden_ref, out_ref, total):
    width = w_ref.shape[1]
    total[...] = jnp.dot(inner_ref[...], w_ref[...], preferred_element_type=jnp.float32)
    rows = hidden_ref.shape[0]
    own = pl.ds(pl.multiple_of(lax.axis_index("dp") * rows, 16), rows)
    total[own, :] += hidden_ref[...].astype(jnp.float32)
    groups = width // 128
    per_rank = out_ref.shape[1] // groups
    for d in range(out_ref.shape[0]):
        pieces = [
            total[d * per_rank : (d + 1) * per_rank, g * 128 : (g + 1) * 128]
            for g in range(groups)
        ]
        out_ref[d] = jnp.concatenate(pieces, 0).astype(out_ref.dtype)


def project_down(inner, w_down, hidden, ranks):
    requests, units = inner.shape
    width = w_down.shape[1]
    return pl.pallas_call(
        down_kernel,
        out_shape=jax.ShapeDtypeStruct(
            (ranks, requests // ranks * (width // 128), 128), jnp.bfloat16
        ),
        in_specs=in_vmem(3),
        out_specs=pl.BlockSpec(memory_space=pltpu.VMEM),
        scratch_shapes=[pltpu.VMEM((requests, width), jnp.float32)],
        compiler_params=kernel_params(12),
        name="project_down",
    )(inner, fetched(w_down), hidden)


def layer_kernel(parts_ref, out_ref, total):
    per_rank, model = out_ref.shape
    ranks = lax.axis_size("tp")
    groups = model // ranks // 128
    for t in range(ranks):
        terms = [
            parts_ref[d, :, :].astype(jnp.float32) for d in range(t, parts_ref.shape[0], ranks)
        ]
        layer = sum(terms[1:], terms[0])
        for g in range(groups):
            at = (t * groups + g) * 128
            total[:, at : at + 128] = layer[g * per_rank : (g + 1) * per_rank, :]
    out_ref[...] = total[...].astype(out_ref.dtype)


def make_layer(parts, per_rank, model):
    return pl.pallas_call(
        layer_kernel,
        out_shape=jax.ShapeDtypeStruct((per_rank, model), jnp.bfloat16),
        in_specs=in_vmem(1),
        out_specs=pl.BlockSpec(memory_space=pltpu.VMEM),
        scratch_shapes=[pltpu.VMEM((per_rank, model), jnp.float32)],
        compiler_params=kernel_params(12),
        name="layer",
    )(parts)


def round_up(value, step):
    return (value + step - 1) // step * step


def swap(parts, axes):
    return lax.all_to_all(parts, axes, split_axis=0, concat_axis=0, tiled=True)


def local(
    residual, queries, paged_latent_cache, lengths, w_uv, w_o, norm_gain, w_gate, w_up, w_down
):
    ranks_dp = lax.axis_size("dp")
    ranks_tp = lax.axis_size("tp")
    ranks = ranks_dp * ranks_tp
    per_rank, model = residual.shape
    requests = per_rank * ranks
    row_length = paged_latent_cache.shape[1]
    heads_all = queries.shape[1] // row_length
    heads_here = w_uv.shape[0]
    units = w_gate.shape[1]
    width = w_o.shape[1]

    groups = width // 128

    query = queries.reshape(per_rank, heads_all, row_length)
    latent = swap(attend(lengths, query, paged_latent_cache.T, ranks), ("dp", "tp"))

    across = heads_here * w_uv.shape[2] // 128
    slot_rows = ranks_tp * round_up(per_rank * ((groups + across - 1) // across), 16)
    values = head_values(latent.reshape(requests * heads_here, C), w_uv, residual, slot_rows)
    values = lax.all_gather(values, "tp", axis=0)
    attn = project_out(values, w_o, requests)
    attn = swap(attn.reshape(ranks_dp, requests // ranks_dp, width), "dp")
    own_hidden = make_hidden(attn, values, slot_rows)
    hidden = lax.all_gather(own_hidden, "dp", axis=0, tiled=True)

    halves = 2 if ranks_tp == 4 else 1
    parts = gate_up(hidden, norm_gain.reshape(-1, 128), w_gate, w_up, halves)
    if halves == 2:
        gate_send, up_send, gate_keep, up_keep = parts
        came = [from_distance(gate_send, "tp", 1), from_distance(up_send, "tp", 2)]
        (gate_send, up_send), (gate_keep, up_keep) = halve([gate_keep, up_keep], came)
        came = [from_distance(gate_send, "tp", 2), from_distance(up_send, "tp", 1)]
        parts = [part[None] for part in (gate_keep, up_keep, *came)]
    else:
        parts = [swap(part.reshape(ranks_tp, -1, part.shape[1]), "tp") for part in parts]
    inner = make_inner(parts, units, model)
    inner = lax.all_gather(inner, "tp", axis=0, tiled=True)
    ffn = swap(project_down(inner, w_down, own_hidden, ranks), ("dp", "tp"))
    return make_layer(ffn, per_rank, model)


def solution(mesh):
    placed = (
        P(("dp", "tp"), None),
        P(("dp", "tp"), None),
        P(("dp", "tp"), None),
        P(),
        P(("dp", "tp"), None, None),
        P("dp", "tp"),
        P(),
        P("tp", "dp"),
        P("tp", "dp"),
        P("dp", "tp"),
    )
    return jax.shard_map(
        local, mesh=mesh, in_specs=placed, out_specs=P(("dp", "tp"), None), check_vma=False
    )
```

```python
import functools

import jax
import jax.numpy as jnp
from jax import lax
from jax.experimental import pallas as pl
from jax.experimental.pallas import tpu as pltpu
from jax.sharding import PartitionSpec as P

C = 512
BLOCK_TOKENS = 64
TILE = 1024

score_scale = 192.0 ** (-0.5)
log2_e = 1.4426950408889634
negative = -1e30


def attention_kernel(
    lens_ref,
    q_ref,
    cache_ref,
    out_ref,
    held,
    score0,
    score1,
    weight0,
    weight1,
    keep0,
    keep1,
    acc,
    done,
    best,
    mass,
    lo,
    hi,
    first,
    last,
    sems,
):
    nreq, heads, _ = q_ref.shape
    tile = held.shape[2]
    factor = score_scale * log2_e

    rank = lax.axis_index("dp") * lax.axis_size("tp") + lax.axis_index("tp")
    begin = jnp.int32(0)
    pairs = jnp.int32(0)
    for r in range(nreq):
        length = lens_ref[rank * nreq + r]
        lo[r] = begin
        hi[r] = begin + length
        first[r] = begin // tile
        last[r] = (begin + length - 1) // tile
        pairs = pairs + (last[r] - first[r] + 1)
        begin = begin + ((length + BLOCK_TOKENS - 1) // BLOCK_TOKENS) * BLOCK_TOKENS
    used = last[nreq - 1] + 1

    def copy(i):
        return pltpu.make_async_copy(
            cache_ref.at[:, pl.ds(pl.multiple_of(i * tile, tile), tile)], held.at[i], sems.at[i]
        )

    @pl.loop(0, used)
    def _(i):
        copy(i).start()

    acc[...] = jnp.zeros_like(acc)
    best[...] = jnp.full_like(best, negative)
    mass[...] = jnp.zeros_like(mass)
    weight1[...] = jnp.zeros_like(weight1)
    keep1[...] = jnp.ones_like(keep1)

    def advance(p, r, i):
        live = p + 1 < pairs
        step = (i == last[r]) & live
        nr = jnp.where(step, r + 1, r)
        ni = jnp.where(step, first[nr], jnp.where(live, i + 1, i))
        return nr, ni, live

    def fetch(r, i, live):
        fresh = live & ((r == 0) | (i > last[jnp.maximum(r - 1, 0)]))

        @pl.when(fresh)
        def _():
            copy(i).wait()

    def scores(r, i, live, target):
        begin_at = jnp.where(live, lo[r], 0)
        end_at = jnp.where(live, hi[r], 0)
        s = jnp.dot(q_ref[r], held[i], preferred_element_type=jnp.float32)
        token = i * tile + lax.broadcasted_iota(jnp.int32, (1, tile), 1)
        target[...] = s + jnp.where((token >= begin_at) & (token < end_at), 0.0, negative)

    def soften(r, source, weights, keeps):
        s = source[...]
        old = best[r]
        new = jnp.maximum(old, jnp.max(s, axis=1, keepdims=True))
        weight = jnp.exp2((s - new[:, :1]) * factor)
        keep = jnp.exp2((old - new) * factor)
        part = weight[:, :128]
        for at in range(128, tile, 128):
            part = part + weight[:, at : at + 128]
        mass[r] = mass[r] * keep + part
        best[r] = new
        weights[...] = weight.astype(weights.dtype)
        keeps[...] = keep.T[:8, :]

    def gather(r, i, weights, keeps):
        values = lax.dot_general(
            held[i, :C, :],
            weights[...],
            (((1,), (1,)), ((), ())),
            preferred_element_type=jnp.float32,
        )
        acc[r] = acc[r] * keeps[:1, :] + values

    zero = jnp.int32(0)
    fetch(zero, zero, pairs > 0)
    scores(zero, zero, pairs > 0, score0)

    def step(j, carry):
        r0, i0, r1, i1 = carry
        p = 2 * j
        r2, i2, live2 = advance(p, r1, i1)
        r3, i3, live3 = advance(p + 1, r2, i2)
        fetch(r2, i2, live2)
        fetch(r3, i3, live3)
        gather(r0, i0, weight1, keep1)
        scores(r2, i2, live2, score1)
        soften(r1, score0, weight0, keep0)
        gather(r1, i1, weight0, keep0)
        scores(r3, i3, live3, score0)
        soften(r2, score1, weight1, keep1)
        return r2, i2, r3, i3

    r0, i0, _, _ = lax.fori_loop(0, (pairs + 1) // 2, step, (zero, zero, zero, zero))
    gather(r0, i0, weight1, keep1)

    share = heads // out_ref.shape[0]
    for r in range(nreq):
        total = jnp.sum(mass[r], axis=1, keepdims=True)
        score0[:, :C] = acc[r].T / total
        for d in range(out_ref.shape[0]):
            done[d, r * share : (r + 1) * share, :] = score0[d * share : (d + 1) * share, :C]
    out_ref[...] = done[...].astype(out_ref.dtype)


def kernel_params(limit):
    return pltpu.CompilerParams(vmem_limit_bytes=limit * 1024 * 1024)


def in_vmem(count):
    return [pl.BlockSpec(memory_space=pltpu.VMEM)] * count


def fetched(weight):
    return pltpu.with_memory_space_constraint(weight, pltpu.VMEM)


def attend(lengths, queries, cache_t, ranks):
    nreq, heads, width = queries.shape
    tokens = cache_t.shape[1]
    tile = TILE
    tiles = tokens // tile
    return pl.pallas_call(
        attention_kernel,
        out_shape=jax.ShapeDtypeStruct((ranks, nreq * heads // ranks, C), jnp.bfloat16),
        in_specs=[pl.BlockSpec(memory_space=pltpu.SMEM)]
        + in_vmem(1)
        + [pl.BlockSpec(memory_space=pltpu.HBM)],
        out_specs=pl.BlockSpec(memory_space=pltpu.VMEM),
        scratch_shapes=[
            pltpu.VMEM((tiles, width, tile), jnp.bfloat16),
            pltpu.VMEM((heads, tile), jnp.float32),
            pltpu.VMEM((heads, tile), jnp.float32),
            pltpu.VMEM((heads, tile), jnp.bfloat16),
            pltpu.VMEM((heads, tile), jnp.bfloat16),
            pltpu.VMEM((8, heads), jnp.float32),
            pltpu.VMEM((8, heads), jnp.float32),
            pltpu.VMEM((nreq, C, heads), jnp.float32),
            pltpu.VMEM((ranks, nreq * heads // ranks, C), jnp.float32),
            pltpu.VMEM((nreq, heads, 128), jnp.float32),
            pltpu.VMEM((nreq, heads, 128), jnp.float32),
            pltpu.SMEM((nreq,), jnp.int32),
            pltpu.SMEM((nreq,), jnp.int32),
            pltpu.SMEM((nreq,), jnp.int32),
            pltpu.SMEM((nreq,), jnp.int32),
            pltpu.SemaphoreType.DMA((tiles,)),
        ],
        compiler_params=kernel_params(26),
        cost_estimate=pl.CostEstimate(
            flops=2 * heads * tokens * (width + C),
            bytes_accessed=2 * tokens * width,
            transcendentals=heads * tokens,
        ),
        name="attention",
    )(
        pltpu.with_memory_space_constraint(lengths, pltpu.HBM),
        fetched(queries),
        pltpu.with_memory_space_constraint(cache_t, pltpu.HBM),
    )


def head_values_kernel(latent_ref, w_ref, residual_ref, out_ref, values, slots):
    heads, _, wide = w_ref.shape
    per_rank, model = residual_ref.shape
    requests = latent_ref.shape[0] // heads
    latent = latent_ref[...]
    for h in range(heads):
        values[...] = jnp.dot(latent, w_ref[h], preferred_element_type=jnp.float32)
        picked = values[pl.ds(h, requests, stride=heads), :]
        out_ref[:requests, h * wide : (h + 1) * wide] = picked.astype(out_ref.dtype)
    ranks = lax.axis_size("tp")
    groups = model // ranks // 128
    rows = (out_ref.shape[0] - requests) // ranks
    across = out_ref.shape[1] // 128
    slots[...] = jnp.zeros_like(slots)
    for t in range(ranks):
        for g in range(groups):
            at = (t * groups + g) * 128
            row = t * rows + (g // across) * per_rank
            column = (g % across) * 128
            slots[row : row + per_rank, column : column + 128] = residual_ref[
                :, at : at + 128
            ].astype(jnp.float32)
    out_ref[requests:, :] = slots[...].astype(out_ref.dtype)


def head_values(latent, w_uv, residual, slot_rows):
    heads, _, wide = w_uv.shape
    requests = latent.shape[0] // heads
    return pl.pallas_call(
        head_values_kernel,
        out_shape=jax.ShapeDtypeStruct((requests + slot_rows, heads * wide), jnp.bfloat16),
        in_specs=in_vmem(3),
        out_specs=pl.BlockSpec(memory_space=pltpu.VMEM),
        scratch_shapes=[
            pltpu.VMEM((latent.shape[0], wide), jnp.float32),
            pltpu.VMEM((slot_rows, heads * wide), jnp.float32),
        ],
        compiler_params=kernel_params(12),
        name="head_values",
    )(latent, w_uv, residual)


def from_distance(piece, axis, distance):
    return lax.ppermute(piece, axis, [(k, k ^ distance) for k in range(lax.axis_size(axis))])


def output_kernel(values_ref, w_ref, out_ref, total):
    steps, _, depth = values_ref.shape
    requests = out_ref.shape[0]
    for k in range(steps):
        term = jnp.dot(
            values_ref[k, :requests, :],
            w_ref[k * depth : (k + 1) * depth, :],
            preferred_element_type=jnp.float32,
        )
        if k == 0:
            total[...] = term
        else:
            total[...] += term
    out_ref[...] = total[...].astype(out_ref.dtype)


def project_out(values, w_o, requests):
    width = w_o.shape[1]
    return pl.pallas_call(
        output_kernel,
        out_shape=jax.ShapeDtypeStruct((requests, width), jnp.bfloat16),
        in_specs=in_vmem(2),
        out_specs=pl.BlockSpec(memory_space=pltpu.VMEM),
        scratch_shapes=[pltpu.VMEM((requests, width), jnp.float32)],
        compiler_params=kernel_params(12),
        name="project_out",
    )(values, fetched(w_o))


def hidden_kernel(parts_ref, values_ref, out_ref, slots):
    ranks = values_ref.shape[0]
    width = out_ref.shape[1]
    per_rank = out_ref.shape[0] // ranks
    across = values_ref.shape[2] // 128
    rows = slots.shape[1]
    requests = values_ref.shape[1] - ranks * rows
    start = pl.multiple_of(requests + lax.axis_index("tp") * rows, 16)
    for s in range(ranks):
        slots[s] = values_ref[s, pl.ds(start, rows), :].astype(jnp.float32)
    for g in range(width // 128):
        at = slice(g * 128, (g + 1) * 128)
        row = (g // across) * per_rank
        column = (g % across) * 128
        terms = [
            slots[s, row : row + per_rank, column : column + 128] for s in range(ranks)
        ]
        total = parts_ref[0, :, at].astype(jnp.float32)
        for d in range(1, parts_ref.shape[0]):
            total = total + parts_ref[d, :, at].astype(jnp.float32)
        total = total + jnp.concatenate(terms, 0)
        out_ref[:, at] = total.astype(out_ref.dtype)


def make_hidden(parts, values, slot_rows):
    ranks = values.shape[0]
    return pl.pallas_call(
        hidden_kernel,
        out_shape=jax.ShapeDtypeStruct(parts.shape[1:], jnp.bfloat16),
        in_specs=in_vmem(2),
        out_specs=pl.BlockSpec(memory_space=pltpu.VMEM),
        scratch_shapes=[pltpu.VMEM((ranks, slot_rows // ranks, values.shape[2]), jnp.float32)],
        compiler_params=kernel_params(12),
        name="hidden",
    )(parts, values)


def scale_kernel(hidden_ref, gain_ref, gate_ref, up_ref, scaled, gate_sum, up_sum, *refs):
    *outs, gains = refs
    ranks = lax.axis_size("tp")
    halves = scaled.shape[0]
    requests, width = hidden_ref.shape
    share = requests // ranks
    groups = width // 128
    me = lax.axis_index("tp")
    places = [[3, 1, 2, 0], [3, 2, 1, 0]] if halves == 2 else [list(range(ranks))]

    gains[...] = gain_ref[...].astype(jnp.float32)
    squares = [None] * ranks
    for k in range(ranks):
        block = me ^ k if halves == 2 else k
        start = block * share if halves == 1 else pl.multiple_of(block * share, 16)
        square = jnp.zeros((share, 128), jnp.float32)
        for g in range(groups):
            at = slice(g * 128, (g + 1) * 128)
            x = hidden_ref[pl.ds(start, share), at].astype(jnp.float32)
            square = square + x * x
            gain = gains[pl.ds(me * groups + g, 1), :]
            value = (x * gain).astype(scaled.dtype)
            for n, place in enumerate(places):
                scaled[n, place[k] * share : (place[k] + 1) * share, at] = value
        squares[places[0][k]] = square
    square = jnp.sum(jnp.concatenate(squares, 0), 1, keepdims=True)
    top = square.astype(jnp.bfloat16).astype(jnp.float32)
    middle = (square - top).astype(jnp.bfloat16).astype(jnp.float32)
    low = square - top - middle
    lane = lax.broadcasted_iota(jnp.int32, (requests, 128), 1)
    digits = jnp.where(lane == 0, top, jnp.where(lane == 1, middle, jnp.where(lane == 2, low, 0.0)))
    gates = [gate_sum, outs[0]] if halves == 2 else [gate_sum]
    ups = [up_sum, outs[1]] if halves == 2 else [up_sum]
    columns = up_sum.shape[1]
    for n, target in enumerate(gates):
        rows = target.shape[0]
        target[:, columns:] = digits[n * rows : (n + 1) * rows].astype(target.dtype)
    products(scaled, gate_ref, up_ref, 0, columns, gates, ups)


def products(scaled, gate_ref, up_ref, first, columns, gates, ups):
    for left, w_ref, targets in ((0, gate_ref, gates), (scaled.shape[0] - 1, up_ref, ups)):
        for at in range(0, columns, 256):
            upto = min(at + 256, columns)
            term = jnp.dot(
                scaled[left],
                w_ref[:, first + at : first + upto],
                preferred_element_type=jnp.float32,
            )
            for n, target in enumerate(targets):
                rows = target.shape[0]
                target[:, at:upto] = term[n * rows : (n + 1) * rows].astype(target.dtype)


def second_kernel(scaled, gate_ref, up_ref, *outs):
    columns = outs[1].shape[1]
    first = gate_ref.shape[1] - columns
    products(scaled, gate_ref, up_ref, first, columns, outs[0::2], outs[1::2])


def gate_up(hidden, gain, w_gate, w_up, halves):
    requests, width = hidden.shape
    units = w_gate.shape[1]
    first = units if halves == 1 else round_up(units // 2, 256)
    w_gate, w_up = fetched(w_gate), fetched(w_up)

    def shapes(columns, extra):
        return [
            jax.ShapeDtypeStruct((requests // halves, columns + more), jnp.bfloat16)
            for _ in range(halves)
            for more in (extra, 0)
        ]

    outs = [jax.ShapeDtypeStruct((halves, requests, width), jnp.bfloat16)] + shapes(first, 128)
    scaled, *parts = pl.pallas_call(
        scale_kernel,
        out_shape=outs,
        in_specs=in_vmem(4),
        out_specs=in_vmem(len(outs)),
        scratch_shapes=[pltpu.VMEM(gain.shape, jnp.float32)],
        compiler_params=kernel_params(12),
        cost_estimate=pl.CostEstimate(
            flops=4 * requests * width * first, bytes_accessed=4 * width * first, transcendentals=0
        ),
        name="gate_up",
    )(hidden, gain, w_gate, w_up)
    if halves == 1:
        return [parts]
    outs = shapes(units - first, 0)
    others = pl.pallas_call(
        second_kernel,
        out_shape=outs,
        in_specs=in_vmem(3),
        out_specs=in_vmem(len(outs)),
        compiler_params=kernel_params(12),
        cost_estimate=pl.CostEstimate(
            flops=4 * requests * width * (units - first),
            bytes_accessed=4 * width * (units - first),
            transcendentals=0,
        ),
        name="gate_up_rest",
    )(scaled, w_gate, w_up)
    return [parts, others]


def halve_kernel(*refs):
    count = len(refs) // 4
    for n in range(count):
        kept, came, send, keep = refs[n], refs[count + n], refs[2 * count + n], refs[3 * count + n]
        rows = send.shape[0]
        for at in range(0, send.shape[1], 128):
            at = slice(at, at + 128)
            total = kept[:, at].astype(jnp.float32) + came[:, at].astype(jnp.float32)
            send[:, at] = total[:rows].astype(send.dtype)
            keep[:, at] = total[rows:]


def halve(kept, came):
    half = [(k.shape[0] // 2, k.shape[1]) for k in kept]
    outs = pl.pallas_call(
        halve_kernel,
        out_shape=[jax.ShapeDtypeStruct(shape, jnp.bfloat16) for shape in half]
        + [jax.ShapeDtypeStruct(shape, jnp.float32) for shape in half],
        in_specs=in_vmem(2 * len(kept)),
        out_specs=in_vmem(2 * len(kept)),
        compiler_params=kernel_params(12),
        name="halve",
    )(*kept, *came)
    return outs[: len(kept)], outs[len(kept) :]


def inner_kernel(model, counts, *refs):
    *parts, out_ref = refs
    factor = None
    at = 0
    for count in counts:
        gates, ups, parts = parts[0:count:2], parts[1:count:2], parts[count:]
        columns = ups[0].shape[2]

        def total(parts, at):
            terms = [
                part[n, :, at].astype(jnp.float32) for part in parts for n in range(part.shape[0])
            ]
            return sum(terms[1:], terms[0])

        if factor is None:
            square = jnp.sum(total(gates, slice(columns, columns + 128)), 1, keepdims=True)
            factor = lax.rsqrt(square / model + 1e-06)
        for start in range(0, columns, 128):
            span = slice(start, start + 128)
            gate = total(gates, span) * factor
            up = total(ups, span) * factor
            value = gate / (1.0 + jnp.exp(-gate)) * up
            out_ref[:, at + start : at + start + 128] = value.astype(out_ref.dtype)
        at += columns


def make_inner(chunks, units, model):
    parts = [part for chunk in chunks for part in chunk]
    return pl.pallas_call(
        functools.partial(inner_kernel, model, [len(chunk) for chunk in chunks]),
        out_shape=jax.ShapeDtypeStruct((parts[0].shape[1], units), jnp.bfloat16),
        in_specs=in_vmem(len(parts)),
        out_specs=pl.BlockSpec(memory_space=pltpu.VMEM),
        compiler_params=kernel_params(12),
        name="inner",
    )(*parts)


def down_kernel(inner_ref, w_ref, hidden_ref, out_ref, total):
    width = w_ref.shape[1]
    total[...] = jnp.dot(inner_ref[...], w_ref[...], preferred_element_type=jnp.float32)
    rows = hidden_ref.shape[0]
    own = pl.ds(pl.multiple_of(lax.axis_index("dp") * rows, 16), rows)
    total[own, :] += hidden_ref[...].astype(jnp.float32)
    groups = width // 128
    per_rank = out_ref.shape[1] // groups
    for d in range(out_ref.shape[0]):
        pieces = [
            total[d * per_rank : (d + 1) * per_rank, g * 128 : (g + 1) * 128]
            for g in range(groups)
        ]
        out_ref[d] = jnp.concatenate(pieces, 0).astype(out_ref.dtype)


def project_down(inner, w_down, hidden, ranks):
    requests, units = inner.shape
    width = w_down.shape[1]
    return pl.pallas_call(
        down_kernel,
        out_shape=jax.ShapeDtypeStruct(
            (ranks, requests // ranks * (width // 128), 128), jnp.bfloat16
        ),
        in_specs=in_vmem(3),
        out_specs=pl.BlockSpec(memory_space=pltpu.VMEM),
        scratch_shapes=[pltpu.VMEM((requests, width), jnp.float32)],
        compiler_params=kernel_params(12),
        name="project_down",
    )(inner, fetched(w_down), hidden)


def layer_kernel(parts_ref, out_ref, total):
    per_rank, model = out_ref.shape
    ranks = lax.axis_size("tp")
    groups = model // ranks // 128
    for t in range(ranks):
        terms = [
            parts_ref[d, :, :].astype(jnp.float32) for d in range(t, parts_ref.shape[0], ranks)
        ]
        layer = sum(terms[1:], terms[0])
        for g in range(groups):
            at = (t * groups + g) * 128
            total[:, at : at + 128] = layer[g * per_rank : (g + 1) * per_rank, :]
    out_ref[...] = total[...].astype(out_ref.dtype)


def make_layer(parts, per_rank, model):
    return pl.pallas_call(
        layer_kernel,
        out_shape=jax.ShapeDtypeStruct((per_rank, model), jnp.bfloat16),
        in_specs=in_vmem(1),
        out_specs=pl.BlockSpec(memory_space=pltpu.VMEM),
        scratch_shapes=[pltpu.VMEM((per_rank, model), jnp.float32)],
        compiler_params=kernel_params(12),
        name="layer",
    )(parts)


def round_up(value, step):
    return (value + step - 1) // step * step


def swap(parts, axes):
    return lax.all_to_all(parts, axes, split_axis=0, concat_axis=0, tiled=True)


def local(
    residual, queries, paged_latent_cache, lengths, w_uv, w_o, norm_gain, w_gate, w_up, w_down
):
    ranks_dp = lax.axis_size("dp")
    ranks_tp = lax.axis_size("tp")
    ranks = ranks_dp * ranks_tp
    per_rank, model = residual.shape
    requests = per_rank * ranks
    row_length = paged_latent_cache.shape[1]
    heads_all = queries.shape[1] // row_length
    heads_here = w_uv.shape[0]
    units = w_gate.shape[1]
    width = w_o.shape[1]

    groups = width // 128

    query = queries.reshape(per_rank, heads_all, row_length)
    latent = swap(attend(lengths, query, paged_latent_cache.T, ranks), ("dp", "tp"))

    across = heads_here * w_uv.shape[2] // 128
    slot_rows = ranks_tp * round_up(per_rank * ((groups + across - 1) // across), 16)
    values = head_values(latent.reshape(requests * heads_here, C), w_uv, residual, slot_rows)
    values = lax.all_gather(values, "tp", axis=0)
    attn = project_out(values, w_o, requests)
    attn = swap(attn.reshape(ranks_dp, requests // ranks_dp, width), "dp")
    own_hidden = make_hidden(attn, values, slot_rows)
    hidden = lax.all_gather(own_hidden, "dp", axis=0, tiled=True)

    halves = 2 if ranks_tp == 4 else 1
    chunks = gate_up(hidden, norm_gain.reshape(-1, 128), w_gate, w_up, halves)
    if halves == 2:
        sums = []
        for gate_send, up_send, gate_keep, up_keep in chunks:
            came = [from_distance(gate_send, "tp", 1), from_distance(up_send, "tp", 2)]
            (gate_send, up_send), kept = halve([gate_keep, up_keep], came)
            came = [from_distance(gate_send, "tp", 2), from_distance(up_send, "tp", 1)]
            sums.append([part[None] for part in (*kept, *came)])
    else:
        sums = [
            [swap(part.reshape(ranks_tp, -1, part.shape[1]), "tp") for part in chunk]
            for chunk in chunks
        ]
    inner = make_inner(sums, units, model)
    inner = lax.all_gather(inner, "tp", axis=0, tiled=True)
    ffn = swap(project_down(inner, w_down, own_hidden, ranks), ("dp", "tp"))
    return make_layer(ffn, per_rank, model)


def solution(mesh):
    placed = (
        P(("dp", "tp"), None),
        P(("dp", "tp"), None),
        P(("dp", "tp"), None),
        P(),
        P(("dp", "tp"), None, None),
        P("dp", "tp"),
        P(),
        P("tp", "dp"),
        P("tp", "dp"),
        P("dp", "tp"),
    )
    return jax.shard_map(
        local, mesh=mesh, in_specs=placed, out_specs=P(("dp", "tp"), None), check_vma=False
    )
```

```python
import functools

import jax
import jax.numpy as jnp
from jax import lax
from jax.experimental import pallas as pl
from jax.experimental.pallas import tpu as pltpu
from jax.sharding import PartitionSpec as P

C = 512
BLOCK_TOKENS = 64
TILE = 1024

score_scale = 192.0 ** (-0.5)
log2_e = 1.4426950408889634
negative = -1e30


def attention_kernel(
    lens_ref,
    q_ref,
    cache_ref,
    out_ref,
    held,
    score0,
    score1,
    weight0,
    weight1,
    keep0,
    keep1,
    acc,
    done,
    best,
    mass,
    lo,
    hi,
    first,
    last,
    sems,
):
    nreq, heads, _ = q_ref.shape
    tile = held.shape[2]
    factor = score_scale * log2_e

    rank = lax.axis_index("dp") * lax.axis_size("tp") + lax.axis_index("tp")
    begin = jnp.int32(0)
    pairs = jnp.int32(0)
    for r in range(nreq):
        length = lens_ref[rank * nreq + r]
        lo[r] = begin
        hi[r] = begin + length
        first[r] = begin // tile
        last[r] = (begin + length - 1) // tile
        pairs = pairs + (last[r] - first[r] + 1)
        begin = begin + ((length + BLOCK_TOKENS - 1) // BLOCK_TOKENS) * BLOCK_TOKENS
    used = last[nreq - 1] + 1

    def copy(i):
        return pltpu.make_async_copy(
            cache_ref.at[:, pl.ds(pl.multiple_of(i * tile, tile), tile)], held.at[i], sems.at[i]
        )

    @pl.loop(0, used)
    def _(i):
        copy(i).start()

    acc[...] = jnp.zeros_like(acc)
    best[...] = jnp.full_like(best, negative)
    mass[...] = jnp.zeros_like(mass)
    weight1[...] = jnp.zeros_like(weight1)
    keep1[...] = jnp.ones_like(keep1)

    def advance(p, r, i):
        live = p + 1 < pairs
        step = (i == last[r]) & live
        nr = jnp.where(step, r + 1, r)
        ni = jnp.where(step, first[nr], jnp.where(live, i + 1, i))
        return nr, ni, live

    def fetch(r, i, live):
        fresh = live & ((r == 0) | (i > last[jnp.maximum(r - 1, 0)]))

        @pl.when(fresh)
        def _():
            copy(i).wait()

    def scores(r, i, live, target):
        begin_at = jnp.where(live, lo[r], 0)
        end_at = jnp.where(live, hi[r], 0)
        s = jnp.dot(q_ref[r], held[i], preferred_element_type=jnp.float32)
        token = i * tile + lax.broadcasted_iota(jnp.int32, (1, tile), 1)
        target[...] = s + jnp.where((token >= begin_at) & (token < end_at), 0.0, negative)

    def soften(r, source, weights, keeps):
        s = source[...]
        old = best[r]
        new = jnp.maximum(old, jnp.max(s, axis=1, keepdims=True))
        weight = jnp.exp2((s - new[:, :1]) * factor)
        keep = jnp.exp2((old - new) * factor)
        part = weight[:, :128]
        for at in range(128, tile, 128):
            part = part + weight[:, at : at + 128]
        mass[r] = mass[r] * keep + part
        best[r] = new
        weights[...] = weight.astype(weights.dtype)
        keeps[...] = keep.T[:8, :]

    def gather(r, i, weights, keeps):
        values = lax.dot_general(
            held[i, :C, :],
            weights[...],
            (((1,), (1,)), ((), ())),
            preferred_element_type=jnp.float32,
        )
        acc[r] = acc[r] * keeps[:1, :] + values

    zero = jnp.int32(0)
    fetch(zero, zero, pairs > 0)
    scores(zero, zero, pairs > 0, score0)

    def step(j, carry):
        r0, i0, r1, i1 = carry
        p = 2 * j
        r2, i2, live2 = advance(p, r1, i1)
        r3, i3, live3 = advance(p + 1, r2, i2)
        fetch(r2, i2, live2)
        fetch(r3, i3, live3)
        gather(r0, i0, weight1, keep1)
        scores(r2, i2, live2, score1)
        soften(r1, score0, weight0, keep0)
        gather(r1, i1, weight0, keep0)
        scores(r3, i3, live3, score0)
        soften(r2, score1, weight1, keep1)
        return r2, i2, r3, i3

    r0, i0, _, _ = lax.fori_loop(0, (pairs + 1) // 2, step, (zero, zero, zero, zero))
    gather(r0, i0, weight1, keep1)

    share = heads // out_ref.shape[0]
    for r in range(nreq):
        total = jnp.sum(mass[r], axis=1, keepdims=True)
        score0[:, :C] = acc[r].T / total
        for d in range(out_ref.shape[0]):
            done[d, r * share : (r + 1) * share, :] = score0[d * share : (d + 1) * share, :C]
    out_ref[...] = done[...].astype(out_ref.dtype)


def kernel_params(limit):
    return pltpu.CompilerParams(vmem_limit_bytes=limit * 1024 * 1024)


def in_vmem(count):
    return [pl.BlockSpec(memory_space=pltpu.VMEM)] * count


def fetched(weight):
    return pltpu.with_memory_space_constraint(weight, pltpu.VMEM)


def attend(lengths, queries, cache_t, ranks):
    nreq, heads, width = queries.shape
    tokens = cache_t.shape[1]
    tile = TILE
    tiles = tokens // tile
    return pl.pallas_call(
        attention_kernel,
        out_shape=jax.ShapeDtypeStruct((ranks, nreq * heads // ranks, C), jnp.bfloat16),
        in_specs=[pl.BlockSpec(memory_space=pltpu.SMEM)]
        + in_vmem(1)
        + [pl.BlockSpec(memory_space=pltpu.HBM)],
        out_specs=pl.BlockSpec(memory_space=pltpu.VMEM),
        scratch_shapes=[
            pltpu.VMEM((tiles, width, tile), jnp.bfloat16),
            pltpu.VMEM((heads, tile), jnp.float32),
            pltpu.VMEM((heads, tile), jnp.float32),
            pltpu.VMEM((heads, tile), jnp.bfloat16),
            pltpu.VMEM((heads, tile), jnp.bfloat16),
            pltpu.VMEM((8, heads), jnp.float32),
            pltpu.VMEM((8, heads), jnp.float32),
            pltpu.VMEM((nreq, C, heads), jnp.float32),
            pltpu.VMEM((ranks, nreq * heads // ranks, C), jnp.float32),
            pltpu.VMEM((nreq, heads, 128), jnp.float32),
            pltpu.VMEM((nreq, heads, 128), jnp.float32),
            pltpu.SMEM((nreq,), jnp.int32),
            pltpu.SMEM((nreq,), jnp.int32),
            pltpu.SMEM((nreq,), jnp.int32),
            pltpu.SMEM((nreq,), jnp.int32),
            pltpu.SemaphoreType.DMA((tiles,)),
        ],
        compiler_params=kernel_params(26),
        cost_estimate=pl.CostEstimate(
            flops=2 * heads * tokens * (width + C),
            bytes_accessed=2 * tokens * width,
            transcendentals=heads * tokens,
        ),
        name="attention",
    )(
        pltpu.with_memory_space_constraint(lengths, pltpu.HBM),
        fetched(queries),
        pltpu.with_memory_space_constraint(cache_t, pltpu.HBM),
    )


def head_values_kernel(latent_ref, w_ref, out_ref, values):
    heads, _, wide = w_ref.shape
    requests = out_ref.shape[0]
    latent = latent_ref[...]
    for h in range(heads):
        values[...] = jnp.dot(latent, w_ref[h], preferred_element_type=jnp.float32)
        picked = values[pl.ds(h, requests, stride=heads), :]
        out_ref[:, h * wide : (h + 1) * wide] = picked.astype(out_ref.dtype)


def head_values(latent, w_uv):
    heads, _, wide = w_uv.shape
    requests = latent.shape[0] // heads
    return pl.pallas_call(
        head_values_kernel,
        out_shape=jax.ShapeDtypeStruct((requests, heads * wide), jnp.bfloat16),
        in_specs=in_vmem(2),
        out_specs=pl.BlockSpec(memory_space=pltpu.VMEM),
        scratch_shapes=[pltpu.VMEM((latent.shape[0], wide), jnp.float32)],
        compiler_params=kernel_params(12),
        name="head_values",
    )(latent, w_uv)


def split_kernel(rows_ref, *out_refs):
    width = out_refs[0].shape[1]
    me = lax.axis_index("tp")
    for k, out_ref in enumerate(out_refs):
        start = pl.multiple_of((me ^ k) * width, 128)
        out_ref[...] = rows_ref[:, pl.ds(start, width)]


def split_columns(rows, ranks):
    shape = jax.ShapeDtypeStruct((rows.shape[0], rows.shape[1] // ranks), rows.dtype)
    return pl.pallas_call(
        split_kernel,
        out_shape=[shape] * ranks,
        in_specs=in_vmem(1),
        out_specs=in_vmem(ranks),
        compiler_params=kernel_params(8),
        name="split_columns",
    )(rows)


def from_distance(piece, axis, distance):
    return lax.ppermute(piece, axis, [(k, k ^ distance) for k in range(lax.axis_size(axis))])


def from_all(piece, axis):
    return [piece] + [from_distance(piece, axis, k) for k in range(1, lax.axis_size(axis))]


def output_kernel(*refs):
    *values, w_ref, out_ref, total = refs
    depth = values[0].shape[1]
    me = lax.axis_index("tp")
    for k, value in enumerate(values):
        rows = pl.ds(pl.multiple_of((me ^ k) * depth, 128), depth)
        term = jnp.dot(value[...], w_ref[rows, :], preferred_element_type=jnp.float32)
        if k == 0:
            total[...] = term
        else:
            total[...] += term
    out_ref[...] = total[...].astype(out_ref.dtype)


def project_out(values, w_o):
    requests = values[0].shape[0]
    width = w_o.shape[1]
    return pl.pallas_call(
        output_kernel,
        out_shape=jax.ShapeDtypeStruct((requests, width), jnp.bfloat16),
        in_specs=in_vmem(len(values) + 1),
        out_specs=pl.BlockSpec(memory_space=pltpu.VMEM),
        scratch_shapes=[pltpu.VMEM((requests, width), jnp.float32)],
        compiler_params=kernel_params(12),
        name="project_out",
    )(*values, fetched(w_o))


def hidden_kernel(parts_ref, *refs):
    *slices, out_ref, added = refs
    per_rank = slices[0].shape[0]
    me = lax.axis_index("tp")
    for k, piece in enumerate(slices):
        added[me ^ k] = piece[...].astype(jnp.float32)
    width = out_ref.shape[1]
    for at in range(0, width, 128):
        at = slice(at, at + 128)
        total = parts_ref[0, :, at].astype(jnp.float32)
        for d in range(1, parts_ref.shape[0]):
            total = total + parts_ref[d, :, at].astype(jnp.float32)
        terms = [added[s, :, at] for s in range(len(slices))]
        out_ref[:, at] = (total + jnp.concatenate(terms, 0)).astype(out_ref.dtype)


def make_hidden(parts, slices):
    return pl.pallas_call(
        hidden_kernel,
        out_shape=jax.ShapeDtypeStruct(parts.shape[1:], jnp.bfloat16),
        in_specs=in_vmem(1 + len(slices)),
        out_specs=pl.BlockSpec(memory_space=pltpu.VMEM),
        scratch_shapes=[pltpu.VMEM((len(slices),) + slices[0].shape, jnp.float32)],
        compiler_params=kernel_params(12),
        name="hidden",
    )(parts, *slices)


def scale_kernel(hidden_ref, gain_ref, gate_ref, up_ref, scaled, gate_sum, up_sum, *refs):
    *outs, gains = refs
    ranks = lax.axis_size("tp")
    halves = scaled.shape[0]
    requests, width = hidden_ref.shape
    share = requests // ranks
    groups = width // 128
    me = lax.axis_index("tp")
    places = [[3, 1, 2, 0], [3, 2, 1, 0]] if halves == 2 else [list(range(ranks))]

    gains[...] = gain_ref[...].astype(jnp.float32)
    squares = [None] * ranks
    for k in range(ranks):
        block = me ^ k if halves == 2 else k
        start = block * share if halves == 1 else pl.multiple_of(block * share, 16)
        square = jnp.zeros((share, 128), jnp.float32)
        for g in range(groups):
            at = slice(g * 128, (g + 1) * 128)
            x = hidden_ref[pl.ds(start, share), at].astype(jnp.float32)
            square = square + x * x
            gain = gains[pl.ds(me * groups + g, 1), :]
            value = (x * gain).astype(scaled.dtype)
            for n, place in enumerate(places):
                scaled[n, place[k] * share : (place[k] + 1) * share, at] = value
        squares[places[0][k]] = square
    square = jnp.sum(jnp.concatenate(squares, 0), 1, keepdims=True)
    top = square.astype(jnp.bfloat16).astype(jnp.float32)
    middle = (square - top).astype(jnp.bfloat16).astype(jnp.float32)
    low = square - top - middle
    lane = lax.broadcasted_iota(jnp.int32, (requests, 128), 1)
    digits = jnp.where(lane == 0, top, jnp.where(lane == 1, middle, jnp.where(lane == 2, low, 0.0)))
    gates = [gate_sum, outs[0]] if halves == 2 else [gate_sum]
    ups = [up_sum, outs[1]] if halves == 2 else [up_sum]
    columns = up_sum.shape[1]
    for n, target in enumerate(gates):
        rows = target.shape[0]
        target[:, columns:] = digits[n * rows : (n + 1) * rows].astype(target.dtype)
    products(scaled, gate_ref, up_ref, 0, columns, gates, ups)


def products(scaled, gate_ref, up_ref, first, columns, gates, ups):
    for left, w_ref, targets in ((0, gate_ref, gates), (scaled.shape[0] - 1, up_ref, ups)):
        for at in range(0, columns, 256):
            upto = min(at + 256, columns)
            term = jnp.dot(
                scaled[left],
                w_ref[:, first + at : first + upto],
                preferred_element_type=jnp.float32,
            )
            for n, target in enumerate(targets):
                rows = target.shape[0]
                target[:, at:upto] = term[n * rows : (n + 1) * rows].astype(target.dtype)


def second_kernel(scaled, gate_ref, up_ref, *outs):
    columns = outs[1].shape[1]
    first = gate_ref.shape[1] - columns
    products(scaled, gate_ref, up_ref, first, columns, outs[0::2], outs[1::2])


def gate_up(hidden, gain, w_gate, w_up, halves):
    requests, width = hidden.shape
    units = w_gate.shape[1]
    first = units if halves == 1 else round_up(units // 2, 256)
    w_gate, w_up = fetched(w_gate), fetched(w_up)

    def shapes(columns, extra):
        return [
            jax.ShapeDtypeStruct((requests // halves, columns + more), jnp.bfloat16)
            for _ in range(halves)
            for more in (extra, 0)
        ]

    outs = [jax.ShapeDtypeStruct((halves, requests, width), jnp.bfloat16)] + shapes(first, 128)
    scaled, *parts = pl.pallas_call(
        scale_kernel,
        out_shape=outs,
        in_specs=in_vmem(4),
        out_specs=in_vmem(len(outs)),
        scratch_shapes=[pltpu.VMEM(gain.shape, jnp.float32)],
        compiler_params=kernel_params(12),
        cost_estimate=pl.CostEstimate(
            flops=4 * requests * width * first, bytes_accessed=4 * width * first, transcendentals=0
        ),
        name="gate_up",
    )(hidden, gain, w_gate, w_up)
    if halves == 1:
        return [parts]
    outs = shapes(units - first, 0)
    others = pl.pallas_call(
        second_kernel,
        out_shape=outs,
        in_specs=in_vmem(3),
        out_specs=in_vmem(len(outs)),
        compiler_params=kernel_params(12),
        cost_estimate=pl.CostEstimate(
            flops=4 * requests * width * (units - first),
            bytes_accessed=4 * width * (units - first),
            transcendentals=0,
        ),
        name="gate_up_rest",
    )(scaled, w_gate, w_up)
    return [parts, others]


def halve_kernel(*refs):
    count = len(refs) // 4
    for n in range(count):
        kept, came, send, keep = refs[n], refs[count + n], refs[2 * count + n], refs[3 * count + n]
        rows = send.shape[0]
        for at in range(0, send.shape[1], 128):
            at = slice(at, at + 128)
            total = kept[:, at].astype(jnp.float32) + came[:, at].astype(jnp.float32)
            send[:, at] = total[:rows].astype(send.dtype)
            keep[:, at] = total[rows:]


def halve(kept, came):
    half = [(k.shape[0] // 2, k.shape[1]) for k in kept]
    outs = pl.pallas_call(
        halve_kernel,
        out_shape=[jax.ShapeDtypeStruct(shape, jnp.bfloat16) for shape in half]
        + [jax.ShapeDtypeStruct(shape, jnp.float32) for shape in half],
        in_specs=in_vmem(2 * len(kept)),
        out_specs=in_vmem(2 * len(kept)),
        compiler_params=kernel_params(12),
        name="halve",
    )(*kept, *came)
    return outs[: len(kept)], outs[len(kept) :]


def inner_kernel(model, given, *refs):
    *parts, out_ref, factor_ref = refs
    gates, ups = parts[given::2], parts[given + 1 :: 2]
    columns = out_ref.shape[1]

    def total(parts, at):
        terms = [
            part[n, :, at].astype(jnp.float32) for part in parts for n in range(part.shape[0])
        ]
        return sum(terms[1:], terms[0])

    if given:
        factor = parts[0][...]
    else:
        square = jnp.sum(total(gates, slice(columns, columns + 128)), 1, keepdims=True)
        factor = jnp.broadcast_to(lax.rsqrt(square / model + 1e-06), factor_ref.shape)
    factor_ref[...] = factor
    for at in range(0, columns, 128):
        at = slice(at, at + 128)
        gate = total(gates, at) * factor
        up = total(ups, at) * factor
        out_ref[:, at] = (gate / (1.0 + jnp.exp(-gate)) * up).astype(out_ref.dtype)


def make_inner(parts, factor, model):
    given = [] if factor is None else [factor]
    rows, columns = parts[1].shape[1:]
    return pl.pallas_call(
        functools.partial(inner_kernel, model, len(given)),
        out_shape=[
            jax.ShapeDtypeStruct((rows, columns), jnp.bfloat16),
            jax.ShapeDtypeStruct((rows, 128), jnp.float32),
        ],
        in_specs=in_vmem(len(given) + len(parts)),
        out_specs=in_vmem(2),
        compiler_params=kernel_params(12),
        name="inner",
    )(*given, *parts)


def down_kernel(chunks, *refs):
    *pieces, w_ref, hidden_ref, out_ref, inner, total = refs
    width = w_ref.shape[1]
    count = len(pieces) // chunks
    share = total.shape[0] // count
    at = 0
    for c in range(chunks):
        columns = pieces[c * count].shape[1]
        for k in range(count):
            inner[k * share : (k + 1) * share, at : at + columns] = pieces[c * count + k][...]
        at += columns
    result = jnp.dot(inner[...], w_ref[...], preferred_element_type=jnp.float32)
    me = lax.axis_index("tp")
    for k in range(count):
        start = pl.multiple_of((me ^ k) * share, 16) if count > 1 else 0
        total[pl.ds(start, share), :] = result[k * share : (k + 1) * share]
    rows = hidden_ref.shape[0]
    own = pl.ds(pl.multiple_of(lax.axis_index("dp") * rows, 16), rows)
    total[own, :] += hidden_ref[...].astype(jnp.float32)
    groups = width // 128
    per_rank = out_ref.shape[1] // groups
    for d in range(out_ref.shape[0]):
        owned = [
            total[d * per_rank : (d + 1) * per_rank, g * 128 : (g + 1) * 128]
            for g in range(groups)
        ]
        out_ref[d] = jnp.concatenate(owned, 0).astype(out_ref.dtype)


def project_down(chunks, w_down, hidden, ranks):
    units, width = w_down.shape
    pieces = [piece for chunk in chunks for piece in chunk]
    requests = sum(piece.shape[0] for piece in chunks[0])
    return pl.pallas_call(
        functools.partial(down_kernel, len(chunks)),
        out_shape=jax.ShapeDtypeStruct(
            (ranks, requests // ranks * (width // 128), 128), jnp.bfloat16
        ),
        in_specs=in_vmem(len(pieces) + 2),
        out_specs=pl.BlockSpec(memory_space=pltpu.VMEM),
        scratch_shapes=[
            pltpu.VMEM((requests, units), jnp.bfloat16),
            pltpu.VMEM((requests, width), jnp.float32),
        ],
        compiler_params=kernel_params(12),
        name="project_down",
    )(*pieces, fetched(w_down), hidden)


def layer_kernel(parts_ref, out_ref, total):
    per_rank, model = out_ref.shape
    ranks = lax.axis_size("tp")
    groups = model // ranks // 128
    for t in range(ranks):
        terms = [
            parts_ref[d, :, :].astype(jnp.float32) for d in range(t, parts_ref.shape[0], ranks)
        ]
        layer = sum(terms[1:], terms[0])
        for g in range(groups):
            at = (t * groups + g) * 128
            total[:, at : at + 128] = layer[g * per_rank : (g + 1) * per_rank, :]
    out_ref[...] = total[...].astype(out_ref.dtype)


def make_layer(parts, per_rank, model):
    return pl.pallas_call(
        layer_kernel,
        out_shape=jax.ShapeDtypeStruct((per_rank, model), jnp.bfloat16),
        in_specs=in_vmem(1),
        out_specs=pl.BlockSpec(memory_space=pltpu.VMEM),
        scratch_shapes=[pltpu.VMEM((per_rank, model), jnp.float32)],
        compiler_params=kernel_params(12),
        name="layer",
    )(parts)


def round_up(value, step):
    return (value + step - 1) // step * step


def swap(parts, axes):
    return lax.all_to_all(parts, axes, split_axis=0, concat_axis=0, tiled=True)


def local(
    residual, queries, paged_latent_cache, lengths, w_uv, w_o, norm_gain, w_gate, w_up, w_down
):
    ranks_dp = lax.axis_size("dp")
    ranks_tp = lax.axis_size("tp")
    ranks = ranks_dp * ranks_tp
    per_rank, model = residual.shape
    requests = per_rank * ranks
    row_length = paged_latent_cache.shape[1]
    heads_all = queries.shape[1] // row_length
    heads_here = w_uv.shape[0]
    units = w_gate.shape[1]
    width = w_o.shape[1]


    query = queries.reshape(per_rank, heads_all, row_length)
    latent = swap(attend(lengths, query, paged_latent_cache.T, ranks), ("dp", "tp"))

    values = head_values(latent.reshape(requests * heads_here, C), w_uv)
    values, residual = lax.optimization_barrier((values, residual))
    values = from_all(values, "tp")
    added = list(split_columns(residual, ranks_tp))
    added = added[:1] + [from_distance(added[k], "tp", k) for k in range(1, ranks_tp)]
    attn, added = lax.optimization_barrier((project_out(values, w_o), added))
    attn = swap(attn.reshape(ranks_dp, requests // ranks_dp, width), "dp")
    own_hidden = make_hidden(attn, added)
    hidden = lax.all_gather(own_hidden, "dp", axis=0, tiled=True)

    halves = 2 if ranks_tp == 4 else 1
    chunks = gate_up(hidden, norm_gain.reshape(-1, 128), w_gate, w_up, halves)
    inner = []
    factor = None
    for chunk in chunks:
        if halves == 2:
            gate_send, up_send, gate_keep, up_keep = chunk
            came = [from_distance(gate_send, "tp", 1), from_distance(up_send, "tp", 2)]
            (gate_send, up_send), kept = halve([gate_keep, up_keep], came)
            came = [from_distance(gate_send, "tp", 2), from_distance(up_send, "tp", 1)]
            own, factor = make_inner([part[None] for part in (*kept, *came)], factor, model)
            far = from_distance(own, "tp", 2)
            inner.append([own, from_distance(own, "tp", 1), far, from_distance(far, "tp", 1)])
        else:
            parts = [swap(part.reshape(ranks_tp, -1, part.shape[1]), "tp") for part in chunk]
            own, factor = make_inner(parts, factor, model)
            inner.append([lax.all_gather(own, "tp", axis=0, tiled=True)])
    ffn = swap(project_down(inner, w_down, own_hidden, ranks), ("dp", "tp"))
    return make_layer(ffn, per_rank, model)


def solution(mesh):
    placed = (
        P(("dp", "tp"), None),
        P(("dp", "tp"), None),
        P(("dp", "tp"), None),
        P(),
        P(("dp", "tp"), None, None),
        P("dp", "tp"),
        P(),
        P("tp", "dp"),
        P("tp", "dp"),
        P("dp", "tp"),
    )
    return jax.shard_map(
        local, mesh=mesh, in_specs=placed, out_specs=P(("dp", "tp"), None), check_vma=False
    )
```

```python
import functools

import jax
import jax.numpy as jnp
from jax import lax
from jax.experimental import pallas as pl
from jax.experimental.pallas import tpu as pltpu
from jax.sharding import PartitionSpec as P

C = 512
BLOCK_TOKENS = 64
TILE = 1024

score_scale = 192.0 ** (-0.5)
log2_e = 1.4426950408889634
negative = -1e30


def attention_kernel(
    lens_ref,
    q_ref,
    cache_ref,
    out_ref,
    held,
    score0,
    score1,
    weight0,
    weight1,
    keep0,
    keep1,
    acc,
    done,
    best,
    mass,
    lo,
    hi,
    first,
    last,
    sems,
):
    nreq, heads, _ = q_ref.shape
    tile = held.shape[2]
    factor = score_scale * log2_e

    rank = lax.axis_index("dp") * lax.axis_size("tp") + lax.axis_index("tp")
    begin = jnp.int32(0)
    pairs = jnp.int32(0)
    for r in range(nreq):
        length = lens_ref[rank * nreq + r]
        lo[r] = begin
        hi[r] = begin + length
        first[r] = begin // tile
        last[r] = (begin + length - 1) // tile
        pairs = pairs + (last[r] - first[r] + 1)
        begin = begin + ((length + BLOCK_TOKENS - 1) // BLOCK_TOKENS) * BLOCK_TOKENS
    used = last[nreq - 1] + 1

    def copy(i):
        return pltpu.make_async_copy(
            cache_ref.at[:, pl.ds(pl.multiple_of(i * tile, tile), tile)], held.at[i], sems.at[i]
        )

    @pl.loop(0, used)
    def _(i):
        copy(i).start()

    acc[...] = jnp.zeros_like(acc)
    best[...] = jnp.full_like(best, negative)
    mass[...] = jnp.zeros_like(mass)
    weight1[...] = jnp.zeros_like(weight1)
    keep1[...] = jnp.ones_like(keep1)

    def advance(p, r, i):
        live = p + 1 < pairs
        step = (i == last[r]) & live
        nr = jnp.where(step, r + 1, r)
        ni = jnp.where(step, first[nr], jnp.where(live, i + 1, i))
        return nr, ni, live

    def fetch(r, i, live):
        fresh = live & ((r == 0) | (i > last[jnp.maximum(r - 1, 0)]))

        @pl.when(fresh)
        def _():
            copy(i).wait()

    def scores(r, i, live, target):
        begin_at = jnp.where(live, lo[r], 0)
        end_at = jnp.where(live, hi[r], 0)
        s = jnp.dot(q_ref[r], held[i], preferred_element_type=jnp.float32)
        token = i * tile + lax.broadcasted_iota(jnp.int32, (1, tile), 1)
        target[...] = s + jnp.where((token >= begin_at) & (token < end_at), 0.0, negative)

    def soften(r, source, weights, keeps):
        s = source[...]
        old = best[r]
        new = jnp.maximum(old, jnp.max(s, axis=1, keepdims=True))
        weight = jnp.exp2((s - new[:, :1]) * factor)
        keep = jnp.exp2((old - new) * factor)
        part = weight[:, :128]
        for at in range(128, tile, 128):
            part = part + weight[:, at : at + 128]
        mass[r] = mass[r] * keep + part
        best[r] = new
        weights[...] = weight.T.astype(weights.dtype)
        keeps[...] = keep.T[:8, :]

    def gather(r, i, weights, keeps):
        values = lax.dot_general(
            held[i, :C, :],
            weights[...],
            (((1,), (0,)), ((), ())),
            preferred_element_type=jnp.float32,
        )
        acc[r] = acc[r] * keeps[:1, :] + values

    zero = jnp.int32(0)
    fetch(zero, zero, pairs > 0)
    scores(zero, zero, pairs > 0, score0)

    def step(j, carry):
        r0, i0, r1, i1 = carry
        p = 2 * j
        r2, i2, live2 = advance(p, r1, i1)
        r3, i3, live3 = advance(p + 1, r2, i2)
        fetch(r2, i2, live2)
        fetch(r3, i3, live3)
        gather(r0, i0, weight1, keep1)
        scores(r2, i2, live2, score1)
        soften(r1, score0, weight0, keep0)
        gather(r1, i1, weight0, keep0)
        scores(r3, i3, live3, score0)
        soften(r2, score1, weight1, keep1)
        return r2, i2, r3, i3

    r0, i0, _, _ = lax.fori_loop(0, (pairs + 1) // 2, step, (zero, zero, zero, zero))
    gather(r0, i0, weight1, keep1)

    share = heads // out_ref.shape[0]
    for r in range(nreq):
        total = jnp.sum(mass[r], axis=1, keepdims=True)
        score0[:, :C] = acc[r].T / total
        for d in range(out_ref.shape[0]):
            done[d, r * share : (r + 1) * share, :] = score0[d * share : (d + 1) * share, :C]
    out_ref[...] = done[...].astype(out_ref.dtype)


def kernel_params(limit):
    return pltpu.CompilerParams(vmem_limit_bytes=limit * 1024 * 1024)


def in_vmem(count):
    return [pl.BlockSpec(memory_space=pltpu.VMEM)] * count


def fetched(weight):
    return pltpu.with_memory_space_constraint(weight, pltpu.VMEM)


def attend(lengths, queries, cache_t, ranks):
    nreq, heads, width = queries.shape
    tokens = cache_t.shape[1]
    tile = TILE
    tiles = tokens // tile
    return pl.pallas_call(
        attention_kernel,
        out_shape=jax.ShapeDtypeStruct((ranks, nreq * heads // ranks, C), jnp.bfloat16),
        in_specs=[pl.BlockSpec(memory_space=pltpu.SMEM)]
        + in_vmem(1)
        + [pl.BlockSpec(memory_space=pltpu.HBM)],
        out_specs=pl.BlockSpec(memory_space=pltpu.VMEM),
        scratch_shapes=[
            pltpu.VMEM((tiles, width, tile), jnp.bfloat16),
            pltpu.VMEM((heads, tile), jnp.float32),
            pltpu.VMEM((heads, tile), jnp.float32),
            pltpu.VMEM((tile, heads), jnp.bfloat16),
            pltpu.VMEM((tile, heads), jnp.bfloat16),
            pltpu.VMEM((8, heads), jnp.float32),
            pltpu.VMEM((8, heads), jnp.float32),
            pltpu.VMEM((nreq, C, heads), jnp.float32),
            pltpu.VMEM((ranks, nreq * heads // ranks, C), jnp.float32),
            pltpu.VMEM((nreq, heads, 128), jnp.float32),
            pltpu.VMEM((nreq, heads, 128), jnp.float32),
            pltpu.SMEM((nreq,), jnp.int32),
            pltpu.SMEM((nreq,), jnp.int32),
            pltpu.SMEM((nreq,), jnp.int32),
            pltpu.SMEM((nreq,), jnp.int32),
            pltpu.SemaphoreType.DMA((tiles,)),
        ],
        compiler_params=kernel_params(26),
        cost_estimate=pl.CostEstimate(
            flops=2 * heads * tokens * (width + C),
            bytes_accessed=2 * tokens * width,
            transcendentals=heads * tokens,
        ),
        name="attention",
    )(
        pltpu.with_memory_space_constraint(lengths, pltpu.HBM),
        fetched(queries),
        pltpu.with_memory_space_constraint(cache_t, pltpu.HBM),
    )


def head_values_kernel(latent_ref, w_ref, out_ref, values):
    heads, _, wide = w_ref.shape
    requests = out_ref.shape[0]
    latent = latent_ref[...]
    for h in range(heads):
        values[...] = jnp.dot(latent, w_ref[h], preferred_element_type=jnp.float32)
        picked = values[pl.ds(h, requests, stride=heads), :]
        out_ref[:, h * wide : (h + 1) * wide] = picked.astype(out_ref.dtype)


def head_values(latent, w_uv):
    heads, _, wide = w_uv.shape
    requests = latent.shape[0] // heads
    return pl.pallas_call(
        head_values_kernel,
        out_shape=jax.ShapeDtypeStruct((requests, heads * wide), jnp.bfloat16),
        in_specs=in_vmem(2),
        out_specs=pl.BlockSpec(memory_space=pltpu.VMEM),
        scratch_shapes=[pltpu.VMEM((latent.shape[0], wide), jnp.float32)],
        compiler_params=kernel_params(12),
        name="head_values",
    )(latent, w_uv)


def split_kernel(rows_ref, *out_refs):
    width = out_refs[0].shape[1]
    me = lax.axis_index("tp")
    for k, out_ref in enumerate(out_refs):
        start = pl.multiple_of((me ^ k) * width, 128)
        out_ref[...] = rows_ref[:, pl.ds(start, width)]


def split_columns(rows, ranks):
    shape = jax.ShapeDtypeStruct((rows.shape[0], rows.shape[1] // ranks), rows.dtype)
    return pl.pallas_call(
        split_kernel,
        out_shape=[shape] * ranks,
        in_specs=in_vmem(1),
        out_specs=in_vmem(ranks),
        compiler_params=kernel_params(8),
        name="split_columns",
    )(rows)


def from_distance(piece, axis, distance):
    return lax.ppermute(piece, axis, [(k, k ^ distance) for k in range(lax.axis_size(axis))])


def from_all(piece, axis):
    return [piece] + [from_distance(piece, axis, k) for k in range(1, lax.axis_size(axis))]


def own_output_kernel(value_ref, w_ref, out_ref):
    depth = value_ref.shape[1]
    rows = pl.ds(pl.multiple_of(lax.axis_index("tp") * depth, 128), depth)
    out_ref[...] = jnp.dot(value_ref[...], w_ref[rows, :], preferred_element_type=jnp.float32)


def output_kernel(*refs):
    own_ref, *values, w_ref, out_ref, total = refs
    depth = values[0].shape[1]
    me = lax.axis_index("tp")
    for k, value in enumerate(values, 1):
        rows = pl.ds(pl.multiple_of((me ^ k) * depth, 128), depth)
        term = jnp.dot(value[...], w_ref[rows, :], preferred_element_type=jnp.float32)
        if k == 1:
            total[...] = own_ref[...] + term
        else:
            total[...] += term
    out_ref[...] = total[...].astype(out_ref.dtype)


def project_out(values, w_o):
    requests, depth = values[0].shape
    width = w_o.shape[1]
    w_o = fetched(w_o)
    own = pl.pallas_call(
        own_output_kernel,
        out_shape=jax.ShapeDtypeStruct((requests, width), jnp.float32),
        in_specs=in_vmem(2),
        out_specs=pl.BlockSpec(memory_space=pltpu.VMEM),
        compiler_params=kernel_params(12),
        cost_estimate=pl.CostEstimate(
            flops=2 * requests * depth * width, bytes_accessed=2 * depth * width, transcendentals=0
        ),
        name="project_own",
    )(values[0], w_o)
    return pl.pallas_call(
        output_kernel,
        out_shape=jax.ShapeDtypeStruct((requests, width), jnp.bfloat16),
        in_specs=in_vmem(len(values) + 1),
        out_specs=pl.BlockSpec(memory_space=pltpu.VMEM),
        scratch_shapes=[pltpu.VMEM((requests, width), jnp.float32)],
        compiler_params=kernel_params(12),
        name="project_out",
    )(own, *values[1:], w_o)


def hidden_kernel(parts_ref, *refs):
    *slices, out_ref, added = refs
    per_rank = slices[0].shape[0]
    me = lax.axis_index("tp")
    for k, piece in enumerate(slices):
        added[me ^ k] = piece[...].astype(jnp.float32)
    width = out_ref.shape[1]
    for at in range(0, width, 128):
        at = slice(at, at + 128)
        total = parts_ref[0, :, at].astype(jnp.float32)
        for d in range(1, parts_ref.shape[0]):
            total = total + parts_ref[d, :, at].astype(jnp.float32)
        terms = [added[s, :, at] for s in range(len(slices))]
        out_ref[:, at] = (total + jnp.concatenate(terms, 0)).astype(out_ref.dtype)


def make_hidden(parts, slices):
    return pl.pallas_call(
        hidden_kernel,
        out_shape=jax.ShapeDtypeStruct(parts.shape[1:], jnp.bfloat16),
        in_specs=in_vmem(1 + len(slices)),
        out_specs=pl.BlockSpec(memory_space=pltpu.VMEM),
        scratch_shapes=[pltpu.VMEM((len(slices),) + slices[0].shape, jnp.float32)],
        compiler_params=kernel_params(12),
        name="hidden",
    )(parts, *slices)


def scale_kernel(hidden_ref, gain_ref, gate_ref, up_ref, scaled, gate_sum, up_sum, *refs):
    *outs, gains = refs
    ranks = lax.axis_size("tp")
    halves = scaled.shape[0]
    requests, width = hidden_ref.shape
    share = requests // ranks
    groups = width // 128
    me = lax.axis_index("tp")
    places = [[3, 1, 2, 0], [3, 2, 1, 0]] if halves == 2 else [list(range(ranks))]

    gains[...] = gain_ref[...].astype(jnp.float32)
    squares = [None] * ranks
    for k in range(ranks):
        block = me ^ k if halves == 2 else k
        start = block * share if halves == 1 else pl.multiple_of(block * share, 16)
        square = jnp.zeros((share, 128), jnp.float32)
        for g in range(groups):
            at = slice(g * 128, (g + 1) * 128)
            x = hidden_ref[pl.ds(start, share), at].astype(jnp.float32)
            square = square + x * x
            gain = gains[pl.ds(me * groups + g, 1), :]
            value = (x * gain).astype(scaled.dtype)
            for n, place in enumerate(places):
                scaled[n, place[k] * share : (place[k] + 1) * share, at] = value
        squares[places[0][k]] = square
    square = jnp.sum(jnp.concatenate(squares, 0), 1, keepdims=True)
    top = square.astype(jnp.bfloat16).astype(jnp.float32)
    middle = (square - top).astype(jnp.bfloat16).astype(jnp.float32)
    low = square - top - middle
    lane = lax.broadcasted_iota(jnp.int32, (requests, 128), 1)
    digits = jnp.where(lane == 0, top, jnp.where(lane == 1, middle, jnp.where(lane == 2, low, 0.0)))
    gates = [gate_sum, outs[0]] if halves == 2 else [gate_sum]
    ups = [up_sum, outs[1]] if halves == 2 else [up_sum]
    columns = up_sum.shape[1]
    for n, target in enumerate(gates):
        rows = target.shape[0]
        target[:, columns:] = digits[n * rows : (n + 1) * rows].astype(target.dtype)
    products(scaled, gate_ref, up_ref, 0, columns, gates, ups)


def products(scaled, gate_ref, up_ref, first, columns, gates, ups):
    for left, w_ref, targets in ((0, gate_ref, gates), (scaled.shape[0] - 1, up_ref, ups)):
        for at in range(0, columns, 256):
            upto = min(at + 256, columns)
            term = jnp.dot(
                scaled[left],
                w_ref[:, first + at : first + upto],
                preferred_element_type=jnp.float32,
            )
            for n, target in enumerate(targets):
                rows = target.shape[0]
                target[:, at:upto] = term[n * rows : (n + 1) * rows].astype(target.dtype)


def second_kernel(scaled, gate_ref, up_ref, *outs):
    columns = outs[1].shape[1]
    first = gate_ref.shape[1] - columns
    products(scaled, gate_ref, up_ref, first, columns, outs[0::2], outs[1::2])


def gate_up(hidden, gain, w_gate, w_up, halves):
    requests, width = hidden.shape
    units = w_gate.shape[1]
    first = units if halves == 1 else round_up(units * 5 // 8, 256)
    w_gate, w_up = fetched(w_gate), fetched(w_up)

    def shapes(columns, extra):
        return [
            jax.ShapeDtypeStruct((requests // halves, columns + more), jnp.bfloat16)
            for _ in range(halves)
            for more in (extra, 0)
        ]

    outs = [jax.ShapeDtypeStruct((halves, requests, width), jnp.bfloat16)] + shapes(first, 128)
    scaled, *parts = pl.pallas_call(
        scale_kernel,
        out_shape=outs,
        in_specs=in_vmem(4),
        out_specs=in_vmem(len(outs)),
        scratch_shapes=[pltpu.VMEM(gain.shape, jnp.float32)],
        compiler_params=kernel_params(12),
        cost_estimate=pl.CostEstimate(
            flops=4 * requests * width * first, bytes_accessed=4 * width * first, transcendentals=0
        ),
        name="gate_up",
    )(hidden, gain, w_gate, w_up)
    if halves == 1:
        return [parts]
    outs = shapes(units - first, 0)
    others = pl.pallas_call(
        second_kernel,
        out_shape=outs,
        in_specs=in_vmem(3),
        out_specs=in_vmem(len(outs)),
        compiler_params=kernel_params(12),
        cost_estimate=pl.CostEstimate(
            flops=4 * requests * width * (units - first),
            bytes_accessed=4 * width * (units - first),
            transcendentals=0,
        ),
        name="gate_up_rest",
    )(scaled, w_gate, w_up)
    return [parts, others]


def halve_kernel(*refs):
    count = len(refs) // 4
    for n in range(count):
        kept, came, send, keep = refs[n], refs[count + n], refs[2 * count + n], refs[3 * count + n]
        rows = send.shape[0]
        for at in range(0, send.shape[1], 128):
            at = slice(at, at + 128)
            total = kept[:, at].astype(jnp.float32) + came[:, at].astype(jnp.float32)
            send[:, at] = total[:rows].astype(send.dtype)
            keep[:, at] = total[rows:]


def halve(kept, came):
    half = [(k.shape[0] // 2, k.shape[1]) for k in kept]
    outs = pl.pallas_call(
        halve_kernel,
        out_shape=[jax.ShapeDtypeStruct(shape, jnp.bfloat16) for shape in half]
        + [jax.ShapeDtypeStruct(shape, jnp.float32) for shape in half],
        in_specs=in_vmem(2 * len(kept)),
        out_specs=in_vmem(2 * len(kept)),
        compiler_params=kernel_params(12),
        name="halve",
    )(*kept, *came)
    return outs[: len(kept)], outs[len(kept) :]


def inner_kernel(model, given, *refs):
    *parts, out_ref, factor_ref = refs
    gates, ups = parts[given::2], parts[given + 1 :: 2]
    columns = out_ref.shape[1]

    def total(parts, at):
        terms = [
            part[n, :, at].astype(jnp.float32) for part in parts for n in range(part.shape[0])
        ]
        return sum(terms[1:], terms[0])

    if given:
        factor = parts[0][...]
    else:
        square = jnp.sum(total(gates, slice(columns, columns + 128)), 1, keepdims=True)
        factor = jnp.broadcast_to(lax.rsqrt(square / model + 1e-06), factor_ref.shape)
    factor_ref[...] = factor
    for at in range(0, columns, 128):
        at = slice(at, at + 128)
        gate = total(gates, at) * factor
        up = total(ups, at) * factor
        out_ref[:, at] = (gate / (1.0 + jnp.exp(-gate)) * up).astype(out_ref.dtype)


def make_inner(parts, factor, model):
    given = [] if factor is None else [factor]
    rows, columns = parts[1].shape[1:]
    return pl.pallas_call(
        functools.partial(inner_kernel, model, len(given)),
        out_shape=[
            jax.ShapeDtypeStruct((rows, columns), jnp.bfloat16),
            jax.ShapeDtypeStruct((rows, 128), jnp.float32),
        ],
        in_specs=in_vmem(len(given) + len(parts)),
        out_specs=in_vmem(2),
        compiler_params=kernel_params(12),
        name="inner",
    )(*given, *parts)


def down_kernel(chunks, *refs):
    *pieces, w_ref, hidden_ref, out_ref, inner, total = refs
    width = w_ref.shape[1]
    count = len(pieces) // chunks
    share = total.shape[0] // count
    at = 0
    for c in range(chunks):
        columns = pieces[c * count].shape[1]
        for k in range(count):
            inner[k * share : (k + 1) * share, at : at + columns] = pieces[c * count + k][...]
        at += columns
    result = jnp.dot(inner[...], w_ref[...], preferred_element_type=jnp.float32)
    me = lax.axis_index("tp")
    for k in range(count):
        start = pl.multiple_of((me ^ k) * share, 16) if count > 1 else 0
        total[pl.ds(start, share), :] = result[k * share : (k + 1) * share]
    rows = hidden_ref.shape[0]
    own = pl.ds(pl.multiple_of(lax.axis_index("dp") * rows, 16), rows)
    total[own, :] += hidden_ref[...].astype(jnp.float32)
    groups = width // 128
    per_rank = out_ref.shape[1] // groups
    for d in range(out_ref.shape[0]):
        owned = [
            total[d * per_rank : (d + 1) * per_rank, g * 128 : (g + 1) * 128]
            for g in range(groups)
        ]
        out_ref[d] = jnp.concatenate(owned, 0).astype(out_ref.dtype)


def project_down(chunks, w_down, hidden, ranks):
    units, width = w_down.shape
    pieces = [piece for chunk in chunks for piece in chunk]
    requests = sum(piece.shape[0] for piece in chunks[0])
    return pl.pallas_call(
        functools.partial(down_kernel, len(chunks)),
        out_shape=jax.ShapeDtypeStruct(
            (ranks, requests // ranks * (width // 128), 128), jnp.bfloat16
        ),
        in_specs=in_vmem(len(pieces) + 2),
        out_specs=pl.BlockSpec(memory_space=pltpu.VMEM),
        scratch_shapes=[
            pltpu.VMEM((requests, units), jnp.bfloat16),
            pltpu.VMEM((requests, width), jnp.float32),
        ],
        compiler_params=kernel_params(12),
        name="project_down",
    )(*pieces, fetched(w_down), hidden)


def layer_kernel(parts_ref, out_ref, total):
    per_rank, model = out_ref.shape
    ranks = lax.axis_size("tp")
    groups = model // ranks // 128
    for t in range(ranks):
        terms = [
            parts_ref[d, :, :].astype(jnp.float32) for d in range(t, parts_ref.shape[0], ranks)
        ]
        layer = sum(terms[1:], terms[0])
        for g in range(groups):
            at = (t * groups + g) * 128
            total[:, at : at + 128] = layer[g * per_rank : (g + 1) * per_rank, :]
    out_ref[...] = total[...].astype(out_ref.dtype)


def make_layer(parts, per_rank, model):
    return pl.pallas_call(
        layer_kernel,
        out_shape=jax.ShapeDtypeStruct((per_rank, model), jnp.bfloat16),
        in_specs=in_vmem(1),
        out_specs=pl.BlockSpec(memory_space=pltpu.VMEM),
        scratch_shapes=[pltpu.VMEM((per_rank, model), jnp.float32)],
        compiler_params=kernel_params(12),
        name="layer",
    )(parts)


def round_up(value, step):
    return (value + step - 1) // step * step


def swap(parts, axes):
    return lax.all_to_all(parts, axes, split_axis=0, concat_axis=0, tiled=True)


def local(
    residual, queries, paged_latent_cache, lengths, w_uv, w_o, norm_gain, w_gate, w_up, w_down
):
    ranks_dp = lax.axis_size("dp")
    ranks_tp = lax.axis_size("tp")
    ranks = ranks_dp * ranks_tp
    per_rank, model = residual.shape
    requests = per_rank * ranks
    row_length = paged_latent_cache.shape[1]
    heads_all = queries.shape[1] // row_length
    heads_here = w_uv.shape[0]
    units = w_gate.shape[1]
    width = w_o.shape[1]


    query = queries.reshape(per_rank, heads_all, row_length)
    latent = swap(attend(lengths, query, paged_latent_cache.T, ranks), ("dp", "tp"))

    values = head_values(latent.reshape(requests * heads_here, C), w_uv)
    values, residual = lax.optimization_barrier((values, residual))
    values = from_all(values, "tp")
    added = list(split_columns(residual, ranks_tp))
    added = added[:1] + [from_distance(added[k], "tp", k) for k in range(1, ranks_tp)]
    attn, added = lax.optimization_barrier((project_out(values, w_o), added))
    attn = swap(attn.reshape(ranks_dp, requests // ranks_dp, width), "dp")
    own_hidden = make_hidden(attn, added)
    hidden = lax.all_gather(own_hidden, "dp", axis=0, tiled=True)

    halves = 2 if ranks_tp == 4 else 1
    chunks = gate_up(hidden, norm_gain.reshape(-1, 128), w_gate, w_up, halves)
    inner = []
    factor = None
    for chunk in chunks:
        if halves == 2:
            gate_send, up_send, gate_keep, up_keep = chunk
            came = [from_distance(gate_send, "tp", 1), from_distance(up_send, "tp", 2)]
            (gate_send, up_send), kept = halve([gate_keep, up_keep], came)
            came = [from_distance(gate_send, "tp", 2), from_distance(up_send, "tp", 1)]
            own, factor = make_inner([part[None] for part in (*kept, *came)], factor, model)
            far = from_distance(own, "tp", 2)
            inner.append([own, from_distance(own, "tp", 1), far, from_distance(far, "tp", 1)])
        else:
            parts = [swap(part.reshape(ranks_tp, -1, part.shape[1]), "tp") for part in chunk]
            own, factor = make_inner(parts, factor, model)
            inner.append([lax.all_gather(own, "tp", axis=0, tiled=True)])
    ffn = swap(project_down(inner, w_down, own_hidden, ranks), ("dp", "tp"))
    return make_layer(ffn, per_rank, model)


def solution(mesh):
    placed = (
        P(("dp", "tp"), None),
        P(("dp", "tp"), None),
        P(("dp", "tp"), None),
        P(),
        P(("dp", "tp"), None, None),
        P("dp", "tp"),
        P(),
        P("tp", "dp"),
        P("tp", "dp"),
        P("dp", "tp"),
    )
    return jax.shard_map(
        local, mesh=mesh, in_specs=placed, out_specs=P(("dp", "tp"), None), check_vma=False
    )
```

```python
import functools

import jax
import jax.numpy as jnp
from jax import lax
from jax.experimental import pallas as pl
from jax.experimental.pallas import tpu as pltpu
from jax.sharding import PartitionSpec as P

C = 512
BLOCK_TOKENS = 64
TILE = 512

score_scale = 192.0 ** (-0.5)
log2_e = 1.4426950408889634
negative = -1e30


def attention_kernel(
    lens_ref,
    raw_ref,
    cache_ref,
    out_ref,
    q_ref,
    pairs_of_heads,
    rows_of_heads,
    held,
    score0,
    score1,
    weight0,
    weight1,
    keep0,
    keep1,
    acc,
    done,
    best,
    mass,
    lo,
    hi,
    first,
    last,
    sems,
):
    nreq, heads, _ = q_ref.shape
    tile = held.shape[2]
    factor = score_scale * log2_e

    rank = lax.axis_index("dp") * lax.axis_size("tp") + lax.axis_index("tp")
    begin = jnp.int32(0)
    pairs = jnp.int32(0)
    for r in range(nreq):
        length = lens_ref[rank * nreq + r]
        lo[r] = begin
        hi[r] = begin + length
        first[r] = begin // tile
        last[r] = (begin + length - 1) // tile
        pairs = pairs + (last[r] - first[r] + 1)
        begin = begin + ((length + BLOCK_TOKENS - 1) // BLOCK_TOKENS) * BLOCK_TOKENS
    used = last[nreq - 1] + 1

    def copy(i):
        return pltpu.make_async_copy(
            cache_ref.at[:, pl.ds(pl.multiple_of(i * tile, tile), tile)], held.at[i], sems.at[i]
        )

    @pl.loop(0, used)
    def _(i):
        copy(i).start()

    width = q_ref.shape[2]
    half = heads // 2
    tail = width % 128
    full = width // 128
    for j in range(half):
        for c in range(pairs_of_heads.shape[0]):
            at = 2 * width * j + 128 * c
            pairs_of_heads[c, pl.ds(j, nreq, stride=half), :] = raw_ref[:, at : at + 128].astype(
                jnp.float32
            )
    for r in range(nreq):
        rows = slice(r * half, (r + 1) * half)
        for c in range(full + 1):
            rows_of_heads[c, pl.ds(0, half, stride=2), :] = pairs_of_heads[c, rows, :]
            ahead = min(full + c + 1, pairs_of_heads.shape[0] - 1)
            rows_of_heads[c, pl.ds(1, half, stride=2), :] = jnp.concatenate(
                [pairs_of_heads[full + c, rows, tail:], pairs_of_heads[ahead, rows, :tail]], 1
            )
        for c in range(full):
            q_ref[r, :, c * 128 : (c + 1) * 128] = rows_of_heads[c].astype(q_ref.dtype)
        q_ref[r, :, full * 128 :] = rows_of_heads[full, :, :tail].astype(q_ref.dtype)

    acc[...] = jnp.zeros_like(acc)
    best[...] = jnp.full_like(best, negative)
    mass[...] = jnp.zeros_like(mass)
    weight1[...] = jnp.zeros_like(weight1)
    keep1[...] = jnp.ones_like(keep1)

    def advance(p, r, i):
        live = p + 1 < pairs
        step = (i == last[r]) & live
        nr = jnp.where(step, r + 1, r)
        ni = jnp.where(step, first[nr], jnp.where(live, i + 1, i))
        return nr, ni, live

    def fetch(r, i, live):
        fresh = live & ((r == 0) | (i > last[jnp.maximum(r - 1, 0)]))

        @pl.when(fresh)
        def _():
            copy(i).wait()

    def scores(r, i, live, target):
        begin_at = jnp.where(live, lo[r], 0)
        end_at = jnp.where(live, hi[r], 0)
        s = jnp.dot(q_ref[r], held[i], preferred_element_type=jnp.float32)
        token = i * tile + lax.broadcasted_iota(jnp.int32, (1, tile), 1)
        target[...] = s + jnp.where((token >= begin_at) & (token < end_at), 0.0, negative)

    def soften(r, source, weights, keeps):
        s = source[...]
        old = best[r]
        new = jnp.maximum(old, jnp.max(s, axis=1, keepdims=True))
        weight = jnp.exp2((s - new[:, :1]) * factor)
        keep = jnp.exp2((old - new) * factor)
        part = weight[:, :128]
        for at in range(128, tile, 128):
            part = part + weight[:, at : at + 128]
        mass[r] = mass[r] * keep + part
        best[r] = new
        weights[...] = weight.T.astype(weights.dtype)
        keeps[...] = keep.T[:8, :]

    def gather(r, i, weights, keeps):
        values = lax.dot_general(
            held[i, :C, :],
            weights[...],
            (((1,), (0,)), ((), ())),
            preferred_element_type=jnp.float32,
        )
        acc[r] = acc[r] * keeps[:1, :] + values

    zero = jnp.int32(0)
    fetch(zero, zero, pairs > 0)
    scores(zero, zero, pairs > 0, score0)

    def step(j, carry):
        r0, i0, r1, i1 = carry
        p = 2 * j
        r2, i2, live2 = advance(p, r1, i1)
        r3, i3, live3 = advance(p + 1, r2, i2)
        fetch(r2, i2, live2)
        fetch(r3, i3, live3)
        gather(r0, i0, weight1, keep1)
        scores(r2, i2, live2, score1)
        soften(r1, score0, weight0, keep0)
        gather(r1, i1, weight0, keep0)
        scores(r3, i3, live3, score0)
        soften(r2, score1, weight1, keep1)
        return r2, i2, r3, i3

    r0, i0, _, _ = lax.fori_loop(0, (pairs + 1) // 2, step, (zero, zero, zero, zero))
    gather(r0, i0, weight1, keep1)

    share = heads // out_ref.shape[0]
    for r in range(nreq):
        total = jnp.sum(mass[r], axis=1, keepdims=True)
        score0[:, :C] = acc[r].T / total
        for d in range(out_ref.shape[0]):
            done[d, r * share : (r + 1) * share, :] = score0[d * share : (d + 1) * share, :C]
    out_ref[...] = done[...].astype(out_ref.dtype)


def kernel_params(limit):
    return pltpu.CompilerParams(vmem_limit_bytes=limit * 1024 * 1024)


def in_vmem(count):
    return [pl.BlockSpec(memory_space=pltpu.VMEM)] * count


def fetched(weight):
    return pltpu.with_memory_space_constraint(weight, pltpu.VMEM)


def attend(lengths, queries, cache_t, ranks):
    nreq = queries.shape[0]
    width, tokens = cache_t.shape
    heads = queries.shape[1] // width
    tile = TILE
    tiles = tokens // tile
    return pl.pallas_call(
        attention_kernel,
        out_shape=jax.ShapeDtypeStruct((ranks, nreq * heads // ranks, C), jnp.bfloat16),
        in_specs=[pl.BlockSpec(memory_space=pltpu.SMEM)]
        + in_vmem(1)
        + [pl.BlockSpec(memory_space=pltpu.HBM)],
        out_specs=pl.BlockSpec(memory_space=pltpu.VMEM),
        scratch_shapes=[
            pltpu.VMEM((nreq, heads, width), jnp.bfloat16),
            pltpu.VMEM((2 * width // 128, nreq * heads // 2, 128), jnp.float32),
            pltpu.VMEM((width // 128 + 1, heads, 128), jnp.float32),
            pltpu.VMEM((tiles, width, tile), jnp.bfloat16),
            pltpu.VMEM((heads, tile), jnp.float32),
            pltpu.VMEM((heads, tile), jnp.float32),
            pltpu.VMEM((tile, heads), jnp.bfloat16),
            pltpu.VMEM((tile, heads), jnp.bfloat16),
            pltpu.VMEM((8, heads), jnp.float32),
            pltpu.VMEM((8, heads), jnp.float32),
            pltpu.VMEM((nreq, C, heads), jnp.float32),
            pltpu.VMEM((ranks, nreq * heads // ranks, C), jnp.float32),
            pltpu.VMEM((nreq, heads, 128), jnp.float32),
            pltpu.VMEM((nreq, heads, 128), jnp.float32),
            pltpu.SMEM((nreq,), jnp.int32),
            pltpu.SMEM((nreq,), jnp.int32),
            pltpu.SMEM((nreq,), jnp.int32),
            pltpu.SMEM((nreq,), jnp.int32),
            pltpu.SemaphoreType.DMA((tiles,)),
        ],
        compiler_params=kernel_params(28),
        cost_estimate=pl.CostEstimate(
            flops=2 * heads * tokens * (width + C),
            bytes_accessed=2 * tokens * width,
            transcendentals=heads * tokens,
        ),
        name="attention",
    )(
        pltpu.with_memory_space_constraint(lengths, pltpu.HBM),
        pltpu.with_memory_space_constraint(queries, pltpu.HBM),
        pltpu.with_memory_space_constraint(cache_t, pltpu.HBM),
    )


def head_values_kernel(latent_ref, w_ref, out_ref, values):
    heads, _, wide = w_ref.shape
    requests = out_ref.shape[0]
    latent = latent_ref[...]
    for h in range(heads):
        values[...] = jnp.dot(latent, w_ref[h], preferred_element_type=jnp.float32)
        picked = values[pl.ds(h, requests, stride=heads), :]
        out_ref[:, h * wide : (h + 1) * wide] = picked.astype(out_ref.dtype)


def head_values(latent, w_uv):
    heads, _, wide = w_uv.shape
    requests = latent.shape[0] // heads
    return pl.pallas_call(
        head_values_kernel,
        out_shape=jax.ShapeDtypeStruct((requests, heads * wide), jnp.bfloat16),
        in_specs=in_vmem(2),
        out_specs=pl.BlockSpec(memory_space=pltpu.VMEM),
        scratch_shapes=[pltpu.VMEM((latent.shape[0], wide), jnp.float32)],
        compiler_params=kernel_params(12),
        name="head_values",
    )(latent, w_uv)


def split_kernel(rows_ref, *out_refs):
    width = out_refs[0].shape[1]
    me = lax.axis_index("tp")
    for k, out_ref in enumerate(out_refs):
        start = pl.multiple_of((me ^ k) * width, 128)
        out_ref[...] = rows_ref[:, pl.ds(start, width)]


def split_columns(rows, ranks):
    shape = jax.ShapeDtypeStruct((rows.shape[0], rows.shape[1] // ranks), rows.dtype)
    return pl.pallas_call(
        split_kernel,
        out_shape=[shape] * ranks,
        in_specs=in_vmem(1),
        out_specs=in_vmem(ranks),
        compiler_params=kernel_params(8),
        name="split_columns",
    )(rows)


def from_distance(piece, axis, distance):
    return lax.ppermute(piece, axis, [(k, k ^ distance) for k in range(lax.axis_size(axis))])


def from_all(piece, axis):
    return [piece] + [from_distance(piece, axis, k) for k in range(1, lax.axis_size(axis))]


def own_output_kernel(value_ref, w_ref, out_ref):
    depth = value_ref.shape[1]
    rows = pl.ds(pl.multiple_of(lax.axis_index("tp") * depth, 128), depth)
    out_ref[...] = jnp.dot(value_ref[...], w_ref[rows, :], preferred_element_type=jnp.float32)


def output_kernel(*refs):
    own_ref, *values, w_ref, out_ref, total = refs
    depth = values[0].shape[1]
    me = lax.axis_index("tp")
    for k, value in enumerate(values, 1):
        rows = pl.ds(pl.multiple_of((me ^ k) * depth, 128), depth)
        term = jnp.dot(value[...], w_ref[rows, :], preferred_element_type=jnp.float32)
        if k == 1:
            total[...] = own_ref[...] + term
        else:
            total[...] += term
    out_ref[...] = total[...].astype(out_ref.dtype)


def project_out(values, w_o):
    requests, depth = values[0].shape
    width = w_o.shape[1]
    w_o = fetched(w_o)
    own = pl.pallas_call(
        own_output_kernel,
        out_shape=jax.ShapeDtypeStruct((requests, width), jnp.float32),
        in_specs=in_vmem(2),
        out_specs=pl.BlockSpec(memory_space=pltpu.VMEM),
        compiler_params=kernel_params(12),
        cost_estimate=pl.CostEstimate(
            flops=2 * requests * depth * width, bytes_accessed=2 * depth * width, transcendentals=0
        ),
        name="project_own",
    )(values[0], w_o)
    return pl.pallas_call(
        output_kernel,
        out_shape=jax.ShapeDtypeStruct((requests, width), jnp.bfloat16),
        in_specs=in_vmem(len(values) + 1),
        out_specs=pl.BlockSpec(memory_space=pltpu.VMEM),
        scratch_shapes=[pltpu.VMEM((requests, width), jnp.float32)],
        compiler_params=kernel_params(12),
        name="project_out",
    )(own, *values[1:], w_o)


def hidden_kernel(parts_ref, *refs):
    *slices, out_ref, added = refs
    per_rank = slices[0].shape[0]
    me = lax.axis_index("tp")
    for k, piece in enumerate(slices):
        added[me ^ k] = piece[...].astype(jnp.float32)
    width = out_ref.shape[1]
    for at in range(0, width, 128):
        at = slice(at, at + 128)
        total = parts_ref[0, :, at].astype(jnp.float32)
        for d in range(1, parts_ref.shape[0]):
            total = total + parts_ref[d, :, at].astype(jnp.float32)
        terms = [added[s, :, at] for s in range(len(slices))]
        out_ref[:, at] = (total + jnp.concatenate(terms, 0)).astype(out_ref.dtype)


def make_hidden(parts, slices):
    return pl.pallas_call(
        hidden_kernel,
        out_shape=jax.ShapeDtypeStruct(parts.shape[1:], jnp.bfloat16),
        in_specs=in_vmem(1 + len(slices)),
        out_specs=pl.BlockSpec(memory_space=pltpu.VMEM),
        scratch_shapes=[pltpu.VMEM((len(slices),) + slices[0].shape, jnp.float32)],
        compiler_params=kernel_params(12),
        name="hidden",
    )(parts, *slices)


def scale_kernel(hidden_ref, gain_ref, gate_ref, up_ref, scaled, gate_sum, up_sum, *refs):
    *outs, gains = refs
    ranks = lax.axis_size("tp")
    halves = scaled.shape[0]
    requests, width = hidden_ref.shape
    share = requests // ranks
    groups = width // 128
    me = lax.axis_index("tp")
    places = [[3, 1, 2, 0], [3, 2, 1, 0]] if halves == 2 else [list(range(ranks))]

    gains[...] = gain_ref[...].astype(jnp.float32)
    squares = [None] * ranks
    for k in range(ranks):
        block = me ^ k if halves == 2 else k
        start = block * share if halves == 1 else pl.multiple_of(block * share, 16)
        square = jnp.zeros((share, 128), jnp.float32)
        for g in range(groups):
            at = slice(g * 128, (g + 1) * 128)
            x = hidden_ref[pl.ds(start, share), at].astype(jnp.float32)
            square = square + x * x
            gain = gains[pl.ds(me * groups + g, 1), :]
            value = (x * gain).astype(scaled.dtype)
            for n, place in enumerate(places):
                scaled[n, place[k] * share : (place[k] + 1) * share, at] = value
        squares[places[0][k]] = square
    square = jnp.sum(jnp.concatenate(squares, 0), 1, keepdims=True)
    top = square.astype(jnp.bfloat16).astype(jnp.float32)
    middle = (square - top).astype(jnp.bfloat16).astype(jnp.float32)
    low = square - top - middle
    lane = lax.broadcasted_iota(jnp.int32, (requests, 128), 1)
    digits = jnp.where(lane == 0, top, jnp.where(lane == 1, middle, jnp.where(lane == 2, low, 0.0)))
    gates = [gate_sum, outs[0]] if halves == 2 else [gate_sum]
    ups = [up_sum, outs[1]] if halves == 2 else [up_sum]
    columns = up_sum.shape[1]
    for n, target in enumerate(gates):
        rows = target.shape[0]
        target[:, columns:] = digits[n * rows : (n + 1) * rows].astype(target.dtype)
    products(scaled, gate_ref, up_ref, 0, columns, gates, ups)


def products(scaled, gate_ref, up_ref, first, columns, gates, ups):
    for left, w_ref, targets in ((0, gate_ref, gates), (scaled.shape[0] - 1, up_ref, ups)):
        for at in range(0, columns, 256):
            upto = min(at + 256, columns)
            term = jnp.dot(
                scaled[left],
                w_ref[:, first + at : first + upto],
                preferred_element_type=jnp.float32,
            )
            for n, target in enumerate(targets):
                rows = target.shape[0]
                target[:, at:upto] = term[n * rows : (n + 1) * rows].astype(target.dtype)


def second_kernel(scaled, gate_ref, up_ref, *outs):
    columns = outs[1].shape[1]
    first = gate_ref.shape[1] - columns
    products(scaled, gate_ref, up_ref, first, columns, outs[0::2], outs[1::2])


def gate_up(hidden, gain, w_gate, w_up, halves):
    requests, width = hidden.shape
    units = w_gate.shape[1]
    first = units if halves == 1 else round_up(units // 2, 256)
    w_gate, w_up = fetched(w_gate), fetched(w_up)

    def shapes(columns, extra):
        return [
            jax.ShapeDtypeStruct((requests // halves, columns + more), jnp.bfloat16)
            for _ in range(halves)
            for more in (extra, 0)
        ]

    outs = [jax.ShapeDtypeStruct((halves, requests, width), jnp.bfloat16)] + shapes(first, 128)
    scaled, *parts = pl.pallas_call(
        scale_kernel,
        out_shape=outs,
        in_specs=in_vmem(4),
        out_specs=in_vmem(len(outs)),
        scratch_shapes=[pltpu.VMEM(gain.shape, jnp.float32)],
        compiler_params=kernel_params(12),
        cost_estimate=pl.CostEstimate(
            flops=4 * requests * width * first, bytes_accessed=4 * width * first, transcendentals=0
        ),
        name="gate_up",
    )(hidden, gain, w_gate, w_up)
    if halves == 1:
        return [parts]
    outs = shapes(units - first, 0)
    others = pl.pallas_call(
        second_kernel,
        out_shape=outs,
        in_specs=in_vmem(3),
        out_specs=in_vmem(len(outs)),
        compiler_params=kernel_params(12),
        cost_estimate=pl.CostEstimate(
            flops=4 * requests * width * (units - first),
            bytes_accessed=4 * width * (units - first),
            transcendentals=0,
        ),
        name="gate_up_rest",
    )(scaled, w_gate, w_up)
    return [parts, others]


def halve_kernel(*refs):
    count = len(refs) // 4
    for n in range(count):
        kept, came, send, keep = refs[n], refs[count + n], refs[2 * count + n], refs[3 * count + n]
        rows = send.shape[0]
        for at in range(0, send.shape[1], 128):
            at = slice(at, at + 128)
            total = kept[:, at].astype(jnp.float32) + came[:, at].astype(jnp.float32)
            send[:, at] = total[:rows].astype(send.dtype)
            keep[:, at] = total[rows:]


def halve(kept, came):
    half = [(k.shape[0] // 2, k.shape[1]) for k in kept]
    outs = pl.pallas_call(
        halve_kernel,
        out_shape=[jax.ShapeDtypeStruct(shape, jnp.bfloat16) for shape in half]
        + [jax.ShapeDtypeStruct(shape, jnp.float32) for shape in half],
        in_specs=in_vmem(2 * len(kept)),
        out_specs=in_vmem(2 * len(kept)),
        compiler_params=kernel_params(12),
        name="halve",
    )(*kept, *came)
    return outs[: len(kept)], outs[len(kept) :]


def inner_kernel(model, given, *refs):
    *parts, out_ref, factor_ref = refs
    gates, ups = parts[given::2], parts[given + 1 :: 2]
    columns = out_ref.shape[1]

    def total(parts, at):
        terms = [
            part[n, :, at].astype(jnp.float32) for part in parts for n in range(part.shape[0])
        ]
        return sum(terms[1:], terms[0])

    if given:
        factor = parts[0][...]
    else:
        square = jnp.sum(total(gates, slice(columns, columns + 128)), 1, keepdims=True)
        factor = jnp.broadcast_to(lax.rsqrt(square / model + 1e-06), factor_ref.shape)
    factor_ref[...] = factor
    for at in range(0, columns, 128):
        at = slice(at, at + 128)
        gate = total(gates, at) * factor
        up = total(ups, at) * factor
        out_ref[:, at] = (gate / (1.0 + jnp.exp(-gate)) * up).astype(out_ref.dtype)


def make_inner(parts, factor, model):
    given = [] if factor is None else [factor]
    rows, columns = parts[1].shape[1:]
    return pl.pallas_call(
        functools.partial(inner_kernel, model, len(given)),
        out_shape=[
            jax.ShapeDtypeStruct((rows, columns), jnp.bfloat16),
            jax.ShapeDtypeStruct((rows, 128), jnp.float32),
        ],
        in_specs=in_vmem(len(given) + len(parts)),
        out_specs=in_vmem(2),
        compiler_params=kernel_params(12),
        name="inner",
    )(*given, *parts)


def down_kernel(chunks, *refs):
    *pieces, w_ref, hidden_ref, out_ref, inner, total = refs
    width = w_ref.shape[1]
    count = len(pieces) // chunks
    share = total.shape[0] // count
    at = 0
    for c in range(chunks):
        columns = pieces[c * count].shape[1]
        for k in range(count):
            inner[k * share : (k + 1) * share, at : at + columns] = pieces[c * count + k][...]
        at += columns
    result = jnp.dot(inner[...], w_ref[...], preferred_element_type=jnp.float32)
    me = lax.axis_index("tp")
    for k in range(count):
        start = pl.multiple_of((me ^ k) * share, 16) if count > 1 else 0
        total[pl.ds(start, share), :] = result[k * share : (k + 1) * share]
    rows = hidden_ref.shape[0]
    own = pl.ds(pl.multiple_of(lax.axis_index("dp") * rows, 16), rows)
    total[own, :] += hidden_ref[...].astype(jnp.float32)
    groups = width // 128
    per_rank = out_ref.shape[1] // groups
    for d in range(out_ref.shape[0]):
        owned = [
            total[d * per_rank : (d + 1) * per_rank, g * 128 : (g + 1) * 128]
            for g in range(groups)
        ]
        out_ref[d] = jnp.concatenate(owned, 0).astype(out_ref.dtype)


def project_down(chunks, w_down, hidden, ranks):
    units, width = w_down.shape
    pieces = [piece for chunk in chunks for piece in chunk]
    requests = sum(piece.shape[0] for piece in chunks[0])
    return pl.pallas_call(
        functools.partial(down_kernel, len(chunks)),
        out_shape=jax.ShapeDtypeStruct(
            (ranks, requests // ranks * (width // 128), 128), jnp.bfloat16
        ),
        in_specs=in_vmem(len(pieces) + 2),
        out_specs=pl.BlockSpec(memory_space=pltpu.VMEM),
        scratch_shapes=[
            pltpu.VMEM((requests, units), jnp.bfloat16),
            pltpu.VMEM((requests, width), jnp.float32),
        ],
        compiler_params=kernel_params(12),
        name="project_down",
    )(*pieces, fetched(w_down), hidden)


def layer_kernel(parts_ref, out_ref, total):
    per_rank, model = out_ref.shape
    ranks = lax.axis_size("tp")
    groups = model // ranks // 128
    for t in range(ranks):
        terms = [
            parts_ref[d, :, :].astype(jnp.float32) for d in range(t, parts_ref.shape[0], ranks)
        ]
        layer = sum(terms[1:], terms[0])
        for g in range(groups):
            at = (t * groups + g) * 128
            total[:, at : at + 128] = layer[g * per_rank : (g + 1) * per_rank, :]
    out_ref[...] = total[...].astype(out_ref.dtype)


def make_layer(parts, per_rank, model):
    return pl.pallas_call(
        layer_kernel,
        out_shape=jax.ShapeDtypeStruct((per_rank, model), jnp.bfloat16),
        in_specs=in_vmem(1),
        out_specs=pl.BlockSpec(memory_space=pltpu.VMEM),
        scratch_shapes=[pltpu.VMEM((per_rank, model), jnp.float32)],
        compiler_params=kernel_params(12),
        name="layer",
    )(parts)


def round_up(value, step):
    return (value + step - 1) // step * step


def swap(parts, axes):
    return lax.all_to_all(parts, axes, split_axis=0, concat_axis=0, tiled=True)


def local(
    residual, queries, paged_latent_cache, lengths, w_uv, w_o, norm_gain, w_gate, w_up, w_down
):
    ranks_dp = lax.axis_size("dp")
    ranks_tp = lax.axis_size("tp")
    ranks = ranks_dp * ranks_tp
    per_rank, model = residual.shape
    requests = per_rank * ranks
    heads_here = w_uv.shape[0]
    units = w_gate.shape[1]
    width = w_o.shape[1]


    latent = swap(attend(lengths, queries, paged_latent_cache.T, ranks), ("dp", "tp"))

    values = head_values(latent.reshape(requests * heads_here, C), w_uv)
    values, residual = lax.optimization_barrier((values, residual))
    values = from_all(values, "tp")
    added = list(split_columns(residual, ranks_tp))
    added = added[:1] + [from_distance(added[k], "tp", k) for k in range(1, ranks_tp)]
    attn, added = lax.optimization_barrier((project_out(values, w_o), added))
    attn = swap(attn.reshape(ranks_dp, requests // ranks_dp, width), "dp")
    own_hidden = make_hidden(attn, added)
    hidden = lax.all_gather(own_hidden, "dp", axis=0, tiled=True)

    halves = 2 if ranks_tp == 4 else 1
    chunks = gate_up(hidden, norm_gain.reshape(-1, 128), w_gate, w_up, halves)
    if halves == 2:
        first, second = chunks
        kept, second = lax.optimization_barrier((first[2:], second))
        chunks = [[*first[:2], *kept], second]
    inner = []
    factor = None
    for chunk in chunks:
        if halves == 2:
            gate_send, up_send, gate_keep, up_keep = chunk
            came = [from_distance(gate_send, "tp", 1), from_distance(up_send, "tp", 2)]
            (gate_send, up_send), kept = halve([gate_keep, up_keep], came)
            came = [from_distance(gate_send, "tp", 2), from_distance(up_send, "tp", 1)]
            own, factor = make_inner([part[None] for part in (*kept, *came)], factor, model)
            far = from_distance(own, "tp", 2)
            inner.append([own, from_distance(own, "tp", 1), far, from_distance(far, "tp", 1)])
        else:
            parts = [swap(part.reshape(ranks_tp, -1, part.shape[1]), "tp") for part in chunk]
            own, factor = make_inner(parts, factor, model)
            inner.append([lax.all_gather(own, "tp", axis=0, tiled=True)])
    ffn = swap(project_down(inner, w_down, own_hidden, ranks), ("dp", "tp"))
    return make_layer(ffn, per_rank, model)


def solution(mesh):
    placed = (
        P(("dp", "tp"), None),
        P(("dp", "tp"), None),
        P(("dp", "tp"), None),
        P(),
        P(("dp", "tp"), None, None),
        P("dp", "tp"),
        P(),
        P("tp", "dp"),
        P("tp", "dp"),
        P("dp", "tp"),
    )
    return jax.shard_map(
        local, mesh=mesh, in_specs=placed, out_specs=P(("dp", "tp"), None), check_vma=False
    )
```

```python
import functools

import jax
import jax.numpy as jnp
from jax import lax
from jax.experimental import pallas as pl
from jax.experimental.pallas import tpu as pltpu
from jax.sharding import PartitionSpec as P

C = 512
BLOCK_TOKENS = 64
TILE = 512

score_scale = 192.0 ** (-0.5)
log2_e = 1.4426950408889634
negative = -1e30


def attention_kernel(
    lens_ref,
    raw_ref,
    cache_ref,
    out_ref,
    q_ref,
    pairs_of_heads,
    rows_of_heads,
    held,
    score0,
    score1,
    weight0,
    weight1,
    keep0,
    keep1,
    acc,
    done,
    best,
    mass0,
    mass1,
    lo,
    hi,
    first,
    last,
    sems,
):
    nreq, heads, _ = q_ref.shape
    tile = held.shape[2]
    factor = score_scale * log2_e

    rank = lax.axis_index("dp") * lax.axis_size("tp") + lax.axis_index("tp")
    begin = jnp.int32(0)
    pairs = jnp.int32(0)
    for r in range(nreq):
        length = lens_ref[rank * nreq + r]
        lo[r] = begin
        hi[r] = begin + length
        first[r] = begin // tile
        last[r] = (begin + length - 1) // tile
        pairs = pairs + (last[r] - first[r] + 1)
        begin = begin + ((length + BLOCK_TOKENS - 1) // BLOCK_TOKENS) * BLOCK_TOKENS
    used = last[nreq - 1] + 1

    def copy(i):
        return pltpu.make_async_copy(
            cache_ref.at[:, pl.ds(pl.multiple_of(i * tile, tile), tile)], held.at[i], sems.at[i]
        )

    @pl.loop(0, used)
    def _(i):
        copy(i).start()

    width = q_ref.shape[2]
    half = heads // 2
    tail = width % 128
    full = width // 128
    for j in range(half):
        for c in range(pairs_of_heads.shape[0]):
            at = 2 * width * j + 128 * c
            pairs_of_heads[c, pl.ds(j, nreq, stride=half), :] = raw_ref[:, at : at + 128].astype(
                jnp.float32
            )
    for r in range(nreq):
        rows = slice(r * half, (r + 1) * half)
        for c in range(full + 1):
            rows_of_heads[c, pl.ds(0, half, stride=2), :] = pairs_of_heads[c, rows, :]
            ahead = min(full + c + 1, pairs_of_heads.shape[0] - 1)
            rows_of_heads[c, pl.ds(1, half, stride=2), :] = jnp.concatenate(
                [pairs_of_heads[full + c, rows, tail:], pairs_of_heads[ahead, rows, :tail]], 1
            )
        for c in range(full):
            q_ref[r, :, c * 128 : (c + 1) * 128] = rows_of_heads[c].astype(q_ref.dtype)
        q_ref[r, :, full * 128 :] = rows_of_heads[full, :, :tail].astype(q_ref.dtype)

    for ref in (acc, mass0, mass1, keep0, keep1, weight0, weight1):
        ref[...] = jnp.zeros_like(ref)
    best[...] = jnp.full_like(best, negative)

    def advance(p, r, i):
        live = p + 1 < pairs
        step = (i == last[r]) & live
        nr = jnp.where(step, r + 1, r)
        ni = jnp.where(step, first[nr], jnp.where(live, i + 1, i))
        return nr, ni, live

    def fetch(r, i, live):
        fresh = live & ((r == 0) | (i > last[jnp.maximum(r - 1, 0)]))

        @pl.when(fresh)
        def _():
            copy(i).wait()

    def scores(r, i, live):
        begin_at = jnp.where(live, lo[r], 0)
        end_at = jnp.where(live, hi[r], 0)
        token = i * tile + lax.broadcasted_iota(jnp.int32, (1, tile), 1)
        bias = jnp.where((token >= begin_at) & (token < end_at), 0.0, negative)
        return jnp.dot(q_ref[r], held[i], preferred_element_type=jnp.float32) + bias

    def gather(i, weights):
        return jnp.dot(held[i, :C, :], weights[...], preferred_element_type=jnp.float32)

    def half_step(before, now, after, given, found, used, made):
        (r0, i0), (r1, i1, live1), (r2, i2, live2) = before, now, after
        weights0, keeps0, masses0 = used
        weights1, keeps1, masses1 = made
        values = gather(i0, weights0)
        ahead = scores(r2, i2, live2)

        s = given[...]
        old = jnp.where(live1 & (i1 == first[r1]), negative, best[...])
        new = jnp.maximum(old, jnp.max(s, axis=1, keepdims=True))
        weight = jnp.exp2((s - new[:, :1]) * factor)
        keep = jnp.exp2((old - new) * factor)
        part = weight[:, :128]
        for at in range(128, tile, 128):
            part = part + weight[:, at : at + 128]

        acc[...] = acc[...] * keeps0[:1, :] + values
        found[...] = ahead
        weights1[...] = weight.T.astype(weights1.dtype)
        keeps1[...] = keep.T[:8, :]
        masses1[...] = masses0[...] * keep + part
        best[...] = new

        @pl.when(r1 != r0)
        def _():
            close(r0, masses0)

    def close(r, masses):
        total = jnp.sum(masses[...], axis=1, keepdims=True)
        done[r] = acc[...].T / total

    zero = jnp.int32(0)
    fetch(zero, zero, pairs > 0)
    score0[...] = scores(zero, zero, pairs > 0)
    stage0 = (weight0, keep0, mass0)
    stage1 = (weight1, keep1, mass1)

    def step(j, carry):
        r0, i0, r1, i1, live1 = carry
        p = 2 * j
        r2, i2, live2 = advance(p, r1, i1)
        r3, i3, live3 = advance(p + 1, r2, i2)
        fetch(r2, i2, live2)
        half_step((r0, i0), (r1, i1, live1), (r2, i2, live2), score0, score1, stage1, stage0)
        fetch(r3, i3, live3)
        half_step((r1, i1), (r2, i2, live2), (r3, i3, live3), score1, score0, stage0, stage1)
        return r2, i2, r3, i3, live3

    r0, i0, _, _, _ = lax.fori_loop(
        0, (pairs + 1) // 2, step, (zero, zero, zero, zero, pairs > 0)
    )
    acc[...] = acc[...] * keep1[:1, :] + gather(i0, weight1)
    close(r0, mass1)

    share = heads // out_ref.shape[0]
    for d in range(out_ref.shape[0]):
        rows = [done[r, d * share : (d + 1) * share, :] for r in range(nreq)]
        out_ref[d] = jnp.concatenate(rows, 0).astype(out_ref.dtype)


def kernel_params(limit):
    return pltpu.CompilerParams(vmem_limit_bytes=limit * 1024 * 1024)


def in_vmem(count):
    return [pl.BlockSpec(memory_space=pltpu.VMEM)] * count


def fetched(weight):
    return pltpu.with_memory_space_constraint(weight, pltpu.VMEM)


def attend(lengths, queries, cache_t, ranks):
    nreq = queries.shape[0]
    width, tokens = cache_t.shape
    heads = queries.shape[1] // width
    tile = TILE
    tiles = tokens // tile
    return pl.pallas_call(
        attention_kernel,
        out_shape=jax.ShapeDtypeStruct((ranks, nreq * heads // ranks, C), jnp.bfloat16),
        in_specs=[pl.BlockSpec(memory_space=pltpu.SMEM)]
        + in_vmem(1)
        + [pl.BlockSpec(memory_space=pltpu.HBM)],
        out_specs=pl.BlockSpec(memory_space=pltpu.VMEM),
        scratch_shapes=[
            pltpu.VMEM((nreq, heads, width), jnp.bfloat16),
            pltpu.VMEM((2 * width // 128, nreq * heads // 2, 128), jnp.float32),
            pltpu.VMEM((width // 128 + 1, heads, 128), jnp.float32),
            pltpu.VMEM((tiles, width, tile), jnp.bfloat16),
            pltpu.VMEM((heads, tile), jnp.float32),
            pltpu.VMEM((heads, tile), jnp.float32),
            pltpu.VMEM((tile, heads), jnp.bfloat16),
            pltpu.VMEM((tile, heads), jnp.bfloat16),
            pltpu.VMEM((8, heads), jnp.float32),
            pltpu.VMEM((8, heads), jnp.float32),
            pltpu.VMEM((C, heads), jnp.float32),
            pltpu.VMEM((nreq, heads, C), jnp.float32),
            pltpu.VMEM((heads, 128), jnp.float32),
            pltpu.VMEM((heads, 128), jnp.float32),
            pltpu.VMEM((heads, 128), jnp.float32),
            pltpu.SMEM((nreq,), jnp.int32),
            pltpu.SMEM((nreq,), jnp.int32),
            pltpu.SMEM((nreq,), jnp.int32),
            pltpu.SMEM((nreq,), jnp.int32),
            pltpu.SemaphoreType.DMA((tiles,)),
        ],
        compiler_params=kernel_params(28),
        cost_estimate=pl.CostEstimate(
            flops=2 * heads * tokens * (width + C),
            bytes_accessed=2 * tokens * width,
            transcendentals=heads * tokens,
        ),
        name="attention",
    )(
        pltpu.with_memory_space_constraint(lengths, pltpu.HBM),
        pltpu.with_memory_space_constraint(queries, pltpu.HBM),
        pltpu.with_memory_space_constraint(cache_t, pltpu.HBM),
    )


def head_values_kernel(latent_ref, w_ref, out_ref, values):
    heads, _, wide = w_ref.shape
    requests = out_ref.shape[0]
    latent = latent_ref[...]
    for h in range(heads):
        values[...] = jnp.dot(latent, w_ref[h], preferred_element_type=jnp.float32)
        picked = values[pl.ds(h, requests, stride=heads), :]
        out_ref[:, h * wide : (h + 1) * wide] = picked.astype(out_ref.dtype)


def head_values(latent, w_uv):
    heads, _, wide = w_uv.shape
    requests = latent.shape[0] // heads
    return pl.pallas_call(
        head_values_kernel,
        out_shape=jax.ShapeDtypeStruct((requests, heads * wide), jnp.bfloat16),
        in_specs=in_vmem(2),
        out_specs=pl.BlockSpec(memory_space=pltpu.VMEM),
        scratch_shapes=[pltpu.VMEM((latent.shape[0], wide), jnp.float32)],
        compiler_params=kernel_params(12),
        name="head_values",
    )(latent, w_uv)


def split_kernel(rows_ref, *out_refs):
    width = out_refs[0].shape[1]
    me = lax.axis_index("tp")
    for k, out_ref in enumerate(out_refs):
        start = pl.multiple_of((me ^ k) * width, 128)
        out_ref[...] = rows_ref[:, pl.ds(start, width)]


def split_columns(rows, ranks):
    shape = jax.ShapeDtypeStruct((rows.shape[0], rows.shape[1] // ranks), rows.dtype)
    return pl.pallas_call(
        split_kernel,
        out_shape=[shape] * ranks,
        in_specs=in_vmem(1),
        out_specs=in_vmem(ranks),
        compiler_params=kernel_params(8),
        name="split_columns",
    )(rows)


def from_distance(piece, axis, distance):
    return lax.ppermute(piece, axis, [(k, k ^ distance) for k in range(lax.axis_size(axis))])


def from_all(piece, axis):
    if lax.axis_size(axis) == 4:
        far = from_distance(piece, axis, 2)
        return [piece, from_distance(piece, axis, 1), far, from_distance(far, axis, 1)]
    return [piece] + [from_distance(piece, axis, k) for k in range(1, lax.axis_size(axis))]


def own_output_kernel(value_ref, w_ref, out_ref):
    depth = value_ref.shape[1]
    rows = pl.ds(pl.multiple_of(lax.axis_index("tp") * depth, 128), depth)
    out_ref[...] = jnp.dot(value_ref[...], w_ref[rows, :], preferred_element_type=jnp.float32)


def output_kernel(*refs):
    own_ref, *values, w_ref, out_ref, total = refs
    depth = values[0].shape[1]
    me = lax.axis_index("tp")
    for k, value in enumerate(values, 1):
        rows = pl.ds(pl.multiple_of((me ^ k) * depth, 128), depth)
        term = jnp.dot(value[...], w_ref[rows, :], preferred_element_type=jnp.float32)
        if k == 1:
            total[...] = own_ref[...] + term
        else:
            total[...] += term
    out_ref[...] = total[...].astype(out_ref.dtype)


def project_out(values, w_o):
    requests, depth = values[0].shape
    width = w_o.shape[1]
    w_o = fetched(w_o)
    own = pl.pallas_call(
        own_output_kernel,
        out_shape=jax.ShapeDtypeStruct((requests, width), jnp.float32),
        in_specs=in_vmem(2),
        out_specs=pl.BlockSpec(memory_space=pltpu.VMEM),
        compiler_params=kernel_params(12),
        cost_estimate=pl.CostEstimate(
            flops=2 * requests * depth * width, bytes_accessed=2 * depth * width, transcendentals=0
        ),
        name="project_own",
    )(values[0], w_o)
    return pl.pallas_call(
        output_kernel,
        out_shape=jax.ShapeDtypeStruct((requests, width), jnp.bfloat16),
        in_specs=in_vmem(len(values) + 1),
        out_specs=pl.BlockSpec(memory_space=pltpu.VMEM),
        scratch_shapes=[pltpu.VMEM((requests, width), jnp.float32)],
        compiler_params=kernel_params(12),
        name="project_out",
    )(own, *values[1:], w_o)


def hidden_kernel(parts_ref, *refs):
    *slices, out_ref, added = refs
    per_rank = slices[0].shape[0]
    me = lax.axis_index("tp")
    for k, piece in enumerate(slices):
        added[me ^ k] = piece[...].astype(jnp.float32)
    width = out_ref.shape[1]
    for at in range(0, width, 128):
        at = slice(at, at + 128)
        total = parts_ref[0, :, at].astype(jnp.float32)
        for d in range(1, parts_ref.shape[0]):
            total = total + parts_ref[d, :, at].astype(jnp.float32)
        terms = [added[s, :, at] for s in range(len(slices))]
        out_ref[:, at] = (total + jnp.concatenate(terms, 0)).astype(out_ref.dtype)


def make_hidden(parts, slices):
    return pl.pallas_call(
        hidden_kernel,
        out_shape=jax.ShapeDtypeStruct(parts.shape[1:], jnp.bfloat16),
        in_specs=in_vmem(1 + len(slices)),
        out_specs=pl.BlockSpec(memory_space=pltpu.VMEM),
        scratch_shapes=[pltpu.VMEM((len(slices),) + slices[0].shape, jnp.float32)],
        compiler_params=kernel_params(12),
        name="hidden",
    )(parts, *slices)


def scale_kernel(hidden_ref, gain_ref, gate_ref, up_ref, scaled, gate_sum, up_sum, *refs):
    *outs, gains = refs
    ranks = lax.axis_size("tp")
    halves = scaled.shape[0]
    requests, width = hidden_ref.shape
    share = requests // ranks
    groups = width // 128
    me = lax.axis_index("tp")
    places = [[3, 1, 2, 0], [3, 2, 1, 0]] if halves == 2 else [list(range(ranks))]

    gains[...] = gain_ref[...].astype(jnp.float32)
    squares = [None] * ranks
    for k in range(ranks):
        block = me ^ k if halves == 2 else k
        start = block * share if halves == 1 else pl.multiple_of(block * share, 16)
        square = jnp.zeros((share, 128), jnp.float32)
        for g in range(groups):
            at = slice(g * 128, (g + 1) * 128)
            x = hidden_ref[pl.ds(start, share), at].astype(jnp.float32)
            square = square + x * x
            gain = gains[pl.ds(me * groups + g, 1), :]
            value = (x * gain).astype(scaled.dtype)
            for n, place in enumerate(places):
                scaled[n, place[k] * share : (place[k] + 1) * share, at] = value
        squares[places[0][k]] = square
    square = jnp.sum(jnp.concatenate(squares, 0), 1, keepdims=True)
    top = square.astype(jnp.bfloat16).astype(jnp.float32)
    middle = (square - top).astype(jnp.bfloat16).astype(jnp.float32)
    low = square - top - middle
    lane = lax.broadcasted_iota(jnp.int32, (requests, 128), 1)
    digits = jnp.where(lane == 0, top, jnp.where(lane == 1, middle, jnp.where(lane == 2, low, 0.0)))
    gates = [gate_sum, outs[0]] if halves == 2 else [gate_sum]
    ups = [up_sum, outs[1]] if halves == 2 else [up_sum]
    columns = up_sum.shape[1]
    for n, target in enumerate(gates):
        rows = target.shape[0]
        target[:, columns:] = digits[n * rows : (n + 1) * rows].astype(target.dtype)
    products(scaled, gate_ref, up_ref, 0, columns, gates, ups)


def products(scaled, gate_ref, up_ref, first, columns, gates, ups):
    for left, w_ref, targets in ((0, gate_ref, gates), (scaled.shape[0] - 1, up_ref, ups)):
        for at in range(0, columns, 256):
            upto = min(at + 256, columns)
            term = jnp.dot(
                scaled[left],
                w_ref[:, first + at : first + upto],
                preferred_element_type=jnp.float32,
            )
            for n, target in enumerate(targets):
                rows = target.shape[0]
                target[:, at:upto] = term[n * rows : (n + 1) * rows].astype(target.dtype)


def second_kernel(scaled, gate_ref, up_ref, *outs):
    columns = outs[1].shape[1]
    first = gate_ref.shape[1] - columns
    products(scaled, gate_ref, up_ref, first, columns, outs[0::2], outs[1::2])


def gate_up(hidden, gain, w_gate, w_up, halves):
    requests, width = hidden.shape
    units = w_gate.shape[1]
    first = units if halves == 1 else round_up(units // 2, 256)
    w_gate, w_up = fetched(w_gate), fetched(w_up)

    def shapes(columns, extra):
        return [
            jax.ShapeDtypeStruct((requests // halves, columns + more), jnp.bfloat16)
            for _ in range(halves)
            for more in (extra, 0)
        ]

    outs = [jax.ShapeDtypeStruct((halves, requests, width), jnp.bfloat16)] + shapes(first, 128)
    scaled, *parts = pl.pallas_call(
        scale_kernel,
        out_shape=outs,
        in_specs=in_vmem(4),
        out_specs=in_vmem(len(outs)),
        scratch_shapes=[pltpu.VMEM(gain.shape, jnp.float32)],
        compiler_params=kernel_params(12),
        cost_estimate=pl.CostEstimate(
            flops=4 * requests * width * first, bytes_accessed=4 * width * first, transcendentals=0
        ),
        name="gate_up",
    )(hidden, gain, w_gate, w_up)
    if halves == 1:
        return [parts]
    outs = shapes(units - first, 0)
    others = pl.pallas_call(
        second_kernel,
        out_shape=outs,
        in_specs=in_vmem(3),
        out_specs=in_vmem(len(outs)),
        compiler_params=kernel_params(12),
        cost_estimate=pl.CostEstimate(
            flops=4 * requests * width * (units - first),
            bytes_accessed=4 * width * (units - first),
            transcendentals=0,
        ),
        name="gate_up_rest",
    )(scaled, w_gate, w_up)
    return [parts, others]


def halve_kernel(*refs):
    count = len(refs) // 4
    for n in range(count):
        kept, came, send, keep = refs[n], refs[count + n], refs[2 * count + n], refs[3 * count + n]
        rows = send.shape[0]
        for at in range(0, send.shape[1], 128):
            at = slice(at, at + 128)
            total = kept[:, at].astype(jnp.float32) + came[:, at].astype(jnp.float32)
            send[:, at] = total[:rows].astype(send.dtype)
            keep[:, at] = total[rows:]


def halve(kept, came):
    half = [(k.shape[0] // 2, k.shape[1]) for k in kept]
    outs = pl.pallas_call(
        halve_kernel,
        out_shape=[jax.ShapeDtypeStruct(shape, jnp.bfloat16) for shape in half]
        + [jax.ShapeDtypeStruct(shape, jnp.float32) for shape in half],
        in_specs=in_vmem(2 * len(kept)),
        out_specs=in_vmem(2 * len(kept)),
        compiler_params=kernel_params(12),
        name="halve",
    )(*kept, *came)
    return outs[: len(kept)], outs[len(kept) :]


def inner_kernel(model, given, *refs):
    *parts, out_ref, factor_ref = refs
    gates, ups = parts[given::2], parts[given + 1 :: 2]
    columns = out_ref.shape[1]

    def total(parts, at):
        terms = [
            part[n, :, at].astype(jnp.float32) for part in parts for n in range(part.shape[0])
        ]
        return sum(terms[1:], terms[0])

    if given:
        factor = parts[0][...]
    else:
        square = jnp.sum(total(gates, slice(columns, columns + 128)), 1, keepdims=True)
        factor = jnp.broadcast_to(lax.rsqrt(square / model + 1e-06), factor_ref.shape)
    factor_ref[...] = factor
    for at in range(0, columns, 128):
        at = slice(at, at + 128)
        gate = total(gates, at) * factor
        up = total(ups, at) * factor
        out_ref[:, at] = (gate / (1.0 + jnp.exp(-gate)) * up).astype(out_ref.dtype)


def make_inner(parts, factor, model):
    given = [] if factor is None else [factor]
    rows, columns = parts[1].shape[1:]
    return pl.pallas_call(
        functools.partial(inner_kernel, model, len(given)),
        out_shape=[
            jax.ShapeDtypeStruct((rows, columns), jnp.bfloat16),
            jax.ShapeDtypeStruct((rows, 128), jnp.float32),
        ],
        in_specs=in_vmem(len(given) + len(parts)),
        out_specs=in_vmem(2),
        compiler_params=kernel_params(12),
        name="inner",
    )(*given, *parts)


def down_kernel(chunks, *refs):
    *pieces, w_ref, hidden_ref, out_ref, inner, total = refs
    width = w_ref.shape[1]
    count = len(pieces) // chunks
    share = total.shape[0] // count
    at = 0
    for c in range(chunks):
        columns = pieces[c * count].shape[1]
        for k in range(count):
            inner[k * share : (k + 1) * share, at : at + columns] = pieces[c * count + k][...]
        at += columns
    result = jnp.dot(inner[...], w_ref[...], preferred_element_type=jnp.float32)
    me = lax.axis_index("tp")
    for k in range(count):
        start = pl.multiple_of((me ^ k) * share, 16) if count > 1 else 0
        total[pl.ds(start, share), :] = result[k * share : (k + 1) * share]
    rows = hidden_ref.shape[0]
    own = pl.ds(pl.multiple_of(lax.axis_index("dp") * rows, 16), rows)
    total[own, :] += hidden_ref[...].astype(jnp.float32)
    groups = width // 128
    per_rank = out_ref.shape[1] // groups
    for d in range(out_ref.shape[0]):
        owned = [
            total[d * per_rank : (d + 1) * per_rank, g * 128 : (g + 1) * 128]
            for g in range(groups)
        ]
        out_ref[d] = jnp.concatenate(owned, 0).astype(out_ref.dtype)


def project_down(chunks, w_down, hidden, ranks):
    units, width = w_down.shape
    pieces = [piece for chunk in chunks for piece in chunk]
    requests = sum(piece.shape[0] for piece in chunks[0])
    return pl.pallas_call(
        functools.partial(down_kernel, len(chunks)),
        out_shape=jax.ShapeDtypeStruct(
            (ranks, requests // ranks * (width // 128), 128), jnp.bfloat16
        ),
        in_specs=in_vmem(len(pieces) + 2),
        out_specs=pl.BlockSpec(memory_space=pltpu.VMEM),
        scratch_shapes=[
            pltpu.VMEM((requests, units), jnp.bfloat16),
            pltpu.VMEM((requests, width), jnp.float32),
        ],
        compiler_params=kernel_params(12),
        name="project_down",
    )(*pieces, fetched(w_down), hidden)


def layer_kernel(parts_ref, out_ref, total):
    per_rank, model = out_ref.shape
    ranks = lax.axis_size("tp")
    groups = model // ranks // 128
    for t in range(ranks):
        terms = [
            parts_ref[d, :, :].astype(jnp.float32) for d in range(t, parts_ref.shape[0], ranks)
        ]
        layer = sum(terms[1:], terms[0])
        for g in range(groups):
            at = (t * groups + g) * 128
            total[:, at : at + 128] = layer[g * per_rank : (g + 1) * per_rank, :]
    out_ref[...] = total[...].astype(out_ref.dtype)


def make_layer(parts, per_rank, model):
    return pl.pallas_call(
        layer_kernel,
        out_shape=jax.ShapeDtypeStruct((per_rank, model), jnp.bfloat16),
        in_specs=in_vmem(1),
        out_specs=pl.BlockSpec(memory_space=pltpu.VMEM),
        scratch_shapes=[pltpu.VMEM((per_rank, model), jnp.float32)],
        compiler_params=kernel_params(12),
        name="layer",
    )(parts)


def round_up(value, step):
    return (value + step - 1) // step * step


def swap(parts, axes):
    return lax.all_to_all(parts, axes, split_axis=0, concat_axis=0, tiled=True)


def local(
    residual, queries, paged_latent_cache, lengths, w_uv, w_o, norm_gain, w_gate, w_up, w_down
):
    ranks_dp = lax.axis_size("dp")
    ranks_tp = lax.axis_size("tp")
    ranks = ranks_dp * ranks_tp
    per_rank, model = residual.shape
    requests = per_rank * ranks
    heads_here = w_uv.shape[0]
    units = w_gate.shape[1]
    width = w_o.shape[1]


    latent = swap(attend(lengths, queries, paged_latent_cache.T, ranks), ("dp", "tp"))

    values = head_values(latent.reshape(requests * heads_here, C), w_uv)
    values, residual = lax.optimization_barrier((values, residual))
    values = from_all(values, "tp")
    added = list(split_columns(residual, ranks_tp))
    added = added[:1] + [from_distance(added[k], "tp", k) for k in range(1, ranks_tp)]
    attn, added = lax.optimization_barrier((project_out(values, w_o), added))
    attn = swap(attn.reshape(ranks_dp, requests // ranks_dp, width), "dp")
    own_hidden = make_hidden(attn, added)
    hidden = lax.all_gather(own_hidden, "dp", axis=0, tiled=True)

    halves = 2 if ranks_tp == 4 else 1
    chunks = gate_up(hidden, norm_gain.reshape(-1, 128), w_gate, w_up, halves)
    if halves == 2:
        first, second = chunks
        kept, second = lax.optimization_barrier((first[2:], second))
        chunks = [[*first[:2], *kept], second]
    inner = []
    factor = None
    for chunk in chunks:
        if halves == 2:
            gate_send, up_send, gate_keep, up_keep = chunk
            came = [from_distance(gate_send, "tp", 1), from_distance(up_send, "tp", 2)]
            (gate_send, up_send), kept = halve([gate_keep, up_keep], came)
            came = [from_distance(gate_send, "tp", 2), from_distance(up_send, "tp", 1)]
            own, factor = make_inner([part[None] for part in (*kept, *came)], factor, model)
            inner.append(from_all(own, "tp"))
        else:
            parts = [swap(part.reshape(ranks_tp, -1, part.shape[1]), "tp") for part in chunk]
            own, factor = make_inner(parts, factor, model)
            inner.append([lax.all_gather(own, "tp", axis=0, tiled=True)])
    ffn = swap(project_down(inner, w_down, own_hidden, ranks), ("dp", "tp"))
    return make_layer(ffn, per_rank, model)


def solution(mesh):
    placed = (
        P(("dp", "tp"), None),
        P(("dp", "tp"), None),
        P(("dp", "tp"), None),
        P(),
        P(("dp", "tp"), None, None),
        P("dp", "tp"),
        P(),
        P("tp", "dp"),
        P("tp", "dp"),
        P("dp", "tp"),
    )
    return jax.shard_map(
        local, mesh=mesh, in_specs=placed, out_specs=P(("dp", "tp"), None), check_vma=False
    )
```

```python
import functools

import jax
import jax.numpy as jnp
from jax import lax
from jax.experimental import pallas as pl
from jax.experimental.pallas import tpu as pltpu
from jax.sharding import PartitionSpec as P

C = 512
BLOCK_TOKENS = 64
TILE = 512

score_scale = 192.0 ** (-0.5)
log2_e = 1.4426950408889634
negative = -1e30


def attention_kernel(
    lens_ref,
    raw_ref,
    cache_ref,
    out_ref,
    q_ref,
    pairs_of_heads,
    rows_of_heads,
    held,
    score0,
    score1,
    weight0,
    weight1,
    keep0,
    keep1,
    acc,
    done,
    best,
    mass,
    lo,
    hi,
    first,
    last,
    sems,
):
    nreq, heads, _ = q_ref.shape
    tile = held.shape[2]
    factor = score_scale * log2_e

    rank = lax.axis_index("dp") * lax.axis_size("tp") + lax.axis_index("tp")
    begin = jnp.int32(0)
    pairs = jnp.int32(0)
    for r in range(nreq):
        length = lens_ref[rank * nreq + r]
        lo[r] = begin
        hi[r] = begin + length
        first[r] = begin // tile
        last[r] = (begin + length - 1) // tile
        pairs = pairs + (last[r] - first[r] + 1)
        begin = begin + ((length + BLOCK_TOKENS - 1) // BLOCK_TOKENS) * BLOCK_TOKENS
    used = last[nreq - 1] + 1

    def copy(i):
        return pltpu.make_async_copy(
            cache_ref.at[:, pl.ds(pl.multiple_of(i * tile, tile), tile)], held.at[i], sems.at[i]
        )

    @pl.loop(0, used)
    def _(i):
        copy(i).start()

    width = q_ref.shape[2]
    half = heads // 2
    tail = width % 128
    full = width // 128
    for j in range(half):
        for c in range(pairs_of_heads.shape[0]):
            at = 2 * width * j + 128 * c
            pairs_of_heads[c, pl.ds(j, nreq, stride=half), :] = raw_ref[:, at : at + 128].astype(
                jnp.float32
            )
    for r in range(nreq):
        rows = slice(r * half, (r + 1) * half)
        for c in range(full + 1):
            rows_of_heads[c, pl.ds(0, half, stride=2), :] = pairs_of_heads[c, rows, :]
            ahead = min(full + c + 1, pairs_of_heads.shape[0] - 1)
            rows_of_heads[c, pl.ds(1, half, stride=2), :] = jnp.concatenate(
                [pairs_of_heads[full + c, rows, tail:], pairs_of_heads[ahead, rows, :tail]], 1
            )
        for c in range(full):
            q_ref[r, :, c * 128 : (c + 1) * 128] = rows_of_heads[c].astype(q_ref.dtype)
        q_ref[r, :, full * 128 :] = rows_of_heads[full, :, :tail].astype(q_ref.dtype)

    acc[...] = jnp.zeros_like(acc)
    best[...] = jnp.full_like(best, negative)
    mass[...] = jnp.zeros_like(mass)
    weight1[...] = jnp.zeros_like(weight1)
    keep1[...] = jnp.ones_like(keep1)

    def advance(p, r, i):
        live = p + 1 < pairs
        step = (i == last[r]) & live
        nr = jnp.where(step, r + 1, r)
        ni = jnp.where(step, first[nr], jnp.where(live, i + 1, i))
        return nr, ni, live

    def fetch(r, i, live):
        fresh = live & ((r == 0) | (i > last[jnp.maximum(r - 1, 0)]))

        @pl.when(fresh)
        def _():
            copy(i).wait()

    def scores(r, i, live, target):
        begin_at = jnp.where(live, lo[r], 0)
        end_at = jnp.where(live, hi[r], 0)
        s = jnp.dot(q_ref[r, :, :C], held[i, :C, :], preferred_element_type=jnp.float32)
        s = s + jnp.dot(q_ref[r, :, C:], held[i, C:, :], preferred_element_type=jnp.float32)
        token = i * tile + lax.broadcasted_iota(jnp.int32, (1, tile), 1)
        target[...] = s + jnp.where((token >= begin_at) & (token < end_at), 0.0, negative)

    def soften(r, source, weights, keeps):
        s = source[...]
        old = best[r]
        new = jnp.maximum(old, jnp.max(s, axis=1, keepdims=True))
        weight = jnp.exp2((s - new[:, :1]) * factor)
        keep = jnp.exp2((old - new) * factor)
        part = weight[:, :128]
        for at in range(128, tile, 128):
            part = part + weight[:, at : at + 128]
        mass[r] = mass[r] * keep + part
        best[r] = new
        weights[...] = weight.T.astype(weights.dtype)
        keeps[...] = keep.T[:8, :]

    def gather(r, i, weights, keeps):
        values = lax.dot_general(
            held[i, :C, :],
            weights[...],
            (((1,), (0,)), ((), ())),
            preferred_element_type=jnp.float32,
        )
        acc[r] = acc[r] * keeps[:1, :] + values

    zero = jnp.int32(0)
    fetch(zero, zero, pairs > 0)
    scores(zero, zero, pairs > 0, score0)

    def step(j, carry):
        r0, i0, r1, i1 = carry
        p = 2 * j
        r2, i2, live2 = advance(p, r1, i1)
        r3, i3, live3 = advance(p + 1, r2, i2)
        fetch(r2, i2, live2)
        fetch(r3, i3, live3)
        gather(r0, i0, weight1, keep1)
        scores(r2, i2, live2, score1)
        soften(r1, score0, weight0, keep0)
        gather(r1, i1, weight0, keep0)
        scores(r3, i3, live3, score0)
        soften(r2, score1, weight1, keep1)
        return r2, i2, r3, i3

    r0, i0, _, _ = lax.fori_loop(0, (pairs + 1) // 2, step, (zero, zero, zero, zero))
    gather(r0, i0, weight1, keep1)

    share = heads // out_ref.shape[0]
    for r in range(nreq):
        total = jnp.sum(mass[r], axis=1, keepdims=True)
        score0[:, :C] = acc[r].T / total
        for d in range(out_ref.shape[0]):
            done[d, r * share : (r + 1) * share, :] = score0[d * share : (d + 1) * share, :C]
    out_ref[...] = done[...].astype(out_ref.dtype)


def kernel_params(limit):
    return pltpu.CompilerParams(vmem_limit_bytes=limit * 1024 * 1024)


def in_vmem(count):
    return [pl.BlockSpec(memory_space=pltpu.VMEM)] * count


def fetched(weight):
    return pltpu.with_memory_space_constraint(weight, pltpu.VMEM)


def attend(lengths, queries, cache_t, ranks):
    nreq = queries.shape[0]
    width, tokens = cache_t.shape
    heads = queries.shape[1] // width
    tile = TILE
    tiles = tokens // tile
    return pl.pallas_call(
        attention_kernel,
        out_shape=jax.ShapeDtypeStruct((ranks, nreq * heads // ranks, C), jnp.bfloat16),
        in_specs=[pl.BlockSpec(memory_space=pltpu.SMEM)]
        + in_vmem(1)
        + [pl.BlockSpec(memory_space=pltpu.HBM)],
        out_specs=pl.BlockSpec(memory_space=pltpu.VMEM),
        scratch_shapes=[
            pltpu.VMEM((nreq, heads, width), jnp.bfloat16),
            pltpu.VMEM((2 * width // 128, nreq * heads // 2, 128), jnp.float32),
            pltpu.VMEM((width // 128 + 1, heads, 128), jnp.float32),
            pltpu.VMEM((tiles, width, tile), jnp.bfloat16),
            pltpu.VMEM((heads, tile), jnp.float32),
            pltpu.VMEM((heads, tile), jnp.float32),
            pltpu.VMEM((tile, heads), jnp.bfloat16),
            pltpu.VMEM((tile, heads), jnp.bfloat16),
            pltpu.VMEM((8, heads), jnp.float32),
            pltpu.VMEM((8, heads), jnp.float32),
            pltpu.VMEM((nreq, C, heads), jnp.float32),
            pltpu.VMEM((ranks, nreq * heads // ranks, C), jnp.float32),
            pltpu.VMEM((nreq, heads, 128), jnp.float32),
            pltpu.VMEM((nreq, heads, 128), jnp.float32),
            pltpu.SMEM((nreq,), jnp.int32),
            pltpu.SMEM((nreq,), jnp.int32),
            pltpu.SMEM((nreq,), jnp.int32),
            pltpu.SMEM((nreq,), jnp.int32),
            pltpu.SemaphoreType.DMA((tiles,)),
        ],
        compiler_params=kernel_params(28),
        cost_estimate=pl.CostEstimate(
            flops=2 * heads * tokens * (width + C),
            bytes_accessed=2 * tokens * width,
            transcendentals=heads * tokens,
        ),
        name="attention",
    )(
        pltpu.with_memory_space_constraint(lengths, pltpu.HBM),
        pltpu.with_memory_space_constraint(queries, pltpu.HBM),
        pltpu.with_memory_space_constraint(cache_t, pltpu.HBM),
    )


def head_values_kernel(latent_ref, w_ref, out_ref, values):
    heads, _, wide = w_ref.shape
    requests = out_ref.shape[0]
    latent = latent_ref[...]
    for h in range(heads):
        values[...] = jnp.dot(latent, w_ref[h], preferred_element_type=jnp.float32)
        picked = values[pl.ds(h, requests, stride=heads), :]
        out_ref[:, h * wide : (h + 1) * wide] = picked.astype(out_ref.dtype)


def head_values(latent, w_uv):
    heads, _, wide = w_uv.shape
    requests = latent.shape[0] // heads
    return pl.pallas_call(
        head_values_kernel,
        out_shape=jax.ShapeDtypeStruct((requests, heads * wide), jnp.bfloat16),
        in_specs=in_vmem(2),
        out_specs=pl.BlockSpec(memory_space=pltpu.VMEM),
        scratch_shapes=[pltpu.VMEM((latent.shape[0], wide), jnp.float32)],
        compiler_params=kernel_params(12),
        name="head_values",
    )(latent, w_uv)


def split_kernel(rows_ref, *out_refs):
    width = out_refs[0].shape[1]
    me = lax.axis_index("tp")
    for k, out_ref in enumerate(out_refs):
        start = pl.multiple_of((me ^ k) * width, 128)
        out_ref[...] = rows_ref[:, pl.ds(start, width)]


def split_columns(rows, ranks):
    shape = jax.ShapeDtypeStruct((rows.shape[0], rows.shape[1] // ranks), rows.dtype)
    return pl.pallas_call(
        split_kernel,
        out_shape=[shape] * ranks,
        in_specs=in_vmem(1),
        out_specs=in_vmem(ranks),
        compiler_params=kernel_params(8),
        name="split_columns",
    )(rows)


def from_distance(piece, axis, distance):
    return lax.ppermute(piece, axis, [(k, k ^ distance) for k in range(lax.axis_size(axis))])


def from_all(piece, axis):
    return [piece] + [from_distance(piece, axis, k) for k in range(1, lax.axis_size(axis))]


def own_output_kernel(value_ref, w_ref, out_ref):
    depth = value_ref.shape[1]
    rows = pl.ds(pl.multiple_of(lax.axis_index("tp") * depth, 128), depth)
    out_ref[...] = jnp.dot(value_ref[...], w_ref[rows, :], preferred_element_type=jnp.float32)


def output_kernel(*refs):
    own_ref, *values, w_ref, out_ref, total = refs
    depth = values[0].shape[1]
    me = lax.axis_index("tp")
    for k, value in enumerate(values, 1):
        rows = pl.ds(pl.multiple_of((me ^ k) * depth, 128), depth)
        term = jnp.dot(value[...], w_ref[rows, :], preferred_element_type=jnp.float32)
        if k == 1:
            total[...] = own_ref[...] + term
        else:
            total[...] += term
    out_ref[...] = total[...].astype(out_ref.dtype)


def project_out(values, w_o):
    requests, depth = values[0].shape
    width = w_o.shape[1]
    w_o = fetched(w_o)
    own = pl.pallas_call(
        own_output_kernel,
        out_shape=jax.ShapeDtypeStruct((requests, width), jnp.float32),
        in_specs=in_vmem(2),
        out_specs=pl.BlockSpec(memory_space=pltpu.VMEM),
        compiler_params=kernel_params(12),
        cost_estimate=pl.CostEstimate(
            flops=2 * requests * depth * width, bytes_accessed=2 * depth * width, transcendentals=0
        ),
        name="project_own",
    )(values[0], w_o)
    return pl.pallas_call(
        output_kernel,
        out_shape=jax.ShapeDtypeStruct((requests, width), jnp.bfloat16),
        in_specs=in_vmem(len(values) + 1),
        out_specs=pl.BlockSpec(memory_space=pltpu.VMEM),
        scratch_shapes=[pltpu.VMEM((requests, width), jnp.float32)],
        compiler_params=kernel_params(12),
        name="project_out",
    )(own, *values[1:], w_o)


def hidden_kernel(parts_ref, *refs):
    *slices, out_ref, added = refs
    per_rank = slices[0].shape[0]
    me = lax.axis_index("tp")
    for k, piece in enumerate(slices):
        added[me ^ k] = piece[...].astype(jnp.float32)
    width = out_ref.shape[1]
    for at in range(0, width, 128):
        at = slice(at, at + 128)
        total = parts_ref[0, :, at].astype(jnp.float32)
        for d in range(1, parts_ref.shape[0]):
            total = total + parts_ref[d, :, at].astype(jnp.float32)
        terms = [added[s, :, at] for s in range(len(slices))]
        out_ref[:, at] = (total + jnp.concatenate(terms, 0)).astype(out_ref.dtype)


def make_hidden(parts, slices):
    return pl.pallas_call(
        hidden_kernel,
        out_shape=jax.ShapeDtypeStruct(parts.shape[1:], jnp.bfloat16),
        in_specs=in_vmem(1 + len(slices)),
        out_specs=pl.BlockSpec(memory_space=pltpu.VMEM),
        scratch_shapes=[pltpu.VMEM((len(slices),) + slices[0].shape, jnp.float32)],
        compiler_params=kernel_params(12),
        name="hidden",
    )(parts, *slices)


def scale_kernel(hidden_ref, gain_ref, gate_ref, up_ref, scaled, gate_sum, up_sum, *refs):
    *outs, gains = refs
    ranks = lax.axis_size("tp")
    halves = scaled.shape[0]
    requests, width = hidden_ref.shape
    share = requests // ranks
    groups = width // 128
    me = lax.axis_index("tp")
    places = [[3, 1, 2, 0], [3, 2, 1, 0]] if halves == 2 else [list(range(ranks))]

    gains[...] = gain_ref[...].astype(jnp.float32)
    squares = [None] * ranks
    for k in range(ranks):
        block = me ^ k if halves == 2 else k
        start = block * share if halves == 1 else pl.multiple_of(block * share, 16)
        square = jnp.zeros((share, 128), jnp.float32)
        for g in range(groups):
            at = slice(g * 128, (g + 1) * 128)
            x = hidden_ref[pl.ds(start, share), at].astype(jnp.float32)
            square = square + x * x
            gain = gains[pl.ds(me * groups + g, 1), :]
            value = (x * gain).astype(scaled.dtype)
            for n, place in enumerate(places):
                scaled[n, place[k] * share : (place[k] + 1) * share, at] = value
        squares[places[0][k]] = square
    square = jnp.sum(jnp.concatenate(squares, 0), 1, keepdims=True)
    top = square.astype(jnp.bfloat16).astype(jnp.float32)
    middle = (square - top).astype(jnp.bfloat16).astype(jnp.float32)
    low = square - top - middle
    lane = lax.broadcasted_iota(jnp.int32, (requests, 128), 1)
    digits = jnp.where(lane == 0, top, jnp.where(lane == 1, middle, jnp.where(lane == 2, low, 0.0)))
    gates = [gate_sum, outs[0]] if halves == 2 else [gate_sum]
    ups = [up_sum, outs[1]] if halves == 2 else [up_sum]
    columns = up_sum.shape[1]
    for n, target in enumerate(gates):
        rows = target.shape[0]
        target[:, columns:] = digits[n * rows : (n + 1) * rows].astype(target.dtype)
    products(scaled, gate_ref, up_ref, 0, columns, gates, ups)


def products(scaled, gate_ref, up_ref, first, columns, gates, ups):
    for left, w_ref, targets in ((0, gate_ref, gates), (scaled.shape[0] - 1, up_ref, ups)):
        for at in range(0, columns, 256):
            upto = min(at + 256, columns)
            term = jnp.dot(
                scaled[left],
                w_ref[:, first + at : first + upto],
                preferred_element_type=jnp.float32,
            )
            for n, target in enumerate(targets):
                rows = target.shape[0]
                target[:, at:upto] = term[n * rows : (n + 1) * rows].astype(target.dtype)


def second_kernel(scaled, gate_ref, up_ref, *outs):
    columns = outs[1].shape[1]
    first = gate_ref.shape[1] - columns
    products(scaled, gate_ref, up_ref, first, columns, outs[0::2], outs[1::2])


def gate_up(hidden, gain, w_gate, w_up, halves):
    requests, width = hidden.shape
    units = w_gate.shape[1]
    first = units if halves == 1 else round_up(units // 2, 256)
    w_gate, w_up = fetched(w_gate), fetched(w_up)

    def shapes(columns, extra):
        return [
            jax.ShapeDtypeStruct((requests // halves, columns + more), jnp.bfloat16)
            for _ in range(halves)
            for more in (extra, 0)
        ]

    outs = [jax.ShapeDtypeStruct((halves, requests, width), jnp.bfloat16)] + shapes(first, 128)
    scaled, *parts = pl.pallas_call(
        scale_kernel,
        out_shape=outs,
        in_specs=in_vmem(4),
        out_specs=in_vmem(len(outs)),
        scratch_shapes=[pltpu.VMEM(gain.shape, jnp.float32)],
        compiler_params=kernel_params(12),
        cost_estimate=pl.CostEstimate(
            flops=4 * requests * width * first, bytes_accessed=4 * width * first, transcendentals=0
        ),
        name="gate_up",
    )(hidden, gain, w_gate, w_up)
    if halves == 1:
        return [parts]
    outs = shapes(units - first, 0)
    others = pl.pallas_call(
        second_kernel,
        out_shape=outs,
        in_specs=in_vmem(3),
        out_specs=in_vmem(len(outs)),
        compiler_params=kernel_params(12),
        cost_estimate=pl.CostEstimate(
            flops=4 * requests * width * (units - first),
            bytes_accessed=4 * width * (units - first),
            transcendentals=0,
        ),
        name="gate_up_rest",
    )(scaled, w_gate, w_up)
    return [parts, others]


def halve_kernel(*refs):
    count = len(refs) // 4
    for n in range(count):
        kept, came, send, keep = refs[n], refs[count + n], refs[2 * count + n], refs[3 * count + n]
        rows = send.shape[0]
        for at in range(0, send.shape[1], 128):
            at = slice(at, at + 128)
            total = kept[:, at].astype(jnp.float32) + came[:, at].astype(jnp.float32)
            send[:, at] = total[:rows].astype(send.dtype)
            keep[:, at] = total[rows:]


def halve(kept, came):
    half = [(k.shape[0] // 2, k.shape[1]) for k in kept]
    outs = pl.pallas_call(
        halve_kernel,
        out_shape=[jax.ShapeDtypeStruct(shape, jnp.bfloat16) for shape in half]
        + [jax.ShapeDtypeStruct(shape, jnp.float32) for shape in half],
        in_specs=in_vmem(2 * len(kept)),
        out_specs=in_vmem(2 * len(kept)),
        compiler_params=kernel_params(12),
        name="halve",
    )(*kept, *came)
    return outs[: len(kept)], outs[len(kept) :]


def inner_kernel(model, given, *refs):
    *parts, out_ref, factor_ref = refs
    gates, ups = parts[given::2], parts[given + 1 :: 2]
    columns = out_ref.shape[1]

    def total(parts, at):
        terms = [
            part[n, :, at].astype(jnp.float32) for part in parts for n in range(part.shape[0])
        ]
        return sum(terms[1:], terms[0])

    if given:
        factor = parts[0][...]
    else:
        square = jnp.sum(total(gates, slice(columns, columns + 128)), 1, keepdims=True)
        factor = jnp.broadcast_to(lax.rsqrt(square / model + 1e-06), factor_ref.shape)
    factor_ref[...] = factor
    for at in range(0, columns, 128):
        at = slice(at, at + 128)
        gate = total(gates, at) * factor
        up = total(ups, at) * factor
        out_ref[:, at] = (gate / (1.0 + jnp.exp(-gate)) * up).astype(out_ref.dtype)


def make_inner(parts, factor, model):
    given = [] if factor is None else [factor]
    rows, columns = parts[1].shape[1:]
    return pl.pallas_call(
        functools.partial(inner_kernel, model, len(given)),
        out_shape=[
            jax.ShapeDtypeStruct((rows, columns), jnp.bfloat16),
            jax.ShapeDtypeStruct((rows, 128), jnp.float32),
        ],
        in_specs=in_vmem(len(given) + len(parts)),
        out_specs=in_vmem(2),
        compiler_params=kernel_params(12),
        name="inner",
    )(*given, *parts)


def down_kernel(chunks, *refs):
    *pieces, w_ref, hidden_ref, out_ref, inner, total = refs
    width = w_ref.shape[1]
    count = len(pieces) // chunks
    share = total.shape[0] // count
    at = 0
    for c in range(chunks):
        columns = pieces[c * count].shape[1]
        for k in range(count):
            inner[k * share : (k + 1) * share, at : at + columns] = pieces[c * count + k][...]
        at += columns
    result = jnp.dot(inner[...], w_ref[...], preferred_element_type=jnp.float32)
    me = lax.axis_index("tp")
    for k in range(count):
        start = pl.multiple_of((me ^ k) * share, 16) if count > 1 else 0
        total[pl.ds(start, share), :] = result[k * share : (k + 1) * share]
    rows = hidden_ref.shape[0]
    own = pl.ds(pl.multiple_of(lax.axis_index("dp") * rows, 16), rows)
    total[own, :] += hidden_ref[...].astype(jnp.float32)
    per_rank = out_ref.shape[1]
    for d in range(out_ref.shape[0]):
        out_ref[d] = total[d * per_rank : (d + 1) * per_rank, :].astype(out_ref.dtype)


def project_down(chunks, w_down, hidden, ranks):
    units, width = w_down.shape
    pieces = [piece for chunk in chunks for piece in chunk]
    requests = sum(piece.shape[0] for piece in chunks[0])
    return pl.pallas_call(
        functools.partial(down_kernel, len(chunks)),
        out_shape=jax.ShapeDtypeStruct((ranks, requests // ranks, width), jnp.bfloat16),
        in_specs=in_vmem(len(pieces) + 2),
        out_specs=pl.BlockSpec(memory_space=pltpu.VMEM),
        scratch_shapes=[
            pltpu.VMEM((requests, units), jnp.bfloat16),
            pltpu.VMEM((requests, width), jnp.float32),
        ],
        compiler_params=kernel_params(12),
        name="project_down",
    )(*pieces, fetched(w_down), hidden)


def layer_kernel(parts_ref, out_ref):
    ranks = lax.axis_size("tp")
    width = parts_ref.shape[2]
    for t in range(ranks):
        terms = [parts_ref[d].astype(jnp.float32) for d in range(t, parts_ref.shape[0], ranks)]
        layer = sum(terms[1:], terms[0])
        out_ref[:, t * width : (t + 1) * width] = layer.astype(out_ref.dtype)


def make_layer(parts, per_rank, model):
    return pl.pallas_call(
        layer_kernel,
        out_shape=jax.ShapeDtypeStruct((per_rank, model), jnp.bfloat16),
        in_specs=in_vmem(1),
        out_specs=pl.BlockSpec(memory_space=pltpu.VMEM),
        compiler_params=kernel_params(12),
        name="layer",
    )(parts)


def round_up(value, step):
    return (value + step - 1) // step * step


def swap(parts, axes):
    return lax.all_to_all(parts, axes, split_axis=0, concat_axis=0, tiled=True)


def local(
    residual, queries, paged_latent_cache, lengths, w_uv, w_o, norm_gain, w_gate, w_up, w_down
):
    ranks_dp = lax.axis_size("dp")
    ranks_tp = lax.axis_size("tp")
    ranks = ranks_dp * ranks_tp
    per_rank, model = residual.shape
    requests = per_rank * ranks
    heads_here = w_uv.shape[0]
    units = w_gate.shape[1]
    width = w_o.shape[1]


    latent = swap(attend(lengths, queries, paged_latent_cache.T, ranks), ("dp", "tp"))

    values = head_values(latent.reshape(requests * heads_here, C), w_uv)
    values, residual = lax.optimization_barrier((values, residual))
    values = from_all(values, "tp")
    added = list(split_columns(residual, ranks_tp))
    added = added[:1] + [from_distance(added[k], "tp", k) for k in range(1, ranks_tp)]
    attn, added = lax.optimization_barrier((project_out(values, w_o), added))
    attn = swap(attn.reshape(ranks_dp, requests // ranks_dp, width), "dp")
    own_hidden = make_hidden(attn, added)
    hidden = lax.all_gather(own_hidden, "dp", axis=0, tiled=True)

    halves = 2 if ranks_tp == 4 else 1
    chunks = gate_up(hidden, norm_gain.reshape(-1, 128), w_gate, w_up, halves)
    if halves == 2:
        first, second = chunks
        kept, second = lax.optimization_barrier((first[2:], second))
        chunks = [[*first[:2], *kept], second]
    inner = []
    factor = None
    for chunk in chunks:
        if halves == 2:
            gate_send, up_send, gate_keep, up_keep = chunk
            came = [from_distance(gate_send, "tp", 1), from_distance(up_send, "tp", 2)]
            (gate_send, up_send), kept = halve([gate_keep, up_keep], came)
            came = [from_distance(gate_send, "tp", 2), from_distance(up_send, "tp", 1)]
            own, factor = make_inner([part[None] for part in (*kept, *came)], factor, model)
            far = from_distance(own, "tp", 2)
            inner.append([own, from_distance(own, "tp", 1), far, from_distance(far, "tp", 1)])
        else:
            parts = [swap(part.reshape(ranks_tp, -1, part.shape[1]), "tp") for part in chunk]
            own, factor = make_inner(parts, factor, model)
            inner.append([lax.all_gather(own, "tp", axis=0, tiled=True)])
    ffn = swap(project_down(inner, w_down, own_hidden, ranks), ("dp", "tp"))
    return make_layer(ffn, per_rank, model)


def solution(mesh):
    placed = (
        P(("dp", "tp"), None),
        P(("dp", "tp"), None),
        P(("dp", "tp"), None),
        P(),
        P(("dp", "tp"), None, None),
        P("dp", "tp"),
        P(),
        P("tp", "dp"),
        P("tp", "dp"),
        P("dp", "tp"),
    )
    return jax.shard_map(
        local, mesh=mesh, in_specs=placed, out_specs=P(("dp", "tp"), None), check_vma=False
    )
```

```python
import functools

import jax
import jax.numpy as jnp
from jax import lax
from jax.experimental import pallas as pl
from jax.experimental.pallas import tpu as pltpu
from jax.sharding import PartitionSpec as P

C = 512
BLOCK_TOKENS = 64
TILE = 512

score_scale = 192.0 ** (-0.5)
log2_e = 1.4426950408889634
negative = -1e30


def attention_kernel(
    lens_ref,
    raw_ref,
    cache_ref,
    out_ref,
    q_ref,
    pairs_of_heads,
    rows_of_heads,
    held,
    score0,
    score1,
    weight0,
    weight1,
    keep0,
    keep1,
    acc,
    done,
    best,
    mass0,
    mass1,
    lo,
    hi,
    first,
    last,
    sems,
):
    nreq, heads, _ = q_ref.shape
    tile = held.shape[2]
    factor = score_scale * log2_e

    rank = lax.axis_index("dp") * lax.axis_size("tp") + lax.axis_index("tp")
    begin = jnp.int32(0)
    pairs = jnp.int32(0)
    for r in range(nreq):
        length = lens_ref[rank * nreq + r]
        lo[r] = begin
        hi[r] = begin + length
        first[r] = begin // tile
        last[r] = (begin + length - 1) // tile
        pairs = pairs + (last[r] - first[r] + 1)
        begin = begin + ((length + BLOCK_TOKENS - 1) // BLOCK_TOKENS) * BLOCK_TOKENS
    used = last[nreq - 1] + 1

    def copy(i):
        return pltpu.make_async_copy(
            cache_ref.at[:, pl.ds(pl.multiple_of(i * tile, tile), tile)], held.at[i], sems.at[i]
        )

    @pl.loop(0, used)
    def _(i):
        copy(i).start()

    width = q_ref.shape[2]
    half = heads // 2
    tail = width % 128
    full = width // 128
    for j in range(half):
        for c in range(pairs_of_heads.shape[0]):
            at = 2 * width * j + 128 * c
            pairs_of_heads[c, pl.ds(j, nreq, stride=half), :] = raw_ref[:, at : at + 128].astype(
                jnp.float32
            )
    for r in range(nreq):
        rows = slice(r * half, (r + 1) * half)
        for c in range(full + 1):
            rows_of_heads[c, pl.ds(0, half, stride=2), :] = pairs_of_heads[c, rows, :]
            ahead = min(full + c + 1, pairs_of_heads.shape[0] - 1)
            rows_of_heads[c, pl.ds(1, half, stride=2), :] = jnp.concatenate(
                [pairs_of_heads[full + c, rows, tail:], pairs_of_heads[ahead, rows, :tail]], 1
            )
        for c in range(full):
            q_ref[r, :, c * 128 : (c + 1) * 128] = rows_of_heads[c].astype(q_ref.dtype)
        q_ref[r, :, full * 128 :] = rows_of_heads[full, :, :tail].astype(q_ref.dtype)

    for ref in (acc, mass0, mass1, keep0, keep1, weight0, weight1):
        ref[...] = jnp.zeros_like(ref)
    best[...] = jnp.full_like(best, negative)

    def advance(p, r, i):
        live = p + 1 < pairs
        step = (i == last[r]) & live
        nr = jnp.where(step, r + 1, r)
        ni = jnp.where(step, first[nr], jnp.where(live, i + 1, i))
        return nr, ni, live

    def fetch(r, i, live):
        fresh = live & ((r == 0) | (i > last[jnp.maximum(r - 1, 0)]))

        @pl.when(fresh)
        def _():
            copy(i).wait()

    def scores(r, i, live):
        begin_at = jnp.where(live, lo[r], 0)
        end_at = jnp.where(live, hi[r], 0)
        token = i * tile + lax.broadcasted_iota(jnp.int32, (1, tile), 1)
        bias = jnp.where((token >= begin_at) & (token < end_at), 0.0, negative)
        return jnp.dot(q_ref[r], held[i], preferred_element_type=jnp.float32) + bias

    def gather(i, weights):
        return jnp.dot(held[i, :C, :], weights[...], preferred_element_type=jnp.float32)

    def half_step(before, now, after, given, found, used, made):
        (r0, i0), (r1, i1, live1), (r2, i2, live2) = before, now, after
        weights0, keeps0, masses0 = used
        weights1, keeps1, masses1 = made
        acc[...] = acc[...] * keeps0[:1, :] + gather(i0, weights0)
        found[...] = scores(r2, i2, live2)

        s = given[...]
        old = jnp.where(live1 & (i1 == first[r1]), negative, best[...])
        new = jnp.maximum(old, jnp.max(s, axis=1, keepdims=True))
        weight = jnp.exp2((s - new[:, :1]) * factor)
        keep = jnp.exp2((old - new) * factor)
        part = weight[:, :128]
        for at in range(128, tile, 128):
            part = part + weight[:, at : at + 128]

        weights1[...] = weight.T.astype(weights1.dtype)
        keeps1[...] = keep.T[:8, :]
        masses1[...] = masses0[...] * keep + part
        best[...] = new

        @pl.when(r1 != r0)
        def _():
            close(r0, masses0)

    def close(r, masses):
        total = jnp.sum(masses[...], axis=1, keepdims=True)
        done[r] = acc[...].T / total

    zero = jnp.int32(0)
    fetch(zero, zero, pairs > 0)
    score0[...] = scores(zero, zero, pairs > 0)
    stage0 = (weight0, keep0, mass0)
    stage1 = (weight1, keep1, mass1)

    def step(j, carry):
        r0, i0, r1, i1, live1 = carry
        p = 2 * j
        r2, i2, live2 = advance(p, r1, i1)
        r3, i3, live3 = advance(p + 1, r2, i2)
        fetch(r2, i2, live2)
        half_step((r0, i0), (r1, i1, live1), (r2, i2, live2), score0, score1, stage1, stage0)
        fetch(r3, i3, live3)
        half_step((r1, i1), (r2, i2, live2), (r3, i3, live3), score1, score0, stage0, stage1)
        return r2, i2, r3, i3, live3

    r0, i0, _, _, _ = lax.fori_loop(
        0, (pairs + 1) // 2, step, (zero, zero, zero, zero, pairs > 0)
    )
    acc[...] = acc[...] * keep1[:1, :] + gather(i0, weight1)
    close(r0, mass1)

    share = heads // out_ref.shape[0]
    for d in range(out_ref.shape[0]):
        rows = [done[r, d * share : (d + 1) * share, :] for r in range(nreq)]
        out_ref[d] = jnp.concatenate(rows, 0).astype(out_ref.dtype)


def kernel_params(limit):
    return pltpu.CompilerParams(vmem_limit_bytes=limit * 1024 * 1024)


def in_vmem(count):
    return [pl.BlockSpec(memory_space=pltpu.VMEM)] * count


def fetched(weight):
    return pltpu.with_memory_space_constraint(weight, pltpu.VMEM)


def attend(lengths, queries, cache_t, ranks):
    nreq = queries.shape[0]
    width, tokens = cache_t.shape
    heads = queries.shape[1] // width
    tile = TILE
    tiles = tokens // tile
    return pl.pallas_call(
        attention_kernel,
        out_shape=jax.ShapeDtypeStruct((ranks, nreq * heads // ranks, C), jnp.bfloat16),
        in_specs=[pl.BlockSpec(memory_space=pltpu.SMEM)]
        + in_vmem(1)
        + [pl.BlockSpec(memory_space=pltpu.HBM)],
        out_specs=pl.BlockSpec(memory_space=pltpu.VMEM),
        scratch_shapes=[
            pltpu.VMEM((nreq, heads, width), jnp.bfloat16),
            pltpu.VMEM((2 * width // 128, nreq * heads // 2, 128), jnp.float32),
            pltpu.VMEM((width // 128 + 1, heads, 128), jnp.float32),
            pltpu.VMEM((tiles, width, tile), jnp.bfloat16),
            pltpu.VMEM((heads, tile), jnp.float32),
            pltpu.VMEM((heads, tile), jnp.float32),
            pltpu.VMEM((tile, heads), jnp.bfloat16),
            pltpu.VMEM((tile, heads), jnp.bfloat16),
            pltpu.VMEM((8, heads), jnp.float32),
            pltpu.VMEM((8, heads), jnp.float32),
            pltpu.VMEM((C, heads), jnp.float32),
            pltpu.VMEM((nreq, heads, C), jnp.float32),
            pltpu.VMEM((heads, 128), jnp.float32),
            pltpu.VMEM((heads, 128), jnp.float32),
            pltpu.VMEM((heads, 128), jnp.float32),
            pltpu.SMEM((nreq,), jnp.int32),
            pltpu.SMEM((nreq,), jnp.int32),
            pltpu.SMEM((nreq,), jnp.int32),
            pltpu.SMEM((nreq,), jnp.int32),
            pltpu.SemaphoreType.DMA((tiles,)),
        ],
        compiler_params=kernel_params(28),
        cost_estimate=pl.CostEstimate(
            flops=2 * heads * tokens * (width + C),
            bytes_accessed=2 * tokens * width,
            transcendentals=heads * tokens,
        ),
        name="attention",
    )(
        pltpu.with_memory_space_constraint(lengths, pltpu.HBM),
        pltpu.with_memory_space_constraint(queries, pltpu.HBM),
        pltpu.with_memory_space_constraint(cache_t, pltpu.HBM),
    )


def head_values_kernel(latent_ref, w_ref, out_ref, values):
    heads, _, wide = w_ref.shape
    requests = out_ref.shape[0]
    latent = latent_ref[...]
    for h in range(heads):
        values[...] = jnp.dot(latent, w_ref[h], preferred_element_type=jnp.float32)
        picked = values[pl.ds(h, requests, stride=heads), :]
        out_ref[:, h * wide : (h + 1) * wide] = picked.astype(out_ref.dtype)


def head_values(latent, w_uv):
    heads, _, wide = w_uv.shape
    requests = latent.shape[0] // heads
    return pl.pallas_call(
        head_values_kernel,
        out_shape=jax.ShapeDtypeStruct((requests, heads * wide), jnp.bfloat16),
        in_specs=in_vmem(2),
        out_specs=pl.BlockSpec(memory_space=pltpu.VMEM),
        scratch_shapes=[pltpu.VMEM((latent.shape[0], wide), jnp.float32)],
        compiler_params=kernel_params(12),
        name="head_values",
    )(latent, w_uv)


def split_kernel(rows_ref, *out_refs):
    width = out_refs[0].shape[1]
    me = lax.axis_index("tp")
    for k, out_ref in enumerate(out_refs):
        start = pl.multiple_of((me ^ k) * width, 128)
        out_ref[...] = rows_ref[:, pl.ds(start, width)]


def split_columns(rows, ranks):
    shape = jax.ShapeDtypeStruct((rows.shape[0], rows.shape[1] // ranks), rows.dtype)
    return pl.pallas_call(
        split_kernel,
        out_shape=[shape] * ranks,
        in_specs=in_vmem(1),
        out_specs=in_vmem(ranks),
        compiler_params=kernel_params(8),
        name="split_columns",
    )(rows)


def from_distance(piece, axis, distance):
    return lax.ppermute(piece, axis, [(k, k ^ distance) for k in range(lax.axis_size(axis))])


def from_all(piece, axis):
    if lax.axis_size(axis) == 4:
        far = from_distance(piece, axis, 2)
        return [piece, from_distance(piece, axis, 1), far, from_distance(far, axis, 1)]
    return [piece] + [from_distance(piece, axis, k) for k in range(1, lax.axis_size(axis))]


def own_output_kernel(value_ref, w_ref, out_ref):
    depth = value_ref.shape[1]
    rows = pl.ds(pl.multiple_of(lax.axis_index("tp") * depth, 128), depth)
    out_ref[...] = jnp.dot(value_ref[...], w_ref[rows, :], preferred_element_type=jnp.float32)


def output_kernel(*refs):
    own_ref, *values, w_ref, out_ref, total = refs
    depth = values[0].shape[1]
    me = lax.axis_index("tp")
    for k, value in enumerate(values, 1):
        rows = pl.ds(pl.multiple_of((me ^ k) * depth, 128), depth)
        term = jnp.dot(value[...], w_ref[rows, :], preferred_element_type=jnp.float32)
        if k == 1:
            total[...] = own_ref[...] + term
        else:
            total[...] += term
    out_ref[...] = total[...].astype(out_ref.dtype)


def project_out(values, w_o):
    requests, depth = values[0].shape
    width = w_o.shape[1]
    w_o = fetched(w_o)
    own = pl.pallas_call(
        own_output_kernel,
        out_shape=jax.ShapeDtypeStruct((requests, width), jnp.float32),
        in_specs=in_vmem(2),
        out_specs=pl.BlockSpec(memory_space=pltpu.VMEM),
        compiler_params=kernel_params(12),
        cost_estimate=pl.CostEstimate(
            flops=2 * requests * depth * width, bytes_accessed=2 * depth * width, transcendentals=0
        ),
        name="project_own",
    )(values[0], w_o)
    return pl.pallas_call(
        output_kernel,
        out_shape=jax.ShapeDtypeStruct((requests, width), jnp.bfloat16),
        in_specs=in_vmem(len(values) + 1),
        out_specs=pl.BlockSpec(memory_space=pltpu.VMEM),
        scratch_shapes=[pltpu.VMEM((requests, width), jnp.float32)],
        compiler_params=kernel_params(12),
        name="project_out",
    )(own, *values[1:], w_o)


def hidden_kernel(parts_ref, *refs):
    *slices, out_ref, added = refs
    per_rank = slices[0].shape[0]
    me = lax.axis_index("tp")
    for k, piece in enumerate(slices):
        added[me ^ k] = piece[...].astype(jnp.float32)
    width = out_ref.shape[1]
    for at in range(0, width, 128):
        at = slice(at, at + 128)
        total = parts_ref[0, :, at].astype(jnp.float32)
        for d in range(1, parts_ref.shape[0]):
            total = total + parts_ref[d, :, at].astype(jnp.float32)
        terms = [added[s, :, at] for s in range(len(slices))]
        out_ref[:, at] = (total + jnp.concatenate(terms, 0)).astype(out_ref.dtype)


def make_hidden(parts, slices):
    return pl.pallas_call(
        hidden_kernel,
        out_shape=jax.ShapeDtypeStruct(parts.shape[1:], jnp.bfloat16),
        in_specs=in_vmem(1 + len(slices)),
        out_specs=pl.BlockSpec(memory_space=pltpu.VMEM),
        scratch_shapes=[pltpu.VMEM((len(slices),) + slices[0].shape, jnp.float32)],
        compiler_params=kernel_params(12),
        name="hidden",
    )(parts, *slices)


def scale_kernel(hidden_ref, gain_ref, gate_ref, up_ref, scaled, gate_sum, up_sum, *refs):
    *outs, gains = refs
    ranks = lax.axis_size("tp")
    halves = scaled.shape[0]
    requests, width = hidden_ref.shape
    share = requests // ranks
    groups = width // 128
    me = lax.axis_index("tp")
    places = [[3, 1, 2, 0], [3, 2, 1, 0]] if halves == 2 else [list(range(ranks))]

    gains[...] = gain_ref[...].astype(jnp.float32)
    squares = [None] * ranks
    for k in range(ranks):
        block = me ^ k if halves == 2 else k
        start = block * share if halves == 1 else pl.multiple_of(block * share, 16)
        square = jnp.zeros((share, 128), jnp.float32)
        for g in range(groups):
            at = slice(g * 128, (g + 1) * 128)
            x = hidden_ref[pl.ds(start, share), at].astype(jnp.float32)
            square = square + x * x
            gain = gains[pl.ds(me * groups + g, 1), :]
            value = (x * gain).astype(scaled.dtype)
            for n, place in enumerate(places):
                scaled[n, place[k] * share : (place[k] + 1) * share, at] = value
        squares[places[0][k]] = square
    square = jnp.sum(jnp.concatenate(squares, 0), 1, keepdims=True)
    top = square.astype(jnp.bfloat16).astype(jnp.float32)
    middle = (square - top).astype(jnp.bfloat16).astype(jnp.float32)
    low = square - top - middle
    lane = lax.broadcasted_iota(jnp.int32, (requests, 128), 1)
    digits = jnp.where(lane == 0, top, jnp.where(lane == 1, middle, jnp.where(lane == 2, low, 0.0)))
    gates = [gate_sum, outs[0]] if halves == 2 else [gate_sum]
    ups = [up_sum, outs[1]] if halves == 2 else [up_sum]
    columns = up_sum.shape[1]
    for n, target in enumerate(gates):
        rows = target.shape[0]
        target[:, columns:] = digits[n * rows : (n + 1) * rows].astype(target.dtype)
    products(scaled, gate_ref, up_ref, 0, columns, gates, ups)


def products(scaled, gate_ref, up_ref, first, columns, gates, ups):
    for left, w_ref, targets in ((0, gate_ref, gates), (scaled.shape[0] - 1, up_ref, ups)):
        for at in range(0, columns, 256):
            upto = min(at + 256, columns)
            term = jnp.dot(
                scaled[left],
                w_ref[:, first + at : first + upto],
                preferred_element_type=jnp.float32,
            )
            for n, target in enumerate(targets):
                rows = target.shape[0]
                target[:, at:upto] = term[n * rows : (n + 1) * rows].astype(target.dtype)


def second_kernel(scaled, gate_ref, up_ref, *outs):
    columns = outs[1].shape[1]
    first = gate_ref.shape[1] - columns
    products(scaled, gate_ref, up_ref, first, columns, outs[0::2], outs[1::2])


def gate_up(hidden, gain, w_gate, w_up, halves):
    requests, width = hidden.shape
    units = w_gate.shape[1]
    first = units if halves == 1 else round_up(units // 2, 256)
    w_gate, w_up = fetched(w_gate), fetched(w_up)

    def shapes(columns, extra):
        return [
            jax.ShapeDtypeStruct((requests // halves, columns + more), jnp.bfloat16)
            for _ in range(halves)
            for more in (extra, 0)
        ]

    outs = [jax.ShapeDtypeStruct((halves, requests, width), jnp.bfloat16)] + shapes(first, 128)
    scaled, *parts = pl.pallas_call(
        scale_kernel,
        out_shape=outs,
        in_specs=in_vmem(4),
        out_specs=in_vmem(len(outs)),
        scratch_shapes=[pltpu.VMEM(gain.shape, jnp.float32)],
        compiler_params=kernel_params(12),
        cost_estimate=pl.CostEstimate(
            flops=4 * requests * width * first, bytes_accessed=4 * width * first, transcendentals=0
        ),
        name="gate_up",
    )(hidden, gain, w_gate, w_up)
    if halves == 1:
        return [parts]
    outs = shapes(units - first, 0)
    others = pl.pallas_call(
        second_kernel,
        out_shape=outs,
        in_specs=in_vmem(3),
        out_specs=in_vmem(len(outs)),
        compiler_params=kernel_params(12),
        cost_estimate=pl.CostEstimate(
            flops=4 * requests * width * (units - first),
            bytes_accessed=4 * width * (units - first),
            transcendentals=0,
        ),
        name="gate_up_rest",
    )(scaled, w_gate, w_up)
    return [parts, others]


def halve_kernel(*refs):
    count = len(refs) // 4
    for n in range(count):
        kept, came, send, keep = refs[n], refs[count + n], refs[2 * count + n], refs[3 * count + n]
        rows = send.shape[0]
        for at in range(0, send.shape[1], 128):
            at = slice(at, at + 128)
            total = kept[:, at].astype(jnp.float32) + came[:, at].astype(jnp.float32)
            send[:, at] = total[:rows].astype(send.dtype)
            keep[:, at] = total[rows:]


def halve(kept, came):
    half = [(k.shape[0] // 2, k.shape[1]) for k in kept]
    outs = pl.pallas_call(
        halve_kernel,
        out_shape=[jax.ShapeDtypeStruct(shape, jnp.bfloat16) for shape in half]
        + [jax.ShapeDtypeStruct(shape, jnp.float32) for shape in half],
        in_specs=in_vmem(2 * len(kept)),
        out_specs=in_vmem(2 * len(kept)),
        compiler_params=kernel_params(12),
        name="halve",
    )(*kept, *came)
    return outs[: len(kept)], outs[len(kept) :]


def inner_kernel(model, given, *refs):
    *parts, out_ref, factor_ref = refs
    gates, ups = parts[given::2], parts[given + 1 :: 2]
    columns = out_ref.shape[1]

    def total(parts, at):
        terms = [
            part[n, :, at].astype(jnp.float32) for part in parts for n in range(part.shape[0])
        ]
        return sum(terms[1:], terms[0])

    if given:
        factor = parts[0][...]
    else:
        square = jnp.sum(total(gates, slice(columns, columns + 128)), 1, keepdims=True)
        factor = jnp.broadcast_to(lax.rsqrt(square / model + 1e-06), factor_ref.shape)
    factor_ref[...] = factor
    for at in range(0, columns, 128):
        at = slice(at, at + 128)
        gate = total(gates, at) * factor
        up = total(ups, at) * factor
        out_ref[:, at] = (gate / (1.0 + jnp.exp(-gate)) * up).astype(out_ref.dtype)


def make_inner(parts, factor, model):
    given = [] if factor is None else [factor]
    rows, columns = parts[1].shape[1:]
    return pl.pallas_call(
        functools.partial(inner_kernel, model, len(given)),
        out_shape=[
            jax.ShapeDtypeStruct((rows, columns), jnp.bfloat16),
            jax.ShapeDtypeStruct((rows, 128), jnp.float32),
        ],
        in_specs=in_vmem(len(given) + len(parts)),
        out_specs=in_vmem(2),
        compiler_params=kernel_params(12),
        name="inner",
    )(*given, *parts)


def down_kernel(chunks, *refs):
    *pieces, w_ref, hidden_ref, out_ref, inner, total = refs
    width = w_ref.shape[1]
    count = len(pieces) // chunks
    share = total.shape[0] // count
    at = 0
    for c in range(chunks):
        columns = pieces[c * count].shape[1]
        for k in range(count):
            inner[k * share : (k + 1) * share, at : at + columns] = pieces[c * count + k][...]
        at += columns
    result = jnp.dot(inner[...], w_ref[...], preferred_element_type=jnp.float32)
    me = lax.axis_index("tp")
    for k in range(count):
        start = pl.multiple_of((me ^ k) * share, 16) if count > 1 else 0
        total[pl.ds(start, share), :] = result[k * share : (k + 1) * share]
    rows = hidden_ref.shape[0]
    own = pl.ds(pl.multiple_of(lax.axis_index("dp") * rows, 16), rows)
    total[own, :] += hidden_ref[...].astype(jnp.float32)
    groups = width // 128
    per_rank = out_ref.shape[1] // groups
    for d in range(out_ref.shape[0]):
        owned = [
            total[d * per_rank : (d + 1) * per_rank, g * 128 : (g + 1) * 128]
            for g in range(groups)
        ]
        out_ref[d] = jnp.concatenate(owned, 0).astype(out_ref.dtype)


def project_down(chunks, w_down, hidden, ranks):
    units, width = w_down.shape
    pieces = [piece for chunk in chunks for piece in chunk]
    requests = sum(piece.shape[0] for piece in chunks[0])
    return pl.pallas_call(
        functools.partial(down_kernel, len(chunks)),
        out_shape=jax.ShapeDtypeStruct(
            (ranks, requests // ranks * (width // 128), 128), jnp.bfloat16
        ),
        in_specs=in_vmem(len(pieces) + 2),
        out_specs=pl.BlockSpec(memory_space=pltpu.VMEM),
        scratch_shapes=[
            pltpu.VMEM((requests, units), jnp.bfloat16),
            pltpu.VMEM((requests, width), jnp.float32),
        ],
        compiler_params=kernel_params(12),
        name="project_down",
    )(*pieces, fetched(w_down), hidden)


def layer_kernel(parts_ref, out_ref, total):
    per_rank, model = out_ref.shape
    ranks = lax.axis_size("tp")
    groups = model // ranks // 128
    for t in range(ranks):
        terms = [
            parts_ref[d, :, :].astype(jnp.float32) for d in range(t, parts_ref.shape[0], ranks)
        ]
        layer = sum(terms[1:], terms[0])
        for g in range(groups):
            at = (t * groups + g) * 128
            total[:, at : at + 128] = layer[g * per_rank : (g + 1) * per_rank, :]
    out_ref[...] = total[...].astype(out_ref.dtype)


def make_layer(parts, per_rank, model):
    return pl.pallas_call(
        layer_kernel,
        out_shape=jax.ShapeDtypeStruct((per_rank, model), jnp.bfloat16),
        in_specs=in_vmem(1),
        out_specs=pl.BlockSpec(memory_space=pltpu.VMEM),
        scratch_shapes=[pltpu.VMEM((per_rank, model), jnp.float32)],
        compiler_params=kernel_params(12),
        name="layer",
    )(parts)


def round_up(value, step):
    return (value + step - 1) // step * step


def swap(parts, axes):
    return lax.all_to_all(parts, axes, split_axis=0, concat_axis=0, tiled=True)


def local(
    residual, queries, paged_latent_cache, lengths, w_uv, w_o, norm_gain, w_gate, w_up, w_down
):
    ranks_dp = lax.axis_size("dp")
    ranks_tp = lax.axis_size("tp")
    ranks = ranks_dp * ranks_tp
    per_rank, model = residual.shape
    requests = per_rank * ranks
    heads_here = w_uv.shape[0]
    units = w_gate.shape[1]
    width = w_o.shape[1]


    latent = swap(attend(lengths, queries, paged_latent_cache.T, ranks), ("dp", "tp"))

    values = head_values(latent.reshape(requests * heads_here, C), w_uv)
    values, residual = lax.optimization_barrier((values, residual))
    added = list(split_columns(residual, ranks_tp))
    added = added[:1] + [from_distance(added[k], "tp", k) for k in range(1, ranks_tp)]
    if ranks_tp == 4:
        far, added = lax.optimization_barrier((from_distance(values, "tp", 2), added))
        near = from_distance(values, "tp", 1)
        values = [values, near, far, from_distance(far, "tp", 1)]
    else:
        values = from_all(values, "tp")
    attn, added = lax.optimization_barrier((project_out(values, w_o), added))
    attn = swap(attn.reshape(ranks_dp, requests // ranks_dp, width), "dp")
    own_hidden = make_hidden(attn, added)
    hidden = lax.all_gather(own_hidden, "dp", axis=0, tiled=True)

    halves = 2 if ranks_tp == 4 else 1
    chunks = gate_up(hidden, norm_gain.reshape(-1, 128), w_gate, w_up, halves)
    if halves == 2:
        first, second = chunks
        kept, second = lax.optimization_barrier((first[2:], second))
        chunks = [[*first[:2], *kept], second]
    inner = []
    factor = None
    for chunk in chunks:
        if halves == 2:
            gate_send, up_send, gate_keep, up_keep = chunk
            came = [from_distance(gate_send, "tp", 1), from_distance(up_send, "tp", 2)]
            (gate_send, up_send), kept = halve([gate_keep, up_keep], came)
            came = [from_distance(gate_send, "tp", 2), from_distance(up_send, "tp", 1)]
            own, factor = make_inner([part[None] for part in (*kept, *came)], factor, model)
            inner.append(from_all(own, "tp"))
        else:
            parts = [swap(part.reshape(ranks_tp, -1, part.shape[1]), "tp") for part in chunk]
            own, factor = make_inner(parts, factor, model)
            inner.append([lax.all_gather(own, "tp", axis=0, tiled=True)])
    ffn = swap(project_down(inner, w_down, own_hidden, ranks), ("dp", "tp"))
    return make_layer(ffn, per_rank, model)


def solution(mesh):
    placed = (
        P(("dp", "tp"), None),
        P(("dp", "tp"), None),
        P(("dp", "tp"), None),
        P(),
        P(("dp", "tp"), None, None),
        P("dp", "tp"),
        P(),
        P("tp", "dp"),
        P("tp", "dp"),
        P("dp", "tp"),
    )
    return jax.shard_map(
        local, mesh=mesh, in_specs=placed, out_specs=P(("dp", "tp"), None), check_vma=False
    )
```

```python
import functools

import jax
import jax.numpy as jnp
from jax import lax
from jax.experimental import pallas as pl
from jax.experimental.pallas import tpu as pltpu
from jax.sharding import PartitionSpec as P

C = 512
BLOCK_TOKENS = 64
TILE = 512
UNROLL = 4

score_scale = 192.0 ** (-0.5)
log2_e = 1.4426950408889634
negative = -1e30


def attention_kernel(
    lens_ref,
    raw_ref,
    cache_ref,
    out_ref,
    q_ref,
    pairs_of_heads,
    rows_of_heads,
    held,
    score_bufs,
    weight_bufs,
    keep_bufs,
    acc,
    done,
    best,
    mass,
    lo,
    hi,
    first,
    last,
    sems,
):
    nreq, heads, _ = q_ref.shape
    tile = held.shape[2]
    factor = score_scale * log2_e

    rank = lax.axis_index("dp") * lax.axis_size("tp") + lax.axis_index("tp")
    begin = jnp.int32(0)
    pairs = jnp.int32(0)
    for r in range(nreq):
        length = lens_ref[rank * nreq + r]
        lo[r] = begin
        hi[r] = begin + length
        first[r] = begin // tile
        last[r] = (begin + length - 1) // tile
        pairs = pairs + (last[r] - first[r] + 1)
        begin = begin + ((length + BLOCK_TOKENS - 1) // BLOCK_TOKENS) * BLOCK_TOKENS
    used = last[nreq - 1] + 1

    def copy(i):
        return pltpu.make_async_copy(
            cache_ref.at[:, pl.ds(pl.multiple_of(i * tile, tile), tile)], held.at[i], sems.at[i]
        )

    @pl.loop(0, used)
    def _(i):
        copy(i).start()

    width = q_ref.shape[2]
    half = heads // 2
    tail = width % 128
    full = width // 128
    for j in range(half):
        for c in range(pairs_of_heads.shape[0]):
            at = 2 * width * j + 128 * c
            pairs_of_heads[c, pl.ds(j, nreq, stride=half), :] = raw_ref[:, at : at + 128].astype(
                jnp.float32
            )
    for r in range(nreq):
        rows = slice(r * half, (r + 1) * half)
        for c in range(full + 1):
            rows_of_heads[c, pl.ds(0, half, stride=2), :] = pairs_of_heads[c, rows, :]
            ahead = min(full + c + 1, pairs_of_heads.shape[0] - 1)
            rows_of_heads[c, pl.ds(1, half, stride=2), :] = jnp.concatenate(
                [pairs_of_heads[full + c, rows, tail:], pairs_of_heads[ahead, rows, :tail]], 1
            )
        for c in range(full):
            q_ref[r, :, c * 128 : (c + 1) * 128] = rows_of_heads[c].astype(q_ref.dtype)
        q_ref[r, :, full * 128 :] = rows_of_heads[full, :, :tail].astype(q_ref.dtype)

    acc[...] = jnp.zeros_like(acc)
    best[...] = jnp.full_like(best, negative)
    mass[...] = jnp.zeros_like(mass)
    score_of = [score_bufs.at[k] for k in range(UNROLL)]
    weight_of = [weight_bufs.at[k] for k in range(UNROLL)]
    keep_of = [keep_bufs.at[k] for k in range(UNROLL)]
    weight_of[-1][...] = jnp.zeros(weight_bufs.shape[1:], weight_bufs.dtype)
    keep_of[-1][...] = jnp.ones(keep_bufs.shape[1:], keep_bufs.dtype)

    def advance(p, r, i):
        live = p + 1 < pairs
        step = (i == last[r]) & live
        nr = jnp.where(step, r + 1, r)
        ni = jnp.where(step, first[nr], jnp.where(live, i + 1, i))
        return nr, ni, live

    def fetch(r, i, live):
        fresh = live & ((r == 0) | (i > last[jnp.maximum(r - 1, 0)]))

        @pl.when(fresh)
        def _():
            copy(i).wait()

    def scores(r, i, live, target):
        begin_at = jnp.where(live, lo[r], 0)
        end_at = jnp.where(live, hi[r], 0)
        s = jnp.dot(q_ref[r], held[i], preferred_element_type=jnp.float32)
        token = i * tile + lax.broadcasted_iota(jnp.int32, (1, tile), 1)
        target[...] = s + jnp.where((token >= begin_at) & (token < end_at), 0.0, negative)

    def soften(r, source, weights, keeps):
        s = source[...]
        old = best[r]
        new = jnp.maximum(old, jnp.max(s, axis=1, keepdims=True))
        weight = jnp.exp2((s - new[:, :1]) * factor)
        keep = jnp.exp2((old - new) * factor)
        part = weight[:, :128]
        for at in range(128, tile, 128):
            part = part + weight[:, at : at + 128]
        mass[r] = mass[r] * keep + part
        best[r] = new
        weights[...] = weight.T.astype(weights.dtype)
        keeps[...] = keep.T[:8, :]

    def gather(r, i, weights, keeps):
        values = lax.dot_general(
            held[i, :C, :],
            weights[...],
            (((1,), (0,)), ((), ())),
            preferred_element_type=jnp.float32,
        )
        acc[r] = acc[r] * keeps[:1, :] + values

    zero = jnp.int32(0)
    fetch(zero, zero, pairs > 0)
    scores(zero, zero, pairs > 0, score_of[0])

    def step(j, carry):
        r0, i0, r1, i1 = carry
        places = [(r1, i1, True)]
        for k in range(UNROLL):
            places.append(advance(UNROLL * j + k, *places[-1][:2]))
        for place in places[1:]:
            fetch(*place)
        for k in range(UNROLL):
            gather(r0, i0, weight_of[k - 1], keep_of[k - 1])
            scores(*places[k + 1], score_of[(k + 1) % UNROLL])
            r0, i0, _ = places[k]
            soften(r0, score_of[k], weight_of[k], keep_of[k])
        return (r0, i0) + places[-1][:2]

    steps = (pairs + UNROLL - 1) // UNROLL
    r0, i0, _, _ = lax.fori_loop(0, steps, step, (zero, zero, zero, zero))
    gather(r0, i0, weight_of[-1], keep_of[-1])

    share = heads // out_ref.shape[0]
    for r in range(nreq):
        total = jnp.sum(mass[r], axis=1, keepdims=True)
        score_bufs[0, :, :C] = acc[r].T / total
        for d in range(out_ref.shape[0]):
            done[d, r * share : (r + 1) * share, :] = score_bufs[
                0, d * share : (d + 1) * share, :C
            ]
    out_ref[...] = done[...].astype(out_ref.dtype)


def kernel_params(limit):
    return pltpu.CompilerParams(vmem_limit_bytes=limit * 1024 * 1024)


def in_vmem(count):
    return [pl.BlockSpec(memory_space=pltpu.VMEM)] * count


def fetched(weight):
    return pltpu.with_memory_space_constraint(weight, pltpu.VMEM)


def attend(lengths, queries, cache_t, ranks):
    nreq = queries.shape[0]
    width, tokens = cache_t.shape
    heads = queries.shape[1] // width
    tile = TILE
    tiles = tokens // tile
    return pl.pallas_call(
        attention_kernel,
        out_shape=jax.ShapeDtypeStruct((ranks, nreq * heads // ranks, C), jnp.bfloat16),
        in_specs=[pl.BlockSpec(memory_space=pltpu.SMEM)]
        + in_vmem(1)
        + [pl.BlockSpec(memory_space=pltpu.HBM)],
        out_specs=pl.BlockSpec(memory_space=pltpu.VMEM),
        scratch_shapes=[
            pltpu.VMEM((nreq, heads, width), jnp.bfloat16),
            pltpu.VMEM((2 * width // 128, nreq * heads // 2, 128), jnp.float32),
            pltpu.VMEM((width // 128 + 1, heads, 128), jnp.float32),
            pltpu.VMEM((tiles, width, tile), jnp.bfloat16),
            pltpu.VMEM((UNROLL, heads, tile), jnp.float32),
            pltpu.VMEM((UNROLL, tile, heads), jnp.bfloat16),
            pltpu.VMEM((UNROLL, 8, heads), jnp.float32),
            pltpu.VMEM((nreq, C, heads), jnp.float32),
            pltpu.VMEM((ranks, nreq * heads // ranks, C), jnp.float32),
            pltpu.VMEM((nreq, heads, 128), jnp.float32),
            pltpu.VMEM((nreq, heads, 128), jnp.float32),
            pltpu.SMEM((nreq,), jnp.int32),
            pltpu.SMEM((nreq,), jnp.int32),
            pltpu.SMEM((nreq,), jnp.int32),
            pltpu.SMEM((nreq,), jnp.int32),
            pltpu.SemaphoreType.DMA((tiles,)),
        ],
        compiler_params=kernel_params(28),
        cost_estimate=pl.CostEstimate(
            flops=2 * heads * tokens * (width + C),
            bytes_accessed=2 * tokens * width,
            transcendentals=heads * tokens,
        ),
        name="attention",
    )(
        pltpu.with_memory_space_constraint(lengths, pltpu.HBM),
        pltpu.with_memory_space_constraint(queries, pltpu.HBM),
        pltpu.with_memory_space_constraint(cache_t, pltpu.HBM),
    )


def head_values_kernel(latent_ref, w_ref, out_ref, values):
    heads, _, wide = w_ref.shape
    requests = out_ref.shape[0]
    latent = latent_ref[...]
    for h in range(heads):
        values[...] = jnp.dot(latent, w_ref[h], preferred_element_type=jnp.float32)
        picked = values[pl.ds(h, requests, stride=heads), :]
        out_ref[:, h * wide : (h + 1) * wide] = picked.astype(out_ref.dtype)


def head_values(latent, w_uv):
    heads, _, wide = w_uv.shape
    requests = latent.shape[0] // heads
    return pl.pallas_call(
        head_values_kernel,
        out_shape=jax.ShapeDtypeStruct((requests, heads * wide), jnp.bfloat16),
        in_specs=in_vmem(2),
        out_specs=pl.BlockSpec(memory_space=pltpu.VMEM),
        scratch_shapes=[pltpu.VMEM((latent.shape[0], wide), jnp.float32)],
        compiler_params=kernel_params(12),
        name="head_values",
    )(latent, w_uv)


def split_kernel(rows_ref, *out_refs):
    width = out_refs[0].shape[1]
    me = lax.axis_index("tp")
    for k, out_ref in enumerate(out_refs):
        start = pl.multiple_of((me ^ k) * width, 128)
        out_ref[...] = rows_ref[:, pl.ds(start, width)]


def split_columns(rows, ranks):
    shape = jax.ShapeDtypeStruct((rows.shape[0], rows.shape[1] // ranks), rows.dtype)
    return pl.pallas_call(
        split_kernel,
        out_shape=[shape] * ranks,
        in_specs=in_vmem(1),
        out_specs=in_vmem(ranks),
        compiler_params=kernel_params(8),
        name="split_columns",
    )(rows)


def from_distance(piece, axis, distance):
    return lax.ppermute(piece, axis, [(k, k ^ distance) for k in range(lax.axis_size(axis))])


def from_all(piece, axis):
    return [piece] + [from_distance(piece, axis, k) for k in range(1, lax.axis_size(axis))]


def own_output_kernel(value_ref, w_ref, out_ref):
    depth = value_ref.shape[1]
    rows = pl.ds(pl.multiple_of(lax.axis_index("tp") * depth, 128), depth)
    out_ref[...] = jnp.dot(value_ref[...], w_ref[rows, :], preferred_element_type=jnp.float32)


def output_kernel(*refs):
    own_ref, *values, w_ref, out_ref, total = refs
    depth = values[0].shape[1]
    me = lax.axis_index("tp")
    for k, value in enumerate(values, 1):
        rows = pl.ds(pl.multiple_of((me ^ k) * depth, 128), depth)
        term = jnp.dot(value[...], w_ref[rows, :], preferred_element_type=jnp.float32)
        if k == 1:
            total[...] = own_ref[...] + term
        else:
            total[...] += term
    out_ref[...] = total[...].astype(out_ref.dtype)


def project_out(values, w_o):
    requests, depth = values[0].shape
    width = w_o.shape[1]
    w_o = fetched(w_o)
    own = pl.pallas_call(
        own_output_kernel,
        out_shape=jax.ShapeDtypeStruct((requests, width), jnp.float32),
        in_specs=in_vmem(2),
        out_specs=pl.BlockSpec(memory_space=pltpu.VMEM),
        compiler_params=kernel_params(12),
        cost_estimate=pl.CostEstimate(
            flops=2 * requests * depth * width, bytes_accessed=2 * depth * width, transcendentals=0
        ),
        name="project_own",
    )(values[0], w_o)
    return pl.pallas_call(
        output_kernel,
        out_shape=jax.ShapeDtypeStruct((requests, width), jnp.bfloat16),
        in_specs=in_vmem(len(values) + 1),
        out_specs=pl.BlockSpec(memory_space=pltpu.VMEM),
        scratch_shapes=[pltpu.VMEM((requests, width), jnp.float32)],
        compiler_params=kernel_params(12),
        name="project_out",
    )(own, *values[1:], w_o)


def hidden_kernel(parts_ref, *refs):
    *slices, out_ref, added = refs
    per_rank = slices[0].shape[0]
    me = lax.axis_index("tp")
    for k, piece in enumerate(slices):
        added[me ^ k] = piece[...].astype(jnp.float32)
    width = out_ref.shape[1]
    for at in range(0, width, 128):
        at = slice(at, at + 128)
        total = parts_ref[0, :, at].astype(jnp.float32)
        for d in range(1, parts_ref.shape[0]):
            total = total + parts_ref[d, :, at].astype(jnp.float32)
        terms = [added[s, :, at] for s in range(len(slices))]
        out_ref[:, at] = (total + jnp.concatenate(terms, 0)).astype(out_ref.dtype)


def make_hidden(parts, slices):
    return pl.pallas_call(
        hidden_kernel,
        out_shape=jax.ShapeDtypeStruct(parts.shape[1:], jnp.bfloat16),
        in_specs=in_vmem(1 + len(slices)),
        out_specs=pl.BlockSpec(memory_space=pltpu.VMEM),
        scratch_shapes=[pltpu.VMEM((len(slices),) + slices[0].shape, jnp.float32)],
        compiler_params=kernel_params(12),
        name="hidden",
    )(parts, *slices)


def scale_kernel(hidden_ref, gain_ref, gate_ref, up_ref, scaled, gate_sum, up_sum, *refs):
    *outs, gains = refs
    ranks = lax.axis_size("tp")
    halves = scaled.shape[0]
    requests, width = hidden_ref.shape
    share = requests // ranks
    groups = width // 128
    me = lax.axis_index("tp")
    places = [[3, 1, 2, 0], [3, 2, 1, 0]] if halves == 2 else [list(range(ranks))]

    gains[...] = gain_ref[...].astype(jnp.float32)
    squares = [None] * ranks
    for k in range(ranks):
        block = me ^ k if halves == 2 else k
        start = block * share if halves == 1 else pl.multiple_of(block * share, 16)
        square = jnp.zeros((share, 128), jnp.float32)
        for g in range(groups):
            at = slice(g * 128, (g + 1) * 128)
            x = hidden_ref[pl.ds(start, share), at].astype(jnp.float32)
            square = square + x * x
            gain = gains[pl.ds(me * groups + g, 1), :]
            value = (x * gain).astype(scaled.dtype)
            for n, place in enumerate(places):
                scaled[n, place[k] * share : (place[k] + 1) * share, at] = value
        squares[places[0][k]] = square
    square = jnp.sum(jnp.concatenate(squares, 0), 1, keepdims=True)
    top = square.astype(jnp.bfloat16).astype(jnp.float32)
    middle = (square - top).astype(jnp.bfloat16).astype(jnp.float32)
    low = square - top - middle
    lane = lax.broadcasted_iota(jnp.int32, (requests, 128), 1)
    digits = jnp.where(lane == 0, top, jnp.where(lane == 1, middle, jnp.where(lane == 2, low, 0.0)))
    gates = [gate_sum, outs[0]] if halves == 2 else [gate_sum]
    ups = [up_sum, outs[1]] if halves == 2 else [up_sum]
    columns = up_sum.shape[1]
    for n, target in enumerate(gates):
        rows = target.shape[0]
        target[:, columns:] = digits[n * rows : (n + 1) * rows].astype(target.dtype)
    products(scaled, gate_ref, up_ref, 0, columns, gates, ups)


def products(scaled, gate_ref, up_ref, first, columns, gates, ups):
    for left, w_ref, targets in ((0, gate_ref, gates), (scaled.shape[0] - 1, up_ref, ups)):
        for at in range(0, columns, 256):
            upto = min(at + 256, columns)
            term = jnp.dot(
                scaled[left],
                w_ref[:, first + at : first + upto],
                preferred_element_type=jnp.float32,
            )
            for n, target in enumerate(targets):
                rows = target.shape[0]
                target[:, at:upto] = term[n * rows : (n + 1) * rows].astype(target.dtype)


def second_kernel(scaled, gate_ref, up_ref, *outs):
    columns = outs[1].shape[1]
    first = gate_ref.shape[1] - columns
    products(scaled, gate_ref, up_ref, first, columns, outs[0::2], outs[1::2])


def gate_up(hidden, gain, w_gate, w_up, halves):
    requests, width = hidden.shape
    units = w_gate.shape[1]
    first = units if halves == 1 else round_up(units // 2, 256)
    w_gate, w_up = fetched(w_gate), fetched(w_up)

    def shapes(columns, extra):
        return [
            jax.ShapeDtypeStruct((requests // halves, columns + more), jnp.bfloat16)
            for _ in range(halves)
            for more in (extra, 0)
        ]

    outs = [jax.ShapeDtypeStruct((halves, requests, width), jnp.bfloat16)] + shapes(first, 128)
    scaled, *parts = pl.pallas_call(
        scale_kernel,
        out_shape=outs,
        in_specs=in_vmem(4),
        out_specs=in_vmem(len(outs)),
        scratch_shapes=[pltpu.VMEM(gain.shape, jnp.float32)],
        compiler_params=kernel_params(12),
        cost_estimate=pl.CostEstimate(
            flops=4 * requests * width * first, bytes_accessed=4 * width * first, transcendentals=0
        ),
        name="gate_up",
    )(hidden, gain, w_gate, w_up)
    if halves == 1:
        return [parts]
    outs = shapes(units - first, 0)
    others = pl.pallas_call(
        second_kernel,
        out_shape=outs,
        in_specs=in_vmem(3),
        out_specs=in_vmem(len(outs)),
        compiler_params=kernel_params(12),
        cost_estimate=pl.CostEstimate(
            flops=4 * requests * width * (units - first),
            bytes_accessed=4 * width * (units - first),
            transcendentals=0,
        ),
        name="gate_up_rest",
    )(scaled, w_gate, w_up)
    return [parts, others]


def halve_kernel(*refs):
    count = len(refs) // 4
    for n in range(count):
        kept, came, send, keep = refs[n], refs[count + n], refs[2 * count + n], refs[3 * count + n]
        rows = send.shape[0]
        for at in range(0, send.shape[1], 128):
            at = slice(at, at + 128)
            total = kept[:, at].astype(jnp.float32) + came[:, at].astype(jnp.float32)
            send[:, at] = total[:rows].astype(send.dtype)
            keep[:, at] = total[rows:]


def halve(kept, came):
    half = [(k.shape[0] // 2, k.shape[1]) for k in kept]
    outs = pl.pallas_call(
        halve_kernel,
        out_shape=[jax.ShapeDtypeStruct(shape, jnp.bfloat16) for shape in half]
        + [jax.ShapeDtypeStruct(shape, jnp.float32) for shape in half],
        in_specs=in_vmem(2 * len(kept)),
        out_specs=in_vmem(2 * len(kept)),
        compiler_params=kernel_params(12),
        name="halve",
    )(*kept, *came)
    return outs[: len(kept)], outs[len(kept) :]


def inner_kernel(model, given, *refs):
    *parts, out_ref, factor_ref = refs
    gates, ups = parts[given::2], parts[given + 1 :: 2]
    columns = out_ref.shape[1]

    def total(parts, at):
        terms = [
            part[n, :, at].astype(jnp.float32) for part in parts for n in range(part.shape[0])
        ]
        return sum(terms[1:], terms[0])

    if given:
        factor = parts[0][...]
    else:
        square = jnp.sum(total(gates, slice(columns, columns + 128)), 1, keepdims=True)
        factor = jnp.broadcast_to(lax.rsqrt(square / model + 1e-06), factor_ref.shape)
    factor_ref[...] = factor
    for at in range(0, columns, 128):
        at = slice(at, at + 128)
        gate = total(gates, at) * factor
        up = total(ups, at) * factor
        out_ref[:, at] = (gate / (1.0 + jnp.exp(-gate)) * up).astype(out_ref.dtype)


def make_inner(parts, factor, model):
    given = [] if factor is None else [factor]
    rows, columns = parts[1].shape[1:]
    return pl.pallas_call(
        functools.partial(inner_kernel, model, len(given)),
        out_shape=[
            jax.ShapeDtypeStruct((rows, columns), jnp.bfloat16),
            jax.ShapeDtypeStruct((rows, 128), jnp.float32),
        ],
        in_specs=in_vmem(len(given) + len(parts)),
        out_specs=in_vmem(2),
        compiler_params=kernel_params(12),
        name="inner",
    )(*given, *parts)


def down_kernel(chunks, *refs):
    *pieces, w_ref, hidden_ref, out_ref, inner, total = refs
    width = w_ref.shape[1]
    count = len(pieces) // chunks
    share = total.shape[0] // count
    at = 0
    for c in range(chunks):
        columns = pieces[c * count].shape[1]
        for k in range(count):
            inner[k * share : (k + 1) * share, at : at + columns] = pieces[c * count + k][...]
        at += columns
    result = jnp.dot(inner[...], w_ref[...], preferred_element_type=jnp.float32)
    me = lax.axis_index("tp")
    for k in range(count):
        start = pl.multiple_of((me ^ k) * share, 16) if count > 1 else 0
        total[pl.ds(start, share), :] = result[k * share : (k + 1) * share]
    rows = hidden_ref.shape[0]
    own = pl.ds(pl.multiple_of(lax.axis_index("dp") * rows, 16), rows)
    total[own, :] += hidden_ref[...].astype(jnp.float32)
    per_rank = out_ref.shape[1]
    for d in range(out_ref.shape[0]):
        out_ref[d] = total[d * per_rank : (d + 1) * per_rank, :].astype(out_ref.dtype)


def project_down(chunks, w_down, hidden, ranks):
    units, width = w_down.shape
    pieces = [piece for chunk in chunks for piece in chunk]
    requests = sum(piece.shape[0] for piece in chunks[0])
    return pl.pallas_call(
        functools.partial(down_kernel, len(chunks)),
        out_shape=jax.ShapeDtypeStruct((ranks, requests // ranks, width), jnp.bfloat16),
        in_specs=in_vmem(len(pieces) + 2),
        out_specs=pl.BlockSpec(memory_space=pltpu.VMEM),
        scratch_shapes=[
            pltpu.VMEM((requests, units), jnp.bfloat16),
            pltpu.VMEM((requests, width), jnp.float32),
        ],
        compiler_params=kernel_params(12),
        name="project_down",
    )(*pieces, fetched(w_down), hidden)


def layer_kernel(parts_ref, out_ref):
    ranks = lax.axis_size("tp")
    width = parts_ref.shape[2]
    for t in range(ranks):
        terms = [parts_ref[d].astype(jnp.float32) for d in range(t, parts_ref.shape[0], ranks)]
        layer = sum(terms[1:], terms[0])
        out_ref[:, t * width : (t + 1) * width] = layer.astype(out_ref.dtype)


def make_layer(parts, per_rank, model):
    return pl.pallas_call(
        layer_kernel,
        out_shape=jax.ShapeDtypeStruct((per_rank, model), jnp.bfloat16),
        in_specs=in_vmem(1),
        out_specs=pl.BlockSpec(memory_space=pltpu.VMEM),
        compiler_params=kernel_params(12),
        name="layer",
    )(parts)


def round_up(value, step):
    return (value + step - 1) // step * step


def swap(parts, axes):
    return lax.all_to_all(parts, axes, split_axis=0, concat_axis=0, tiled=True)


def local(
    residual, queries, paged_latent_cache, lengths, w_uv, w_o, norm_gain, w_gate, w_up, w_down
):
    ranks_dp = lax.axis_size("dp")
    ranks_tp = lax.axis_size("tp")
    ranks = ranks_dp * ranks_tp
    per_rank, model = residual.shape
    requests = per_rank * ranks
    heads_here = w_uv.shape[0]
    units = w_gate.shape[1]
    width = w_o.shape[1]


    latent = swap(attend(lengths, queries, paged_latent_cache.T, ranks), ("dp", "tp"))

    values = head_values(latent.reshape(requests * heads_here, C), w_uv)
    values, residual = lax.optimization_barrier((values, residual))
    values = from_all(values, "tp")
    added = list(split_columns(residual, ranks_tp))
    added = added[:1] + [from_distance(added[k], "tp", k) for k in range(1, ranks_tp)]
    attn, added = lax.optimization_barrier((project_out(values, w_o), added))
    attn = swap(attn.reshape(ranks_dp, requests // ranks_dp, width), "dp")
    own_hidden = make_hidden(attn, added)
    hidden = lax.all_gather(own_hidden, "dp", axis=0, tiled=True)

    halves = 2 if ranks_tp == 4 else 1
    chunks = gate_up(hidden, norm_gain.reshape(-1, 128), w_gate, w_up, halves)
    if halves == 2:
        first, second = chunks
        kept, second = lax.optimization_barrier((first[2:], second))
        chunks = [[*first[:2], *kept], second]
    inner = []
    factor = None
    for chunk in chunks:
        if halves == 2:
            gate_send, up_send, gate_keep, up_keep = chunk
            came = [from_distance(gate_send, "tp", 1), from_distance(up_send, "tp", 2)]
            (gate_send, up_send), kept = halve([gate_keep, up_keep], came)
            came = [from_distance(gate_send, "tp", 2), from_distance(up_send, "tp", 1)]
            own, factor = make_inner([part[None] for part in (*kept, *came)], factor, model)
            far = from_distance(own, "tp", 2)
            inner.append([own, from_distance(own, "tp", 1), far, from_distance(far, "tp", 1)])
        else:
            parts = [swap(part.reshape(ranks_tp, -1, part.shape[1]), "tp") for part in chunk]
            own, factor = make_inner(parts, factor, model)
            inner.append([lax.all_gather(own, "tp", axis=0, tiled=True)])
    ffn = swap(project_down(inner, w_down, own_hidden, ranks), ("dp", "tp"))
    return make_layer(ffn, per_rank, model)


def solution(mesh):
    placed = (
        P(("dp", "tp"), None),
        P(("dp", "tp"), None),
        P(("dp", "tp"), None),
        P(),
        P(("dp", "tp"), None, None),
        P("dp", "tp"),
        P(),
        P("tp", "dp"),
        P("tp", "dp"),
        P("dp", "tp"),
    )
    return jax.shard_map(
        local, mesh=mesh, in_specs=placed, out_specs=P(("dp", "tp"), None), check_vma=False
    )
```

```python
import functools

import jax
import jax.numpy as jnp
from jax import lax
from jax.experimental import pallas as pl
from jax.experimental.pallas import tpu as pltpu
from jax.sharding import PartitionSpec as P

C = 512
BLOCK_TOKENS = 64
TILE = 512

score_scale = 192.0 ** (-0.5)
log2_e = 1.4426950408889634
negative = -1e30


def attention_kernel(
    lens_ref,
    raw_ref,
    cache_ref,
    out_ref,
    q_ref,
    pairs_of_heads,
    rows_of_heads,
    held,
    score0,
    score1,
    weight0,
    weight1,
    keep0,
    keep1,
    acc,
    done,
    best,
    mass,
    lo,
    hi,
    first,
    last,
    sems,
):
    nreq, heads, _ = q_ref.shape
    tile = held.shape[2]
    factor = score_scale * log2_e

    rank = lax.axis_index("dp") * lax.axis_size("tp") + lax.axis_index("tp")
    begin = jnp.int32(0)
    pairs = jnp.int32(0)
    for r in range(nreq):
        length = lens_ref[rank * nreq + r]
        lo[r] = begin
        hi[r] = begin + length
        first[r] = begin // tile
        last[r] = (begin + length - 1) // tile
        pairs = pairs + (last[r] - first[r] + 1)
        begin = begin + ((length + BLOCK_TOKENS - 1) // BLOCK_TOKENS) * BLOCK_TOKENS
    used = last[nreq - 1] + 1

    def copy(i):
        return pltpu.make_async_copy(
            cache_ref.at[:, pl.ds(pl.multiple_of(i * tile, tile), tile)], held.at[i], sems.at[i]
        )

    @pl.loop(0, used)
    def _(i):
        copy(i).start()

    width = q_ref.shape[2]
    half = heads // 2
    tail = width % 128
    full = width // 128
    for j in range(half):
        for c in range(pairs_of_heads.shape[0]):
            at = 2 * width * j + 128 * c
            pairs_of_heads[c, pl.ds(j, nreq, stride=half), :] = raw_ref[:, at : at + 128].astype(
                jnp.float32
            )
    for r in range(nreq):
        rows = slice(r * half, (r + 1) * half)
        for c in range(full + 1):
            rows_of_heads[c, pl.ds(0, half, stride=2), :] = pairs_of_heads[c, rows, :]
            ahead = min(full + c + 1, pairs_of_heads.shape[0] - 1)
            rows_of_heads[c, pl.ds(1, half, stride=2), :] = jnp.concatenate(
                [pairs_of_heads[full + c, rows, tail:], pairs_of_heads[ahead, rows, :tail]], 1
            )
        for c in range(full):
            q_ref[r, :, c * 128 : (c + 1) * 128] = rows_of_heads[c].astype(q_ref.dtype)
        q_ref[r, :, full * 128 :] = rows_of_heads[full, :, :tail].astype(q_ref.dtype)

    acc[...] = jnp.zeros_like(acc)
    best[...] = jnp.full_like(best, negative)
    mass[...] = jnp.zeros_like(mass)
    weight1[...] = jnp.zeros_like(weight1)
    keep1[...] = jnp.ones_like(keep1)

    def advance(p, r, i):
        live = p + 1 < pairs
        step = (i == last[r]) & live
        nr = jnp.where(step, r + 1, r)
        ni = jnp.where(step, first[nr], jnp.where(live, i + 1, i))
        return nr, ni, live

    def fetch(r, i, live):
        fresh = live & ((r == 0) | (i > last[jnp.maximum(r - 1, 0)]))

        @pl.when(fresh)
        def _():
            copy(i).wait()

    def scores(r, i, live, target):
        begin_at = jnp.where(live, lo[r], 0)
        end_at = jnp.where(live, hi[r], 0)
        s = jnp.dot(q_ref[r, :, :C], held[i, :C, :], preferred_element_type=jnp.float32)
        s = s + jnp.dot(q_ref[r, :, C:], held[i, C:, :], preferred_element_type=jnp.float32)
        token = i * tile + lax.broadcasted_iota(jnp.int32, (1, tile), 1)
        target[...] = s + jnp.where((token >= begin_at) & (token < end_at), 0.0, negative)

    def soften(r, source, weights, keeps):
        s = source[...]
        old = best[r]
        new = jnp.maximum(old, jnp.max(s, axis=1, keepdims=True))
        weight = jnp.exp2((s - new[:, :1]) * factor)
        keep = jnp.exp2((old - new) * factor)
        part = weight[:, :128]
        for at in range(128, tile, 128):
            part = part + weight[:, at : at + 128]
        mass[r] = mass[r] * keep + part
        best[r] = new
        weights[...] = weight.T.astype(weights.dtype)
        keeps[...] = keep.T[:8, :]

    def gather(r, i, weights, keeps):
        values = lax.dot_general(
            held[i, :C, :],
            weights[...],
            (((1,), (0,)), ((), ())),
            preferred_element_type=jnp.float32,
        )
        acc[r] = acc[r] * keeps[:1, :] + values

    zero = jnp.int32(0)
    fetch(zero, zero, pairs > 0)
    scores(zero, zero, pairs > 0, score0)

    def step(j, carry):
        r0, i0, r1, i1 = carry
        p = 2 * j
        r2, i2, live2 = advance(p, r1, i1)
        r3, i3, live3 = advance(p + 1, r2, i2)
        fetch(r2, i2, live2)
        fetch(r3, i3, live3)
        gather(r0, i0, weight1, keep1)
        scores(r2, i2, live2, score1)
        soften(r1, score0, weight0, keep0)
        gather(r1, i1, weight0, keep0)
        scores(r3, i3, live3, score0)
        soften(r2, score1, weight1, keep1)
        return r2, i2, r3, i3

    r0, i0, _, _ = lax.fori_loop(0, (pairs + 1) // 2, step, (zero, zero, zero, zero))
    gather(r0, i0, weight1, keep1)

    share = heads // out_ref.shape[0]
    for r in range(nreq):
        total = jnp.sum(mass[r], axis=1, keepdims=True)
        score0[:, :C] = acc[r].T / total
        for d in range(out_ref.shape[0]):
            done[d, r * share : (r + 1) * share, :] = score0[d * share : (d + 1) * share, :C]
    out_ref[...] = done[...].astype(out_ref.dtype)


def kernel_params(limit):
    return pltpu.CompilerParams(vmem_limit_bytes=limit * 1024 * 1024)


def in_vmem(count):
    return [pl.BlockSpec(memory_space=pltpu.VMEM)] * count


def fetched(weight):
    return pltpu.with_memory_space_constraint(weight, pltpu.VMEM)


def attend(lengths, queries, cache_t, ranks):
    nreq = queries.shape[0]
    width, tokens = cache_t.shape
    heads = queries.shape[1] // width
    tile = TILE
    tiles = tokens // tile
    return pl.pallas_call(
        attention_kernel,
        out_shape=jax.ShapeDtypeStruct((ranks, nreq * heads // ranks, C), jnp.bfloat16),
        in_specs=[pl.BlockSpec(memory_space=pltpu.SMEM)]
        + in_vmem(1)
        + [pl.BlockSpec(memory_space=pltpu.HBM)],
        out_specs=pl.BlockSpec(memory_space=pltpu.VMEM),
        scratch_shapes=[
            pltpu.VMEM((nreq, heads, width), jnp.bfloat16),
            pltpu.VMEM((2 * width // 128, nreq * heads // 2, 128), jnp.float32),
            pltpu.VMEM((width // 128 + 1, heads, 128), jnp.float32),
            pltpu.VMEM((tiles, width, tile), jnp.bfloat16),
            pltpu.VMEM((heads, tile), jnp.float32),
            pltpu.VMEM((heads, tile), jnp.float32),
            pltpu.VMEM((tile, heads), jnp.bfloat16),
            pltpu.VMEM((tile, heads), jnp.bfloat16),
            pltpu.VMEM((8, heads), jnp.float32),
            pltpu.VMEM((8, heads), jnp.float32),
            pltpu.VMEM((nreq, C, heads), jnp.float32),
            pltpu.VMEM((ranks, nreq * heads // ranks, C), jnp.float32),
            pltpu.VMEM((nreq, heads, 128), jnp.float32),
            pltpu.VMEM((nreq, heads, 128), jnp.float32),
            pltpu.SMEM((nreq,), jnp.int32),
            pltpu.SMEM((nreq,), jnp.int32),
            pltpu.SMEM((nreq,), jnp.int32),
            pltpu.SMEM((nreq,), jnp.int32),
            pltpu.SemaphoreType.DMA((tiles,)),
        ],
        compiler_params=kernel_params(28),
        cost_estimate=pl.CostEstimate(
            flops=2 * heads * tokens * (width + C),
            bytes_accessed=2 * tokens * width,
            transcendentals=heads * tokens,
        ),
        name="attention",
    )(
        pltpu.with_memory_space_constraint(lengths, pltpu.HBM),
        pltpu.with_memory_space_constraint(queries, pltpu.HBM),
        pltpu.with_memory_space_constraint(cache_t, pltpu.HBM),
    )


def head_values_kernel(latent_ref, w_ref, out_ref, values):
    heads, _, wide = w_ref.shape
    requests = out_ref.shape[0]
    latent = latent_ref[...]
    for h in range(heads):
        values[...] = jnp.dot(latent, w_ref[h], preferred_element_type=jnp.float32)
        picked = values[pl.ds(h, requests, stride=heads), :]
        out_ref[:, h * wide : (h + 1) * wide] = picked.astype(out_ref.dtype)


def head_values(latent, w_uv):
    heads, _, wide = w_uv.shape
    requests = latent.shape[0] // heads
    return pl.pallas_call(
        head_values_kernel,
        out_shape=jax.ShapeDtypeStruct((requests, heads * wide), jnp.bfloat16),
        in_specs=in_vmem(2),
        out_specs=pl.BlockSpec(memory_space=pltpu.VMEM),
        scratch_shapes=[pltpu.VMEM((latent.shape[0], wide), jnp.float32)],
        compiler_params=kernel_params(12),
        name="head_values",
    )(latent, w_uv)


def split_kernel(rows_ref, *out_refs):
    width = out_refs[0].shape[1]
    me = lax.axis_index("tp")
    for k, out_ref in enumerate(out_refs):
        start = pl.multiple_of((me ^ k) * width, 128)
        out_ref[...] = rows_ref[:, pl.ds(start, width)]


def split_columns(rows, ranks):
    shape = jax.ShapeDtypeStruct((rows.shape[0], rows.shape[1] // ranks), rows.dtype)
    return pl.pallas_call(
        split_kernel,
        out_shape=[shape] * ranks,
        in_specs=in_vmem(1),
        out_specs=in_vmem(ranks),
        compiler_params=kernel_params(8),
        name="split_columns",
    )(rows)


def from_distance(piece, axis, distance):
    return lax.ppermute(piece, axis, [(k, k ^ distance) for k in range(lax.axis_size(axis))])


def from_all(piece, axis):
    return [piece] + [from_distance(piece, axis, k) for k in range(1, lax.axis_size(axis))]


def own_output_kernel(value_ref, w_ref, out_ref):
    depth = value_ref.shape[1]
    rows = pl.ds(pl.multiple_of(lax.axis_index("tp") * depth, 128), depth)
    out_ref[...] = jnp.dot(value_ref[...], w_ref[rows, :], preferred_element_type=jnp.float32)


def output_kernel(*refs):
    own_ref, *values, w_ref, out_ref, total = refs
    depth = values[0].shape[1]
    me = lax.axis_index("tp")
    for k, value in enumerate(values, 1):
        rows = pl.ds(pl.multiple_of((me ^ k) * depth, 128), depth)
        term = jnp.dot(value[...], w_ref[rows, :], preferred_element_type=jnp.float32)
        if k == 1:
            total[...] = own_ref[...] + term
        else:
            total[...] += term
    out_ref[...] = total[...].astype(out_ref.dtype)


def project_out(values, w_o):
    requests, depth = values[0].shape
    width = w_o.shape[1]
    w_o = fetched(w_o)
    own = pl.pallas_call(
        own_output_kernel,
        out_shape=jax.ShapeDtypeStruct((requests, width), jnp.float32),
        in_specs=in_vmem(2),
        out_specs=pl.BlockSpec(memory_space=pltpu.VMEM),
        compiler_params=kernel_params(12),
        cost_estimate=pl.CostEstimate(
            flops=2 * requests * depth * width, bytes_accessed=2 * depth * width, transcendentals=0
        ),
        name="project_own",
    )(values[0], w_o)
    return pl.pallas_call(
        output_kernel,
        out_shape=jax.ShapeDtypeStruct((requests, width), jnp.bfloat16),
        in_specs=in_vmem(len(values) + 1),
        out_specs=pl.BlockSpec(memory_space=pltpu.VMEM),
        scratch_shapes=[pltpu.VMEM((requests, width), jnp.float32)],
        compiler_params=kernel_params(12),
        name="project_out",
    )(own, *values[1:], w_o)


def hidden_kernel(parts_ref, *refs):
    *slices, out_ref, added = refs
    per_rank = slices[0].shape[0]
    me = lax.axis_index("tp")
    for k, piece in enumerate(slices):
        added[me ^ k] = piece[...].astype(jnp.float32)
    width = out_ref.shape[1]
    for at in range(0, width, 128):
        at = slice(at, at + 128)
        total = parts_ref[0, :, at].astype(jnp.float32)
        for d in range(1, parts_ref.shape[0]):
            total = total + parts_ref[d, :, at].astype(jnp.float32)
        terms = [added[s, :, at] for s in range(len(slices))]
        out_ref[:, at] = (total + jnp.concatenate(terms, 0)).astype(out_ref.dtype)


def make_hidden(parts, slices):
    return pl.pallas_call(
        hidden_kernel,
        out_shape=jax.ShapeDtypeStruct(parts.shape[1:], jnp.bfloat16),
        in_specs=in_vmem(1 + len(slices)),
        out_specs=pl.BlockSpec(memory_space=pltpu.VMEM),
        scratch_shapes=[pltpu.VMEM((len(slices),) + slices[0].shape, jnp.float32)],
        compiler_params=kernel_params(12),
        name="hidden",
    )(parts, *slices)


def scale_kernel(hidden_ref, gain_ref, gate_ref, up_ref, scaled, gate_sum, up_sum, *refs):
    *outs, gains = refs
    ranks = lax.axis_size("tp")
    halves = scaled.shape[0]
    requests, width = hidden_ref.shape
    share = requests // ranks
    groups = width // 128
    me = lax.axis_index("tp")
    places = [[3, 1, 2, 0], [3, 2, 1, 0]] if halves == 2 else [list(range(ranks))]

    gains[...] = gain_ref[...].astype(jnp.float32)
    squares = [None] * ranks
    for k in range(ranks):
        block = me ^ k if halves == 2 else k
        start = block * share if halves == 1 else pl.multiple_of(block * share, 16)
        square = jnp.zeros((share, 128), jnp.float32)
        for g in range(groups):
            at = slice(g * 128, (g + 1) * 128)
            x = hidden_ref[pl.ds(start, share), at].astype(jnp.float32)
            square = square + x * x
            gain = gains[pl.ds(me * groups + g, 1), :]
            value = (x * gain).astype(scaled.dtype)
            for n, place in enumerate(places):
                scaled[n, place[k] * share : (place[k] + 1) * share, at] = value
        squares[places[0][k]] = square
    square = jnp.sum(jnp.concatenate(squares, 0), 1, keepdims=True)
    top = square.astype(jnp.bfloat16).astype(jnp.float32)
    middle = (square - top).astype(jnp.bfloat16).astype(jnp.float32)
    low = square - top - middle
    lane = lax.broadcasted_iota(jnp.int32, (requests, 128), 1)
    digits = jnp.where(lane == 0, top, jnp.where(lane == 1, middle, jnp.where(lane == 2, low, 0.0)))
    gates = [gate_sum, outs[0]] if halves == 2 else [gate_sum]
    ups = [up_sum, outs[1]] if halves == 2 else [up_sum]
    columns = up_sum.shape[1]
    for n, target in enumerate(gates):
        rows = target.shape[0]
        target[:, columns:] = digits[n * rows : (n + 1) * rows].astype(target.dtype)
    products(scaled, gate_ref, up_ref, 0, columns, gates, ups)


def products(scaled, gate_ref, up_ref, first, columns, gates, ups):
    for left, w_ref, targets in ((0, gate_ref, gates), (scaled.shape[0] - 1, up_ref, ups)):
        for at in range(0, columns, 256):
            upto = min(at + 256, columns)
            term = jnp.dot(
                scaled[left],
                w_ref[:, first + at : first + upto],
                preferred_element_type=jnp.float32,
            )
            for n, target in enumerate(targets):
                rows = target.shape[0]
                target[:, at:upto] = term[n * rows : (n + 1) * rows].astype(target.dtype)


def second_kernel(scaled, gate_ref, up_ref, *outs):
    columns = outs[1].shape[1]
    first = gate_ref.shape[1] - columns
    products(scaled, gate_ref, up_ref, first, columns, outs[0::2], outs[1::2])


def gate_up(hidden, gain, w_gate, w_up, halves):
    requests, width = hidden.shape
    units = w_gate.shape[1]
    first = units if halves == 1 else round_up(units * 5 // 8, 256)
    w_gate, w_up = fetched(w_gate), fetched(w_up)

    def shapes(columns, extra):
        return [
            jax.ShapeDtypeStruct((requests // halves, columns + more), jnp.bfloat16)
            for _ in range(halves)
            for more in (extra, 0)
        ]

    outs = [jax.ShapeDtypeStruct((halves, requests, width), jnp.bfloat16)] + shapes(first, 128)
    scaled, *parts = pl.pallas_call(
        scale_kernel,
        out_shape=outs,
        in_specs=in_vmem(4),
        out_specs=in_vmem(len(outs)),
        scratch_shapes=[pltpu.VMEM(gain.shape, jnp.float32)],
        compiler_params=kernel_params(12),
        cost_estimate=pl.CostEstimate(
            flops=4 * requests * width * first, bytes_accessed=4 * width * first, transcendentals=0
        ),
        name="gate_up",
    )(hidden, gain, w_gate, w_up)
    if halves == 1:
        return [parts]
    outs = shapes(units - first, 0)
    others = pl.pallas_call(
        second_kernel,
        out_shape=outs,
        in_specs=in_vmem(3),
        out_specs=in_vmem(len(outs)),
        compiler_params=kernel_params(12),
        cost_estimate=pl.CostEstimate(
            flops=4 * requests * width * (units - first),
            bytes_accessed=4 * width * (units - first),
            transcendentals=0,
        ),
        name="gate_up_rest",
    )(scaled, w_gate, w_up)
    return [parts, others]


def halve_kernel(*refs):
    count = len(refs) // 4
    for n in range(count):
        kept, came, send, keep = refs[n], refs[count + n], refs[2 * count + n], refs[3 * count + n]
        rows = send.shape[0]
        for at in range(0, send.shape[1], 128):
            at = slice(at, at + 128)
            total = kept[:, at].astype(jnp.float32) + came[:, at].astype(jnp.float32)
            send[:, at] = total[:rows].astype(send.dtype)
            keep[:, at] = total[rows:]


def halve(kept, came):
    half = [(k.shape[0] // 2, k.shape[1]) for k in kept]
    outs = pl.pallas_call(
        halve_kernel,
        out_shape=[jax.ShapeDtypeStruct(shape, jnp.bfloat16) for shape in half]
        + [jax.ShapeDtypeStruct(shape, jnp.float32) for shape in half],
        in_specs=in_vmem(2 * len(kept)),
        out_specs=in_vmem(2 * len(kept)),
        compiler_params=kernel_params(12),
        name="halve",
    )(*kept, *came)
    return outs[: len(kept)], outs[len(kept) :]


def inner_kernel(model, given, *refs):
    *parts, out_ref, factor_ref = refs
    gates, ups = parts[given::2], parts[given + 1 :: 2]
    columns = out_ref.shape[1]

    def total(parts, at):
        terms = [
            part[n, :, at].astype(jnp.float32) for part in parts for n in range(part.shape[0])
        ]
        return sum(terms[1:], terms[0])

    if given:
        factor = parts[0][...]
    else:
        square = jnp.sum(total(gates, slice(columns, columns + 128)), 1, keepdims=True)
        factor = jnp.broadcast_to(lax.rsqrt(square / model + 1e-06), factor_ref.shape)
    factor_ref[...] = factor
    for at in range(0, columns, 128):
        at = slice(at, at + 128)
        gate = total(gates, at) * factor
        up = total(ups, at) * factor
        out_ref[:, at] = (gate / (1.0 + jnp.exp(-gate)) * up).astype(out_ref.dtype)


def make_inner(parts, factor, model):
    given = [] if factor is None else [factor]
    rows, columns = parts[1].shape[1:]
    return pl.pallas_call(
        functools.partial(inner_kernel, model, len(given)),
        out_shape=[
            jax.ShapeDtypeStruct((rows, columns), jnp.bfloat16),
            jax.ShapeDtypeStruct((rows, 128), jnp.float32),
        ],
        in_specs=in_vmem(len(given) + len(parts)),
        out_specs=in_vmem(2),
        compiler_params=kernel_params(12),
        name="inner",
    )(*given, *parts)


def down_kernel(chunks, *refs):
    *pieces, w_ref, hidden_ref, out_ref, inner, total = refs
    width = w_ref.shape[1]
    count = len(pieces) // chunks
    share = total.shape[0] // count
    at = 0
    for c in range(chunks):
        columns = pieces[c * count].shape[1]
        for k in range(count):
            inner[k * share : (k + 1) * share, at : at + columns] = pieces[c * count + k][...]
        at += columns
    result = jnp.dot(inner[...], w_ref[...], preferred_element_type=jnp.float32)
    me = lax.axis_index("tp")
    for k in range(count):
        start = pl.multiple_of((me ^ k) * share, 16) if count > 1 else 0
        total[pl.ds(start, share), :] = result[k * share : (k + 1) * share]
    rows = hidden_ref.shape[0]
    own = pl.ds(pl.multiple_of(lax.axis_index("dp") * rows, 16), rows)
    total[own, :] += hidden_ref[...].astype(jnp.float32)
    per_rank = out_ref.shape[1]
    for d in range(out_ref.shape[0]):
        out_ref[d] = total[d * per_rank : (d + 1) * per_rank, :].astype(out_ref.dtype)


def project_down(chunks, w_down, hidden, ranks):
    units, width = w_down.shape
    pieces = [piece for chunk in chunks for piece in chunk]
    requests = sum(piece.shape[0] for piece in chunks[0])
    return pl.pallas_call(
        functools.partial(down_kernel, len(chunks)),
        out_shape=jax.ShapeDtypeStruct((ranks, requests // ranks, width), jnp.bfloat16),
        in_specs=in_vmem(len(pieces) + 2),
        out_specs=pl.BlockSpec(memory_space=pltpu.VMEM),
        scratch_shapes=[
            pltpu.VMEM((requests, units), jnp.bfloat16),
            pltpu.VMEM((requests, width), jnp.float32),
        ],
        compiler_params=kernel_params(12),
        name="project_down",
    )(*pieces, fetched(w_down), hidden)


def layer_kernel(parts_ref, out_ref):
    ranks = lax.axis_size("tp")
    width = parts_ref.shape[2]
    for t in range(ranks):
        terms = [parts_ref[d].astype(jnp.float32) for d in range(t, parts_ref.shape[0], ranks)]
        layer = sum(terms[1:], terms[0])
        out_ref[:, t * width : (t + 1) * width] = layer.astype(out_ref.dtype)


def make_layer(parts, per_rank, model):
    return pl.pallas_call(
        layer_kernel,
        out_shape=jax.ShapeDtypeStruct((per_rank, model), jnp.bfloat16),
        in_specs=in_vmem(1),
        out_specs=pl.BlockSpec(memory_space=pltpu.VMEM),
        compiler_params=kernel_params(12),
        name="layer",
    )(parts)


def round_up(value, step):
    return (value + step - 1) // step * step


def swap(parts, axes):
    return lax.all_to_all(parts, axes, split_axis=0, concat_axis=0, tiled=True)


def local(
    residual, queries, paged_latent_cache, lengths, w_uv, w_o, norm_gain, w_gate, w_up, w_down
):
    ranks_dp = lax.axis_size("dp")
    ranks_tp = lax.axis_size("tp")
    ranks = ranks_dp * ranks_tp
    per_rank, model = residual.shape
    requests = per_rank * ranks
    heads_here = w_uv.shape[0]
    units = w_gate.shape[1]
    width = w_o.shape[1]


    latent = swap(attend(lengths, queries, paged_latent_cache.T, ranks), ("dp", "tp"))

    values = head_values(latent.reshape(requests * heads_here, C), w_uv)
    values, residual = lax.optimization_barrier((values, residual))
    values = from_all(values, "tp")
    added = list(split_columns(residual, ranks_tp))
    added = added[:1] + [from_distance(added[k], "tp", k) for k in range(1, ranks_tp)]
    attn, added = lax.optimization_barrier((project_out(values, w_o), added))
    attn = swap(attn.reshape(ranks_dp, requests // ranks_dp, width), "dp")
    own_hidden = make_hidden(attn, added)
    hidden = lax.all_gather(own_hidden, "dp", axis=0, tiled=True)

    halves = 2 if ranks_tp == 4 else 1
    chunks = gate_up(hidden, norm_gain.reshape(-1, 128), w_gate, w_up, halves)
    if halves == 2:
        first, second = chunks
        kept, second = lax.optimization_barrier((first[2:], second))
        chunks = [[*first[:2], *kept], second]
    inner = []
    factor = None
    for chunk in chunks:
        if halves == 2:
            gate_send, up_send, gate_keep, up_keep = chunk
            came = [from_distance(gate_send, "tp", 1), from_distance(up_send, "tp", 2)]
            (gate_send, up_send), kept = halve([gate_keep, up_keep], came)
            came = [from_distance(gate_send, "tp", 2), from_distance(up_send, "tp", 1)]
            own, factor = make_inner([part[None] for part in (*kept, *came)], factor, model)
            far = from_distance(own, "tp", 2)
            inner.append([own, from_distance(own, "tp", 1), far, from_distance(far, "tp", 1)])
        else:
            parts = [swap(part.reshape(ranks_tp, -1, part.shape[1]), "tp") for part in chunk]
            own, factor = make_inner(parts, factor, model)
            inner.append([lax.all_gather(own, "tp", axis=0, tiled=True)])
    ffn = swap(project_down(inner, w_down, own_hidden, ranks), ("dp", "tp"))
    return make_layer(ffn, per_rank, model)


def solution(mesh):
    placed = (
        P(("dp", "tp"), None),
        P(("dp", "tp"), None),
        P(("dp", "tp"), None),
        P(),
        P(("dp", "tp"), None, None),
        P("dp", "tp"),
        P(),
        P("tp", "dp"),
        P("tp", "dp"),
        P("dp", "tp"),
    )
    return jax.shard_map(
        local, mesh=mesh, in_specs=placed, out_specs=P(("dp", "tp"), None), check_vma=False
    )
```

```python
import functools

import jax
import jax.numpy as jnp
from jax import lax
from jax.experimental import pallas as pl
from jax.experimental.pallas import tpu as pltpu
from jax.sharding import PartitionSpec as P

C = 512
BLOCK_TOKENS = 64
TILE = 512

score_scale = 192.0 ** (-0.5)
log2_e = 1.4426950408889634
negative = -1e30


def attention_kernel(
    lens_ref,
    raw_ref,
    cache_ref,
    out_ref,
    q_ref,
    pairs_of_heads,
    rows_of_heads,
    held,
    score0,
    score1,
    weight0,
    weight1,
    keep0,
    keep1,
    acc,
    done,
    best,
    mass,
    lo,
    hi,
    first,
    last,
    sems,
):
    nreq, heads, _ = q_ref.shape
    tile = held.shape[2]
    factor = score_scale * log2_e

    rank = lax.axis_index("dp") * lax.axis_size("tp") + lax.axis_index("tp")
    begin = jnp.int32(0)
    pairs = jnp.int32(0)
    for r in range(nreq):
        length = lens_ref[rank * nreq + r]
        lo[r] = begin
        hi[r] = begin + length
        first[r] = begin // tile
        last[r] = (begin + length - 1) // tile
        pairs = pairs + (last[r] - first[r] + 1)
        begin = begin + ((length + BLOCK_TOKENS - 1) // BLOCK_TOKENS) * BLOCK_TOKENS
    used = last[nreq - 1] + 1

    def copy(i):
        return pltpu.make_async_copy(
            cache_ref.at[:, pl.ds(pl.multiple_of(i * tile, tile), tile)], held.at[i], sems.at[i]
        )

    @pl.loop(0, used)
    def _(i):
        copy(i).start()

    width = q_ref.shape[2]
    half = heads // 2
    tail = width % 128
    full = width // 128
    for j in range(half):
        for c in range(pairs_of_heads.shape[0]):
            at = 2 * width * j + 128 * c
            pairs_of_heads[c, pl.ds(j, nreq, stride=half), :] = raw_ref[:, at : at + 128].astype(
                jnp.float32
            )
    for r in range(nreq):
        rows = slice(r * half, (r + 1) * half)
        for c in range(full + 1):
            rows_of_heads[c, pl.ds(0, half, stride=2), :] = pairs_of_heads[c, rows, :]
            ahead = min(full + c + 1, pairs_of_heads.shape[0] - 1)
            rows_of_heads[c, pl.ds(1, half, stride=2), :] = jnp.concatenate(
                [pairs_of_heads[full + c, rows, tail:], pairs_of_heads[ahead, rows, :tail]], 1
            )
        for c in range(full):
            q_ref[r, :, c * 128 : (c + 1) * 128] = rows_of_heads[c].astype(q_ref.dtype)
        q_ref[r, :, full * 128 :] = rows_of_heads[full, :, :tail].astype(q_ref.dtype)

    acc[...] = jnp.zeros_like(acc)
    best[...] = jnp.full_like(best, negative)
    mass[...] = jnp.zeros_like(mass)
    weight1[...] = jnp.zeros_like(weight1)
    keep1[...] = jnp.ones_like(keep1)

    def advance(p, r, i):
        live = p + 1 < pairs
        step = (i == last[r]) & live
        nr = jnp.where(step, r + 1, r)
        ni = jnp.where(step, first[nr], jnp.where(live, i + 1, i))
        return nr, ni, live

    def fetch(r, i, live):
        fresh = live & ((r == 0) | (i > last[jnp.maximum(r - 1, 0)]))

        @pl.when(fresh)
        def _():
            copy(i).wait()

    def scores(r, i, live, target):
        begin_at = jnp.where(live, lo[r], 0)
        end_at = jnp.where(live, hi[r], 0)
        s = jnp.dot(q_ref[r, :, :C], held[i, :C, :], preferred_element_type=jnp.float32)
        s = s + jnp.dot(q_ref[r, :, C:], held[i, C:, :], preferred_element_type=jnp.float32)
        token = i * tile + lax.broadcasted_iota(jnp.int32, (1, tile), 1)
        target[...] = s + jnp.where((token >= begin_at) & (token < end_at), 0.0, negative)

    def soften(r, source, weights, keeps):
        s = source[...]
        old = best[r]
        new = jnp.maximum(old, jnp.max(s, axis=1, keepdims=True))
        weight = jnp.exp2((s - new[:, :1]) * factor)
        keep = jnp.exp2((old - new) * factor)
        part = weight[:, :128]
        for at in range(128, tile, 128):
            part = part + weight[:, at : at + 128]
        mass[r] = mass[r] * keep + part
        best[r] = new
        weights[...] = weight.T.astype(weights.dtype)
        keeps[...] = keep.T[:8, :]

    def gather(r, i, weights, keeps):
        values = lax.dot_general(
            held[i, :C, :],
            weights[...],
            (((1,), (0,)), ((), ())),
            preferred_element_type=jnp.float32,
        )
        acc[r] = acc[r] * keeps[:1, :] + values

    zero = jnp.int32(0)
    fetch(zero, zero, pairs > 0)
    scores(zero, zero, pairs > 0, score0)

    def step(j, carry):
        r0, i0, r1, i1 = carry
        p = 2 * j
        r2, i2, live2 = advance(p, r1, i1)
        r3, i3, live3 = advance(p + 1, r2, i2)
        fetch(r2, i2, live2)
        fetch(r3, i3, live3)
        gather(r0, i0, weight1, keep1)
        scores(r2, i2, live2, score1)
        soften(r1, score0, weight0, keep0)
        gather(r1, i1, weight0, keep0)
        scores(r3, i3, live3, score0)
        soften(r2, score1, weight1, keep1)
        return r2, i2, r3, i3

    r0, i0, _, _ = lax.fori_loop(0, (pairs + 1) // 2, step, (zero, zero, zero, zero))
    gather(r0, i0, weight1, keep1)

    share = heads // out_ref.shape[0]
    for r in range(nreq):
        total = jnp.sum(mass[r], axis=1, keepdims=True)
        score0[:, :C] = acc[r].T / total
        for d in range(out_ref.shape[0]):
            done[d, r * share : (r + 1) * share, :] = score0[d * share : (d + 1) * share, :C]
    out_ref[...] = done[...].astype(out_ref.dtype)


def kernel_params(limit):
    return pltpu.CompilerParams(vmem_limit_bytes=limit * 1024 * 1024)


def in_vmem(count):
    return [pl.BlockSpec(memory_space=pltpu.VMEM)] * count


def fetched(weight):
    return pltpu.with_memory_space_constraint(weight, pltpu.VMEM)


def attend(lengths, queries, cache_t, ranks):
    nreq = queries.shape[0]
    width, tokens = cache_t.shape
    heads = queries.shape[1] // width
    tile = TILE
    tiles = tokens // tile
    return pl.pallas_call(
        attention_kernel,
        out_shape=jax.ShapeDtypeStruct((ranks, nreq * heads // ranks, C), jnp.bfloat16),
        in_specs=[pl.BlockSpec(memory_space=pltpu.SMEM)]
        + in_vmem(1)
        + [pl.BlockSpec(memory_space=pltpu.HBM)],
        out_specs=pl.BlockSpec(memory_space=pltpu.VMEM),
        scratch_shapes=[
            pltpu.VMEM((nreq, heads, width), jnp.bfloat16),
            pltpu.VMEM((2 * width // 128, nreq * heads // 2, 128), jnp.float32),
            pltpu.VMEM((width // 128 + 1, heads, 128), jnp.float32),
            pltpu.VMEM((tiles, width, tile), jnp.bfloat16),
            pltpu.VMEM((heads, tile), jnp.float32),
            pltpu.VMEM((heads, tile), jnp.float32),
            pltpu.VMEM((tile, heads), jnp.bfloat16),
            pltpu.VMEM((tile, heads), jnp.bfloat16),
            pltpu.VMEM((8, heads), jnp.float32),
            pltpu.VMEM((8, heads), jnp.float32),
            pltpu.VMEM((nreq, C, heads), jnp.float32),
            pltpu.VMEM((ranks, nreq * heads // ranks, C), jnp.float32),
            pltpu.VMEM((nreq, heads, 128), jnp.float32),
            pltpu.VMEM((nreq, heads, 128), jnp.float32),
            pltpu.SMEM((nreq,), jnp.int32),
            pltpu.SMEM((nreq,), jnp.int32),
            pltpu.SMEM((nreq,), jnp.int32),
            pltpu.SMEM((nreq,), jnp.int32),
            pltpu.SemaphoreType.DMA((tiles,)),
        ],
        compiler_params=kernel_params(28),
        cost_estimate=pl.CostEstimate(
            flops=2 * heads * tokens * (width + C),
            bytes_accessed=2 * tokens * width,
            transcendentals=heads * tokens,
        ),
        name="attention",
    )(
        pltpu.with_memory_space_constraint(lengths, pltpu.HBM),
        pltpu.with_memory_space_constraint(queries, pltpu.HBM),
        pltpu.with_memory_space_constraint(cache_t, pltpu.HBM),
    )


def head_values_kernel(latent_ref, w_ref, out_ref, values):
    heads, _, wide = w_ref.shape
    requests = out_ref.shape[0]
    latent = latent_ref[...]
    for h in range(heads):
        values[...] = jnp.dot(latent, w_ref[h], preferred_element_type=jnp.float32)
        picked = values[pl.ds(h, requests, stride=heads), :]
        out_ref[:, h * wide : (h + 1) * wide] = picked.astype(out_ref.dtype)


def head_values(latent, w_uv):
    heads, _, wide = w_uv.shape
    requests = latent.shape[0] // heads
    return pl.pallas_call(
        head_values_kernel,
        out_shape=jax.ShapeDtypeStruct((requests, heads * wide), jnp.bfloat16),
        in_specs=in_vmem(2),
        out_specs=pl.BlockSpec(memory_space=pltpu.VMEM),
        scratch_shapes=[pltpu.VMEM((latent.shape[0], wide), jnp.float32)],
        compiler_params=kernel_params(12),
        name="head_values",
    )(latent, w_uv)


def split_kernel(rows_ref, *out_refs):
    width = out_refs[0].shape[1]
    me = lax.axis_index("tp")
    for k, out_ref in enumerate(out_refs):
        start = pl.multiple_of((me ^ k) * width, 128)
        out_ref[...] = rows_ref[:, pl.ds(start, width)]


def split_columns(rows, ranks):
    shape = jax.ShapeDtypeStruct((rows.shape[0], rows.shape[1] // ranks), rows.dtype)
    return pl.pallas_call(
        split_kernel,
        out_shape=[shape] * ranks,
        in_specs=in_vmem(1),
        out_specs=in_vmem(ranks),
        compiler_params=kernel_params(8),
        name="split_columns",
    )(rows)


def from_distance(piece, axis, distance):
    return lax.ppermute(piece, axis, [(k, k ^ distance) for k in range(lax.axis_size(axis))])


def from_all(piece, axis):
    return [piece] + [from_distance(piece, axis, k) for k in range(1, lax.axis_size(axis))]


def own_output_kernel(value_ref, w_ref, out_ref):
    depth = value_ref.shape[1]
    rows = pl.ds(pl.multiple_of(lax.axis_index("tp") * depth, 128), depth)
    out_ref[...] = jnp.dot(value_ref[...], w_ref[rows, :], preferred_element_type=jnp.float32)


def output_kernel(*refs):
    own_ref, *values, w_ref, out_ref, total = refs
    depth = values[0].shape[1]
    me = lax.axis_index("tp")
    for k, value in enumerate(values, 1):
        rows = pl.ds(pl.multiple_of((me ^ k) * depth, 128), depth)
        term = jnp.dot(value[...], w_ref[rows, :], preferred_element_type=jnp.float32)
        if k == 1:
            total[...] = own_ref[...] + term
        else:
            total[...] += term
    out_ref[...] = total[...].astype(out_ref.dtype)


def project_out(values, w_o):
    requests, depth = values[0].shape
    width = w_o.shape[1]
    w_o = fetched(w_o)
    own = pl.pallas_call(
        own_output_kernel,
        out_shape=jax.ShapeDtypeStruct((requests, width), jnp.float32),
        in_specs=in_vmem(2),
        out_specs=pl.BlockSpec(memory_space=pltpu.VMEM),
        compiler_params=kernel_params(12),
        cost_estimate=pl.CostEstimate(
            flops=2 * requests * depth * width, bytes_accessed=2 * depth * width, transcendentals=0
        ),
        name="project_own",
    )(values[0], w_o)
    return pl.pallas_call(
        output_kernel,
        out_shape=jax.ShapeDtypeStruct((requests, width), jnp.bfloat16),
        in_specs=in_vmem(len(values) + 1),
        out_specs=pl.BlockSpec(memory_space=pltpu.VMEM),
        scratch_shapes=[pltpu.VMEM((requests, width), jnp.float32)],
        compiler_params=kernel_params(12),
        name="project_out",
    )(own, *values[1:], w_o)


def hidden_kernel(parts_ref, *refs):
    *slices, out_ref, added = refs
    per_rank = slices[0].shape[0]
    me = lax.axis_index("tp")
    for k, piece in enumerate(slices):
        added[me ^ k] = piece[...].astype(jnp.float32)
    width = out_ref.shape[1]
    for at in range(0, width, 128):
        at = slice(at, at + 128)
        total = parts_ref[0, :, at].astype(jnp.float32)
        for d in range(1, parts_ref.shape[0]):
            total = total + parts_ref[d, :, at].astype(jnp.float32)
        terms = [added[s, :, at] for s in range(len(slices))]
        out_ref[:, at] = (total + jnp.concatenate(terms, 0)).astype(out_ref.dtype)


def make_hidden(parts, slices):
    return pl.pallas_call(
        hidden_kernel,
        out_shape=jax.ShapeDtypeStruct(parts.shape[1:], jnp.bfloat16),
        in_specs=in_vmem(1 + len(slices)),
        out_specs=pl.BlockSpec(memory_space=pltpu.VMEM),
        scratch_shapes=[pltpu.VMEM((len(slices),) + slices[0].shape, jnp.float32)],
        compiler_params=kernel_params(12),
        name="hidden",
    )(parts, *slices)


def scale_kernel(hidden_ref, gain_ref, gate_ref, up_ref, scaled, gate_sum, up_sum, *refs):
    *outs, gains = refs
    ranks = lax.axis_size("tp")
    halves = scaled.shape[0]
    requests, width = hidden_ref.shape
    share = requests // ranks
    groups = width // 128
    me = lax.axis_index("tp")
    places = [[3, 1, 2, 0], [3, 2, 1, 0]] if halves == 2 else [list(range(ranks))]

    gains[...] = gain_ref[...].astype(jnp.float32)
    squares = [None] * ranks
    for k in range(ranks):
        block = me ^ k if halves == 2 else k
        start = block * share if halves == 1 else pl.multiple_of(block * share, 16)
        square = jnp.zeros((share, 128), jnp.float32)
        for g in range(groups):
            at = slice(g * 128, (g + 1) * 128)
            x = hidden_ref[pl.ds(start, share), at].astype(jnp.float32)
            square = square + x * x
            gain = gains[pl.ds(me * groups + g, 1), :]
            value = (x * gain).astype(scaled.dtype)
            for n, place in enumerate(places):
                scaled[n, place[k] * share : (place[k] + 1) * share, at] = value
        squares[places[0][k]] = square
    square = jnp.sum(jnp.concatenate(squares, 0), 1, keepdims=True)
    top = square.astype(jnp.bfloat16).astype(jnp.float32)
    middle = (square - top).astype(jnp.bfloat16).astype(jnp.float32)
    low = square - top - middle
    lane = lax.broadcasted_iota(jnp.int32, (requests, 128), 1)
    digits = jnp.where(lane == 0, top, jnp.where(lane == 1, middle, jnp.where(lane == 2, low, 0.0)))
    gates = [gate_sum, outs[0]] if halves == 2 else [gate_sum]
    ups = [up_sum, outs[1]] if halves == 2 else [up_sum]
    columns = up_sum.shape[1]
    for n, target in enumerate(gates):
        rows = target.shape[0]
        target[:, columns:] = digits[n * rows : (n + 1) * rows].astype(target.dtype)
    products(scaled, gate_ref, up_ref, 0, columns, gates, ups)


def products(scaled, gate_ref, up_ref, first, columns, gates, ups):
    for left, w_ref, targets in ((0, gate_ref, gates), (scaled.shape[0] - 1, up_ref, ups)):
        for at in range(0, columns, 256):
            upto = min(at + 256, columns)
            term = jnp.dot(
                scaled[left],
                w_ref[:, first + at : first + upto],
                preferred_element_type=jnp.float32,
            )
            for n, target in enumerate(targets):
                rows = target.shape[0]
                target[:, at:upto] = term[n * rows : (n + 1) * rows].astype(target.dtype)


def second_kernel(scaled, gate_ref, up_ref, *outs):
    columns = outs[1].shape[1]
    first = gate_ref.shape[1] - columns
    products(scaled, gate_ref, up_ref, first, columns, outs[0::2], outs[1::2])


def gate_up(hidden, gain, w_gate, w_up, halves):
    requests, width = hidden.shape
    units = w_gate.shape[1]
    first = units if halves == 1 else round_up(units // 2, 256)
    w_gate, w_up = fetched(w_gate), fetched(w_up)

    def shapes(columns, extra):
        return [
            jax.ShapeDtypeStruct((requests // halves, columns + more), jnp.bfloat16)
            for _ in range(halves)
            for more in (extra, 0)
        ]

    outs = [jax.ShapeDtypeStruct((halves, requests, width), jnp.bfloat16)] + shapes(first, 128)
    scaled, *parts = pl.pallas_call(
        scale_kernel,
        out_shape=outs,
        in_specs=in_vmem(4),
        out_specs=in_vmem(len(outs)),
        scratch_shapes=[pltpu.VMEM(gain.shape, jnp.float32)],
        compiler_params=kernel_params(12),
        cost_estimate=pl.CostEstimate(
            flops=4 * requests * width * first, bytes_accessed=4 * width * first, transcendentals=0
        ),
        name="gate_up",
    )(hidden, gain, w_gate, w_up)
    if halves == 1:
        return [parts]
    outs = shapes(units - first, 0)
    others = pl.pallas_call(
        second_kernel,
        out_shape=outs,
        in_specs=in_vmem(3),
        out_specs=in_vmem(len(outs)),
        compiler_params=kernel_params(12),
        cost_estimate=pl.CostEstimate(
            flops=4 * requests * width * (units - first),
            bytes_accessed=4 * width * (units - first),
            transcendentals=0,
        ),
        name="gate_up_rest",
    )(scaled, w_gate, w_up)
    return [parts, others]


def halve_kernel(*refs):
    count = len(refs) // 4
    for n in range(count):
        kept, came, send, keep = refs[n], refs[count + n], refs[2 * count + n], refs[3 * count + n]
        rows = send.shape[0]
        for at in range(0, send.shape[1], 128):
            at = slice(at, at + 128)
            total = kept[:, at].astype(jnp.float32) + came[:, at].astype(jnp.float32)
            send[:, at] = total[:rows].astype(send.dtype)
            keep[:, at] = total[rows:]


def halve(kept, came):
    half = [(k.shape[0] // 2, k.shape[1]) for k in kept]
    outs = pl.pallas_call(
        halve_kernel,
        out_shape=[jax.ShapeDtypeStruct(shape, jnp.bfloat16) for shape in half]
        + [jax.ShapeDtypeStruct(shape, jnp.float32) for shape in half],
        in_specs=in_vmem(2 * len(kept)),
        out_specs=in_vmem(2 * len(kept)),
        compiler_params=kernel_params(12),
        name="halve",
    )(*kept, *came)
    return outs[: len(kept)], outs[len(kept) :]


def inner_kernel(model, given, *refs):
    *parts, out_ref = refs if given else refs[:-1]
    gates, ups = parts[given::2], parts[given + 1 :: 2]
    columns = out_ref.shape[1]

    def total(parts, at):
        terms = [
            part[n, :, at].astype(jnp.float32) for part in parts for n in range(part.shape[0])
        ]
        return sum(terms[1:], terms[0])

    if given:
        factor = parts[0][...]
    else:
        square = jnp.sum(total(gates, slice(columns, columns + 128)), 1, keepdims=True)
        factor = jnp.broadcast_to(lax.rsqrt(square / model + 1e-06), refs[-1].shape)
        refs[-1][...] = factor
    for at in range(0, columns, 128):
        at = slice(at, at + 128)
        gate = total(gates, at) * factor
        up = total(ups, at) * factor
        out_ref[:, at] = (gate / (1.0 + jnp.exp(-gate)) * up).astype(out_ref.dtype)


def make_inner(parts, factor, model):
    given = [] if factor is None else [factor]
    rows, columns = parts[1].shape[1:]
    shapes = [
        jax.ShapeDtypeStruct((rows, columns), jnp.bfloat16),
        jax.ShapeDtypeStruct((rows, 128), jnp.float32),
    ][: 2 - len(given)]
    outs = pl.pallas_call(
        functools.partial(inner_kernel, model, len(given)),
        out_shape=shapes,
        in_specs=in_vmem(len(given) + len(parts)),
        out_specs=in_vmem(len(shapes)),
        compiler_params=kernel_params(12),
        name="inner",
    )(*given, *parts)
    return [*outs, *given]


def down_kernel(chunks, *refs):
    *pieces, w_ref, hidden_ref, out_ref, inner, total = refs
    width = w_ref.shape[1]
    count = len(pieces) // chunks
    share = total.shape[0] // count
    at = 0
    for c in range(chunks):
        columns = pieces[c * count].shape[1]
        for k in range(count):
            inner[k * share : (k + 1) * share, at : at + columns] = pieces[c * count + k][...]
        at += columns
    result = jnp.dot(inner[...], w_ref[...], preferred_element_type=jnp.float32)
    me = lax.axis_index("tp")
    for k in range(count):
        start = pl.multiple_of((me ^ k) * share, 16) if count > 1 else 0
        total[pl.ds(start, share), :] = result[k * share : (k + 1) * share]
    rows = hidden_ref.shape[0]
    own = pl.ds(pl.multiple_of(lax.axis_index("dp") * rows, 16), rows)
    total[own, :] += hidden_ref[...].astype(jnp.float32)
    per_rank = out_ref.shape[1]
    for d in range(out_ref.shape[0]):
        out_ref[d] = total[d * per_rank : (d + 1) * per_rank, :].astype(out_ref.dtype)


def project_down(chunks, w_down, hidden, ranks):
    units, width = w_down.shape
    pieces = [piece for chunk in chunks for piece in chunk]
    requests = sum(piece.shape[0] for piece in chunks[0])
    return pl.pallas_call(
        functools.partial(down_kernel, len(chunks)),
        out_shape=jax.ShapeDtypeStruct((ranks, requests // ranks, width), jnp.bfloat16),
        in_specs=in_vmem(len(pieces) + 2),
        out_specs=pl.BlockSpec(memory_space=pltpu.VMEM),
        scratch_shapes=[
            pltpu.VMEM((requests, units), jnp.bfloat16),
            pltpu.VMEM((requests, width), jnp.float32),
        ],
        compiler_params=kernel_params(12),
        name="project_down",
    )(*pieces, fetched(w_down), hidden)


def layer_kernel(parts_ref, out_ref):
    ranks = lax.axis_size("tp")
    width = parts_ref.shape[2]
    for t in range(ranks):
        terms = [parts_ref[d].astype(jnp.float32) for d in range(t, parts_ref.shape[0], ranks)]
        layer = sum(terms[1:], terms[0])
        out_ref[:, t * width : (t + 1) * width] = layer.astype(out_ref.dtype)


def make_layer(parts, per_rank, model):
    return pl.pallas_call(
        layer_kernel,
        out_shape=jax.ShapeDtypeStruct((per_rank, model), jnp.bfloat16),
        in_specs=in_vmem(1),
        out_specs=pl.BlockSpec(memory_space=pltpu.VMEM),
        compiler_params=kernel_params(12),
        name="layer",
    )(parts)


def round_up(value, step):
    return (value + step - 1) // step * step


def swap(parts, axes):
    return lax.all_to_all(parts, axes, split_axis=0, concat_axis=0, tiled=True)


def local(
    residual, queries, paged_latent_cache, lengths, w_uv, w_o, norm_gain, w_gate, w_up, w_down
):
    ranks_dp = lax.axis_size("dp")
    ranks_tp = lax.axis_size("tp")
    ranks = ranks_dp * ranks_tp
    per_rank, model = residual.shape
    requests = per_rank * ranks
    heads_here = w_uv.shape[0]
    units = w_gate.shape[1]
    width = w_o.shape[1]


    latent = swap(attend(lengths, queries, paged_latent_cache.T, ranks), ("dp", "tp"))

    values = head_values(latent.reshape(requests * heads_here, C), w_uv)
    values, residual = lax.optimization_barrier((values, residual))
    values = from_all(values, "tp")
    added = list(split_columns(residual, ranks_tp))
    added = added[:1] + [from_distance(added[k], "tp", k) for k in range(1, ranks_tp)]
    attn, added = lax.optimization_barrier((project_out(values, w_o), added))
    attn = swap(attn.reshape(ranks_dp, requests // ranks_dp, width), "dp")
    own_hidden = make_hidden(attn, added)
    hidden = lax.all_gather(own_hidden, "dp", axis=0, tiled=True)

    halves = 2 if ranks_tp == 4 else 1
    chunks = gate_up(hidden, norm_gain.reshape(-1, 128), w_gate, w_up, halves)
    if halves == 2:
        first, second = chunks
        kept, second = lax.optimization_barrier((first[2:], second))
        chunks = [[*first[:2], *kept], second]
    inner = []
    factor = None
    for chunk in chunks:
        if halves == 2:
            gate_send, up_send, gate_keep, up_keep = chunk
            came = [from_distance(gate_send, "tp", 1), from_distance(up_send, "tp", 2)]
            (gate_send, up_send), kept = halve([gate_keep, up_keep], came)
            came = [from_distance(gate_send, "tp", 2), from_distance(up_send, "tp", 1)]
            own, factor = make_inner([part[None] for part in (*kept, *came)], factor, model)
            far = from_distance(own, "tp", 2)
            inner.append([own, from_distance(own, "tp", 1), far, from_distance(far, "tp", 1)])
        else:
            parts = [swap(part.reshape(ranks_tp, -1, part.shape[1]), "tp") for part in chunk]
            own, factor = make_inner(parts, factor, model)
            inner.append([lax.all_gather(own, "tp", axis=0, tiled=True)])
    ffn = swap(project_down(inner, w_down, own_hidden, ranks), ("dp", "tp"))
    return make_layer(ffn, per_rank, model)


def solution(mesh):
    placed = (
        P(("dp", "tp"), None),
        P(("dp", "tp"), None),
        P(("dp", "tp"), None),
        P(),
        P(("dp", "tp"), None, None),
        P("dp", "tp"),
        P(),
        P("tp", "dp"),
        P("tp", "dp"),
        P("dp", "tp"),
    )
    return jax.shard_map(
        local, mesh=mesh, in_specs=placed, out_specs=P(("dp", "tp"), None), check_vma=False
    )
```
